32 devices in a mesh: seq: 8 (over y, x, core), shard: 4 (over z).
Axes of the slice: x: 2, y: 2, z: 4, core: 2. Of those that a mesh axis runs over, the one named last changes fastest.
Arguments:
- tokens: bfloat16 [4, 1536, 1536], P('shard', 'seq'), may hold values from -6 to 6
- out_grad: bfloat16 [4, 1536, 1536], P('shard', 'seq'), may hold values from -6 to 6
- deal_order: int32 [4, 1536], P('shard'), may hold values from 0 to 1535, each once within a row
- lengths: int32 [4, 4], P('shard'), may hold values from 1 to 1024, 1536 in all within a row
- routes: int32 [4, 1536, 6], P('shard', 'seq'), may hold values from 0 to 63, all different within a row; in each aligned block of 192 rows (0 to 191, 192 to 383, ..., all dimensions but the last counted through in order) at most 30 rows name the same one
- norm_in: bfloat16 [1536], P('shard'), may hold values from 0.5 to 1.5
- w_in: bfloat16 [1536, 6400], P('shard'), may hold values from -0.15625 to 0.15625
- w_dt: bfloat16 [1536, 48], P('shard'), may hold values from -0.15625 to 0.15625
- conv_w: bfloat16 [3328, 4], P('shard'), may hold values from -0.5 to 0.5
- conv_b: bfloat16 [3328], P('shard'), may hold values from -0.5 to 0.5
- dt_bias: bfloat16 [48], P('shard'), may hold values from -6.5 to -2.5
- a_log: bfloat16 [48], P('shard'), may hold values from 0 to 2.765625
- d_skip: bfloat16 [48], P('shard'), may hold values from 0.5 to 1.5
- norm_gate: bfloat16 [3072], P('shard'), may hold values from 0.5 to 1.5
- w_out: bfloat16 [3072, 1536], P('shard'), may hold values from -0.109375 to 0.109375
- norm_moe: bfloat16 [1536], P('shard'), may hold values from 0.5 to 1.5
- w_router: bfloat16 [1536, 64], P('shard'), may hold values from -0.078125 to 0.078125
- w_shared: bfloat16 [1536, 2048], P('shard'), may hold values from -0.15625 to 0.15625
- w_shared_down: bfloat16 [1024, 1536], P('shard'), may hold values from -0.375 to 0.375
- w_experts: bfloat16 [64, 1536, 1024], P('seq', 'shard'), may hold values from -0.15625 to 0.15625
- w_experts_down: bfloat16 [64, 512, 1536], P('seq', 'shard'), may hold values from -1 to 1
Outputs:
- layer_out: bfloat16 [4, 1536, 1536], P('shard', 'seq')
- tokens_grad: bfloat16 [4, 1536, 1536], P('shard', 'seq')
- norm_in_grad: float32 [1536], P('shard')
- w_in_grad: float32 [1536, 6400], P('shard')
- w_dt_grad: float32 [1536, 48], P('shard')
- conv_w_grad: float32 [3328, 4], P('shard')
- conv_b_grad: float32 [3328], P('shard')
- dt_bias_grad: float32 [48], P('shard')
- a_log_grad: float32 [48], P('shard')
- d_skip_grad: float32 [48], P('shard')
- norm_gate_grad: float32 [3072], P('shard')
- w_out_grad: float32 [3072, 1536], P('shard')
- norm_moe_grad: float32 [1536], P('shard')
- w_router_grad: float32 [1536, 64], P('shard')
- w_shared_grad: float32 [1536, 2048], P('shard')
- w_shared_down_grad: float32 [1024, 1536], P('shard')
- w_experts_grad: float32 [64, 1536, 1024], P('seq', 'shard')
- w_experts_down_grad: float32 [64, 512, 1536], P('seq', 'shard')
The draws below stay inside these ranges and needn't reach their ends.
Inputs may be any that keep to these rules, and one draw needn't show every extreme that they name: Each group's row holds every token number of the group once: dealt position i holds the group's token deal_order[i] in sequence order. A group's 4 lengths sum to 1536; its longest is exactly 1024. `routes`: A token names 6 different experts; among the tokens of one device no expert is named more than 30 times, a bound that some block reaches.
All inputs are finite; a program needn't handle non-finite values.
Results may differ from the reference program's by a relative error of at most 0.02.
Values may be sent and summed in bfloat16 or wider, within the bound.
A program may use at most 320 MiB of HBM per device.

```python
import math
import jax
import jax.numpy as jnp
import numpy as np
from jax import lax

D = 1536
HEADS = 48
HEAD_DIM = 64
STATE = 128
CONV = 4
F = 512
FS = 1024
TOP = 6
TOK_DEV = 192
NSEQ = 4
STRETCH = 256
DI = 3072
XBC = 3328
EXPERTS = 64
GROUPS = 4
GROUP_TOK = 1536
HEADS_DEV = 6
CAP = 30
LONGEST = 1024
N_SEQ = 8


def steps_of(key, extent, shards, low, high):
    def one(axis_at, shards_of):
        draws = jax.random.uniform(jax.random.fold_in(jax.random.fold_in(key, 6), axis_at), (shards_of,), jnp.float32, low / len(shards), high / len(shards))
        return jnp.repeat(jnp.exp(draws), extent[axis_at] // shards_of).reshape((-1,) + (1,) * (len(extent) - axis_at - 1))

    factor_of = one(*shards[0])
    for cut in shards[1:]:
        factor_of = factor_of * one(*cut)
    return factor_of


def length_profile(number_of, total, bound, lean):
    loads = [(1 << 20) // math.isqrt(standing ** lean) + 1 for standing in range(2, number_of + 1)]
    surplus, holding = total - bound - (number_of - 1), [1] * (number_of - 1)
    while surplus > 0:
        free = [i for i in range(number_of - 1) if holding[i] < bound]
        pool, budget = sum([loads[i] for i in free]), surplus
        for i in free:
            extra = min(bound - holding[i], max(1, budget * loads[i] // pool), surplus)
            holding[i] = holding[i] + extra
            surplus = surplus - extra
    return np.array([bound] + holding)


def uneven(own_key, number_of, total, bound, skew):
    if number_of == 2:
        one = jax.random.randint(own_key, (), max(1, total - bound), min(bound, total - 1) + 1)
        return jnp.stack([one, total - one])
    tallies = jnp.asarray(length_profile(number_of, total, bound, skew), jnp.int32)
    couples = (number_of - 1) // 2
    source_of, receiver = tallies[1:1 + 2 * couples:2], tallies[2:2 + 2 * couples:2]
    margin = jnp.minimum(source_of - 1, bound - receiver)
    moved = jax.random.randint(jax.random.fold_in(own_key, 1), (couples,), 0, 1 << 20) % (margin + 1)
    tallies = tallies.at[1:1 + 2 * couples:2].set(source_of - moved).at[2:2 + 2 * couples:2].set(receiver + moved)
    return tallies[jax.random.permutation(jax.random.fold_in(own_key, 2), number_of)]


def shared_out(stream_key, own, number, rows, count, top, limit, skew):
    order = jax.random.permutation(stream_key, count)
    packed, ordinary = portions_of(count, rows * top, limit, skew, True), portions_of(count, rows * top, limit, skew, False)
    places = jnp.arange(count)

    def named(sizes, offset_by):
        used = int((sizes > 0).sum())
        fixed = max(1, used // 4)
        moved = fixed + (places - fixed + offset_by * (used - fixed)) % max(1, count - fixed)
        return jnp.zeros((count,), jnp.int32).at[order[jnp.where(places < fixed, places, moved)]].set(jnp.asarray(sizes, jnp.int32))

    sizes = jnp.where(number % 4 == 0, named(packed, number // 4), named(ordinary, number - number // 4 - 1))
    mixed = jax.random.permutation(jax.random.fold_in(own, 3), count)
    donor, receiver = mixed[0:count // 2 * 2:2], mixed[1:count // 2 * 2:2]
    margin = jnp.minimum(sizes[donor] - 1, limit - sizes[receiver]) // 2
    margin = jnp.where((donor == order[0]) | (receiver == order[0]) | (sizes[receiver] == 0), 0, jnp.maximum(margin, 0))
    moved = jax.random.randint(jax.random.fold_in(own, 4), (count // 2,), 0, 1 << 20) % (margin + 1)
    sizes = sizes.at[donor].add(-moved).at[receiver].add(moved)
    labels = jnp.searchsorted(jnp.cumsum(sizes), jnp.arange(rows * top), side="right").astype(jnp.int32)
    table = labels.reshape(top, rows).T
    table = table[jax.random.permutation(jax.random.fold_in(own, 1), rows)]
    offset_by = jax.random.randint(jax.random.fold_in(own, 2), (rows, 1), 0, top)
    return jnp.take_along_axis(table, (jnp.arange(top)[None, :] + offset_by) % top, axis=1)


def portions_of(amount, total, limit, skew, full):
    loads = [(1 << 20) // math.isqrt(rank ** skew) + 1 for rank in range(1, amount + 1)]
    largest = limit if full else min(limit, max(-(-total // amount), total * loads[0] // sum(loads)))
    least = 1 if total - largest >= amount - 1 else 0
    holding, spare = [largest] + [least] * (amount - 1), total - largest - least * (amount - 1)
    while spare > 0:
        free = [i for i in range(1, amount) if holding[i] < largest] or [i for i in range(1, amount) if holding[i] < limit]
        pool, left = sum([loads[i] for i in free]), spare
        for i in free:
            more = min(limit - holding[i], max(1, left * loads[i] // pool), spare)
            holding[i] = holding[i] + more
            spare = spare - more
    return np.array(holding)


def noise(rng, dims, deviation, reach, split=(), kind=jnp.bfloat16):
    drawn = deviation * jax.random.normal(rng, dims, jnp.float32)
    if split:
        drawn = drawn * steps_of(rng, dims, split, -0.22, 0.18)
    return jnp.clip(drawn, -reach, reach).astype(kind)


def setup_inputs(seed: int = 0) -> dict:
    key_of = jax.random.split(jax.random.key(seed), 22)
    tokens = noise(key_of[0], (GROUPS, GROUP_TOK, D), 1.0, 6.0, ((0, 4), (1, 8)))
    out_grad = noise(key_of[1], (GROUPS, GROUP_TOK, D), 1.0, 6.0, ((0, 4), (1, 8)))
    deal_order = jax.vmap(lambda own: jax.random.permutation(own, GROUP_TOK))(jax.random.split(key_of[2], GROUPS)).reshape((GROUPS, GROUP_TOK)).astype(jnp.int32)
    lengths = jax.vmap(lambda own: uneven(own, NSEQ, GROUP_TOK, LONGEST, 2))(jax.random.split(key_of[3], GROUPS)).reshape((GROUPS, NSEQ)).astype(jnp.int32)
    routes_keys = jax.random.split(jax.random.fold_in(key_of[4], 1), GROUPS * GROUP_TOK // TOK_DEV)
    routes_turns = jax.random.permutation(jax.random.fold_in(key_of[4], 3), GROUPS * GROUP_TOK // TOK_DEV)
    routes = jax.vmap(lambda own, number: shared_out(jax.random.fold_in(key_of[4], 2), own, number, TOK_DEV, EXPERTS, TOP, CAP, 2))(routes_keys, routes_turns).reshape((GROUPS, GROUP_TOK, TOP))
    norm_in = jnp.clip(1.0 + 0.1 * jax.random.normal(key_of[5], (D,), jnp.float32), 0.5, 1.5).astype(jnp.bfloat16)
    w_in = noise(key_of[6], (D, 2 * DI + 2 * STATE), D ** -0.5, 0.15625, ((0, 4),))
    w_dt = noise(key_of[7], (D, HEADS), D ** -0.5, 0.15625, ((0, 4),))
    conv_w = jnp.clip(jax.random.uniform(key_of[8], (XBC, CONV), jnp.float32, -0.5, 0.5) * steps_of(key_of[8], (XBC, CONV), ((0, 4),), -0.4, 0.0), -0.5, 0.5).astype(jnp.bfloat16)
    conv_b = jnp.clip(jax.random.uniform(key_of[9], (XBC,), jnp.float32, -0.5, 0.5) * steps_of(key_of[9], (XBC,), ((0, 4),), -0.4, 0.0), -0.5, 0.5).astype(jnp.bfloat16)
    dt_bias = jnp.clip(-6.5 + 4.0 * jax.random.uniform(key_of[10], (HEADS,), jnp.float32) ** steps_of(key_of[10], (HEADS,), ((0, 4),), -0.2, 0.2), -6.5, -2.5).astype(jnp.bfloat16)
    a_log = jnp.clip(2.765625 * jax.random.uniform(key_of[11], (HEADS,), jnp.float32) ** steps_of(key_of[11], (HEADS,), ((0, 4),), -0.2, 0.2), 0.0, 2.765625).astype(jnp.bfloat16)
    d_skip = jnp.clip(0.5 + 1.0 * jax.random.uniform(key_of[12], (HEADS,), jnp.float32) ** steps_of(key_of[12], (HEADS,), ((0, 4),), -0.2, 0.2), 0.5, 1.5).astype(jnp.bfloat16)
    norm_gate = jnp.clip(1.0 + 0.1 * jax.random.normal(key_of[13], (DI,), jnp.float32), 0.5, 1.5).astype(jnp.bfloat16)
    w_out = noise(key_of[14], (DI, D), DI ** -0.5, 0.109375, ((0, 4),))
    norm_moe = jnp.clip(1.0 + 0.1 * jax.random.normal(key_of[15], (D,), jnp.float32), 0.5, 1.5).astype(jnp.bfloat16)
    w_router = noise(key_of[16], (D, EXPERTS), (4 * D) ** -0.5, 0.078125, ((0, 4),))
    w_shared = noise(key_of[17], (D, 2 * FS), D ** -0.5, 0.15625, ((0, 4),))
    w_shared_down = noise(key_of[18], (FS, D), (FS // 4) ** -0.5, 0.375, ((0, 4),))
    w_experts = noise(key_of[19], (EXPERTS, D, 2 * F), D ** -0.5, 0.15625, ((0, 8), (1, 4)))
    w_experts_down = noise(key_of[20], (EXPERTS, F, D), (F // 16) ** -0.5, 1.0, ((0, 8), (1, 4)))
    return {"tokens": tokens, "out_grad": out_grad, "deal_order": deal_order, "lengths": lengths, "routes": routes, "norm_in": norm_in, "w_in": w_in, "w_dt": w_dt, "conv_w": conv_w, "conv_b": conv_b, "dt_bias": dt_bias, "a_log": a_log, "d_skip": d_skip, "norm_gate": norm_gate, "w_out": w_out, "norm_moe": norm_moe, "w_router": w_router, "w_shared": w_shared, "w_shared_down": w_shared_down, "w_experts": w_experts, "w_experts_down": w_experts_down}


EPSILON = 1e-05
HIGHEST = lax.Precision.HIGHEST

@jax.custom_vjp
def low(v):
    return lax.optimization_barrier(v.astype(jnp.bfloat16)).astype(jnp.float32)

@jax.custom_vjp
def low_back(v):
    return v

def low_keep(v):
    return (low(v), None)

def low_pass(kept, grad):
    return (grad,)

def back_keep(v):
    return (v, None)

def back_low(kept, grad):
    return (low(grad),)
low.defvjp(low_keep, low_pass)
low_back.defvjp(back_keep, back_low)

def matmul(left_side, right_side):
    return jnp.dot(left_side, right_side, precision=HIGHEST, preferred_element_type=jnp.float32)

def rms_norm(values, gain_vec):
    scale = lax.rsqrt(lax.optimization_barrier(jnp.mean(values * values, axis=-1, keepdims=True)) + EPSILON)
    return values * scale * gain_vec

def sequence_ids(seq_lengths, row_count):
    seq_ends = jnp.cumsum(seq_lengths).astype(jnp.int32)
    places = jnp.arange(row_count, dtype=jnp.int32)
    return lax.optimization_barrier(jnp.sum((places[:, None] >= seq_ends[None, :]).astype(jnp.int32), axis=1)).astype(jnp.int32)

def causal_conv(inputs, weight_rows, bias_rows, seq_index):
    tap_count = weight_rows.shape[1]
    result = inputs * weight_rows[:, tap_count - 1] + bias_rows
    for offset in range(1, tap_count):
        shifted = jnp.concatenate([jnp.zeros((offset, inputs.shape[1]), inputs.dtype), inputs[:-offset]], axis=0)
        before = jnp.concatenate([jnp.full((offset,), -1, jnp.int32), seq_index[:-offset]], axis=0)
        result = result + jnp.where((before == seq_index)[:, None], shifted, 0.0) * weight_rows[:, tap_count - 1 - offset]
    return result

def stretch_step(carried_in, block_data):
    state_now, last_id = carried_in
    xblock, dtblock, logblock, bblock, cblock, idblock = block_data
    block_len = idblock.shape[0]
    cumulative = jnp.cumsum(logblock, axis=0)
    places = jnp.arange(block_len, dtype=jnp.int32)
    causal = (idblock[:, None] == idblock[None, :]) & (places[:, None] >= places[None, :])
    spread = cumulative[:, None, :] - cumulative[None, :, :]
    decays = jnp.exp(jnp.minimum(spread, 0.0)) * causal[:, :, None].astype(jnp.float32)
    scores = jnp.dot(cblock, bblock.T, precision=HIGHEST, preferred_element_type=jnp.float32)
    weights = decays * scores[:, :, None] * dtblock[None, :, :]
    within = jnp.einsum('ijh,jhp->ihp', weights, xblock, precision=HIGHEST)
    carried = (idblock == last_id).astype(jnp.float32)[:, None] * jnp.exp(cumulative)
    earlier = jnp.einsum('in,hpn->ihp', cblock, state_now, precision=HIGHEST) * carried[:, :, None]
    end_id = idblock[block_len - 1].astype(jnp.int32)
    tail_weight = (idblock == end_id).astype(jnp.float32)[:, None] * jnp.exp(cumulative[block_len - 1][None, :] - cumulative) * dtblock
    keeping = (last_id == end_id).astype(jnp.float32) * jnp.exp(cumulative[block_len - 1])
    added_state = jnp.einsum('jh,jhp,jn->hpn', tail_weight, xblock, bblock, precision=HIGHEST)
    return ((keeping[:, None, None] * state_now + added_state, end_id), within + earlier)

def state_scan(xheads, step_sizes, decay_rate, bvalues, cvalues, seq_index, skip_gain):
    row_count, head_count, head_size = xheads.shape
    block_count = row_count // STRETCH
    log_decay = step_sizes * decay_rate
    inputs = (xheads.reshape(block_count, STRETCH, head_count, head_size), step_sizes.reshape(block_count, STRETCH, head_count), log_decay.reshape(block_count, STRETCH, head_count), bvalues.reshape(block_count, STRETCH, -1), cvalues.reshape(block_count, STRETCH, -1), seq_index.reshape(block_count, STRETCH))
    start_state = (jnp.zeros((head_count, head_size, bvalues.shape[1]), xheads.dtype), jnp.array(-1, jnp.int32))
    final_state, outputs = lax.scan(jax.checkpoint(stretch_step), start_state, inputs)
    return outputs.reshape(row_count, head_count, head_size) + skip_gain[None, :, None] * xheads

def head_side(xs_seq, bc_seq, dtr_seq, conv_part, conv_bias_part, step_part, decay_part, skip_part, seq_index):
    channels = xs_seq.shape[1]
    head_count = dtr_seq.shape[1]
    state_size = bc_seq.shape[1] // 2
    joined = jnp.concatenate([xs_seq, bc_seq], axis=1)
    activated = jax.nn.silu(causal_conv(joined, conv_part, conv_bias_part, seq_index))
    xheads = activated[:, :channels].reshape(-1, head_count, channels // head_count)
    bvalues = activated[:, channels:channels + state_size]
    cvalues = activated[:, channels + state_size:]
    step_sizes = jax.nn.softplus(dtr_seq + step_part)
    outputs = state_scan(xheads, step_sizes, -jnp.exp(decay_part), bvalues, cvalues, seq_index, skip_part)
    return outputs.reshape(-1, channels)

def group_forward(residual, params, deal_rows, seq_lengths, route_ids):
    gain_in, proj_in, proj_dt, conv_weight, conv_bias, step_bias, decay_log, skip_gain, gain_gate, proj_out, gain_moe, router, shared_up, shared_down, expert_up, expert_down = params
    hidden = low(rms_norm(residual, gain_in))
    projected = matmul(hidden, proj_in)
    gate_in = low_back(projected[:, :DI])
    xs_all = low_back(low(projected[:, DI:2 * DI]))
    bc_all = low_back(low(projected[:, 2 * DI:]))
    dtr_all = low_back(low(matmul(hidden, proj_dt)))
    inverse = jnp.zeros((GROUP_TOK,), jnp.int32).at[deal_rows].set(jnp.arange(GROUP_TOK, dtype=jnp.int32))
    seq_index = sequence_ids(seq_lengths, GROUP_TOK)
    group_width = HEADS_DEV * HEAD_DIM
    xs_groups = jnp.transpose(xs_all[inverse].reshape(GROUP_TOK, N_SEQ, group_width), (1, 0, 2))
    dtr_groups = jnp.transpose(dtr_all[inverse].reshape(GROUP_TOK, N_SEQ, HEADS_DEV), (1, 0, 2))
    bc_copies = low_back(jnp.broadcast_to(bc_all[inverse][None], (N_SEQ, GROUP_TOK, 2 * STATE)))
    conv_rows = jnp.concatenate([conv_weight[:DI].reshape(N_SEQ, group_width, CONV), jnp.broadcast_to(conv_weight[DI:][None], (N_SEQ, 2 * STATE, CONV))], axis=1)
    bias_rows = jnp.concatenate([conv_bias[:DI].reshape(N_SEQ, group_width), jnp.broadcast_to(conv_bias[DI:][None], (N_SEQ, 2 * STATE))], axis=1)
    head_out = jax.vmap(head_side, in_axes=(0, 0, 0, 0, 0, 0, 0, 0, None))(xs_groups, bc_copies, dtr_groups, conv_rows, bias_rows, step_bias.reshape(N_SEQ, HEADS_DEV), decay_log.reshape(N_SEQ, HEADS_DEV), skip_gain.reshape(N_SEQ, HEADS_DEV), seq_index)
    mixed_seq = jnp.transpose(head_out, (1, 0, 2)).reshape(GROUP_TOK, DI)
    mixed_back = low_back(low(mixed_seq[deal_rows]))
    normed = low(rms_norm(mixed_back * jax.nn.silu(gate_in), gain_gate))
    after_mix = residual + low_back(matmul(normed, proj_out))
    moe_in = low(rms_norm(after_mix, gain_moe))
    logits = low_back(matmul(moe_in, router))
    gate_values = jax.nn.softmax(jnp.take_along_axis(logits, route_ids, axis=1), axis=1)
    shared_gu = matmul(moe_in, shared_up)
    shared_act = low(jax.nn.silu(low_back(shared_gu[:, :FS])) * low_back(shared_gu[:, FS:]))
    shared_res = matmul(shared_act, shared_down)
    flat_routes = route_ids.reshape(-1)
    assigned = GROUP_TOK * TOP
    onehot = (flat_routes[:, None] == jnp.arange(EXPERTS, dtype=jnp.int32)[None, :]).astype(jnp.int32)
    per_block = onehot.reshape(N_SEQ, TOK_DEV * TOP, EXPERTS)
    slot_ranks = lax.optimization_barrier(jnp.sum((jnp.cumsum(per_block, axis=1) - per_block) * per_block, axis=2)).reshape(-1).astype(jnp.int32)
    slot_index = jnp.arange(assigned, dtype=jnp.int32) // (TOK_DEV * TOP) * CAP + slot_ranks
    sources = jnp.full((EXPERTS, N_SEQ * CAP), assigned, jnp.int32).at[flat_routes, slot_index].set(jnp.arange(assigned, dtype=jnp.int32))
    padded = jnp.concatenate([moe_in, jnp.zeros((1, D), moe_in.dtype)], axis=0)
    expert_rows = low_back(padded[sources // TOP])
    expert_gu = jnp.einsum('erd,edf->erf', expert_rows, expert_up, precision=HIGHEST)
    expert_act = low(jax.nn.silu(low_back(expert_gu[..., :F])) * low_back(expert_gu[..., F:]))
    expert_res = low_back(low(jnp.einsum('erf,efd->erd', expert_act, expert_down, precision=HIGHEST)))
    picked = expert_res[flat_routes, slot_index].reshape(GROUP_TOK, TOP, D)
    routed = lax.optimization_barrier(jnp.sum(gate_values[:, :, None] * picked, axis=1))
    return after_mix + routed + shared_res

def reference(tokens, out_grad, deal_order, lengths, routes, norm_in, w_in, w_dt, conv_w, conv_b, dt_bias, a_log, d_skip, norm_gate, w_out, norm_moe, w_router, w_shared, w_shared_down, w_experts, w_experts_down):
    weight_list = tuple((tensor.astype(jnp.float32) for tensor in (norm_in, w_in, w_dt, conv_w, conv_b, dt_bias, a_log, d_skip, norm_gate, w_out, norm_moe, w_router, w_shared, w_shared_down, w_experts, w_experts_down)))

    def forward(residual, params):

        def group_step(carried_in, group_data):
            return (carried_in, group_forward(group_data[0], params, group_data[1], group_data[2], group_data[3]))
        final_carry, outputs = lax.scan(jax.checkpoint(group_step), jnp.zeros((), jnp.float32), (residual, deal_order, lengths, routes))
        return outputs
    result, pullback = jax.vjp(forward, tokens.astype(jnp.float32), weight_list)
    token_grad, grads = pullback(out_grad.astype(jnp.float32))
    return (result.astype(jnp.bfloat16), token_grad.astype(jnp.bfloat16), grads[0], grads[1], grads[2], grads[3], grads[4], grads[5], grads[6], grads[7], grads[8], grads[9], grads[10], grads[11], grads[12], grads[13], grads[14], grads[15])
```

```python
import functools

import jax
import jax.numpy as jnp
from jax import lax
from jax.experimental import pallas as pl
from jax.experimental.pallas import tpu as pltpu
from jax.sharding import PartitionSpec as P

STRETCH = 256
INNER = 4
EPSILON = 1e-05
HIGHEST = lax.Precision.HIGHEST


def matmul(left_side, right_side):
    return jnp.dot(left_side, right_side, preferred_element_type=jnp.float32)


def left_contract(left_side, right_side):
    return lax.dot_general(
        left_side, right_side, (((0,), (0,)), ((), ())), preferred_element_type=jnp.float32
    )


def right_contract(left_side, right_side):
    return lax.dot_general(
        left_side, right_side, (((1,), (1,)), ((), ())), preferred_element_type=jnp.float32
    )


def to_low(values):
    return values.astype(jnp.bfloat16)


def to_full(values):
    return values.astype(jnp.float32)


def norm_scale(values):
    return lax.rsqrt(jnp.mean(values * values, axis=-1, keepdims=True) + EPSILON)


LANES = 128
VMEM_BYTES = 56 * 1024 * 1024


def dot_rows(left_side, right_side, precision=None):
    return lax.dot_general(
        left_side,
        right_side,
        (((0,), (0,)), ((), ())),
        precision=precision,
        preferred_element_type=jnp.float32,
    )


def dot_lanes(left_side, right_side, precision=None):
    return lax.dot_general(
        left_side,
        right_side,
        (((1,), (1,)), ((), ())),
        precision=precision,
        preferred_element_type=jnp.float32,
    )


def dot_full(left_side, right_side, precision=None):
    return jnp.dot(
        left_side, right_side, precision=precision, preferred_element_type=jnp.float32
    )


def iota_of(shape, axis):
    return lax.broadcasted_iota(jnp.int32, shape, axis)


def ids_at(places, ends_ref):
    total = jnp.zeros(places.shape, jnp.int32)
    for seq in range(ends_ref.shape[0]):
        total = total + (places >= ends_ref[seq]).astype(jnp.int32)
    return total


def id_at(place, ends_ref):
    total = jnp.int32(0)
    for seq in range(ends_ref.shape[0]):
        total = total + (place >= ends_ref[seq]).astype(jnp.int32)
    return total


class Stretch:
    def __init__(self, start, rows, before, conv_ref, head_ref, ends_ref, channels):
        length = rows.shape[0]
        self.channels = channels
        self.heads = channels // 64
        width = conv_ref.shape[1]
        state = (width - channels) // 2
        places = start + iota_of((length, 1), 0)
        self.ids = ids_at(places, ends_ref)
        self.ids_row = ids_at(start + iota_of((1, length), 1), ends_ref)
        inputs = rows[:, :width]
        joined = jnp.concatenate([before[:, :width], inputs], axis=0)
        self.shifted = [inputs]
        value = conv_ref[4:5, :] + inputs * conv_ref[3:4, :]
        for offset in range(1, 4):
            same = (ids_at(places - offset, ends_ref) == self.ids) & (places >= offset)
            moved = pltpu.roll(joined, offset, 0)[8:, :]
            moved = jnp.where(same, moved, 0.0)
            self.shifted.append(moved)
            value = value + moved * conv_ref[3 - offset : 4 - offset, :]
        self.value = value
        self.sig = jax.nn.sigmoid(value)
        act = value * self.sig
        self.x = act[:, :channels]
        self.b = act[:, channels : channels + state]
        self.c = act[:, channels + state :]
        self.b_low = to_low(self.b)
        self.c_low = to_low(self.c)
        self.dt_in = rows[:, width:] + head_ref[0:1, :]
        self.dt = jnp.maximum(self.dt_in, 0.0) + jnp.log1p(jnp.exp(-jnp.abs(self.dt_in)))
        self.rate = head_ref[1:2, :]
        rows_at = iota_of((length, length), 0)
        columns_at = iota_of((length, length), 1)
        lower = (rows_at >= columns_at).astype(jnp.float32)
        self.cum = dot_full(lower, self.dt * self.rate, HIGHEST)
        self.cum_rows = self.cum.T[:8, :]
        self.dt_rows = self.dt.T[:8, :]
        self.causal = (self.ids == self.ids_row) & (rows_at >= columns_at)
        self.scores = dot_lanes(self.c_low, self.b_low)
        last_id = jnp.where(start > 0, id_at(start - 1, ends_ref), -1)
        end_id = id_at(start + length - 1, ends_ref)
        self.enter = jnp.where(self.ids == last_id, jnp.exp(self.cum), 0.0)
        end_cum = self.cum[length - 1 : length, :]
        self.tail = jnp.where(self.ids == end_id, jnp.exp(end_cum - self.cum), 0.0)
        self.tail_weight = self.tail * self.dt
        self.keep = jnp.where(last_id == end_id, jnp.exp(end_cum), 0.0)

    def decay(self, head):
        spread = self.cum[:, head : head + 1] - self.cum_rows[head : head + 1, :]
        return jnp.where(self.causal, jnp.exp(jnp.minimum(spread, 0.0)), 0.0)

    def per_channel(self, by_head):
        return jnp.concatenate(
            [
                jnp.broadcast_to(by_head[:, head : head + 1], (by_head.shape[0], 64))
                for head in range(self.heads)
            ],
            axis=1,
        )

    def state_keep(self):
        return jnp.concatenate(
            [
                jnp.broadcast_to(self.keep[:, head : head + 1], (64, LANES))
                for head in range(self.heads)
            ],
            axis=0,
        )


def head_lanes(channels):
    return (iota_of((channels, LANES), 0) // 64 == iota_of((channels, LANES), 1)).astype(
        jnp.float32
    )


def pick_rows(deal_ref, start, length):
    places = start + iota_of((length, 1), 0)
    return jnp.where(deal_ref[...] == places, 1.0, 0.0).astype(jnp.bfloat16)


def scan_forward_kernel(
    ends_ref, deal_ref, rows_ref, conv_ref, head_ref, y_ref, seq_ref, states_ref, before, state, total
):
    step = pl.program_id(0)
    length = seq_ref.shape[0]
    channels = y_ref.shape[1]
    start = step * length

    @pl.when(step == 0)
    def _():
        before[...] = jnp.zeros_like(before)
        state[...] = jnp.zeros_like(state)
        total[...] = jnp.zeros_like(total)

    picks = pick_rows(deal_ref, start, length)
    rows = dot_full(picks, rows_ref[...])
    seq_ref[...] = to_low(rows)
    part = Stretch(start, rows, before[...], conv_ref, head_ref, ends_ref, channels)
    before[...] = rows[length - 8 :, :]
    state_now = state[...]
    states_ref[0] = state_now
    x_low = to_low(part.x)
    outs = []
    lane = iota_of((length, LANES), 1)
    for pair in range(channels // LANES):
        x_pair = x_low[:, pair * LANES : (pair + 1) * LANES]
        halves = []
        for head in (2 * pair, 2 * pair + 1):
            weights = part.decay(head) * part.scores * part.dt_rows[head : head + 1, :]
            halves.append(dot_full(to_low(weights), x_pair))
        outs.append(jnp.where(lane < 64, halves[0], halves[1]))
    earlier = dot_lanes(part.c_low, to_low(state_now))
    skip = part.per_channel(head_ref[2:3, :])
    y = jnp.concatenate(outs, axis=1) + part.per_channel(part.enter) * earlier + skip * part.x
    state[...] = part.state_keep() * state_now + dot_rows(
        to_low(part.per_channel(part.tail_weight) * part.x), part.b_low
    )
    total[...] += dot_rows(picks, to_low(y))

    @pl.when(step == pl.num_programs(0) - 1)
    def _():
        y_ref[...] = to_low(total[...])


def scan_forward(ends, deal_row, rows, conv_table, head_table, channels):
    group_rows, width = rows.shape
    steps = group_rows // STRETCH
    state_rows = (channels, LANES)
    whole = lambda shape: pl.BlockSpec(shape, lambda step: (0,) * len(shape))
    return pl.pallas_call(
        scan_forward_kernel,
        grid=(steps,),
        in_specs=[
            pl.BlockSpec(memory_space=pltpu.SMEM),
            whole(deal_row.shape),
            whole(rows.shape),
            whole(conv_table.shape),
            whole(head_table.shape),
        ],
        out_specs=[
            whole((group_rows, channels)),
            pl.BlockSpec((STRETCH, width), lambda step: (step, 0)),
            pl.BlockSpec((1,) + state_rows, lambda step: (step, 0, 0)),
        ],
        out_shape=[
            jax.ShapeDtypeStruct((group_rows, channels), jnp.bfloat16),
            jax.ShapeDtypeStruct((group_rows, width), jnp.bfloat16),
            jax.ShapeDtypeStruct((steps,) + state_rows, jnp.float32),
        ],
        scratch_shapes=[
            pltpu.VMEM((8, width), jnp.float32),
            pltpu.VMEM(state_rows, jnp.float32),
            pltpu.VMEM((group_rows, channels), jnp.float32),
        ],
        compiler_params=pltpu.CompilerParams(vmem_limit_bytes=VMEM_BYTES),
        name="scan_forward",
    )(ends, deal_row, rows, conv_table, head_table)


def scan_backward_kernel(
    ends_ref,
    deal_ref,
    seq_ref,
    states_ref,
    dy_ref,
    conv_ref,
    head_ref,
    drows_ref,
    conv_grad_ref,
    head_grad_ref,
    after,
    state_grad,
    total,
):
    order = pl.program_id(0)
    steps = pl.num_programs(0)
    step = steps - 1 - order
    length = STRETCH
    channels = dy_ref.shape[1]
    width = conv_ref.shape[1]
    state_width = (width - channels) // 2
    start = pl.multiple_of(step * length, length)

    @pl.when(order == 0)
    def _():
        after[...] = jnp.zeros_like(after)
        state_grad[...] = jnp.zeros_like(state_grad)
        total[...] = jnp.zeros_like(total)
        conv_grad_ref[...] = jnp.zeros_like(conv_grad_ref)
        head_grad_ref[...] = jnp.zeros_like(head_grad_ref)

    picks = pick_rows(deal_ref, start, length)
    dy = dot_full(picks, dy_ref[...])
    rows = seq_ref[pl.ds(start, length), :].astype(jnp.float32)
    place = pl.multiple_of(jnp.maximum(start - 16, 0), 16)
    before = seq_ref[pl.ds(place, 16), :].astype(jnp.float32)[8:, :]
    part = Stretch(start, rows, before, conv_ref, head_ref, ends_ref, channels)
    state_now = states_ref[0]
    state_low = to_low(state_now)
    next_grad = state_grad[...]
    next_low = to_low(next_grad)
    lanes_of = head_lanes(channels)
    x_low = to_low(part.x)
    dy_low = to_low(dy)
    lane = iota_of((length, LANES), 1)

    enter = part.per_channel(part.enter)
    tail_weight = part.per_channel(part.tail_weight)
    earlier = dot_lanes(part.c_low, state_low)
    enter_grad = dot_full(dy * earlier, lanes_of, HIGHEST)
    entered = to_low(enter * dy)
    c_grad = dot_full(entered, state_low)
    state_grad[...] = part.state_keep() * next_grad + dot_rows(entered, part.c_low)
    onward = dot_lanes(part.b_low, next_low)
    x_grad = part.per_channel(head_ref[2:3, :]) * dy + tail_weight * onward
    tail_grad = dot_full(part.x * onward, lanes_of, HIGHEST)
    b_grad = dot_full(to_low(tail_weight * part.x), next_low)
    tail_part = tail_grad * part.tail_weight
    cum_grad = enter_grad * part.enter - tail_part
    dt_grad = tail_grad * part.tail
    kept = dot_lanes(jnp.ones((8, LANES), jnp.float32), next_grad * state_now, HIGHEST)
    keep_grad = dot_full(kept, lanes_of, HIGHEST)[:1, :]
    end_grad = jnp.sum(tail_part, axis=0, keepdims=True) + keep_grad * part.keep

    score_grad = jnp.zeros((length, length), jnp.float32)
    cum_columns, cum_rows, dt_rows, outs = [], [], [], []
    for pair in range(channels // LANES):
        x_pair = x_low[:, pair * LANES : (pair + 1) * LANES]
        dy_pair = dy_low[:, pair * LANES : (pair + 1) * LANES]
        halves = []
        for half, head in enumerate((2 * pair, 2 * pair + 1)):
            mine = (lane < 64) if half == 0 else (lane >= 64)
            weight_grad = dot_lanes(jnp.where(mine, dy_pair, jnp.zeros_like(dy_pair)), x_pair)
            decay = part.decay(head)
            dt_row = part.dt_rows[head : head + 1, :]
            by_decay = weight_grad * decay
            by_dt = by_decay * part.scores
            by_spread = by_dt * dt_row
            dt_rows.append(jnp.sum(by_dt, axis=0, keepdims=True))
            cum_rows.append(jnp.sum(by_spread, axis=0, keepdims=True))
            cum_columns.append(jnp.sum(by_spread, axis=1, keepdims=True))
            score_grad = score_grad + by_decay * dt_row
            halves.append(dot_rows(to_low(decay * part.scores * dt_row), dy_pair))
        outs.append(jnp.where(lane < 64, halves[0], halves[1]))
    x_grad = x_grad + jnp.concatenate(outs, axis=1)
    score_low = to_low(score_grad)
    c_grad = c_grad + dot_full(score_low, part.b_low)
    b_grad = b_grad + dot_rows(score_low, part.c_low)

    heads = len(dt_rows)
    blank = jnp.zeros((LANES - heads, length), jnp.float32)
    dt_grad = dt_grad + jnp.concatenate(dt_rows + [blank], axis=0).T
    cum_grad = cum_grad - jnp.concatenate(cum_rows + [blank], axis=0).T
    for head in range(heads):
        cum_grad = cum_grad + jnp.where(lane == head, cum_columns[head], 0.0)
    at_end = iota_of((length, 1), 0) == length - 1
    cum_grad = cum_grad + jnp.where(at_end, end_grad, 0.0)
    upper = (iota_of((length, length), 1) >= iota_of((length, length), 0)).astype(jnp.float32)
    log_grad = dot_full(upper, cum_grad, HIGHEST)
    dt_grad = dt_grad + log_grad * part.rate
    dt_in_grad = dt_grad * jax.nn.sigmoid(part.dt_in)
    dt_in_grad = jnp.where(lane < heads, dt_in_grad, 0.0)
    head_grad_ref[0:1, :] += jnp.sum(dt_in_grad, axis=0, keepdims=True)
    head_grad_ref[1:2, :] += jnp.sum(log_grad * part.dt, axis=0, keepdims=True) * part.rate
    skip_sum = jnp.broadcast_to(jnp.sum(dy * part.x, axis=0, keepdims=True), (8, channels))
    head_grad_ref[2:3, :] += dot_full(skip_sum, lanes_of, HIGHEST)[:1, :]

    act_grad = jnp.concatenate([x_grad, b_grad, c_grad], axis=1)
    value_grad = act_grad * part.sig * (1.0 + part.value * (1.0 - part.sig))
    conv_grad_ref[4:5, :] += jnp.sum(value_grad, axis=0, keepdims=True)
    for offset in range(4):
        conv_grad_ref[3 - offset : 4 - offset, :] += jnp.sum(
            value_grad * part.shifted[offset], axis=0, keepdims=True
        )
    joined = jnp.concatenate([value_grad, after[...]], axis=0)
    places = start + iota_of((length, 1), 0)
    rows_grad = value_grad * conv_ref[3:4, :]
    for offset in range(1, 4):
        moved = pltpu.roll(joined, length + 8 - offset, 0)[:length, :]
        same = (ids_at(places + offset, ends_ref) == part.ids) & (
            places + offset < steps * length
        )
        rows_grad = rows_grad + jnp.where(same, moved, 0.0) * conv_ref[3 - offset : 4 - offset, :]
    after[...] = value_grad[:8, :]
    total[...] += dot_rows(picks, to_low(jnp.concatenate([rows_grad, dt_in_grad], axis=1)))

    @pl.when(order == steps - 1)
    def _():
        drows_ref[...] = to_low(total[...])


def scan_backward(ends, deal_row, seq_rows, states, dy, conv_table, head_table):
    group_rows, width = seq_rows.shape
    channels = dy.shape[1]
    steps = group_rows // STRETCH
    whole = lambda shape: pl.BlockSpec(shape, lambda step: (0,) * len(shape))
    return pl.pallas_call(
        scan_backward_kernel,
        grid=(steps,),
        in_specs=[
            pl.BlockSpec(memory_space=pltpu.SMEM),
            whole(deal_row.shape),
            whole(seq_rows.shape),
            pl.BlockSpec((1, channels, LANES), lambda step: (steps - 1 - step, 0, 0)),
            whole(dy.shape),
            whole(conv_table.shape),
            whole(head_table.shape),
        ],
        out_specs=[
            whole((group_rows, width)),
            whole(conv_table.shape),
            whole(head_table.shape),
        ],
        out_shape=[
            jax.ShapeDtypeStruct((group_rows, width), jnp.bfloat16),
            jax.ShapeDtypeStruct(conv_table.shape, jnp.float32),
            jax.ShapeDtypeStruct(head_table.shape, jnp.float32),
        ],
        scratch_shapes=[
            pltpu.VMEM((8, conv_table.shape[1]), jnp.float32),
            pltpu.VMEM((channels, LANES), jnp.float32),
            pltpu.VMEM((group_rows, width), jnp.float32),
        ],
        compiler_params=pltpu.CompilerParams(vmem_limit_bytes=VMEM_BYTES),
        name="scan_backward",
    )(ends, deal_row, seq_rows, states, dy, conv_table, head_table)


MESH = pl.DeviceIdType.MESH
FLIPS = (1, 2, 4)


def flipped(place, flip):
    result = place
    for bit in FLIPS:
        if flip & bit:
            result = result + bit - 2 * bit * lax.rem(lax.div(place, bit), 2)
    return result


def own_shard_group(inner):
    shard = lax.axis_index("shard")
    place = lax.rem(shard, inner)
    return place, shard - place


def peers_in_order(place, inner):
    if inner == 1:
        return []
    if inner == 4:
        half = lax.div(place, 2)
        return [flipped(place, 1), 2 - half, 3 - 3 * half]
    return [lax.rem(place + shift, inner) for shift in range(1, inner)]


def greet(inner):
    barrier = pltpu.get_barrier_semaphore()
    part = lax.axis_index("seq")
    place, first = own_shard_group(inner)
    for flip in FLIPS:
        pl.semaphore_signal(
            barrier, inc=1, device_id={"seq": flipped(part, flip)}, device_id_type=MESH
        )
    for peer in peers_in_order(place, inner):
        pl.semaphore_signal(
            barrier, inc=1, device_id={"shard": first + peer}, device_id_type=MESH
        )
    pl.semaphore_wait(barrier, len(FLIPS) + inner - 1)


def gather_kernel(inner, x_ref, out_ref, own_sem, zsend, zrecv, send, recv):
    part = lax.axis_index("seq")
    place, first = own_shard_group(inner)
    rows = x_ref.shape[0]
    half = rows // 2
    spans = [pl.ds(0, half), pl.ds(half, half)]
    others = peers_in_order(place, inner)
    sources = [place] + others
    greet(inner)
    own = pltpu.make_async_copy(x_ref, out_ref.at[place, part], own_sem)
    own.start()
    across = []
    for order, peer in enumerate(others):
        copy = pltpu.make_async_remote_copy(
            src_ref=x_ref,
            dst_ref=out_ref.at[place, part],
            send_sem=zsend.at[order],
            recv_sem=zrecv.at[place],
            device_id={"shard": first + peer},
            device_id_type=MESH,
        )
        copy.start()
        across.append(copy)

    def copy_of(order, kind, block, span, flip, from_input=False):
        whole = out_ref.at[sources[order], block, spans[span]]
        return pltpu.make_async_remote_copy(
            src_ref=x_ref.at[spans[span]] if from_input else whole,
            dst_ref=whole,
            send_sem=send.at[order, kind],
            recv_sem=recv.at[order, kind],
            device_id={"seq": flipped(part, flip)},
            device_id_type=MESH,
        )

    started = []

    def push(order, kind, block, span, flip, from_input=False):
        copy = copy_of(order, kind, block, span, flip, from_input)
        copy.start()
        started.append(copy)

    def arrived(order, kind, block, span, flip):
        copy_of(order, kind, block, span, flip).wait_recv()

    def stage_a(order):
        if order:
            arrive = pltpu.make_async_remote_copy(
                src_ref=x_ref,
                dst_ref=out_ref.at[sources[order], part],
                send_sem=zsend.at[order - 1],
                recv_sem=zrecv.at[sources[order]],
                device_id={"shard": first + sources[order]},
                device_id_type=MESH,
            )
            arrive.wait_recv()
        direct = order == 0
        push(order, 3, part, 1, 2, direct)
        push(order, 4, part, 0, 4, direct)
        push(order, 2, part, 0, 2, direct)
        push(order, 5, part, 1, 4, direct)
        push(order, 0, part, 0, 1, direct)
        push(order, 1, part, 1, 1, direct)

    def stage_b(order):
        side, over = flipped(part, 2), flipped(part, 4)
        arrived(order, 3, side, 1, 2)
        push(order, 6, side, 1, 4)
        arrived(order, 4, over, 0, 4)
        push(order, 7, over, 0, 2)
        push(order, 9, side, 1, 1)
        push(order, 10, over, 0, 1)
        arrived(order, 2, side, 0, 2)
        push(order, 8, side, 0, 1)
        arrived(order, 5, over, 1, 4)
        push(order, 11, over, 1, 1)

    def stage_c(order):
        far = flipped(part, 6)
        arrived(order, 6, far, 1, 4)
        push(order, 13, far, 1, 1)
        arrived(order, 7, far, 0, 2)
        push(order, 12, far, 0, 1)

    def stage_d(order):
        for kind, flip, span in (
            (0, 1, 0),
            (1, 1, 1),
            (9, 3, 1),
            (10, 5, 0),
            (8, 3, 0),
            (11, 5, 1),
            (13, 7, 1),
            (12, 7, 0),
        ):
            arrived(order, kind, flipped(part, flip), span, 1)

    count = len(sources)
    stage_a(0)
    stage_b(0)
    for order in range(1, count):
        stage_a(order)
        stage_c(order - 1)
        stage_b(order)
    stage_c(count - 1)
    for order in range(count):
        stage_d(order)
    for copy in started:
        copy.wait_send()
    for copy in across:
        copy.wait_send()
    own.wait()


def gather_rows(x, inner, collective):
    rows, width = x.shape
    seq_devices = lax.axis_size("seq")
    return pl.pallas_call(
        functools.partial(gather_kernel, inner),
        in_specs=[pl.BlockSpec(memory_space=pl.ANY)],
        out_specs=pl.BlockSpec(memory_space=pl.ANY),
        out_shape=jax.ShapeDtypeStruct((inner, seq_devices, rows, width), x.dtype),
        scratch_shapes=[
            pltpu.SemaphoreType.DMA(()),
            pltpu.SemaphoreType.DMA((max(1, inner - 1),)),
            pltpu.SemaphoreType.DMA((inner,)),
            pltpu.SemaphoreType.DMA((inner, 14)),
            pltpu.SemaphoreType.DMA((inner, 14)),
        ],
        compiler_params=pltpu.CompilerParams(collective_id=collective, has_side_effects=True),
        name="gather_rows",
    )(x)


def reduce_kernel(
    inner,
    p_ref,
    out_ref,
    held,
    paired,
    turned,
    crossed,
    sums,
    summed,
    load,
    core_send,
    core_recv,
    turn_send,
    turn_recv,
    cross_send,
    cross_recv,
    zsend,
    zrecv,
):
    part = lax.axis_index("seq")
    place, first = own_shard_group(inner)
    rows = out_ref.shape[0]
    half = rows // 2
    spans = [pl.ds(0, half), pl.ds(half, half)]
    targets = list(reversed(peers_in_order(place, inner))) + [place]
    evens = (6, 2, 4, 0)
    greet(inner)
    loads, cores = {}, {}
    for order, target in enumerate(targets):
        for slot, flip in enumerate(evens):
            copy = pltpu.make_async_remote_copy(
                src_ref=p_ref.at[target, flipped(part, flip + 1)],
                dst_ref=paired.at[order, slot],
                send_sem=core_send.at[order, slot],
                recv_sem=core_recv.at[order, slot],
                device_id={"seq": flipped(part, 1)},
                device_id_type=MESH,
            )
            copy.start()
            cores[order, slot] = copy
            copy = pltpu.make_async_copy(
                p_ref.at[target, flipped(part, flip)], held.at[order, slot], load.at[order, slot]
            )
            copy.start()
            loads[order, slot] = copy

    def total_of(order, slot):
        loads[order, slot].wait()
        cores[order, slot].wait_recv()
        return to_full(held[order, slot]) + to_full(paired[order, slot])

    sends = []

    def push(source, target, send_sem, recv_sem, flip):
        copy = pltpu.make_async_remote_copy(
            src_ref=source,
            dst_ref=target,
            send_sem=send_sem,
            recv_sem=recv_sem,
            device_id={"seq": flipped(part, flip)},
            device_id_type=MESH,
        )
        copy.start()
        sends.append(copy)
        return copy

    turns, crosses, across = {}, {}, []

    def stage_a(order):
        held[order, 0] = to_low(total_of(order, 0))
        for span, flip in ((0, 2), (1, 4)):
            turns[order, span] = push(
                held.at[order, 0, spans[span]],
                turned.at[order, span],
                turn_send.at[order, span],
                turn_recv.at[order, span],
                flip,
            )
        held[order, 1] = to_low(total_of(order, 1))
        held[order, 2] = to_low(total_of(order, 2))
        for kind, slot, flip, span in ((0, 1, 2, 0), (1, 2, 4, 1)):
            crosses[order, kind] = push(
                held.at[order, slot, spans[span]],
                crossed.at[order, kind],
                cross_send.at[order, kind],
                cross_recv.at[order, kind],
                flip,
            )

    def stage_b(order):
        for kind, slot, flip, span in ((2, 2, 4, 0), (3, 1, 2, 1)):
            turns[order, span].wait_recv()
            held[order, slot, spans[span]] = to_low(
                to_full(held[order, slot, spans[span]]) + to_full(turned[order, span])
            )
            crosses[order, kind] = push(
                held.at[order, slot, spans[span]],
                crossed.at[order, kind],
                cross_send.at[order, kind],
                cross_recv.at[order, kind],
                flip,
            )

    def stage_c(order):
        total = total_of(order, 3)
        for kind in range(4):
            crosses[order, kind].wait_recv()
        low_part = to_full(crossed[order, 0]) + to_full(crossed[order, 2])
        high_part = to_full(crossed[order, 1]) + to_full(crossed[order, 3])
        total = total + jnp.concatenate([low_part, high_part], axis=0)
        if order == inner - 1:
            return total
        sums[order] = to_low(total)
        copy = pltpu.make_async_remote_copy(
            src_ref=sums.at[order],
            dst_ref=summed.at[place],
            send_sem=zsend.at[order],
            recv_sem=zrecv.at[place],
            device_id={"shard": first + targets[order]},
            device_id_type=MESH,
        )
        copy.start()
        across.append(copy)
        return None

    stage_a(0)
    for order in range(1, inner):
        stage_a(order)
        stage_b(order - 1)
        if order > 1:
            stage_c(order - 2)
    stage_b(inner - 1)
    if inner > 1:
        stage_c(inner - 2)
    total = stage_c(inner - 1)
    for peer in peers_in_order(place, inner):
        arrive = pltpu.make_async_remote_copy(
            src_ref=sums.at[0],
            dst_ref=summed.at[peer],
            send_sem=zsend.at[0],
            recv_sem=zrecv.at[peer],
            device_id={"shard": first + peer},
            device_id_type=MESH,
        )
        arrive.wait_recv()
        total = total + to_full(summed[peer])
    out_ref[...] = total
    for copy in sends:
        copy.wait_send()
    for copy in cores.values():
        copy.wait_send()
    for copy in across:
        copy.wait_send()


def reduce_rows(partial, collective):
    inner, seq_devices, rows, width = partial.shape
    low = jnp.bfloat16
    sems = lambda *shape: pltpu.SemaphoreType.DMA(shape)
    return pl.pallas_call(
        functools.partial(reduce_kernel, inner),
        in_specs=[pl.BlockSpec(memory_space=pl.ANY)],
        out_specs=pl.BlockSpec(memory_space=pltpu.VMEM),
        out_shape=jax.ShapeDtypeStruct((rows, width), jnp.float32),
        scratch_shapes=[
            pltpu.VMEM((inner, 4, rows, width), low),
            pltpu.VMEM((inner, 4, rows, width), low),
            pltpu.VMEM((inner, 2, rows // 2, width), low),
            pltpu.VMEM((inner, 4, rows // 2, width), low),
            pltpu.VMEM((max(1, inner - 1), rows, width), low),
            pltpu.VMEM((inner, rows, width), low),
            sems(inner, 4),
            sems(inner, 4),
            sems(inner, 4),
            sems(inner, 2),
            sems(inner, 2),
            sems(inner, 4),
            sems(inner, 4),
            sems(max(1, inner - 1)),
            sems(inner),
        ],
        compiler_params=pltpu.CompilerParams(
            collective_id=collective, has_side_effects=True, vmem_limit_bytes=VMEM_BYTES
        ),
        name="reduce_rows",
    )(partial)


def whole(shape):
    return pl.BlockSpec(shape, lambda *steps: (0,) * len(shape))


def params_of(limit=VMEM_BYTES):
    return pltpu.CompilerParams(vmem_limit_bytes=limit)


def project_kernel(x_ref, gain_ref, w_ref, hidden_ref, gate_ref, rows_ref):
    x = to_full(x_ref[...])
    hidden = to_low(x * norm_scale(x) * gain_ref[...])
    hidden_ref[...] = hidden
    projected = dot_full(hidden, w_ref[...])
    gate_width = gate_ref.shape[1]
    gate_ref[...] = projected[:, :gate_width]
    rows_ref[...] = to_low(projected[:, gate_width:])


def project(x, gain, weights, gate_width):
    rows, width = x.shape
    columns = weights.shape[1]
    tile = 256
    block = lambda extent: pl.BlockSpec((tile, extent), lambda step: (step, 0))
    return pl.pallas_call(
        project_kernel,
        grid=(rows // tile,),
        in_specs=[block(width), whole(gain.shape), whole(weights.shape)],
        out_specs=[block(width), block(gate_width), block(columns - gate_width)],
        out_shape=[
            jax.ShapeDtypeStruct((rows, width), jnp.bfloat16),
            jax.ShapeDtypeStruct((rows, gate_width), jnp.float32),
            jax.ShapeDtypeStruct((rows, columns - gate_width), jnp.bfloat16),
        ],
        compiler_params=params_of(),
        name="project",
    )(x, gain, weights)


def put_split(columns, rows):
    lane = iota_of((rows, LANES), 1)
    result = jnp.zeros((rows, LANES), jnp.float32)
    for place, column in enumerate(columns):
        high = to_full(to_low(column))
        result = jnp.where(lane == 2 * place, high, result)
        result = jnp.where(lane == 2 * place + 1, column - high, result)
    return to_low(result)


def mix_out_kernel(y_ref, gate_ref, gain_ref, w_ref, part_ref):
    width = w_ref.shape[1]
    gated = to_full(y_ref[...]) * jax.nn.silu(gate_ref[...])
    part_ref[0, :, :width] = to_low(dot_full(to_low(gated * gain_ref[...]), w_ref[...]))
    squares = jnp.sum(gated * gated, axis=1, keepdims=True)
    part_ref[0, :, width:] = put_split([squares], y_ref.shape[0])


def mix_out(y, gate, gain, weights, blocks):
    rows, channels = y.shape
    width = weights.shape[1]
    tile = rows // blocks
    block = pl.BlockSpec((tile, channels), lambda step: (step, 0))
    return pl.pallas_call(
        mix_out_kernel,
        grid=(blocks,),
        in_specs=[block, block, whole(gain.shape), whole(weights.shape)],
        out_specs=pl.BlockSpec((1, tile, width + LANES), lambda step: (step, 0, 0)),
        out_shape=jax.ShapeDtypeStruct((blocks, tile, width + LANES), jnp.bfloat16),
        compiler_params=params_of(),
        name="mix_out",
    )(y, gate, gain, weights)


def mix_back_kernel(
    mix_ref, y_ref, gate_ref, gain_ref, w_ref, dy_ref, dgate_ref, w_grad_ref, gain_grad_ref, total
):
    step = pl.program_id(0)
    width = w_ref.shape[1]

    @pl.when(step == 0)
    def _():
        total[...] = jnp.zeros_like(total)
        gain_grad_ref[...] = jnp.zeros_like(gain_grad_ref)

    mix = mix_ref[0, :, :width]
    extra = to_full(mix_ref[0, :, width:])
    share = extra[:, 0:1] + extra[:, 1:2]
    scale = extra[:, 2:3] + extra[:, 3:4]
    normed_grad = dot_lanes(mix, w_ref[...])
    y = to_full(y_ref[...])
    gate = gate_ref[...]
    sig = jax.nn.sigmoid(gate)
    act = gate * sig
    unit = y * act * scale
    gain = gain_ref[...]
    gain_grad_ref[0:1, :] += jnp.sum(normed_grad * unit, axis=0, keepdims=True)
    gated_grad = scale * (normed_grad * gain - unit * share)
    dy_ref[...] = to_low(gated_grad * act)
    dgate_ref[...] = to_low(gated_grad * y * sig * (1.0 + gate * (1.0 - sig)))
    total[...] += dot_rows(to_low(unit * gain), mix)

    @pl.when(step == pl.num_programs(0) - 1)
    def _():
        w_grad_ref[...] = to_low(total[...])


def mix_back(mix, y, gate, gain, weights):
    blocks, tile, wide = mix.shape
    rows, channels = y.shape
    block = pl.BlockSpec((tile, channels), lambda step: (step, 0))
    return pl.pallas_call(
        mix_back_kernel,
        grid=(blocks,),
        in_specs=[
            pl.BlockSpec((1, tile, wide), lambda step: (step, 0, 0)),
            block,
            block,
            whole(gain.shape),
            whole(weights.shape),
        ],
        out_specs=[block, block, whole(weights.shape), whole((8, channels))],
        out_shape=[
            jax.ShapeDtypeStruct((rows, channels), jnp.bfloat16),
            jax.ShapeDtypeStruct((rows, channels), jnp.bfloat16),
            jax.ShapeDtypeStruct(weights.shape, jnp.bfloat16),
            jax.ShapeDtypeStruct((8, channels), jnp.float32),
        ],
        scratch_shapes=[pltpu.VMEM(weights.shape, jnp.float32)],
        compiler_params=params_of(),
        name="mix_back",
    )(mix, y, gate, gain, weights)


def project_back_kernel(dgate_ref, drows_ref, hidden_ref, w_ref, part_ref, w_grad_ref, total):
    step = pl.program_id(0)

    @pl.when(step == 0)
    def _():
        total[...] = jnp.zeros_like(total)

    grads = jnp.concatenate([dgate_ref[...], drows_ref[...]], axis=1)
    part_ref[0] = to_low(dot_lanes(grads, w_ref[...]))
    total[...] += dot_rows(hidden_ref[...], grads)

    @pl.when(step == pl.num_programs(0) - 1)
    def _():
        w_grad_ref[...] = to_low(total[...])


def project_back(dgate, drows, hidden, weights, blocks):
    rows, width = hidden.shape
    tile = rows // blocks
    block = lambda extent: pl.BlockSpec((tile, extent), lambda step: (step, 0))
    return pl.pallas_call(
        project_back_kernel,
        grid=(blocks,),
        in_specs=[
            block(dgate.shape[1]),
            block(drows.shape[1]),
            block(width),
            whole(weights.shape),
        ],
        out_specs=[
            pl.BlockSpec((1, tile, width), lambda step: (step, 0, 0)),
            whole(weights.shape),
        ],
        out_shape=[
            jax.ShapeDtypeStruct((blocks, tile, width), jnp.bfloat16),
            jax.ShapeDtypeStruct(weights.shape, jnp.bfloat16),
        ],
        scratch_shapes=[pltpu.VMEM(weights.shape, jnp.float32)],
        compiler_params=params_of(),
        name="project_back",
    )(dgate, drows, hidden, weights)


def shared_kernel(
    rows_ref, grad_ref, up_ref, down_ref, res_ref, back_ref, up_grad_ref, down_grad_ref, up_sum, down_sum
):
    step = pl.program_id(0)

    @pl.when(step == 0)
    def _():
        up_sum[...] = jnp.zeros_like(up_sum)
        down_sum[...] = jnp.zeros_like(down_sum)

    width = grad_ref.shape[2]
    hidden = down_ref.shape[0]
    rows = rows_ref[0, :, :width]
    grad = grad_ref[0]
    joined = dot_full(rows, up_ref[...])
    gate, up = joined[:, :hidden], joined[:, hidden:]
    sig = jax.nn.sigmoid(gate)
    act = gate * sig
    acted = to_low(act * up)
    res_ref[0] = to_low(dot_full(acted, down_ref[...]))
    down_sum[...] += dot_rows(acted, grad)
    act_grad = dot_lanes(grad, down_ref[...])
    joined_grad = to_low(
        jnp.concatenate(
            [act_grad * up * sig * (1.0 + gate * (1.0 - sig)), act_grad * act], axis=1
        )
    )
    up_sum[...] += dot_rows(rows, joined_grad)
    back_ref[0] = to_low(dot_lanes(joined_grad, up_ref[...]))

    @pl.when(step == pl.num_programs(0) - 1)
    def _():
        up_grad_ref[...] = to_low(up_sum[...])
        down_grad_ref[...] = to_low(down_sum[...])


def shared_expert(rows, grad, up, down):
    blocks, tile, wide = rows.shape
    width = grad.shape[2]
    block = lambda extent: pl.BlockSpec((1, tile, extent), lambda step: (step, 0, 0))
    return pl.pallas_call(
        shared_kernel,
        grid=(blocks,),
        in_specs=[block(wide), block(width), whole(up.shape), whole(down.shape)],
        out_specs=[block(width), block(width), whole(up.shape), whole(down.shape)],
        out_shape=[
            jax.ShapeDtypeStruct((blocks, tile, width), jnp.bfloat16),
            jax.ShapeDtypeStruct((blocks, tile, width), jnp.bfloat16),
            jax.ShapeDtypeStruct(up.shape, jnp.bfloat16),
            jax.ShapeDtypeStruct(down.shape, jnp.bfloat16),
        ],
        scratch_shapes=[
            pltpu.VMEM(up.shape, jnp.float32),
            pltpu.VMEM(down.shape, jnp.float32),
        ],
        compiler_params=params_of(),
        name="shared_expert",
    )(rows, grad, up, down)


def dispatch_kernel(
    first_ref, rows_ref, grad_ref, x_ref, g_ref, picks_ref, *, top_count, slots
):
    per_device = x_ref.shape[0]
    tok_rows = rows_ref.shape[1]
    width = grad_ref.shape[2]
    block = rows_ref[0]
    extra = to_full(block[:, width:])
    lane = iota_of((tok_rows, LANES), 1)
    named = (lane >= 2 * top_count) & (lane < 3 * top_count)
    member = jnp.zeros((tok_rows, LANES), jnp.float32)
    for expert in range(per_device):
        own = to_full(first_ref[0] + expert)
        hit = jnp.sum(jnp.where(named & (extra == own), 1.0, 0.0), axis=1, keepdims=True)
        member = jnp.where(lane // slots == expert, hit, member)
    before = iota_of((tok_rows, tok_rows), 0) > iota_of((tok_rows, tok_rows), 1)
    ranks = dot_full(to_low(jnp.where(before, 1.0, 0.0)), to_low(member))
    picks = jnp.where(
        (ranks == to_full(lane % slots)) & (member > 0.0), 1.0, 0.0
    ).astype(jnp.bfloat16)
    picks_ref[0] = picks
    rows = to_low(dot_rows(picks, block))
    grads = to_low(dot_rows(picks, grad_ref[0]))
    for expert in range(per_device):
        x_ref[expert] = rows[expert * slots : (expert + 1) * slots]
        g_ref[expert] = grads[expert * slots : (expert + 1) * slots]


def dispatch(first, rows, grad, per_device, top_count, slots):
    blocks, tok_rows, wide = rows.shape
    width = grad.shape[2]
    block = lambda extent: pl.BlockSpec((1, tok_rows, extent), lambda step: (step, 0, 0))
    taken = lambda extent: pl.BlockSpec((per_device, slots, extent), lambda step: (0, step, 0))
    return pl.pallas_call(
        functools.partial(dispatch_kernel, top_count=top_count, slots=slots),
        grid=(blocks,),
        in_specs=[pl.BlockSpec(memory_space=pltpu.SMEM), block(wide), block(width)],
        out_specs=[taken(wide), taken(width), block(LANES)],
        out_shape=[
            jax.ShapeDtypeStruct((per_device, blocks * slots, wide), jnp.bfloat16),
            jax.ShapeDtypeStruct((per_device, blocks * slots, width), jnp.bfloat16),
            jax.ShapeDtypeStruct((blocks, tok_rows, LANES), jnp.bfloat16),
        ],
        compiler_params=params_of(),
        name="dispatch",
    )(first, rows, grad)


def experts_kernel(first_ref, place_ref, *refs, count, top_count):
    x_ref, g_ref = refs[:2]
    ups, downs = refs[2 : 2 + count], refs[2 + count : 2 + 2 * count]
    refs = refs[2 + 2 * count :]
    res_ref, dx_ref = refs[:2]
    up_outs, down_outs = refs[2 : 2 + count], refs[2 + count : 2 + 2 * count]
    up_held, down_held, up_sum, down_sum, up_low, down_low, up_sems, down_sems = refs[
        2 + 2 * count :
    ]
    expert, step = pl.program_id(0), pl.program_id(1)
    experts, steps = pl.num_programs(0), pl.num_programs(1)
    slot = lax.rem(expert, 2)
    width, double = up_held.shape[1:]
    hidden = double // 2
    tile = x_ref.shape[1]

    def spans(extent):
        piece = extent // count
        return [
            pl.ds(
                pl.multiple_of(lax.rem(place_ref[0] + count - shift, count) * piece, piece), piece
            )
            for shift in range(count)
        ]

    def fetch(which, into):
        copies = []
        for shift, span in enumerate(spans(width)):
            copies.append(
                pltpu.make_async_copy(
                    ups[shift].at[which], up_held.at[into, span], up_sems.at[into, shift]
                )
            )
        for shift, span in enumerate(spans(hidden)):
            copies.append(
                pltpu.make_async_copy(
                    downs[shift].at[which], down_held.at[into, span], down_sems.at[into, shift]
                )
            )
        return copies

    @pl.when(step == 0)
    def _():
        @pl.when(expert == 0)
        def _():
            for copy in fetch(expert, slot):
                copy.start()

        for copy in fetch(expert, slot):
            copy.wait()

        @pl.when(expert + 1 < experts)
        def _():
            for copy in fetch(expert + 1, 1 - slot):
                copy.start()

        up_sum[...] = jnp.zeros_like(up_sum)
        down_sum[...] = jnp.zeros_like(down_sum)

    up, down = up_held.at[slot], down_held.at[slot]
    rows = x_ref[0, :, :width]
    extra = to_full(x_ref[0, :, width:])
    lane = iota_of((tile, LANES), 1)
    own = first_ref[0] + expert
    hits = jnp.where((lane < 3 * top_count) & (extra == to_full(own)), 1.0, 0.0)
    gate_slot = jnp.zeros((tile, 1), jnp.float32)
    for route in range(top_count):
        place = 2 * top_count + route
        value = extra[:, 2 * route : 2 * route + 1] + extra[:, 2 * route + 1 : 2 * route + 2]
        gate_slot = gate_slot + hits[:, place : place + 1] * value
    joined = dot_full(rows, up[...])
    gate, lift = joined[:, :hidden], joined[:, hidden:]
    sig = jax.nn.sigmoid(gate)
    act = gate * sig
    acted = to_low(act * lift)
    res = to_low(dot_full(acted, down[...]))
    grads = g_ref[0]
    wide_grads = to_full(grads)
    wide_res = to_full(res)
    gate_grad = jnp.sum(wide_res * wide_grads, axis=1, keepdims=True)
    res_ref[0] = to_low(wide_res * gate_slot)
    weighted = to_low(wide_grads * gate_slot)
    act_grad = dot_lanes(weighted, down[...])
    down_sum[...] += dot_rows(acted, weighted)
    joined_grad = to_low(
        jnp.concatenate(
            [act_grad * lift * sig * (1.0 + gate * (1.0 - sig)), act_grad * act], axis=1
        )
    )
    dx_ref[0, :, :width] = to_low(dot_lanes(joined_grad, up[...]))
    high = to_full(to_low(gate_grad))
    half = LANES // 2
    dx_ref[0, :, width:] = to_low(
        jnp.where(lane == own, high, 0.0) + jnp.where(lane == own + half, gate_grad - high, 0.0)
    )
    up_sum[...] += dot_rows(rows, joined_grad)

    @pl.when(step == steps - 1)
    def _():
        up_low[...] = to_low(up_sum[...])
        down_low[...] = to_low(down_sum[...])
        copies = []
        for shift, span in enumerate(spans(width)):
            copies.append(
                pltpu.make_async_copy(
                    up_low.at[span], up_outs[shift].at[expert], up_sems.at[2, shift]
                )
            )
        for shift, span in enumerate(spans(hidden)):
            copies.append(
                pltpu.make_async_copy(
                    down_low.at[span], down_outs[shift].at[expert], down_sems.at[2, shift]
                )
            )
        for copy in copies:
            copy.start()
        for copy in copies:
            copy.wait()


def experts(first, place, x, g, ups, downs, top_count):
    per_device, rows, wide = x.shape
    width = g.shape[2]
    count = len(ups)
    double = ups[0].shape[2]
    hidden = double // 2
    tile = min(rows, 256)
    block = lambda extent: pl.BlockSpec((1, tile, extent), lambda e, step: (e, step, 0))
    anywhere = pl.BlockSpec(memory_space=pl.ANY)
    scalars = pl.BlockSpec(memory_space=pltpu.SMEM)
    low = jnp.bfloat16
    outs = pl.pallas_call(
        functools.partial(experts_kernel, count=count, top_count=top_count),
        grid=(per_device, rows // tile),
        in_specs=[scalars, scalars, block(wide), block(width)] + [anywhere] * (2 * count),
        out_specs=[block(width), block(wide)] + [anywhere] * (2 * count),
        out_shape=[
            jax.ShapeDtypeStruct((per_device, rows, width), low),
            jax.ShapeDtypeStruct((per_device, rows, wide), low),
        ]
        + [jax.ShapeDtypeStruct(piece.shape, low) for piece in list(ups) + list(downs)],
        scratch_shapes=[
            pltpu.VMEM((2, width, double), low),
            pltpu.VMEM((2, hidden, width), low),
            pltpu.VMEM((width, double), jnp.float32),
            pltpu.VMEM((hidden, width), jnp.float32),
            pltpu.VMEM((width, double), low),
            pltpu.VMEM((hidden, width), low),
            pltpu.SemaphoreType.DMA((3, count)),
            pltpu.SemaphoreType.DMA((3, count)),
        ],
        compiler_params=params_of(),
        name="experts",
    )(first, place, x, g, *ups, *downs)
    return outs[0], outs[1], outs[2 : 2 + count], outs[2 + count :]


def combine_kernel(place_ref, picks_ref, res_ref, dx_ref, sres_ref, sback_ref, out_ref, back_ref):
    step = pl.program_id(0)
    width = out_ref.shape[2]
    per_device, slots = res_ref.shape[:2]
    taken = per_device * slots
    picks = picks_ref[0, :, :taken]
    out = dot_full(picks, res_ref[...].reshape(taken, width))
    back = dot_full(picks, dx_ref[...].reshape(taken, width + LANES))
    out_ref[0] = to_low(out)
    back_ref[0] = to_low(back)

    @pl.when(lax.div(step, sres_ref.shape[0]) == place_ref[0])
    def _():
        block = lax.rem(step, sres_ref.shape[0])
        out_ref[0] = to_low(out + to_full(sres_ref[block]))
        back_ref[0, :, :width] = to_low(back[:, :width] + to_full(sback_ref[block]))


def combine(place, picks, res, dx, shared_res, shared_back):
    blocks, tok_rows, _ = picks.shape
    per_device, rows, width = res.shape
    slots = rows // blocks
    block = lambda extent: pl.BlockSpec((1, tok_rows, extent), lambda step: (step, 0, 0))
    taken = lambda extent: pl.BlockSpec((per_device, slots, extent), lambda step: (0, step, 0))
    return pl.pallas_call(
        combine_kernel,
        grid=(blocks,),
        in_specs=[
            pl.BlockSpec(memory_space=pltpu.SMEM),
            block(LANES),
            taken(width),
            taken(width + LANES),
            whole(shared_res.shape),
            whole(shared_back.shape),
        ],
        out_specs=[block(width), block(width + LANES)],
        out_shape=[
            jax.ShapeDtypeStruct((blocks, tok_rows, width), jnp.bfloat16),
            jax.ShapeDtypeStruct((blocks, tok_rows, width + LANES), jnp.bfloat16),
        ],
        compiler_params=params_of(),
        name="combine",
    )(place, picks, res, dx, shared_res, shared_back)


def gather_small(arrays):
    flat = jnp.concatenate([piece.reshape(-1) for piece in arrays])
    joined = lax.all_gather(flat, "shard")
    results, start = [], 0
    for piece in arrays:
        part = joined[:, start : start + piece.size]
        results.append(part.reshape((-1,) + piece.shape[1:]))
        start += piece.size
    return results


def rows_to_owner(shard_rows, part):
    seq_devices = lax.axis_size("seq")
    shard_devices = lax.axis_size("shard")
    rows, width = shard_rows.shape
    own_rows = rows * shard_devices // seq_devices
    halves = max(1, rows // own_rows)
    fine = rows // halves // seq_devices
    mine = lax.dynamic_index_in_dim(
        shard_rows.reshape(halves, seq_devices, fine, width), part, 1, keepdims=False
    )
    spread = lax.all_gather(mine, "shard").reshape(seq_devices, -1, width)
    return (
        lax.all_to_all(spread, "seq", split_axis=0, concat_axis=0, tiled=True)
        .reshape(seq_devices, own_rows // fine // seq_devices, fine, width)
        .transpose(1, 0, 2, 3)
        .reshape(own_rows, width)
    )


def rows_from_owner(own, part_rows):
    seq_devices = lax.axis_size("seq")
    shard_devices = lax.axis_size("shard")
    own_rows, width = own.shape
    halves = max(1, part_rows // own_rows)
    fine = part_rows // halves // seq_devices
    pieces = own.reshape(own_rows // fine // seq_devices, seq_devices, fine, width)
    pieces = pieces.transpose(1, 0, 2, 3).reshape(seq_devices, -1, width)
    spread = lax.all_to_all(pieces, "seq", split_axis=0, concat_axis=0, tiled=True)
    mine = lax.psum_scatter(
        spread.reshape(shard_devices, halves * fine, width), "shard", tiled=True
    )
    joined = lax.all_gather(mine.reshape(halves, fine, width), "seq", axis=1)
    return joined.reshape(part_rows, width)


def inner_groups(inner):
    count = lax.axis_size("shard")
    return [list(range(start, start + inner)) for start in range(0, count, inner)]


def outer_groups(inner):
    count = lax.axis_size("shard")
    return [list(range(start, count, inner)) for start in range(inner)]


def exchange(pieces, inner):
    received = [pieces[0]]
    for shift in range(1, inner):
        pairs = [
            (group[place], group[(place + shift) % inner])
            for group in inner_groups(inner)
            for place in range(inner)
        ]
        received.append(lax.ppermute(pieces[shift], "shard", pairs))
    return received


def by_place(received, place, inner):
    return jnp.stack(received)[lax.rem(place + inner - jnp.arange(inner), inner)]


def local(
    tokens,
    out_grad,
    deal_order,
    lengths,
    routes,
    norm_in,
    w_in,
    w_dt,
    conv_w,
    conv_b,
    dt_bias,
    a_log,
    d_skip,
    norm_gate,
    w_out,
    norm_moe,
    w_router,
    w_shared,
    w_shared_down,
    w_experts,
    w_experts_down,
):
    seq_devices = lax.axis_size("seq")
    shard_devices = lax.axis_size("shard")
    part = lax.axis_index("seq")
    shard = lax.axis_index("shard")
    inner = min(shard_devices, INNER)
    outer = shard_devices // inner
    place = lax.rem(shard, inner)
    residual = to_full(tokens[0])
    tok_rows, width = residual.shape
    group_rows = tok_rows * seq_devices
    inner_width = w_out.shape[0] * shard_devices
    channels = inner_width // seq_devices
    head_total = w_dt.shape[1]
    heads = head_total // seq_devices
    shared_width = w_shared_down.shape[0] * shard_devices
    shared_part = shared_width // seq_devices
    depth_rows = w_in.shape[0]
    expert_total = w_router.shape[1]
    local_experts, _, double = w_experts.shape
    hidden = double // 2
    hidden_rows = w_experts_down.shape[1]
    top_count = routes.shape[2]
    per_device = local_experts // inner
    blocks = inner * seq_devices

    def own_columns(array, start, extent):
        return lax.dynamic_slice_in_dim(array, start + part * extent, extent, 1)

    def own_rows(array, extent):
        return lax.dynamic_slice_in_dim(array, part * extent, extent, 0)

    x_group = gather_rows(tokens[0], 1, 1).reshape(group_rows, width)
    (
        gain_in,
        conv_weight,
        conv_bias,
        step_bias,
        decay_log,
        skip_gain,
        gain_gate,
        gain_moe,
        router,
    ) = gather_small(
        [norm_in, conv_w, conv_b, dt_bias, a_log, d_skip, norm_gate, norm_moe, w_router]
    )
    in_columns = jnp.concatenate(
        [
            own_columns(w_in, 0, channels),
            own_columns(w_in, inner_width, channels),
            w_in[:, 2 * inner_width :],
            own_columns(w_dt, 0, heads),
            jnp.zeros((depth_rows, LANES - heads), jnp.bfloat16),
        ],
        axis=1,
    )
    proj_in = lax.all_gather(in_columns, "shard", tiled=True)
    out_rows = rows_to_owner(w_out, part)
    shared_up = lax.all_gather(
        jnp.concatenate(
            [
                own_columns(w_shared, 0, shared_part),
                own_columns(w_shared, shared_width, shared_part),
            ],
            axis=1,
        ),
        "shard",
        tiled=True,
    )
    shared_down = rows_to_owner(w_shared_down, part)
    if outer == 1:
        grad_all = lax.all_gather(out_grad[0], ("shard", "seq"))
    else:
        grad_all = lax.all_gather(
            lax.all_gather(out_grad[0], "shard", axis_index_groups=inner_groups(inner)),
            "seq",
            axis=1,
        )
    grad_all = grad_all.reshape(blocks, tok_rows, width)

    def experts_of(array, shift):
        start = lax.rem(place + shift, inner) * per_device
        return lax.dynamic_slice_in_dim(array, start, per_device, 0)

    up_pieces = exchange([experts_of(w_experts, shift) for shift in range(inner)], inner)
    down_pieces = exchange([experts_of(w_experts_down, shift) for shift in range(inner)], inner)
    if outer > 1:

        def assembled(pieces):
            joined = lax.all_gather(
                by_place(pieces, place, inner), "shard", axis_index_groups=outer_groups(inner)
            )
            return [
                joined.transpose(2, 0, 1, 3, 4).reshape(per_device, -1, joined.shape[-1])
            ]

        up_pieces, down_pieces = assembled(up_pieces), assembled(down_pieces)

    gain_row = to_full(gain_in)[None]
    hidden_in, gate_in, rows_in = project(x_group, gain_row, proj_in, channels)
    ends = jnp.cumsum(lengths[0]).astype(jnp.int32)
    conv_part = jnp.concatenate(
        [own_rows(conv_weight, channels), conv_weight[inner_width:]], axis=0
    )
    bias_part = jnp.concatenate([own_rows(conv_bias, channels), conv_bias[inner_width:]], axis=0)
    conv_table = to_full(
        jnp.pad(jnp.concatenate([conv_part.T, bias_part[None]], axis=0), ((0, 3), (0, 0)))
    )
    head_table = jnp.pad(
        jnp.stack(
            [
                to_full(own_rows(step_bias, heads)),
                -jnp.exp(to_full(own_rows(decay_log, heads))),
                to_full(own_rows(skip_gain, heads)),
            ]
        ),
        ((0, 5), (0, LANES - heads)),
    )
    y, seq_rows, states = scan_forward(
        ends, deal_order, rows_in, conv_table, head_table, channels
    )
    gate_gain = to_full(own_rows(gain_gate, channels))[None]
    mixed = reduce_rows(mix_out(y, gate_in, gate_gain, out_rows, seq_devices)[None], 2)
    gate_scale = lax.rsqrt(
        (mixed[:, width : width + 1] + mixed[:, width + 1 : width + 2]) / inner_width + EPSILON
    )
    mix_sum = mixed[:, :width] * gate_scale
    after_mix = residual + mix_sum

    gain_moe = to_full(gain_moe)
    moe_scale = norm_scale(after_mix)
    moe_unit = after_mix * moe_scale
    moe_in = to_low(moe_unit * gain_moe)
    logits = matmul(moe_in, router)
    route_ids = routes[0]
    chosen = to_full(
        route_ids[:, :, None] == jnp.arange(expert_total, dtype=jnp.int32)[None, None, :]
    )
    gate_values = jax.nn.softmax(jnp.sum(chosen * logits[:, None, :], axis=2), axis=1)
    gate_high = to_low(gate_values)
    gate_rest = to_low(gate_values - to_full(gate_high))
    extra = jnp.concatenate(
        [
            jnp.stack([gate_high, gate_rest], axis=2).reshape(tok_rows, 2 * top_count),
            route_ids.astype(jnp.bfloat16),
            jnp.zeros((tok_rows, LANES - 3 * top_count), jnp.bfloat16),
        ],
        axis=1,
    )
    moe_all = gather_rows(jnp.concatenate([moe_in, extra], axis=1), inner, 3)
    moe_all = moe_all.reshape(blocks, tok_rows, width + LANES)
    moe_group = lax.dynamic_slice_in_dim(moe_all, place * seq_devices, seq_devices, 0)
    grad_group = lax.dynamic_slice_in_dim(grad_all, place * seq_devices, seq_devices, 0)
    shared_res, shared_back, shared_up_grad, shared_down_grad = shared_expert(
        moe_group, grad_group, shared_up, shared_down
    )
    capacity = min(tok_rows, max(2, tok_rows * top_count * 5 // (expert_total * 3)))
    slots = -(-capacity // 16) * 16
    first = (part * local_experts + place * per_device).astype(jnp.int32)[None]
    place_row = place.astype(jnp.int32)[None]
    expert_rows, grad_rows, picks = dispatch(
        first, moe_all, grad_all, per_device, top_count, slots
    )
    expert_res, expert_back, up_grads, down_grads = experts(
        first, place_row, expert_rows, grad_rows, up_pieces, down_pieces, top_count
    )
    out_part, back_part = combine(
        place_row, picks, expert_res, expert_back, shared_res, shared_back
    )
    back = reduce_rows(back_part.reshape(inner, seq_devices, tok_rows, -1), 4)
    if outer == 1:
        out_sum = lax.psum_scatter(
            out_part.reshape(blocks * tok_rows, width), ("shard", "seq"), tiled=True
        )
    else:
        out_sum = lax.psum_scatter(
            lax.psum_scatter(
                out_part.reshape(inner, seq_devices, tok_rows, width),
                "seq",
                scatter_dimension=1,
            ),
            "shard",
            axis_index_groups=inner_groups(inner),
        )
    layer_out = to_low(after_mix + to_full(out_sum))

    if outer > 1:

        def scattered(grads):
            full = grads[0]
            piece = full.shape[1] // shard_devices
            split = full.reshape(per_device, outer, inner, piece, full.shape[2])
            own = lax.psum_scatter(
                split.transpose(1, 2, 0, 3, 4),
                "shard",
                axis_index_groups=outer_groups(inner),
            )
            return [
                lax.dynamic_index_in_dim(own, lax.rem(place + shift, inner), 0, keepdims=False)
                for shift in range(inner)
            ]

        up_back, down_back = scattered(up_grads), scattered(down_grads)
    else:
        turned = lambda pieces: [pieces[(inner - shift) % inner] for shift in range(inner)]
        up_back, down_back = turned(up_grads), turned(down_grads)

    def whole_shard(pieces):
        received = by_place(exchange(pieces, inner), place, inner)
        return to_full(received.reshape((local_experts,) + received.shape[2:]))

    experts_grad = whole_shard(up_back)
    experts_down_grad = whole_shard(down_back)

    half = LANES // 2
    gate_grad_all = (
        back[:, width : width + expert_total]
        + back[:, width + half : width + half + expert_total]
    )
    gate_grad = jnp.sum(chosen * gate_grad_all[:, None, :], axis=2)
    mixed_gate = jnp.sum(gate_values * gate_grad, axis=1, keepdims=True)
    logit_grad = to_low(
        jnp.sum(chosen * (gate_values * (gate_grad - mixed_gate))[:, :, None], axis=1)
    )
    router_grad = left_contract(moe_in, logit_grad)
    moe_grad = back[:, :width] + right_contract(logit_grad, router)
    gain_moe_grad = jnp.sum(moe_grad * moe_unit, axis=0)
    moe_scaled = moe_grad * gain_moe
    mix_grad = to_full(out_grad[0]) + moe_scale * (
        moe_scaled - moe_unit * jnp.mean(moe_scaled * moe_unit, axis=1, keepdims=True)
    )
    mix_low = to_low(mix_grad)
    share = jnp.sum(to_full(mix_low) * mix_sum, axis=1, keepdims=True) / inner_width
    carried = put_split([share, gate_scale], tok_rows)

    mix_group = gather_rows(jnp.concatenate([mix_low, carried], axis=1), 1, 5)[0]
    dy, gate_in_grad, proj_out_grad, gain_gate_grad = mix_back(
        mix_group, y, gate_in, gate_gain, out_rows
    )
    rows_grad, conv_grad, head_grad = scan_backward(
        ends, deal_order, seq_rows, states, dy, conv_table, head_table
    )
    hidden_part, proj_in_grad = project_back(
        gate_in_grad, rows_grad, hidden_in, proj_in, seq_devices
    )
    hidden_grad = reduce_rows(hidden_part[None], 6)
    own_scale = norm_scale(residual)
    own_unit = residual * own_scale
    gain_in_grad = jnp.sum(hidden_grad * own_unit, axis=0)
    hidden_scaled = hidden_grad * gain_row
    tokens_grad = to_low(
        mix_grad
        + own_scale
        * (hidden_scaled - own_unit * jnp.mean(hidden_scaled * own_unit, axis=1, keepdims=True))
    )

    own_in_grad = lax.all_gather(
        lax.psum_scatter(proj_in_grad[:, : 2 * channels], "shard", tiled=True), "seq"
    )
    w_in_main = (
        own_in_grad.reshape(seq_devices, depth_rows, 2, channels)
        .transpose(1, 2, 0, 3)
        .reshape(depth_rows, 2 * inner_width)
    )
    own_shared_grad = lax.all_gather(
        lax.psum_scatter(shared_up_grad, "shard", tiled=True), "seq"
    )
    w_shared_grad = to_full(
        own_shared_grad.reshape(seq_devices, depth_rows, 2, shared_part)
        .transpose(1, 2, 0, 3)
        .reshape(depth_rows, 2 * shared_width)
    )
    w_out_grad = to_full(rows_from_owner(proj_out_grad, w_out.shape[0]))
    w_shared_down_grad = to_full(rows_from_owner(shared_down_grad, w_shared_down.shape[0]))

    def spread(values, length, axis=0):
        shape = values.shape[:axis] + (length,) + values.shape[axis + 1 :]
        return lax.dynamic_update_slice_in_dim(
            jnp.zeros(shape, values.dtype), values, part * values.shape[axis], axis
        )

    conv_rows_grad = conv_grad[:5].T
    conv_full = jnp.concatenate(
        [spread(conv_rows_grad[:channels], inner_width), conv_rows_grad[channels:]], axis=0
    )
    small = [
        gain_in_grad,
        spread(proj_in_grad[:, -LANES:][:, :heads], head_total, 1),
        conv_full[:, :4],
        conv_full[:, 4],
        spread(head_grad[0, :heads], head_total),
        spread(head_grad[1, :heads], head_total),
        spread(head_grad[2, :heads], head_total),
        spread(gain_gate_grad[0], inner_width),
        gain_moe_grad,
        router_grad,
        proj_in_grad[:, 2 * channels : -LANES],
    ]
    shapes = [(piece.shape[0] // shard_devices,) + piece.shape[1:] for piece in small]
    packed = jnp.concatenate(
        [to_low(piece).reshape(shard_devices, -1) for piece in small], axis=1
    )
    summed = lax.psum(lax.psum_scatter(packed, "shard", tiled=True), "seq").reshape(-1)
    results, start = [], 0
    for shape in shapes:
        size = 1
        for extent in shape:
            size *= extent
        results.append(to_full(summed[start : start + size]).reshape(shape))
        start += size
    w_in_grad = jnp.concatenate([to_full(w_in_main), results[10]], axis=1)
    return (
        layer_out[None],
        tokens_grad[None],
        results[0],
        w_in_grad,
        results[1],
        results[2],
        results[3],
        results[4],
        results[5],
        results[6],
        results[7],
        w_out_grad,
        results[8],
        results[9],
        w_shared_grad,
        w_shared_down_grad,
        experts_grad,
        experts_down_grad,
    )


def solution(mesh):
    placed = (
        P("shard", "seq", None),
        P("shard", "seq", None),
        P("shard", None),
        P("shard", None),
        P("shard", "seq", None),
        P("shard"),
        P("shard", None),
        P("shard", None),
        P("shard", None),
        P("shard"),
        P("shard"),
        P("shard"),
        P("shard"),
        P("shard"),
        P("shard", None),
        P("shard"),
        P("shard", None),
        P("shard", None),
        P("shard", None),
        P("seq", "shard", None),
        P("seq", "shard", None),
    )
    return jax.shard_map(
        local,
        mesh=mesh,
        in_specs=placed,
        out_specs=(
            P("shard", "seq", None),
            P("shard", "seq", None),
            P("shard"),
            P("shard", None),
            P("shard", None),
            P("shard", None),
            P("shard"),
            P("shard"),
            P("shard"),
            P("shard"),
            P("shard"),
            P("shard", None),
            P("shard"),
            P("shard", None),
            P("shard", None),
            P("shard", None),
            P("seq", "shard", None),
            P("seq", "shard", None),
        ),
        check_vma=False,
    )
```

```python
import functools

import jax
import jax.numpy as jnp
from jax import lax
from jax.experimental import pallas as pl
from jax.experimental.pallas import tpu as pltpu
from jax.sharding import PartitionSpec as P

STRETCH = 256
INNER = 4
EPSILON = 1e-05
HIGHEST = lax.Precision.HIGHEST


def matmul(left_side, right_side):
    return jnp.dot(left_side, right_side, preferred_element_type=jnp.float32)


def left_contract(left_side, right_side):
    return lax.dot_general(
        left_side, right_side, (((0,), (0,)), ((), ())), preferred_element_type=jnp.float32
    )


def right_contract(left_side, right_side):
    return lax.dot_general(
        left_side, right_side, (((1,), (1,)), ((), ())), preferred_element_type=jnp.float32
    )


def to_low(values):
    return values.astype(jnp.bfloat16)


def to_full(values):
    return values.astype(jnp.float32)


def norm_scale(values):
    return lax.rsqrt(jnp.mean(values * values, axis=-1, keepdims=True) + EPSILON)


LANES = 128
VMEM_BYTES = 56 * 1024 * 1024


def cost_of(micros):
    return pl.CostEstimate(flops=0, transcendentals=0, bytes_accessed=int(micros * 3.6e6))


def dot_rows(left_side, right_side, precision=None):
    return lax.dot_general(
        left_side,
        right_side,
        (((0,), (0,)), ((), ())),
        precision=precision,
        preferred_element_type=jnp.float32,
    )


def dot_lanes(left_side, right_side, precision=None):
    return lax.dot_general(
        left_side,
        right_side,
        (((1,), (1,)), ((), ())),
        precision=precision,
        preferred_element_type=jnp.float32,
    )


def dot_full(left_side, right_side, precision=None):
    return jnp.dot(
        left_side, right_side, precision=precision, preferred_element_type=jnp.float32
    )


def iota_of(shape, axis):
    return lax.broadcasted_iota(jnp.int32, shape, axis)


def ids_at(places, ends_ref):
    total = jnp.zeros(places.shape, jnp.int32)
    for seq in range(ends_ref.shape[0]):
        total = total + (places >= ends_ref[seq]).astype(jnp.int32)
    return total


def id_at(place, ends_ref):
    total = jnp.int32(0)
    for seq in range(ends_ref.shape[0]):
        total = total + (place >= ends_ref[seq]).astype(jnp.int32)
    return total


class Stretch:
    def __init__(self, start, rows, before, conv_ref, head_ref, ends_ref, channels):
        length = rows.shape[0]
        self.channels = channels
        self.heads = channels // 64
        width = conv_ref.shape[1]
        state = (width - channels) // 2
        places = start + iota_of((length, 1), 0)
        self.ids = ids_at(places, ends_ref)
        self.ids_row = ids_at(start + iota_of((1, length), 1), ends_ref)
        inputs = rows[:, :width]
        joined = jnp.concatenate([before[:, :width], inputs], axis=0)
        self.shifted = [inputs]
        value = conv_ref[4:5, :] + inputs * conv_ref[3:4, :]
        for offset in range(1, 4):
            same = (ids_at(places - offset, ends_ref) == self.ids) & (places >= offset)
            moved = pltpu.roll(joined, offset, 0)[8:, :]
            moved = jnp.where(same, moved, 0.0)
            self.shifted.append(moved)
            value = value + moved * conv_ref[3 - offset : 4 - offset, :]
        self.value = value
        self.sig = jax.nn.sigmoid(value)
        act = value * self.sig
        self.x = act[:, :channels]
        self.b = act[:, channels : channels + state]
        self.c = act[:, channels + state :]
        self.b_low = to_low(self.b)
        self.c_low = to_low(self.c)
        self.dt_in = rows[:, width:] + head_ref[0:1, :]
        self.dt = jnp.maximum(self.dt_in, 0.0) + jnp.log1p(jnp.exp(-jnp.abs(self.dt_in)))
        self.rate = head_ref[1:2, :]
        rows_at = iota_of((length, length), 0)
        columns_at = iota_of((length, length), 1)
        lower = (rows_at >= columns_at).astype(jnp.float32)
        self.cum = dot_full(lower, self.dt * self.rate, HIGHEST)
        self.cum_rows = self.cum.T[:8, :]
        self.dt_rows = self.dt.T[:8, :]
        self.causal = (self.ids == self.ids_row) & (rows_at >= columns_at)
        self.scores = dot_lanes(self.c_low, self.b_low)
        last_id = jnp.where(start > 0, id_at(start - 1, ends_ref), -1)
        end_id = id_at(start + length - 1, ends_ref)
        self.enter = jnp.where(self.ids == last_id, jnp.exp(self.cum), 0.0)
        end_cum = self.cum[length - 1 : length, :]
        self.tail = jnp.where(self.ids == end_id, jnp.exp(end_cum - self.cum), 0.0)
        self.tail_weight = self.tail * self.dt
        self.keep = jnp.where(last_id == end_id, jnp.exp(end_cum), 0.0)

    def decay(self, head):
        spread = self.cum[:, head : head + 1] - self.cum_rows[head : head + 1, :]
        return jnp.where(self.causal, jnp.exp(jnp.minimum(spread, 0.0)), 0.0)

    def per_channel(self, by_head):
        return jnp.concatenate(
            [
                jnp.broadcast_to(by_head[:, head : head + 1], (by_head.shape[0], 64))
                for head in range(self.heads)
            ],
            axis=1,
        )

    def state_keep(self):
        return jnp.concatenate(
            [
                jnp.broadcast_to(self.keep[:, head : head + 1], (64, LANES))
                for head in range(self.heads)
            ],
            axis=0,
        )


def head_lanes(channels):
    return (iota_of((channels, LANES), 0) // 64 == iota_of((channels, LANES), 1)).astype(
        jnp.float32
    )


def pick_rows(deal_ref, start, length):
    places = start + iota_of((length, 1), 0)
    return jnp.where(deal_ref[...] == places, 1.0, 0.0).astype(jnp.bfloat16)


def scan_forward_kernel(
    ends_ref, deal_ref, rows_ref, conv_ref, head_ref, y_ref, seq_ref, states_ref, before, state, total
):
    step = pl.program_id(0)
    length = seq_ref.shape[0]
    channels = y_ref.shape[1]
    start = step * length

    @pl.when(step == 0)
    def _():
        before[...] = jnp.zeros_like(before)
        state[...] = jnp.zeros_like(state)
        total[...] = jnp.zeros_like(total)

    picks = pick_rows(deal_ref, start, length)
    rows = dot_full(picks, rows_ref[...])
    seq_ref[...] = to_low(rows)
    part = Stretch(start, rows, before[...], conv_ref, head_ref, ends_ref, channels)
    before[...] = rows[length - 8 :, :]
    state_now = state[...]
    states_ref[0] = state_now
    x_low = to_low(part.x)
    outs = []
    lane = iota_of((length, LANES), 1)
    for pair in range(channels // LANES):
        x_pair = x_low[:, pair * LANES : (pair + 1) * LANES]
        halves = []
        for head in (2 * pair, 2 * pair + 1):
            weights = part.decay(head) * part.scores * part.dt_rows[head : head + 1, :]
            halves.append(dot_full(to_low(weights), x_pair))
        outs.append(jnp.where(lane < 64, halves[0], halves[1]))
    earlier = dot_lanes(part.c_low, to_low(state_now))
    skip = part.per_channel(head_ref[2:3, :])
    y = jnp.concatenate(outs, axis=1) + part.per_channel(part.enter) * earlier + skip * part.x
    state[...] = part.state_keep() * state_now + dot_rows(
        to_low(part.per_channel(part.tail_weight) * part.x), part.b_low
    )
    total[...] += dot_rows(picks, to_low(y))

    @pl.when(step == pl.num_programs(0) - 1)
    def _():
        y_ref[...] = to_low(total[...])


def scan_forward(ends, deal_row, rows, conv_table, head_table, channels, freight):
    group_rows, width = rows.shape
    steps = group_rows // STRETCH
    state_rows = (channels, LANES)
    return run(
        scan_forward_kernel,
        (ends, deal_row, rows, conv_table, head_table),
        grid=(steps,),
        in_specs=[
            pl.BlockSpec(memory_space=pltpu.SMEM),
            whole(deal_row.shape),
            whole(rows.shape),
            whole(conv_table.shape),
            whole(head_table.shape),
        ],
        out_specs=[
            whole((group_rows, channels)),
            pl.BlockSpec((STRETCH, width), lambda step: (step, 0)),
            pl.BlockSpec((1,) + state_rows, lambda step: (step, 0, 0)),
        ],
        out_shape=[
            jax.ShapeDtypeStruct((group_rows, channels), jnp.bfloat16),
            jax.ShapeDtypeStruct((group_rows, width), jnp.bfloat16),
            jax.ShapeDtypeStruct((steps,) + state_rows, jnp.float32),
        ],
        scratch=[
            pltpu.VMEM((8, width), jnp.float32),
            pltpu.VMEM(state_rows, jnp.float32),
            pltpu.VMEM((group_rows, channels), jnp.float32),
        ],
        freight=freight,
        micros=25,
        name="scan_forward",
    )


def scan_backward_kernel(
    ends_ref,
    deal_ref,
    seq_ref,
    states_ref,
    dy_ref,
    conv_ref,
    head_ref,
    drows_ref,
    conv_grad_ref,
    head_grad_ref,
    after,
    state_grad,
    total,
):
    order = pl.program_id(0)
    steps = pl.num_programs(0)
    step = steps - 1 - order
    length = STRETCH
    channels = dy_ref.shape[1]
    width = conv_ref.shape[1]
    state_width = (width - channels) // 2
    start = pl.multiple_of(step * length, length)

    @pl.when(order == 0)
    def _():
        after[...] = jnp.zeros_like(after)
        state_grad[...] = jnp.zeros_like(state_grad)
        total[...] = jnp.zeros_like(total)
        conv_grad_ref[...] = jnp.zeros_like(conv_grad_ref)
        head_grad_ref[...] = jnp.zeros_like(head_grad_ref)

    picks = pick_rows(deal_ref, start, length)
    dy = dot_full(picks, dy_ref[...])
    rows = seq_ref[pl.ds(start, length), :].astype(jnp.float32)
    place = pl.multiple_of(jnp.maximum(start - 16, 0), 16)
    before = seq_ref[pl.ds(place, 16), :].astype(jnp.float32)[8:, :]
    part = Stretch(start, rows, before, conv_ref, head_ref, ends_ref, channels)
    state_now = states_ref[0]
    state_low = to_low(state_now)
    next_grad = state_grad[...]
    next_low = to_low(next_grad)
    lanes_of = head_lanes(channels)
    x_low = to_low(part.x)
    dy_low = to_low(dy)
    lane = iota_of((length, LANES), 1)

    enter = part.per_channel(part.enter)
    tail_weight = part.per_channel(part.tail_weight)
    earlier = dot_lanes(part.c_low, state_low)
    enter_grad = dot_full(dy * earlier, lanes_of, HIGHEST)
    entered = to_low(enter * dy)
    c_grad = dot_full(entered, state_low)
    state_grad[...] = part.state_keep() * next_grad + dot_rows(entered, part.c_low)
    onward = dot_lanes(part.b_low, next_low)
    x_grad = part.per_channel(head_ref[2:3, :]) * dy + tail_weight * onward
    tail_grad = dot_full(part.x * onward, lanes_of, HIGHEST)
    b_grad = dot_full(to_low(tail_weight * part.x), next_low)
    tail_part = tail_grad * part.tail_weight
    cum_grad = enter_grad * part.enter - tail_part
    dt_grad = tail_grad * part.tail
    kept = dot_lanes(jnp.ones((8, LANES), jnp.float32), next_grad * state_now, HIGHEST)
    keep_grad = dot_full(kept, lanes_of, HIGHEST)[:1, :]
    end_grad = jnp.sum(tail_part, axis=0, keepdims=True) + keep_grad * part.keep

    score_grad = jnp.zeros((length, length), jnp.float32)
    cum_columns, cum_rows, dt_rows, outs = [], [], [], []
    for pair in range(channels // LANES):
        x_pair = x_low[:, pair * LANES : (pair + 1) * LANES]
        dy_pair = dy_low[:, pair * LANES : (pair + 1) * LANES]
        halves = []
        for half, head in enumerate((2 * pair, 2 * pair + 1)):
            mine = (lane < 64) if half == 0 else (lane >= 64)
            weight_grad = dot_lanes(jnp.where(mine, dy_pair, jnp.zeros_like(dy_pair)), x_pair)
            decay = part.decay(head)
            dt_row = part.dt_rows[head : head + 1, :]
            by_decay = weight_grad * decay
            by_dt = by_decay * part.scores
            by_spread = by_dt * dt_row
            dt_rows.append(jnp.sum(by_dt, axis=0, keepdims=True))
            cum_rows.append(jnp.sum(by_spread, axis=0, keepdims=True))
            cum_columns.append(jnp.sum(by_spread, axis=1, keepdims=True))
            score_grad = score_grad + by_decay * dt_row
            halves.append(dot_rows(to_low(decay * part.scores * dt_row), dy_pair))
        outs.append(jnp.where(lane < 64, halves[0], halves[1]))
    x_grad = x_grad + jnp.concatenate(outs, axis=1)
    score_low = to_low(score_grad)
    c_grad = c_grad + dot_full(score_low, part.b_low)
    b_grad = b_grad + dot_rows(score_low, part.c_low)

    heads = len(dt_rows)
    blank = jnp.zeros((LANES - heads, length), jnp.float32)
    dt_grad = dt_grad + jnp.concatenate(dt_rows + [blank], axis=0).T
    cum_grad = cum_grad - jnp.concatenate(cum_rows + [blank], axis=0).T
    for head in range(heads):
        cum_grad = cum_grad + jnp.where(lane == head, cum_columns[head], 0.0)
    at_end = iota_of((length, 1), 0) == length - 1
    cum_grad = cum_grad + jnp.where(at_end, end_grad, 0.0)
    upper = (iota_of((length, length), 1) >= iota_of((length, length), 0)).astype(jnp.float32)
    log_grad = dot_full(upper, cum_grad, HIGHEST)
    dt_grad = dt_grad + log_grad * part.rate
    dt_in_grad = dt_grad * jax.nn.sigmoid(part.dt_in)
    dt_in_grad = jnp.where(lane < heads, dt_in_grad, 0.0)
    head_grad_ref[0:1, :] += jnp.sum(dt_in_grad, axis=0, keepdims=True)
    head_grad_ref[1:2, :] += jnp.sum(log_grad * part.dt, axis=0, keepdims=True) * part.rate
    skip_sum = jnp.broadcast_to(jnp.sum(dy * part.x, axis=0, keepdims=True), (8, channels))
    head_grad_ref[2:3, :] += dot_full(skip_sum, lanes_of, HIGHEST)[:1, :]

    act_grad = jnp.concatenate([x_grad, b_grad, c_grad], axis=1)
    value_grad = act_grad * part.sig * (1.0 + part.value * (1.0 - part.sig))
    conv_grad_ref[4:5, :] += jnp.sum(value_grad, axis=0, keepdims=True)
    for offset in range(4):
        conv_grad_ref[3 - offset : 4 - offset, :] += jnp.sum(
            value_grad * part.shifted[offset], axis=0, keepdims=True
        )
    joined = jnp.concatenate([value_grad, after[...]], axis=0)
    places = start + iota_of((length, 1), 0)
    rows_grad = value_grad * conv_ref[3:4, :]
    for offset in range(1, 4):
        moved = pltpu.roll(joined, length + 8 - offset, 0)[:length, :]
        same = (ids_at(places + offset, ends_ref) == part.ids) & (
            places + offset < steps * length
        )
        rows_grad = rows_grad + jnp.where(same, moved, 0.0) * conv_ref[3 - offset : 4 - offset, :]
    after[...] = value_grad[:8, :]
    total[...] += dot_rows(picks, to_low(jnp.concatenate([rows_grad, dt_in_grad], axis=1)))

    @pl.when(order == steps - 1)
    def _():
        drows_ref[...] = to_low(total[...])


def scan_backward(ends, deal_row, seq_rows, states, dy, conv_table, head_table, freight):
    group_rows, width = seq_rows.shape
    channels = dy.shape[1]
    steps = group_rows // STRETCH
    return run(
        scan_backward_kernel,
        (ends, deal_row, seq_rows, states, dy, conv_table, head_table),
        grid=(steps,),
        in_specs=[
            pl.BlockSpec(memory_space=pltpu.SMEM),
            whole(deal_row.shape),
            whole(seq_rows.shape),
            pl.BlockSpec((1, channels, LANES), lambda step: (steps - 1 - step, 0, 0)),
            whole(dy.shape),
            whole(conv_table.shape),
            whole(head_table.shape),
        ],
        out_specs=[
            whole((group_rows, width)),
            whole(conv_table.shape),
            whole(head_table.shape),
        ],
        out_shape=[
            jax.ShapeDtypeStruct((group_rows, width), jnp.bfloat16),
            jax.ShapeDtypeStruct(conv_table.shape, jnp.float32),
            jax.ShapeDtypeStruct(head_table.shape, jnp.float32),
        ],
        scratch=[
            pltpu.VMEM((8, conv_table.shape[1]), jnp.float32),
            pltpu.VMEM((channels, LANES), jnp.float32),
            pltpu.VMEM((group_rows, width), jnp.float32),
        ],
        freight=freight,
        micros=40,
        name="scan_backward",
    )


def whole(shape):
    return pl.BlockSpec(shape, lambda *steps: (0,) * len(shape))


MESH = pl.DeviceIdType.MESH
FLIPS = (1, 2, 4)


def flipped(place, flip):
    result = place
    for bit in FLIPS:
        if flip & bit:
            result = result + bit - 2 * bit * lax.rem(lax.div(place, bit), 2)
    return result


def own_shard_group(inner):
    shard = lax.axis_index("shard")
    place = lax.rem(shard, inner)
    return place, shard - place


def peers_in_order(place, inner):
    if inner == 1:
        return []
    if inner == 4:
        half = lax.div(place, 2)
        return [flipped(place, 1), 2 - half, 3 - 3 * half]
    return [lax.rem(place + shift, inner) for shift in range(1, inner)]


def greet(flips, inner):
    barrier = pltpu.get_barrier_semaphore()
    part = lax.axis_index("seq")
    place, first = own_shard_group(inner)
    for flip in flips:
        pl.semaphore_signal(
            barrier, inc=1, device_id={"seq": flipped(part, flip)}, device_id_type=MESH
        )
    for peer in peers_in_order(place, inner):
        pl.semaphore_signal(
            barrier, inc=1, device_id={"shard": first + peer}, device_id_type=MESH
        )
    pl.semaphore_wait(barrier, len(flips) + inner - 1)


class Parcel:
    flips = ()

    def __init__(self, array, shift, inner):
        self.array, self.shift, self.inner = array, shift, inner
        self.sems = 1

    def moves(self, source, target):
        place, first = own_shard_group(self.inner)
        to = lax.rem(place + self.shift, self.inner)
        return [(source, target, target, {"shard": first + to})]

    def stays(self, source, target):
        return []


class PlaneSwap:
    flips = (1, 2, 3, 4, 5, 6, 7)
    inner = 1
    sems = 8

    def __init__(self, array):
        self.array = array

    def moves(self, source, target):
        part = lax.axis_index("seq")
        return [
            (
                source.at[flipped(part, flip)],
                target.at[part],
                target.at[flipped(part, flip)],
                {"seq": flipped(part, flip)},
            )
            for flip in self.flips
        ]

    def stays(self, source, target):
        part = lax.axis_index("seq")
        return [(source.at[part], target.at[part])]


COLLECTIVES = []


def run(
    kernel,
    args,
    *,
    in_specs,
    out_specs,
    out_shape,
    name,
    micros,
    grid=(),
    scratch=(),
    freight=(),
    flips=(),
    inner=1,
):
    freight = list(freight)
    flips = tuple(sorted(set(flips).union(*[item.flips for item in freight])))
    inner = max([inner] + [item.inner for item in freight])
    talks = bool(flips) or inner > 1
    count_in, count_out, count_scratch = len(args), len(out_shape), len(scratch)
    count = len(freight)

    def wrapped(*refs):
        ins, refs = refs[:count_in], refs[count_in:]
        sources, refs = refs[:count], refs[count:]
        outs, refs = refs[:count_out], refs[count_out:]
        targets, refs = refs[:count], refs[count:]
        own, refs = refs[:count_scratch], refs[count_scratch:]

        def remote(item, place, order, source, target, device):
            send, recv = refs[3 * place : 3 * place + 2]
            return pltpu.make_async_remote_copy(
                src_ref=source,
                dst_ref=target,
                send_sem=send.at[order],
                recv_sem=recv.at[order],
                device_id=device,
                device_id_type=MESH,
            )

        def moves():
            for place, item in enumerate(freight):
                for order, move in enumerate(item.moves(sources[place], targets[place])):
                    yield item, place, order, move

        def stays():
            for place, item in enumerate(freight):
                for source, target in item.stays(sources[place], targets[place]):
                    yield pltpu.make_async_copy(source, target, refs[3 * place + 2])

        def depart():
            if talks:
                greet(flips, inner)
            for item, place, order, (source, target, _, device) in moves():
                remote(item, place, order, source, target, device).start()
            for copy in stays():
                copy.start()

        def arrive():
            for item, place, order, (source, target, arrival, device) in moves():
                remote(item, place, order, source, arrival, device).wait_recv()
                remote(item, place, order, source, target, device).wait_send()
            for copy in stays():
                copy.wait()

        if grid:
            at = [pl.program_id(axis) for axis in range(len(grid))]
            first, last = at[0] == 0, at[0] == grid[0] - 1
            for axis in range(1, len(grid)):
                first = first & (at[axis] == 0)
                last = last & (at[axis] == grid[axis] - 1)
            if talks:
                pl.when(first)(depart)
            kernel(*ins, *outs, *own)
            if talks:
                pl.when(last)(arrive)
        else:
            depart()
            kernel(*ins, *outs, *own)
            arrive()

    anywhere = pl.BlockSpec(memory_space=pl.ANY)
    extra = {}
    if talks:
        COLLECTIVES.append(name)
        extra = dict(collective_id=len(COLLECTIVES), has_side_effects=True)
    sems = []
    for item in freight:
        sems += [
            pltpu.SemaphoreType.DMA((item.sems,)),
            pltpu.SemaphoreType.DMA((item.sems,)),
            pltpu.SemaphoreType.DMA(()),
        ]
    results = pl.pallas_call(
        wrapped,
        grid=grid,
        in_specs=list(in_specs) + [anywhere] * count,
        out_specs=list(out_specs) + [anywhere] * count,
        out_shape=list(out_shape)
        + [jax.ShapeDtypeStruct(item.array.shape, item.array.dtype) for item in freight],
        scratch_shapes=list(scratch) + sems,
        compiler_params=pltpu.CompilerParams(vmem_limit_bytes=VMEM_BYTES, **extra),
        cost_estimate=cost_of(micros),
        name=name,
    )(*args, *[item.array for item in freight])
    results = list(results)
    if freight:
        return results[:count_out] + [results[count_out:]]
    return results


def gather_kernel(inner, x_ref, out_ref, own_sem, zsend, zrecv, send, recv):
    part = lax.axis_index("seq")
    place, first = own_shard_group(inner)
    rows = x_ref.shape[0]
    half = rows // 2
    spans = [pl.ds(0, half), pl.ds(half, half)]
    others = peers_in_order(place, inner)
    sources = [place] + others
    own = pltpu.make_async_copy(x_ref, out_ref.at[place, part], own_sem)
    own.start()
    across = []
    for order, peer in enumerate(others):
        copy = pltpu.make_async_remote_copy(
            src_ref=x_ref,
            dst_ref=out_ref.at[place, part],
            send_sem=zsend.at[order],
            recv_sem=zrecv.at[place],
            device_id={"shard": first + peer},
            device_id_type=MESH,
        )
        copy.start()
        across.append(copy)

    def copy_of(order, kind, block, span, flip, from_input=False):
        whole = out_ref.at[sources[order], block, spans[span]]
        return pltpu.make_async_remote_copy(
            src_ref=x_ref.at[spans[span]] if from_input else whole,
            dst_ref=whole,
            send_sem=send.at[order, kind],
            recv_sem=recv.at[order, kind],
            device_id={"seq": flipped(part, flip)},
            device_id_type=MESH,
        )

    started = []

    def push(order, kind, block, span, flip, from_input=False):
        copy = copy_of(order, kind, block, span, flip, from_input)
        copy.start()
        started.append(copy)

    def arrived(order, kind, block, span, flip):
        copy_of(order, kind, block, span, flip).wait_recv()

    def stage_a(order):
        if order:
            arrive = pltpu.make_async_remote_copy(
                src_ref=x_ref,
                dst_ref=out_ref.at[sources[order], part],
                send_sem=zsend.at[order - 1],
                recv_sem=zrecv.at[sources[order]],
                device_id={"shard": first + sources[order]},
                device_id_type=MESH,
            )
            arrive.wait_recv()
        direct = order == 0
        push(order, 3, part, 1, 2, direct)
        push(order, 4, part, 0, 4, direct)
        push(order, 2, part, 0, 2, direct)
        push(order, 5, part, 1, 4, direct)
        push(order, 0, part, 0, 1, direct)
        push(order, 1, part, 1, 1, direct)

    def stage_b(order):
        side, over = flipped(part, 2), flipped(part, 4)
        arrived(order, 3, side, 1, 2)
        push(order, 6, side, 1, 4)
        arrived(order, 4, over, 0, 4)
        push(order, 7, over, 0, 2)
        push(order, 9, side, 1, 1)
        push(order, 10, over, 0, 1)
        arrived(order, 2, side, 0, 2)
        push(order, 8, side, 0, 1)
        arrived(order, 5, over, 1, 4)
        push(order, 11, over, 1, 1)

    def stage_c(order):
        far = flipped(part, 6)
        arrived(order, 6, far, 1, 4)
        push(order, 13, far, 1, 1)
        arrived(order, 7, far, 0, 2)
        push(order, 12, far, 0, 1)

    def stage_d(order):
        for kind, flip, span in (
            (0, 1, 0),
            (1, 1, 1),
            (9, 3, 1),
            (10, 5, 0),
            (8, 3, 0),
            (11, 5, 1),
            (13, 7, 1),
            (12, 7, 0),
        ):
            arrived(order, kind, flipped(part, flip), span, 1)

    count = len(sources)
    stage_a(0)
    stage_b(0)
    for order in range(1, count):
        stage_a(order)
        stage_c(order - 1)
        stage_b(order)
    stage_c(count - 1)
    for order in range(count):
        stage_d(order)
    for copy in started:
        copy.wait_send()
    for copy in across:
        copy.wait_send()
    own.wait()


def gather_rows(x, inner, freight=()):
    rows, width = x.shape
    seq_devices = lax.axis_size("seq")
    return run(
        functools.partial(gather_kernel, inner),
        (x,),
        in_specs=[pl.BlockSpec(memory_space=pl.ANY)],
        out_specs=[pl.BlockSpec(memory_space=pl.ANY)],
        out_shape=[jax.ShapeDtypeStruct((inner, seq_devices, rows, width), x.dtype)],
        scratch=[
            pltpu.SemaphoreType.DMA(()),
            pltpu.SemaphoreType.DMA((max(1, inner - 1),)),
            pltpu.SemaphoreType.DMA((inner,)),
            pltpu.SemaphoreType.DMA((inner, 14)),
            pltpu.SemaphoreType.DMA((inner, 14)),
        ],
        freight=freight,
        flips=FLIPS,
        inner=inner,
        micros=25 * inner,
        name="gather_rows",
    )


def reduce_body(
    inner,
    p_ref,
    held,
    paired,
    turned,
    crossed,
    sums,
    summed,
    load,
    core_send,
    core_recv,
    turn_send,
    turn_recv,
    cross_send,
    cross_recv,
    zsend,
    zrecv,
):
    part = lax.axis_index("seq")
    place, first = own_shard_group(inner)
    rows = held.shape[2]
    half = rows // 2
    spans = [pl.ds(0, half), pl.ds(half, half)]
    targets = list(reversed(peers_in_order(place, inner))) + [place]
    evens = (6, 2, 4, 0)
    loads, cores = {}, {}
    for order, target in enumerate(targets):
        for slot, flip in enumerate(evens):
            copy = pltpu.make_async_remote_copy(
                src_ref=p_ref.at[target, flipped(part, flip + 1)],
                dst_ref=paired.at[order, slot],
                send_sem=core_send.at[order, slot],
                recv_sem=core_recv.at[order, slot],
                device_id={"seq": flipped(part, 1)},
                device_id_type=MESH,
            )
            copy.start()
            cores[order, slot] = copy
            copy = pltpu.make_async_copy(
                p_ref.at[target, flipped(part, flip)], held.at[order, slot], load.at[order, slot]
            )
            copy.start()
            loads[order, slot] = copy

    def total_of(order, slot):
        loads[order, slot].wait()
        cores[order, slot].wait_recv()
        return to_full(held[order, slot]) + to_full(paired[order, slot])

    sends = []

    def push(source, target, send_sem, recv_sem, flip):
        copy = pltpu.make_async_remote_copy(
            src_ref=source,
            dst_ref=target,
            send_sem=send_sem,
            recv_sem=recv_sem,
            device_id={"seq": flipped(part, flip)},
            device_id_type=MESH,
        )
        copy.start()
        sends.append(copy)
        return copy

    turns, crosses, across = {}, {}, []

    def stage_a(order):
        held[order, 0] = to_low(total_of(order, 0))
        for span, flip in ((0, 2), (1, 4)):
            turns[order, span] = push(
                held.at[order, 0, spans[span]],
                turned.at[order, span],
                turn_send.at[order, span],
                turn_recv.at[order, span],
                flip,
            )
        held[order, 1] = to_low(total_of(order, 1))
        held[order, 2] = to_low(total_of(order, 2))
        for kind, slot, flip, span in ((0, 1, 2, 0), (1, 2, 4, 1)):
            crosses[order, kind] = push(
                held.at[order, slot, spans[span]],
                crossed.at[order, kind],
                cross_send.at[order, kind],
                cross_recv.at[order, kind],
                flip,
            )

    def stage_b(order):
        for kind, slot, flip, span in ((2, 2, 4, 0), (3, 1, 2, 1)):
            turns[order, span].wait_recv()
            held[order, slot, spans[span]] = to_low(
                to_full(held[order, slot, spans[span]]) + to_full(turned[order, span])
            )
            crosses[order, kind] = push(
                held.at[order, slot, spans[span]],
                crossed.at[order, kind],
                cross_send.at[order, kind],
                cross_recv.at[order, kind],
                flip,
            )

    def stage_c(order):
        total = total_of(order, 3)
        for kind in range(4):
            crosses[order, kind].wait_recv()
        low_part = to_full(crossed[order, 0]) + to_full(crossed[order, 2])
        high_part = to_full(crossed[order, 1]) + to_full(crossed[order, 3])
        total = total + jnp.concatenate([low_part, high_part], axis=0)
        if order == inner - 1:
            return total
        sums[order] = to_low(total)
        copy = pltpu.make_async_remote_copy(
            src_ref=sums.at[order],
            dst_ref=summed.at[place],
            send_sem=zsend.at[order],
            recv_sem=zrecv.at[place],
            device_id={"shard": first + targets[order]},
            device_id_type=MESH,
        )
        copy.start()
        across.append(copy)
        return None

    stage_a(0)
    for order in range(1, inner):
        stage_a(order)
        stage_b(order - 1)
        if order > 1:
            stage_c(order - 2)
    stage_b(inner - 1)
    if inner > 1:
        stage_c(inner - 2)
    total = stage_c(inner - 1)
    for peer in peers_in_order(place, inner):
        arrive = pltpu.make_async_remote_copy(
            src_ref=sums.at[0],
            dst_ref=summed.at[peer],
            send_sem=zsend.at[0],
            recv_sem=zrecv.at[peer],
            device_id={"shard": first + peer},
            device_id_type=MESH,
        )
        arrive.wait_recv()
        total = total + to_full(summed[peer])
    for copy in sends:
        copy.wait_send()
    for copy in cores.values():
        copy.wait_send()
    for copy in across:
        copy.wait_send()
    return total


def reduce_scratch(inner, rows, width):
    low = jnp.bfloat16
    sems = lambda *shape: pltpu.SemaphoreType.DMA(shape)
    return [
        pltpu.VMEM((inner, 4, rows, width), low),
        pltpu.VMEM((inner, 4, rows, width), low),
        pltpu.VMEM((inner, 2, rows // 2, width), low),
        pltpu.VMEM((inner, 4, rows // 2, width), low),
        pltpu.VMEM((max(1, inner - 1), rows, width), low),
        pltpu.VMEM((inner, rows, width), low),
        sems(inner, 4),
        sems(inner, 4),
        sems(inner, 4),
        sems(inner, 2),
        sems(inner, 2),
        sems(inner, 4),
        sems(inner, 4),
        sems(max(1, inner - 1)),
        sems(inner),
    ]


def reduce_kernel(inner, p_ref, out_ref, *scratch):
    out_ref[...] = reduce_body(inner, p_ref, *scratch)


def reduce_rows(partial, freight=()):
    inner, _, rows, width = partial.shape
    return run(
        functools.partial(reduce_kernel, inner),
        (partial,),
        in_specs=[pl.BlockSpec(memory_space=pl.ANY)],
        out_specs=[pl.BlockSpec(memory_space=pltpu.VMEM)],
        out_shape=[jax.ShapeDtypeStruct((rows, width), jnp.float32)],
        scratch=reduce_scratch(inner, rows, width),
        freight=freight,
        flips=FLIPS,
        inner=inner,
        micros=25 * inner,
        name="reduce_rows",
    )


def plane_gather(own, target, send, recv):
    part = lax.axis_index("seq")
    half = own.shape[0] // 2
    spans = [pl.ds(0, half), pl.ds(half, half)]
    started = []

    def copy_of(kind, block, span, flip, from_own=False):
        place = target(block).at[spans[span]]
        return pltpu.make_async_remote_copy(
            src_ref=own.at[spans[span]] if from_own else place,
            dst_ref=place,
            send_sem=send.at[kind],
            recv_sem=recv.at[kind],
            device_id={"seq": flipped(part, flip)},
            device_id_type=MESH,
        )

    def push(kind, block, span, flip, from_own=False):
        copy = copy_of(kind, block, span, flip, from_own)
        copy.start()
        started.append(copy)

    def arrived(kind, block, span, flip):
        copy_of(kind, block, span, flip).wait_recv()

    def first():
        for kind, span, flip in (
            (3, 1, 2), (4, 0, 4), (2, 0, 2), (5, 1, 4), (0, 0, 1), (1, 1, 1)
        ):
            push(kind, part, span, flip, True)

    def second():
        side, over = flipped(part, 2), flipped(part, 4)
        arrived(3, side, 1, 2)
        push(6, side, 1, 4)
        arrived(4, over, 0, 4)
        push(7, over, 0, 2)
        push(9, side, 1, 1)
        push(10, over, 0, 1)
        arrived(2, side, 0, 2)
        push(8, side, 0, 1)
        arrived(5, over, 1, 4)
        push(11, over, 1, 1)

    def third():
        far = flipped(part, 6)
        arrived(6, far, 1, 4)
        push(13, far, 1, 1)
        arrived(7, far, 0, 2)
        push(12, far, 0, 1)

    def last():
        for kind, flip, span in (
            (0, 1, 0), (1, 1, 1), (9, 3, 1), (10, 5, 0), (8, 3, 0), (11, 5, 1), (13, 7, 1), (12, 7, 0)
        ):
            arrived(kind, flipped(part, flip), span, 1)
        for copy in started:
            copy.wait_send()

    return first, second, third, last


def line_gather(inner, own, target, send, recv):
    place, first = own_shard_group(inner)
    half = own.shape[0] // 2
    spans = [pl.ds(0, half), pl.ds(half, half)]

    def copy_of(way, step, span):
        block = place - step if way == 0 else place + step
        to = place + 1 if way == 0 else place - 1
        spot = target(block).at[spans[span]]
        return pltpu.make_async_remote_copy(
            src_ref=own.at[spans[span]] if step == 0 else spot,
            dst_ref=spot,
            send_sem=send.at[way, step, span],
            recv_sem=recv.at[way, step, span],
            device_id={"shard": first + to},
            device_id_type=MESH,
        )

    def sends(way, step):
        if way == 0:
            return (place < inner - 1) & (place >= step)
        return (place > 0) & (place + step < inner)

    def receives(way, step):
        return place >= step if way == 0 else place + step < inner

    def start(step, span):
        for way in range(2):

            @pl.when(sends(way, step))
            def _():
                copy_of(way, step, span).start()

    def begin():
        for span in range(2):
            start(0, span)

    def onward(step):
        for span in range(2):
            for way in range(2):

                @pl.when(receives(way, step))
                def _():
                    block = place - step if way == 0 else place + step
                    spot = target(block).at[spans[span]]
                    pltpu.make_async_remote_copy(
                        src_ref=spot,
                        dst_ref=spot,
                        send_sem=send.at[way, step - 1, span],
                        recv_sem=recv.at[way, step - 1, span],
                        device_id={"shard": block + first},
                        device_id_type=MESH,
                    ).wait_recv()

            if step < inner - 1:
                start(step, span)

    def finish():
        for step in range(inner - 1):
            for span in range(2):
                for way in range(2):

                    @pl.when(sends(way, step))
                    def _():
                        copy_of(way, step, span).wait_send()

    return begin, onward, finish


def greet_line(inner):
    barrier = pltpu.get_barrier_semaphore()
    part = lax.axis_index("seq")
    place, first = own_shard_group(inner)
    for flip in FLIPS:
        pl.semaphore_signal(
            barrier, inc=1, device_id={"seq": flipped(part, flip)}, device_id_type=MESH
        )

    @pl.when(place > 0)
    def _():
        pl.semaphore_signal(
            barrier, inc=1, device_id={"shard": first + place - 1}, device_id_type=MESH
        )

    @pl.when(place < inner - 1)
    def _():
        pl.semaphore_signal(
            barrier, inc=1, device_id={"shard": first + place + 1}, device_id_type=MESH
        )

    ends = (place == 0).astype(jnp.int32) + (place == inner - 1).astype(jnp.int32)
    pl.semaphore_wait(barrier, len(FLIPS) + 2 - ends)


def begin_kernel(
    inner,
    x_ref,
    w_ref,
    s_ref,
    r_ref,
    x_out,
    w_out,
    s_out,
    r_out,
    own_sems,
    send,
    recv,
    wsend,
    wrecv,
    ssend,
    srecv,
    rsend,
    rrecv,
):
    part = lax.axis_index("seq")
    place, _ = own_shard_group(inner)
    rows = w_ref.shape[0]
    greet_line(inner)
    w_target = lambda p: w_out.at[pl.ds(p * rows, rows)]
    s_target = lambda p: s_out.at[p]
    w_begin, w_onward, w_finish = line_gather(inner, w_ref, w_target, wsend, wrecv)
    r_target = lambda p: r_out.at[p]
    s_begin, s_onward, s_finish = line_gather(inner, s_ref, s_target, ssend, srecv)
    r_begin, r_onward, r_finish = line_gather(inner, r_ref, r_target, rsend, rrecv)
    first, second, third, last = plane_gather(x_ref, lambda b: x_out.at[b], send, recv)
    s_begin()
    w_begin()
    first()
    r_begin()
    owns = [
        pltpu.make_async_copy(x_ref, x_out.at[part], own_sems.at[0]),
        pltpu.make_async_copy(w_ref, w_target(place), own_sems.at[1]),
        pltpu.make_async_copy(s_ref, s_target(place), own_sems.at[2]),
        pltpu.make_async_copy(r_ref, r_target(place), own_sems.at[3]),
    ]
    for copy in owns:
        copy.start()
    s_onward(1)
    w_onward(1)
    second()
    third()
    for step in range(2, inner):
        s_onward(step)
        w_onward(step)
        r_onward(step - 1)
    last()
    r_onward(inner - 1)
    s_finish()
    w_finish()
    r_finish()
    for copy in owns:
        copy.wait()


def begin(x, weights, small, rows, inner):
    seq_devices = lax.axis_size("seq")
    anywhere = pl.BlockSpec(memory_space=pl.ANY)
    steps = inner - 1
    sems = lambda *shape: pltpu.SemaphoreType.DMA(shape)
    COLLECTIVES.append("begin")
    return pl.pallas_call(
        functools.partial(begin_kernel, inner),
        in_specs=[anywhere] * 4,
        out_specs=[anywhere] * 4,
        out_shape=[
            jax.ShapeDtypeStruct((seq_devices,) + x.shape, x.dtype),
            jax.ShapeDtypeStruct((inner * weights.shape[0], weights.shape[1]), weights.dtype),
            jax.ShapeDtypeStruct((inner,) + small.shape, small.dtype),
            jax.ShapeDtypeStruct((inner,) + rows.shape, rows.dtype),
        ],
        scratch_shapes=[
            sems(4),
            sems(14),
            sems(14),
            sems(2, steps, 2),
            sems(2, steps, 2),
            sems(2, steps, 2),
            sems(2, steps, 2),
            sems(2, steps, 2),
            sems(2, steps, 2),
        ],
        compiler_params=pltpu.CompilerParams(
            collective_id=len(COLLECTIVES), has_side_effects=True
        ),
        cost_estimate=cost_of(60),
        name="begin",
    )(x, weights, small, rows)


def sum_across(inner, part_ref, own, inbox, total_low, sems, send, recv):
    place, first = own_shard_group(inner)
    peers = peers_in_order(place, inner)
    mine = pltpu.make_async_copy(part_ref.at[place], own, sems)
    outgoing = [
        pltpu.make_async_remote_copy(
            src_ref=part_ref.at[peer],
            dst_ref=inbox.at[place],
            send_sem=send.at[order],
            recv_sem=recv.at[place],
            device_id={"shard": first + peer},
            device_id_type=MESH,
        )
        for order, peer in enumerate(peers)
    ]

    def depart():
        mine.start()
        for copy in reversed(outgoing):
            copy.start()

    def arrive():
        mine.wait()
        total = to_full(own[...])
        for order, peer in enumerate(peers):
            pltpu.make_async_remote_copy(
                src_ref=part_ref.at[peer],
                dst_ref=inbox.at[peer],
                send_sem=send.at[order],
                recv_sem=recv.at[peer],
                device_id={"shard": first + peer},
                device_id_type=MESH,
            ).wait_recv()
            total = total + to_full(inbox[peer])
        total_low[...] = to_low(total)

    def finish():
        for copy in outgoing:
            copy.wait_send()

    return depart, arrive, finish


def settle_kernel(inner, counts, *refs):
    part = lax.axis_index("seq")
    hidden_ref, refs = refs[0], refs[1:]
    parts, refs = refs[:counts], refs[counts:]
    hidden_out, refs = refs[0], refs[1:]
    outs, refs = refs[:counts], refs[counts:]
    reduce_refs, refs = refs[:15], refs[15:]
    lines, planes, owns = [], [], []
    for index in range(counts):
        own, inbox, low, sem, send, recv, gsend, grecv, here = refs[9 * index : 9 * index + 9]
        lines.append(sum_across(inner, parts[index], own, inbox, low, sem, send, recv))
        out = outs[index]
        planes.append(plane_gather(low, lambda b, out=out: out.at[b], gsend, grecv))
        owns.append(pltpu.make_async_copy(low, out.at[part], here))
    for line in lines:
        line[0]()
    hidden_out[...] = reduce_body(1, hidden_ref, *reduce_refs)
    for index in range(counts):
        lines[index][1]()
        planes[index][0]()
        owns[index].start()
        if index:
            planes[index - 1][1]()
    planes[counts - 1][1]()
    for stage in (2, 3):
        for plane in planes:
            plane[stage]()
    for index in range(counts):
        lines[index][2]()
        owns[index].wait()


def settle(hidden, parts, inner):
    _, _, rows, width = hidden.shape
    seq_devices = lax.axis_size("seq")
    anywhere = pl.BlockSpec(memory_space=pl.ANY)
    low = jnp.bfloat16
    sems = lambda *shape: pltpu.SemaphoreType.DMA(shape)
    scratch = reduce_scratch(1, rows, width)
    for part in parts:
        shape = part.shape[1:]
        scratch += [
            pltpu.VMEM(shape, low),
            pltpu.VMEM(part.shape, low),
            pltpu.VMEM(shape, low),
            sems(),
            sems(inner),
            sems(inner),
            sems(14),
            sems(14),
            sems(),
        ]
    return run(
        functools.partial(settle_kernel, inner, len(parts)),
        (hidden,) + tuple(parts),
        in_specs=[anywhere] * (1 + len(parts)),
        out_specs=[pl.BlockSpec(memory_space=pltpu.VMEM)] + [anywhere] * len(parts),
        out_shape=[jax.ShapeDtypeStruct((rows, width), jnp.float32)]
        + [jax.ShapeDtypeStruct((seq_devices,) + part.shape[1:], low) for part in parts],
        scratch=scratch,
        flips=FLIPS,
        inner=inner,
        micros=90,
        name="settle",
    )


def sum_all_kernel(inner, p_ref, out_ref, total_low, own_sem, send, recv, *reduce_refs):
    part = lax.axis_index("seq")
    total_low[...] = to_low(reduce_body(inner, p_ref, *reduce_refs))
    stages = plane_gather(total_low, lambda b: out_ref.at[b], send, recv)
    own = pltpu.make_async_copy(total_low, out_ref.at[part], own_sem)
    own.start()
    for stage in stages:
        stage()
    own.wait()


def sum_all(partial):
    inner, seq_devices, rows, width = partial.shape
    sems = lambda *shape: pltpu.SemaphoreType.DMA(shape)
    anywhere = pl.BlockSpec(memory_space=pl.ANY)
    return run(
        functools.partial(sum_all_kernel, inner),
        (partial,),
        in_specs=[anywhere],
        out_specs=[anywhere],
        out_shape=[jax.ShapeDtypeStruct((seq_devices, rows, width), jnp.bfloat16)],
        scratch=[pltpu.VMEM((rows, width), jnp.bfloat16), sems(), sems(14), sems(14)]
        + reduce_scratch(inner, rows, width),
        flips=FLIPS,
        inner=inner,
        micros=25,
        name="sum_all",
    )[0]


def params_of(limit=VMEM_BYTES):
    return pltpu.CompilerParams(vmem_limit_bytes=limit)


def project_kernel(x_ref, gain_ref, w_ref, dt_ref, hidden_ref, gate_ref, rows_ref):
    x = to_full(x_ref[...])
    hidden = to_low(x * norm_scale(x) * gain_ref[...])
    hidden_ref[...] = hidden
    projected = dot_full(hidden, w_ref[...])
    gate_width = gate_ref.shape[1]
    gate_ref[...] = projected[:, :gate_width]
    rest = projected.shape[1] - gate_width
    rows_ref[:, :rest] = to_low(projected[:, gate_width:])
    rows_ref[:, rest:] = to_low(dot_full(hidden, dt_ref[...]))


def project(x, gain, weights, dt_weights, gate_width, freight=()):
    rows, width = x.shape
    columns = weights.shape[1] + LANES
    tile = 256
    block = lambda extent: pl.BlockSpec((tile, extent), lambda step: (step, 0))
    return run(
        project_kernel,
        (x, gain, weights, dt_weights,),
        grid=(rows // tile,),
        in_specs=[
            block(width), whole(gain.shape), whole(weights.shape), whole(dt_weights.shape)
        ],
        out_specs=[block(width), block(gate_width), block(columns - gate_width)],
        out_shape=[
            jax.ShapeDtypeStruct((rows, width), jnp.bfloat16),
            jax.ShapeDtypeStruct((rows, gate_width), jnp.float32),
            jax.ShapeDtypeStruct((rows, columns - gate_width), jnp.bfloat16),
        ],
        freight=freight,
        micros=11,
        name="project",
    )


def put_split(columns, rows):
    lane = iota_of((rows, LANES), 1)
    result = jnp.zeros((rows, LANES), jnp.float32)
    for place, column in enumerate(columns):
        high = to_full(to_low(column))
        result = jnp.where(lane == 2 * place, high, result)
        result = jnp.where(lane == 2 * place + 1, column - high, result)
    return to_low(result)


def mix_out_kernel(y_ref, gate_ref, gain_ref, w_ref, part_ref):
    width = w_ref.shape[1]
    gated = to_full(y_ref[...]) * jax.nn.silu(gate_ref[...])
    part_ref[0, :, :width] = to_low(dot_full(to_low(gated * gain_ref[...]), w_ref[...]))
    squares = jnp.sum(gated * gated, axis=1, keepdims=True)
    part_ref[0, :, width:] = put_split([squares], y_ref.shape[0])


def mix_out(y, gate, gain, weights, blocks):
    rows, channels = y.shape
    width = weights.shape[1]
    tile = rows // blocks
    block = pl.BlockSpec((tile, channels), lambda step: (step, 0))
    return pl.pallas_call(
        mix_out_kernel,
        grid=(blocks,),
        in_specs=[block, block, whole(gain.shape), whole(weights.shape)],
        out_specs=pl.BlockSpec((1, tile, width + LANES), lambda step: (step, 0, 0)),
        out_shape=jax.ShapeDtypeStruct((blocks, tile, width + LANES), jnp.bfloat16),
        compiler_params=params_of(),
        cost_estimate=cost_of(9),
        name="mix_out",
    )(y, gate, gain, weights)


def mix_back_kernel(
    mix_ref, y_ref, gate_ref, gain_ref, w_ref, dy_ref, dgate_ref, w_grad_ref, gain_grad_ref, total
):
    step = pl.program_id(0)
    width = w_ref.shape[1]

    @pl.when(step == 0)
    def _():
        total[...] = jnp.zeros_like(total)
        gain_grad_ref[...] = jnp.zeros_like(gain_grad_ref)

    mix = mix_ref[0, :, :width]
    extra = to_full(mix_ref[0, :, width:])
    share = extra[:, 0:1] + extra[:, 1:2]
    scale = extra[:, 2:3] + extra[:, 3:4]
    normed_grad = dot_lanes(mix, w_ref[...])
    y = to_full(y_ref[...])
    gate = gate_ref[...]
    sig = jax.nn.sigmoid(gate)
    act = gate * sig
    unit = y * act * scale
    gain = gain_ref[...]
    gain_grad_ref[0:1, :] += jnp.sum(normed_grad * unit, axis=0, keepdims=True)
    gated_grad = scale * (normed_grad * gain - unit * share)
    dy_ref[...] = to_low(gated_grad * act)
    dgate_ref[...] = to_low(gated_grad * y * sig * (1.0 + gate * (1.0 - sig)))
    total[...] += dot_rows(to_low(unit * gain), mix)

    @pl.when(step == pl.num_programs(0) - 1)
    def _():
        w_grad_ref[...] = to_low(total[...])


def mix_back(mix, y, gate, gain, weights, freight=()):
    blocks, tile, wide = mix.shape
    rows, channels = y.shape
    block = pl.BlockSpec((tile, channels), lambda step: (step, 0))
    return run(
        mix_back_kernel,
        (mix, y, gate, gain, weights,),
        grid=(blocks,),
        in_specs=[
            pl.BlockSpec((1, tile, wide), lambda step: (step, 0, 0)),
            block,
            block,
            whole(gain.shape),
            whole(weights.shape),
        ],
        out_specs=[block, block, whole(weights.shape), whole((8, channels))],
        out_shape=[
            jax.ShapeDtypeStruct((rows, channels), jnp.bfloat16),
            jax.ShapeDtypeStruct((rows, channels), jnp.bfloat16),
            jax.ShapeDtypeStruct(weights.shape, jnp.bfloat16),
            jax.ShapeDtypeStruct((8, channels), jnp.float32),
        ],
        scratch=[pltpu.VMEM(weights.shape, jnp.float32)],
        freight=freight,
        micros=12,
        name="mix_back",
    )


def project_back_kernel(
    dgate_ref, drows_ref, hidden_ref, w_ref, dt_ref, part_ref, main_grad_ref, rest_grad_ref, total
):
    step = pl.program_id(0)

    @pl.when(step == 0)
    def _():
        total[...] = jnp.zeros_like(total)

    grads = jnp.concatenate([dgate_ref[...], drows_ref[...]], axis=1)
    columns = w_ref.shape[1]
    part_ref[0] = to_low(
        dot_lanes(grads[:, :columns], w_ref[...]) + dot_lanes(grads[:, columns:], dt_ref[...])
    )
    total[...] += dot_rows(hidden_ref[...], grads)

    @pl.when(step == pl.num_programs(0) - 1)
    def _():
        main = main_grad_ref.shape[1]
        main_grad_ref[...] = to_low(total[:, :main])
        rest_grad_ref[...] = to_low(total[:, main:])


def project_back(dgate, drows, hidden, weights, dt_weights, blocks, freight=()):
    rows, width = hidden.shape
    tile = rows // blocks
    main = 2 * dgate.shape[1]
    rest = weights.shape[1] + LANES - main
    block = lambda extent: pl.BlockSpec((tile, extent), lambda step: (step, 0))
    return run(
        project_back_kernel,
        (dgate, drows, hidden, weights, dt_weights,),
        grid=(blocks,),
        in_specs=[
            block(dgate.shape[1]),
            block(drows.shape[1]),
            block(width),
            whole(weights.shape),
            whole(dt_weights.shape),
        ],
        out_specs=[
            pl.BlockSpec((1, tile, width), lambda step: (step, 0, 0)),
            whole((width, main)),
            whole((width, rest)),
        ],
        out_shape=[
            jax.ShapeDtypeStruct((blocks, tile, width), jnp.bfloat16),
            jax.ShapeDtypeStruct((width, main), jnp.bfloat16),
            jax.ShapeDtypeStruct((width, rest), jnp.bfloat16),
        ],
        scratch=[pltpu.VMEM((width, main + rest), jnp.float32)],
        freight=freight,
        micros=25,
        name="project_back",
    )


def shared_kernel(
    rows_ref, up_ref, down_ref, res_ref, back_ref, up_grad_ref, down_grad_ref, up_sum, down_sum
):
    step = pl.program_id(0)

    @pl.when(step == 0)
    def _():
        up_sum[...] = jnp.zeros_like(up_sum)
        down_sum[...] = jnp.zeros_like(down_sum)

    hidden, width = down_ref.shape
    rows = rows_ref[0, :, :width]
    grad = rows_ref[0, :, width + LANES :]
    joined = dot_full(rows, up_ref[...])
    gate, up = joined[:, :hidden], joined[:, hidden:]
    sig = jax.nn.sigmoid(gate)
    act = gate * sig
    acted = to_low(act * up)
    res_ref[0] = to_low(dot_full(acted, down_ref[...]))
    down_sum[...] += dot_rows(acted, grad)
    act_grad = dot_lanes(grad, down_ref[...])
    joined_grad = to_low(
        jnp.concatenate(
            [act_grad * up * sig * (1.0 + gate * (1.0 - sig)), act_grad * act], axis=1
        )
    )
    up_sum[...] += dot_rows(rows, joined_grad)
    back_ref[0] = to_low(dot_lanes(joined_grad, up_ref[...]))

    @pl.when(step == pl.num_programs(0) - 1)
    def _():
        up_grad_ref[...] = to_low(up_sum[...])
        down_grad_ref[...] = to_low(down_sum[...])


def shared_expert(rows, up, down, blocks, inner, freight=()):
    _, tile, wide = rows.shape
    width = down.shape[1]
    block = pl.BlockSpec((1, tile, width), lambda step: (step, 0, 0))
    low = jnp.bfloat16
    return run(
        shared_kernel,
        (rows, up, down),
        grid=(blocks,),
        in_specs=[
            pl.BlockSpec(
                (1, tile, wide), lambda step: (own_shard_group(inner)[0] * blocks + step, 0, 0)
            ),
            whole(up.shape),
            whole(down.shape),
        ],
        out_specs=[block, block, whole(up.shape), whole(down.shape)],
        out_shape=[
            jax.ShapeDtypeStruct((blocks, tile, width), low),
            jax.ShapeDtypeStruct((blocks, tile, width), low),
            jax.ShapeDtypeStruct(up.shape, low),
            jax.ShapeDtypeStruct(down.shape, low),
        ],
        scratch=[pltpu.VMEM(up.shape, jnp.float32), pltpu.VMEM(down.shape, jnp.float32)],
        freight=freight,
        micros=18,
        name="shared_expert",
    )


def dispatch_kernel(rows_ref, x_ref, g_ref, picks_ref, *, top_count, slots, own_first):
    per_device = x_ref.shape[0]
    together, tok_rows, _ = rows_ref.shape
    width = g_ref.shape[2]
    wide = width + LANES
    taken = per_device * slots
    lane = iota_of((tok_rows, LANES), 1)
    named = (lane >= 2 * top_count) & (lane < 3 * top_count)
    before = iota_of((tok_rows, tok_rows), 0) > iota_of((tok_rows, tok_rows), 1)
    before = to_low(jnp.where(before, 1.0, 0.0))
    first = own_first()
    for index in range(together):
        extra = to_full(rows_ref[index, :, width:wide])
        member = jnp.zeros((tok_rows, LANES), jnp.float32)
        for expert in range(per_device):
            own = (first + expert).astype(jnp.float32)
            hit = jnp.sum(jnp.where(named & (extra == own), 1.0, 0.0), axis=1, keepdims=True)
            member = jnp.where(lane // slots == expert, hit, member)
        ranks = dot_full(before, to_low(member))
        picks = jnp.where(
            (ranks == to_full(lane % slots)) & (member > 0.0), 1.0, 0.0
        ).astype(jnp.bfloat16)
        picks_ref[index] = picks
        rows = to_low(dot_rows(picks[:, :taken], rows_ref[index]))
        start = index * slots
        for expert in range(per_device):
            part = rows[expert * slots : (expert + 1) * slots]
            x_ref[expert, start : start + slots] = part[:, :wide]
            g_ref[expert, start : start + slots] = part[:, wide:]


def dispatch(rows, width, per_device, top_count, slots, own_first, freight=()):
    blocks, tok_rows, wide = rows.shape
    together = 4
    block = lambda extent: pl.BlockSpec((together, tok_rows, extent), lambda step: (step, 0, 0))
    taken = lambda extent: pl.BlockSpec(
        (per_device, together * slots, extent), lambda step: (0, step, 0)
    )
    return run(
        functools.partial(
            dispatch_kernel, top_count=top_count, slots=slots, own_first=own_first
        ),
        (rows,),
        grid=(blocks // together,),
        in_specs=[block(wide)],
        out_specs=[taken(width + LANES), taken(width), block(LANES)],
        out_shape=[
            jax.ShapeDtypeStruct((per_device, blocks * slots, width + LANES), jnp.bfloat16),
            jax.ShapeDtypeStruct((per_device, blocks * slots, width), jnp.bfloat16),
            jax.ShapeDtypeStruct((blocks, tok_rows, LANES), jnp.bfloat16),
        ],
        freight=freight,
        micros=30,
        name="dispatch",
    )


def join_piece(up, down):
    double = up.shape[-1]
    rows, width = down.shape[-2:]
    half = rows // 2
    rest = width - double
    tail = jnp.concatenate([down[..., :half, double:], down[..., half:, double:]], axis=-1)
    blank = jnp.zeros(tail.shape[:-1] + (double - 2 * rest,), tail.dtype)
    tail = jnp.concatenate([tail, blank], axis=-1)
    return jnp.concatenate([up, down[..., :double], tail], axis=-2)


def piece_parts(piece, up, down, place, count):
    depth, rows = up.shape[0] // count, down.shape[0] // count
    double, width = up.shape[1], down.shape[1]
    half, rest = rows // 2, width - double
    up_start = pl.multiple_of(place * depth, depth)
    down_start = pl.multiple_of(place * rows, rows)
    tail = pl.ds(depth + rows, half)
    return [
        (piece.at[pl.ds(0, depth)], up.at[pl.ds(up_start, depth)]),
        (piece.at[pl.ds(depth, rows)], down.at[pl.ds(down_start, rows), pl.ds(0, double)]),
        (
            piece.at[tail, pl.ds(0, rest)],
            down.at[pl.ds(down_start, half), pl.ds(double, rest)],
        ),
        (
            piece.at[tail, pl.ds(rest, rest)],
            down.at[pl.ds(down_start + half, half), pl.ds(double, rest)],
        ),
    ]


def experts_kernel(*refs, count, per_device, top_count, own_first, inner):
    x_ref, g_ref = refs[:2]
    total = count * per_device
    pieces = refs[2 : 2 + total]
    res_ref, dx_ref = refs[2 + total : 4 + total]
    outs = refs[4 + total : 4 + 2 * total]
    up_held, down_held, up_sum, down_sum, up_low, down_low, sems = refs[4 + 2 * total :]
    own_place, _ = own_shard_group(inner)
    expert, step = pl.program_id(0), pl.program_id(1)
    steps = pl.num_programs(1)
    slot = lax.rem(expert, 2)
    width, double = up_held.shape[1:]
    hidden = double // 2
    tile = x_ref.shape[1]

    def fetch(which):
        copies = []
        for shift in range(count):
            place = lax.rem(own_place + count - shift, count)
            parts = piece_parts(
                pieces[shift * per_device + which],
                up_held.at[which % 2],
                down_held.at[which % 2],
                place,
                count,
            )
            for kind, (piece, held) in enumerate(parts):
                copies.append(
                    pltpu.make_async_copy(piece, held, sems.at[which % 2, shift, kind])
                )
        return copies

    for which in range(per_device):

        @pl.when((step == 0) & (expert == which))
        def _():
            if which == 0:
                for copy in fetch(0):
                    copy.start()
            for copy in fetch(which):
                copy.wait()
            if which + 1 < per_device:
                for copy in fetch(which + 1):
                    copy.start()

    @pl.when(step == 0)
    def _():
        up_sum[...] = jnp.zeros_like(up_sum)
        down_sum[...] = jnp.zeros_like(down_sum)

    up, down = up_held.at[slot], down_held.at[slot]
    rows = x_ref[0, :, :width]
    extra = to_full(x_ref[0, :, width:])
    lane = iota_of((tile, LANES), 1)
    own = own_first() + expert
    hits = jnp.where((lane < 3 * top_count) & (extra == own.astype(jnp.float32)), 1.0, 0.0)
    gate_slot = jnp.zeros((tile, 1), jnp.float32)
    for route in range(top_count):
        place = 2 * top_count + route
        value = extra[:, 2 * route : 2 * route + 1] + extra[:, 2 * route + 1 : 2 * route + 2]
        gate_slot = gate_slot + hits[:, place : place + 1] * value
    joined = dot_full(rows, up[...])
    gate, lift = joined[:, :hidden], joined[:, hidden:]
    sig = jax.nn.sigmoid(gate)
    act = gate * sig
    acted = to_low(act * lift)
    res = to_low(dot_full(acted, down[...]))
    grads = g_ref[0]
    wide_grads = to_full(grads)
    wide_res = to_full(res)
    gate_grad = jnp.sum(wide_res * wide_grads, axis=1, keepdims=True)
    res_ref[0] = to_low(wide_res * gate_slot)
    weighted = to_low(wide_grads * gate_slot)
    act_grad = dot_lanes(weighted, down[...])
    down_sum[...] += dot_rows(acted, weighted)
    joined_grad = to_low(
        jnp.concatenate(
            [act_grad * lift * sig * (1.0 + gate * (1.0 - sig)), act_grad * act], axis=1
        )
    )
    dx_ref[0, :, :width] = to_low(dot_lanes(joined_grad, up[...]))
    high = to_full(to_low(gate_grad))
    half = LANES // 2
    dx_ref[0, :, width:] = to_low(
        jnp.where(lane == own, high, 0.0) + jnp.where(lane == own + half, gate_grad - high, 0.0)
    )
    up_sum[...] += dot_rows(rows, joined_grad)

    for which in range(per_device):

        @pl.when((step == steps - 1) & (expert == which))
        def _():
            up_low[...] = to_low(up_sum[...])
            down_low[...] = to_low(down_sum[...])
            copies = []
            for shift in range(count):
                place = lax.rem(own_place + count - shift, count)
                parts = piece_parts(
                    outs[shift * per_device + which], up_low, down_low, place, count
                )
                for kind, (piece, held) in enumerate(parts):
                    copies.append(pltpu.make_async_copy(held, piece, sems.at[2, shift, kind]))
            for copy in copies:
                copy.start()
            for copy in copies:
                copy.wait()


def experts(x, g, pieces, hidden, top_count, own_first, inner):
    per_device, rows, wide = x.shape
    width = g.shape[2]
    count = len(pieces) // per_device
    double = 2 * hidden
    tile = min(rows, 256)
    block = lambda extent: pl.BlockSpec((1, tile, extent), lambda e, step: (e, step, 0))
    anywhere = pl.BlockSpec(memory_space=pl.ANY)
    low = jnp.bfloat16
    outs = run(
        functools.partial(
            experts_kernel,
            count=count,
            per_device=per_device,
            top_count=top_count,
            own_first=own_first,
            inner=inner,
        ),
        (x, g) + tuple(pieces),
        grid=(per_device, rows // tile),
        in_specs=[block(wide), block(width)] + [anywhere] * len(pieces),
        out_specs=[block(width), block(wide)] + [anywhere] * len(pieces),
        out_shape=[
            jax.ShapeDtypeStruct((per_device, rows, width), low),
            jax.ShapeDtypeStruct((per_device, rows, wide), low),
        ]
        + [jax.ShapeDtypeStruct(piece.shape, low) for piece in pieces],
        scratch=[
            pltpu.VMEM((2, width, double), low),
            pltpu.VMEM((2, hidden, width), low),
            pltpu.VMEM((width, double), jnp.float32),
            pltpu.VMEM((hidden, width), jnp.float32),
            pltpu.VMEM((width, double), low),
            pltpu.VMEM((hidden, width), low),
            pltpu.SemaphoreType.DMA((3, count, 4)),
        ],
        micros=45,
        name="experts",
    )
    return outs[0], outs[1], outs[2:]


def combine_kernel(
    picks_ref, res_ref, dx_ref, sres_ref, sback_ref, out_ref, back_ref, *, slots, inner
):
    step = pl.program_id(0)
    together, _, width = out_ref.shape
    per_device = res_ref.shape[0]
    blocks = sres_ref.shape[0]
    place, _ = own_shard_group(inner)
    for index in range(together):
        picks = picks_ref[index, :, : per_device * slots]
        start = index * slots
        stacked = lambda ref: jnp.concatenate(
            [ref[expert, start : start + slots] for expert in range(per_device)], axis=0
        )
        out_ref[index] = to_low(dot_full(picks, stacked(res_ref)))
        back_ref[index] = to_low(dot_full(picks, stacked(dx_ref)))

    @pl.when(lax.div(step * together, blocks) == place)
    def _():
        first = lax.rem(step * together, blocks)
        for index in range(together):
            out_ref[index] = to_low(to_full(out_ref[index]) + to_full(sres_ref[first + index]))
            back_ref[index, :, :width] = to_low(
                to_full(back_ref[index, :, :width]) + to_full(sback_ref[first + index])
            )


def combine(picks, res, dx, shared_res, shared_back, inner, freight=()):
    blocks, tok_rows, _ = picks.shape
    per_device, rows, width = res.shape
    slots = rows // blocks
    together = 4
    block = lambda extent: pl.BlockSpec((together, tok_rows, extent), lambda step: (step, 0, 0))
    taken = lambda extent: pl.BlockSpec(
        (per_device, together * slots, extent), lambda step: (0, step, 0)
    )
    return run(
        functools.partial(combine_kernel, slots=slots, inner=inner),
        (picks, res, dx, shared_res, shared_back),
        grid=(blocks // together,),
        in_specs=[
            block(LANES),
            taken(width),
            taken(width + LANES),
            whole(shared_res.shape),
            whole(shared_back.shape),
        ],
        out_specs=[block(width), block(width + LANES)],
        out_shape=[
            jax.ShapeDtypeStruct((blocks, tok_rows, width), jnp.bfloat16),
            jax.ShapeDtypeStruct((blocks, tok_rows, width + LANES), jnp.bfloat16),
        ],
        freight=freight,
        micros=30,
        name="combine",
    )


def assemble_kernel(main_ref, small_ref, out_ref):
    seq_devices, rows, double = main_ref.shape
    channels = double // 2
    for device in range(seq_devices):
        for side in range(2):
            start = (side * seq_devices + device) * channels
            out_ref[:, start : start + channels] = to_full(
                main_ref[device, :, side * channels : (side + 1) * channels]
            )
    start = 2 * seq_devices * channels
    out_ref[:, start:] = to_full(small_ref[0, :rows, : out_ref.shape[1] - start])


def assemble(main, small, columns):
    seq_devices, rows, double = main.shape
    tile = rows // seq_devices
    return pl.pallas_call(
        assemble_kernel,
        grid=(seq_devices,),
        in_specs=[
            pl.BlockSpec((seq_devices, tile, double), lambda step: (0, step, 0)),
            pl.BlockSpec((1,) + small.shape[1:], lambda step: (step, 0, 0)),
        ],
        out_specs=pl.BlockSpec((tile, columns), lambda step: (step, 0)),
        out_shape=jax.ShapeDtypeStruct((rows, columns), jnp.float32),
        compiler_params=params_of(),
        cost_estimate=cost_of(6),
        name="assemble",
    )(main, small)


def collect_kernel(place_ref, *refs, per_device):
    del place_ref
    step = pl.program_id(0)
    up_ref, down_ref = refs[-2:]
    depth, double = up_ref.shape[1:]
    rows, width = down_ref.shape[1:]
    half, rest = rows // 2, width - double
    for order, piece in enumerate(refs[:-2]):

        @pl.when(step == order)
        def _():
            up_ref[0] = to_full(piece[:depth])
            down_ref[0, :, :double] = to_full(piece[depth : depth + rows])
            tail = to_full(piece[depth + rows :])
            down_ref[0, :half, double:] = tail[:, :rest]
            down_ref[0, half:, double:] = tail[:, rest : 2 * rest]


def collect(place, pieces, per_device, depth, rows, width):
    count = len(pieces)
    shape = pieces[0].shape

    def here(step, place):
        shift, expert = lax.div(step, per_device), lax.rem(step, per_device)
        return (
            lax.rem(place[0] + shift, count // per_device) * per_device + expert, 0, 0
        )

    up, down = (depth, shape[1]), (rows, width)
    return pl.pallas_call(
        functools.partial(collect_kernel, per_device=per_device),
        grid_spec=pltpu.PrefetchScalarGridSpec(
            num_scalar_prefetch=1,
            grid=(count,),
            in_specs=[pl.BlockSpec(shape, lambda step, place: (0, 0))] * count,
            out_specs=[pl.BlockSpec((1,) + up, here), pl.BlockSpec((1,) + down, here)],
        ),
        out_shape=[
            jax.ShapeDtypeStruct((count,) + up, jnp.float32),
            jax.ShapeDtypeStruct((count,) + down, jnp.float32),
        ],
        compiler_params=params_of(),
        cost_estimate=cost_of(12),
        name="collect",
    )(place, *pieces)


def split_small(joined, arrays):
    results, start = [], 0
    for piece in arrays:
        part = joined[:, start : start + piece.size]
        results.append(part.reshape((-1,) + piece.shape[1:]))
        start += piece.size
    return results


def flat_of(arrays):
    return jnp.concatenate([piece.reshape(-1) for piece in arrays])


def rows_to_send(weights, columns, part):
    seq_devices = lax.axis_size("seq")
    halves = max(1, seq_devices // lax.axis_size("shard"))
    mine = []
    for weight in weights:
        view = weight.reshape(halves, seq_devices, -1, weight.shape[1])
        mine.append(lax.dynamic_index_in_dim(view, part, 1, keepdims=False))
    width = weights[0].shape[1]
    mine = jnp.concatenate(mine, axis=1).reshape(-1, width)
    return jnp.concatenate([mine, columns.reshape(-1, width)], axis=0)


def rows_by_owner(joined, weights):
    seq_devices = lax.axis_size("seq")
    halves = max(1, seq_devices // lax.axis_size("shard"))
    count = halves * sum(weight.shape[0] // halves // seq_devices for weight in weights)
    return joined[:, :count].reshape(seq_devices, -1, joined.shape[2])


def rows_of_owner(taken, weights):
    seq_devices = lax.axis_size("seq")
    halves = max(1, seq_devices // lax.axis_size("shard"))
    fine_rows = [weight.shape[0] // halves // seq_devices for weight in weights]
    width = taken.shape[2]
    taken = taken.reshape(seq_devices, -1, sum(fine_rows), width).transpose(1, 0, 2, 3)
    results, start = [], 0
    for fine in fine_rows:
        results.append(taken[:, :, start : start + fine].reshape(-1, width))
        start += fine
    return results


def rows_from_owner(grads):
    seq_devices = lax.axis_size("seq")
    shard_devices = lax.axis_size("shard")
    width = grads[0].shape[1]
    turns = shard_devices * max(1, seq_devices // shard_devices) // seq_devices
    pieces = [
        grad.reshape(turns, seq_devices, -1, width).transpose(1, 0, 2, 3) for grad in grads
    ]
    return jnp.concatenate(pieces, axis=2).reshape(seq_devices, -1, width)


def rows_of_shard(joined, weights):
    seq_devices = lax.axis_size("seq")
    halves = max(1, seq_devices // lax.axis_size("shard"))
    fine_rows = [weight.shape[0] // halves // seq_devices for weight in weights]
    width = joined.shape[2]
    count = halves * sum(fine_rows)
    spread = joined[:, :count].reshape(seq_devices, halves, -1, width).transpose(1, 0, 2, 3)
    results, start = [], 0
    for fine in fine_rows:
        results.append(to_full(spread[:, :, start : start + fine]).reshape(-1, width))
        start += fine
    return results, joined[:, count:]


def inner_groups(inner):
    count = lax.axis_size("shard")
    return [list(range(start, start + inner)) for start in range(0, count, inner)]


def outer_groups(inner):
    count = lax.axis_size("shard")
    return [list(range(start, count, inner)) for start in range(inner)]


def stacked_pieces(received, place, inner, extents):
    depth, rows, width = extents
    own = jnp.stack(received)[lax.rem(place + inner - jnp.arange(inner), inner)]
    joined = lax.all_gather(own, "shard", axis_index_groups=outer_groups(inner))
    up, down = unjoin(joined.reshape((-1,) + joined.shape[2:]), depth, rows, width)
    return join_piece(up.reshape(-1, up.shape[-1]), down.reshape(-1, width))


def split_piece(grad, shift, place, inner, extents):
    depth, rows, width = extents
    shards = lax.axis_size("shard")
    up, down = unjoin(grad, depth * shards, rows * shards, width)
    up = up.reshape(shards // inner, inner, depth, -1)
    down = down.reshape(shards // inner, inner, rows, width)
    here = lax.rem(place + inner - shift, inner)
    take = lambda array: lax.dynamic_index_in_dim(array, here, 1, keepdims=False)
    return lax.psum_scatter(
        join_piece(take(up), take(down)), "shard", axis_index_groups=outer_groups(inner)
    )


def unjoin(joined, depth, rows, width):
    double = joined.shape[-1]
    rest = width - double
    tail = joined[..., depth + rows :, :]
    tail = jnp.concatenate([tail[..., :rest], tail[..., rest : 2 * rest]], axis=-2)
    down = jnp.concatenate([joined[..., depth : depth + rows, :], tail], axis=-1)
    return joined[..., :depth, :], down


def by_place(received, place, inner):
    return jnp.stack(received)[lax.rem(place + inner - jnp.arange(inner), inner)]


def local(
    tokens,
    out_grad,
    deal_order,
    lengths,
    routes,
    norm_in,
    w_in,
    w_dt,
    conv_w,
    conv_b,
    dt_bias,
    a_log,
    d_skip,
    norm_gate,
    w_out,
    norm_moe,
    w_router,
    w_shared,
    w_shared_down,
    w_experts,
    w_experts_down,
):
    seq_devices = lax.axis_size("seq")
    shard_devices = lax.axis_size("shard")
    part = lax.axis_index("seq")
    shard = lax.axis_index("shard")
    inner = min(shard_devices, INNER)
    outer = shard_devices // inner
    place = lax.rem(shard, inner)
    residual = to_full(tokens[0])
    tok_rows, width = residual.shape
    group_rows = tok_rows * seq_devices
    inner_width = w_out.shape[0] * shard_devices
    channels = inner_width // seq_devices
    head_total = w_dt.shape[1]
    heads = head_total // seq_devices
    shared_width = w_shared_down.shape[0] * shard_devices
    shared_part = shared_width // seq_devices
    depth_rows = w_in.shape[0]
    expert_total = w_router.shape[1]
    local_experts, _, double = w_experts.shape
    hidden = double // 2
    hidden_rows = w_experts_down.shape[1]
    top_count = routes.shape[2]
    per_device = local_experts // inner
    blocks = inner * seq_devices
    COLLECTIVES.clear()

    def own_columns(array, start, extent):
        return lax.dynamic_slice_in_dim(array, start + part * extent, extent, 1)

    def own_rows(array, extent):
        return lax.dynamic_slice_in_dim(array, part * extent, extent, 0)

    small_weights = [
        norm_in, own_columns(w_dt, 0, heads), conv_w, conv_b, dt_bias, a_log, d_skip, norm_gate, norm_moe, w_router
    ]
    in_columns = jnp.concatenate(
        [
            own_columns(w_in, 0, channels),
            own_columns(w_in, inner_width, channels),
            w_in[:, 2 * inner_width :],
        ],
        axis=1,
    )
    flat = flat_of(small_weights)
    shared_columns = jnp.concatenate(
        [
            own_columns(w_shared, 0, shared_part),
            own_columns(w_shared, shared_width, shared_part),
        ],
        axis=1,
    )
    rows_sent = rows_to_send([w_out, w_shared_down], shared_columns, part)
    if outer == 1:
        wide = in_columns.shape[1]
        flat_rows = -(-flat.size // (wide * 32)) * 32
        flat = jnp.pad(flat, (0, flat_rows * wide - flat.size)).reshape(flat_rows, wide)
        x_group, proj_in, joined, rows_joined = begin(
            tokens[0], in_columns, flat, rows_sent, inner
        )
        joined = joined.reshape(inner, -1)
        x_group = x_group.reshape(group_rows, width)
    else:
        x_group = gather_rows(tokens[0], 1)[0].reshape(group_rows, width)
        proj_in = lax.all_gather(in_columns, "shard", tiled=True)
        joined = lax.all_gather(flat, "shard")
        rows_joined = lax.all_gather(rows_sent, "shard")
    (
        gain_in,
        dt_columns,
        conv_weight,
        conv_bias,
        step_bias,
        decay_log,
        skip_gain,
        gain_gate,
        gain_moe,
        router,
    ) = split_small(joined, small_weights)
    shared_up = rows_joined[:, rows_joined.shape[1] - shared_columns.size // width :]
    shared_up = shared_up.reshape(-1, shared_columns.shape[1])
    dt_columns = jnp.pad(dt_columns, ((0, 0), (0, LANES - heads)))
    def piece_of(shift, expert):
        here = lax.rem(place + shift, inner) * per_device + expert
        return join_piece(
            lax.dynamic_index_in_dim(w_experts, here, 0, keepdims=False),
            lax.dynamic_index_in_dim(w_experts_down, here, 0, keepdims=False),
        )

    def own_first():
        here, _ = own_shard_group(inner)
        return lax.axis_index("seq") * local_experts + here * per_device

    pieces = {(0, expert): piece_of(0, expert) for expert in range(per_device)}

    def parcels(*keys):
        return [Parcel(piece_of(*key), key[0], inner) for key in keys]

    def unpack(keys, arrays):
        pieces.update(zip(keys, arrays))

    gain_row = to_full(gain_in)[None]
    hidden_in, gate_in, rows_in = project(
        x_group, gain_row, proj_in, dt_columns, channels
    )
    ends = jnp.cumsum(lengths[0]).astype(jnp.int32)
    conv_part = jnp.concatenate(
        [own_rows(conv_weight, channels), conv_weight[inner_width:]], axis=0
    )
    bias_part = jnp.concatenate([own_rows(conv_bias, channels), conv_bias[inner_width:]], axis=0)
    conv_table = to_full(
        jnp.pad(jnp.concatenate([conv_part.T, bias_part[None]], axis=0), ((0, 3), (0, 0)))
    )
    head_table = jnp.pad(
        jnp.stack(
            [
                to_full(own_rows(step_bias, heads)),
                -jnp.exp(to_full(own_rows(decay_log, heads))),
                to_full(own_rows(skip_gain, heads)),
            ]
        ),
        ((0, 5), (0, LANES - heads)),
    )
    keys = [(1, 0)]
    y, seq_rows, states, (taken, *arrays) = scan_forward(
        ends,
        deal_order,
        rows_in,
        conv_table,
        head_table,
        channels,
        [PlaneSwap(rows_by_owner(rows_joined, [w_out, w_shared_down]))] + parcels(*keys),
    )
    unpack(keys, arrays)
    out_rows, shared_down = rows_of_owner(taken, [w_out, w_shared_down])
    gate_gain = to_full(own_rows(gain_gate, channels))[None]
    keys = [(inner - 1, 0)]
    mixed, arrays = reduce_rows(
        mix_out(y, gate_in, gate_gain, out_rows, seq_devices)[None], parcels(*keys)
    )
    unpack(keys, arrays)
    gate_scale = lax.rsqrt(
        (mixed[:, width : width + 1] + mixed[:, width + 1 : width + 2]) / inner_width + EPSILON
    )
    mix_sum = mixed[:, :width] * gate_scale
    after_mix = residual + mix_sum

    gain_moe = to_full(gain_moe)
    moe_scale = norm_scale(after_mix)
    moe_unit = after_mix * moe_scale
    moe_in = to_low(moe_unit * gain_moe)
    logits = matmul(moe_in, router)
    route_ids = routes[0]
    chosen = to_full(
        route_ids[:, :, None] == jnp.arange(expert_total, dtype=jnp.int32)[None, None, :]
    )
    gate_values = jax.nn.softmax(jnp.sum(chosen * logits[:, None, :], axis=2), axis=1)
    gate_high = to_low(gate_values)
    gate_rest = to_low(gate_values - to_full(gate_high))
    extra = jnp.concatenate(
        [
            jnp.stack([gate_high, gate_rest], axis=2).reshape(tok_rows, 2 * top_count),
            route_ids.astype(jnp.bfloat16),
            jnp.zeros((tok_rows, LANES - 3 * top_count), jnp.bfloat16),
        ],
        axis=1,
    )
    keys = [(1, 1), (2, 0)]
    both_all, arrays = gather_rows(
        jnp.concatenate([moe_in, extra, out_grad[0]], axis=1), inner, parcels(*keys)
    )
    unpack(keys, arrays)
    both_all = both_all.reshape(blocks, tok_rows, 2 * width + LANES)
    capacity = min(tok_rows, max(2, tok_rows * top_count * 5 // (expert_total * 3)))
    slots = -(-capacity // 16) * 16
    keys = [(inner - 1, 1)]
    expert_rows, grad_rows, picks, arrays = dispatch(
        both_all, width, per_device, top_count, slots, own_first, parcels(*keys)
    )
    unpack(keys, arrays)
    keys = [(2, 1)]
    shared_res, shared_back, shared_up_grad, shared_down_grad, arrays = shared_expert(
        both_all, shared_up, shared_down, seq_devices, inner, parcels(*keys)
    )
    unpack(keys, arrays)
    order = [(shift, expert) for shift in range(inner) for expert in range(per_device)]
    pieces = [pieces[key] for key in order]
    if outer > 1:
        pieces = [
            stacked_pieces(
                [pieces[shift * per_device + expert] for shift in range(inner)],
                place,
                inner,
                (depth_rows, hidden_rows, width),
            )
            for expert in range(per_device)
        ]
    expert_res, expert_back, grads = experts(
        expert_rows, grad_rows, pieces, hidden, top_count, own_first, inner
    )
    if outer > 1:
        grads = [
            split_piece(grads[expert], shift, place, inner, (depth_rows, hidden_rows, width))
            for shift in range(inner)
            for expert in range(per_device)
        ]
    grads = dict(zip(order, grads))
    returned = {(0, expert): grads[0, expert] for expert in range(per_device)}

    def back_parcels(*keys):
        return [Parcel(grads[key], inner - key[0], inner) for key in keys]

    def unpack_back(keys, arrays):
        returned.update(zip(keys, arrays))

    keys = [(1, 0)]
    out_part, back_part, arrays = combine(
        picks, expert_res, expert_back, shared_res, shared_back, inner, back_parcels(*keys)
    )
    unpack_back(keys, arrays)
    keys = [(2, 0)]
    back, arrays = reduce_rows(
        back_part.reshape(inner, seq_devices, tok_rows, -1), back_parcels(*keys)
    )
    unpack_back(keys, arrays)
    keys = [(inner - 1, 0)]
    out_sum, arrays = reduce_rows(
        out_part.reshape(inner, seq_devices, tok_rows, -1), back_parcels(*keys)
    )
    unpack_back(keys, arrays)
    layer_out = to_low(after_mix + to_full(out_sum))

    half = LANES // 2
    gate_grad_all = (
        back[:, width : width + expert_total]
        + back[:, width + half : width + half + expert_total]
    )
    gate_grad = jnp.sum(chosen * gate_grad_all[:, None, :], axis=2)
    mixed_gate = jnp.sum(gate_values * gate_grad, axis=1, keepdims=True)
    logit_grad = to_low(
        jnp.sum(chosen * (gate_values * (gate_grad - mixed_gate))[:, :, None], axis=1)
    )
    router_grad = left_contract(moe_in, logit_grad)
    moe_grad = back[:, :width] + right_contract(logit_grad, router)
    gain_moe_grad = jnp.sum(moe_grad * moe_unit, axis=0)
    moe_scaled = moe_grad * gain_moe
    mix_grad = to_full(out_grad[0]) + moe_scale * (
        moe_scaled - moe_unit * jnp.mean(moe_scaled * moe_unit, axis=1, keepdims=True)
    )
    mix_low = to_low(mix_grad)
    share = jnp.sum(to_full(mix_low) * mix_sum, axis=1, keepdims=True) / inner_width
    carried = put_split([share, gate_scale], tok_rows)

    keys = [(inner - 1, 1)]
    mix_group, arrays = gather_rows(
        jnp.concatenate([mix_low, carried], axis=1), 1, back_parcels(*keys)
    )
    unpack_back(keys, arrays)
    dy, gate_in_grad, proj_out_grad, gain_gate_grad = mix_back(
        mix_group[0], y, gate_in, gate_gain, out_rows
    )
    keys = [(2, 1)]
    rows_grad, conv_grad, head_grad, (taken, *arrays) = scan_backward(
        ends,
        deal_order,
        seq_rows,
        states,
        dy,
        conv_table,
        head_table,
        [PlaneSwap(rows_from_owner([proj_out_grad, shared_down_grad]))] + back_parcels(*keys),
    )
    unpack_back(keys, arrays)
    keys = [(1, 1)]
    hidden_part, main_grad, rest_grad, arrays = project_back(
        gate_in_grad, rows_grad, hidden_in, proj_in, dt_columns, seq_devices, back_parcels(*keys)
    )
    unpack_back(keys, arrays)
    experts_grad, experts_down_grad = collect(
        place[None], [returned[key] for key in order], per_device, depth_rows, hidden_rows, width
    )
    rows_part = jnp.concatenate(
        [
            taken.reshape(shard_devices, -1, width),
            shared_up_grad.reshape(shard_devices, -1, width),
        ],
        axis=1,
    )
    main_part = main_grad.reshape(shard_devices, depth_rows, 2 * channels)
    if outer == 1:
        hidden_grad, main_all, rows_all = settle(hidden_part[None], [main_part, rows_part], inner)
    else:
        hidden_grad = reduce_rows(hidden_part[None])[0]
        main_all = lax.all_gather(lax.psum_scatter(main_part, "shard"), "seq")
        rows_all = lax.all_gather(lax.psum_scatter(rows_part, "shard"), "seq")
    (w_out_grad, w_shared_down_grad), shared_columns = rows_of_shard(
        rows_all, [w_out, w_shared_down]
    )
    w_shared_grad = (
        to_full(shared_columns)
        .reshape(seq_devices, depth_rows, 2, shared_part)
        .transpose(1, 2, 0, 3)
        .reshape(depth_rows, 2 * shared_width)
    )
    own_scale = norm_scale(residual)
    own_unit = residual * own_scale
    gain_in_grad = jnp.sum(hidden_grad * own_unit, axis=0)
    hidden_scaled = hidden_grad * gain_row
    tokens_grad = to_low(
        mix_grad
        + own_scale
        * (hidden_scaled - own_unit * jnp.mean(hidden_scaled * own_unit, axis=1, keepdims=True))
    )

    def spread(values, length, axis=0):
        shape = values.shape[:axis] + (length,) + values.shape[axis + 1 :]
        return lax.dynamic_update_slice_in_dim(
            jnp.zeros(shape, values.dtype), values, part * values.shape[axis], axis
        )

    state_columns = rest_grad.shape[1] - LANES
    conv_rows_grad = conv_grad[:5].T
    conv_full = jnp.concatenate(
        [spread(conv_rows_grad[:channels], inner_width), conv_rows_grad[channels:]], axis=0
    )
    by_depth = [
        rest_grad[:, :state_columns],
        to_low(router_grad),
        spread(rest_grad[:, state_columns : state_columns + heads], head_total, 1),
        to_low(jnp.stack([gain_in_grad, gain_moe_grad], axis=1)),
    ]
    by_shard = [
        conv_full[:, :4],
        conv_full[:, 4],
        spread(head_grad[0, :heads], head_total),
        spread(head_grad[1, :heads], head_total),
        spread(head_grad[2, :heads], head_total),
        spread(gain_gate_grad[0], inner_width),
    ]
    shapes = [(piece.shape[0] // shard_devices,) + piece.shape[1:] for piece in by_shard]
    by_shard = jnp.concatenate(
        [to_low(piece).reshape(shard_devices, -1) for piece in by_shard], axis=1
    )
    extents = [piece.shape[1] for piece in by_depth]
    used = sum(extents)
    if outer == 1:
        wide = -(-used // LANES) * LANES
        by_depth.append(jnp.zeros((width, wide - used), jnp.bfloat16))
        by_depth = jnp.concatenate(by_depth, axis=1).reshape(inner, seq_devices, -1, wide)
        depth_each = by_depth.shape[2]
        size = by_shard.shape[1]
        each = -(-size // (seq_devices * wide))
        padded = -(-each // 16) * 16
        by_shard = jnp.pad(by_shard, ((0, 0), (0, each * seq_devices * wide - size)))
        by_shard = by_shard.reshape(inner, seq_devices, each, wide)
        by_shard = jnp.pad(by_shard, ((0, 0), (0, 0), (0, padded - each), (0, 0)))
        small_all = sum_all(jnp.concatenate([by_depth, by_shard], axis=2))
        w_in_grad = assemble(main_all, small_all, w_in.shape[1])
        depth_sum = to_full(small_all[:, :depth_each].reshape(depth_rows, wide))
        shard_sum = small_all[:, depth_each : depth_each + each].reshape(-1)
    else:
        by_depth = jnp.concatenate(by_depth, axis=1).reshape(shard_devices, -1)
        packed = jnp.concatenate([by_depth, by_shard], axis=1)
        summed = lax.psum(lax.psum_scatter(packed, "shard", tiled=True), "seq").reshape(-1)
        depth_sum = to_full(summed[: depth_rows * used]).reshape(depth_rows, used)
        shard_sum = summed[depth_rows * used :]
        w_in_main = (
            main_all.reshape(seq_devices, depth_rows, 2, channels)
            .transpose(1, 2, 0, 3)
            .reshape(depth_rows, 2 * inner_width)
        )
        w_in_grad = jnp.concatenate([to_full(w_in_main), depth_sum[:, :state_columns]], axis=1)
    results, start = [], 0
    for shape in shapes:
        size = 1
        for extent in shape:
            size *= extent
        results.append(to_full(shard_sum[start : start + size]).reshape(shape))
        start += size
    conv_w_grad, conv_b_grad, dt_bias_grad, a_log_grad, d_skip_grad, norm_gate_grad = results
    start = state_columns
    w_router_grad = depth_sum[:, start : start + expert_total]
    start += expert_total
    w_dt_grad = depth_sum[:, start : start + head_total]
    start += head_total
    norm_in_grad, norm_moe_grad = depth_sum[:, start], depth_sum[:, start + 1]
    return (
        layer_out[None],
        tokens_grad[None],
        norm_in_grad,
        w_in_grad,
        w_dt_grad,
        conv_w_grad,
        conv_b_grad,
        dt_bias_grad,
        a_log_grad,
        d_skip_grad,
        norm_gate_grad,
        w_out_grad,
        norm_moe_grad,
        w_router_grad,
        w_shared_grad,
        w_shared_down_grad,
        experts_grad,
        experts_down_grad,
    )


def solution(mesh):
    placed = (
        P("shard", "seq", None),
        P("shard", "seq", None),
        P("shard", None),
        P("shard", None),
        P("shard", "seq", None),
        P("shard"),
        P("shard", None),
        P("shard", None),
        P("shard", None),
        P("shard"),
        P("shard"),
        P("shard"),
        P("shard"),
        P("shard"),
        P("shard", None),
        P("shard"),
        P("shard", None),
        P("shard", None),
        P("shard", None),
        P("seq", "shard", None),
        P("seq", "shard", None),
    )
    return jax.shard_map(
        local,
        mesh=mesh,
        in_specs=placed,
        out_specs=(
            P("shard", "seq", None),
            P("shard", "seq", None),
            P("shard"),
            P("shard", None),
            P("shard", None),
            P("shard", None),
            P("shard"),
            P("shard"),
            P("shard"),
            P("shard"),
            P("shard"),
            P("shard", None),
            P("shard"),
            P("shard", None),
            P("shard", None),
            P("shard", None),
            P("seq", "shard", None),
            P("seq", "shard", None),
        ),
        check_vma=False,
    )
```

```python
import functools

import jax
import jax.numpy as jnp
from jax import lax
from jax.experimental import pallas as pl
from jax.experimental.pallas import tpu as pltpu
from jax.sharding import PartitionSpec as P

STRETCH = 256
INNER = 4
UP, DOWN = 0, 1
EPSILON = 1e-05
HIGHEST = lax.Precision.HIGHEST


def matmul(left_side, right_side):
    return jnp.dot(left_side, right_side, preferred_element_type=jnp.float32)


def left_contract(left_side, right_side):
    return lax.dot_general(
        left_side, right_side, (((0,), (0,)), ((), ())), preferred_element_type=jnp.float32
    )


def right_contract(left_side, right_side):
    return lax.dot_general(
        left_side, right_side, (((1,), (1,)), ((), ())), preferred_element_type=jnp.float32
    )


def to_low(values):
    return values.astype(jnp.bfloat16)


def to_full(values):
    return values.astype(jnp.float32)


def norm_scale(values):
    return lax.rsqrt(jnp.mean(values * values, axis=-1, keepdims=True) + EPSILON)


LANES = 128
VMEM_BYTES = 56 * 1024 * 1024


def cost_of(micros):
    return pl.CostEstimate(flops=0, transcendentals=0, bytes_accessed=int(micros * 3.6e6))


def dot_rows(left_side, right_side, precision=None):
    return lax.dot_general(
        left_side,
        right_side,
        (((0,), (0,)), ((), ())),
        precision=precision,
        preferred_element_type=jnp.float32,
    )


def dot_lanes(left_side, right_side, precision=None):
    return lax.dot_general(
        left_side,
        right_side,
        (((1,), (1,)), ((), ())),
        precision=precision,
        preferred_element_type=jnp.float32,
    )


def dot_full(left_side, right_side, precision=None):
    return jnp.dot(
        left_side, right_side, precision=precision, preferred_element_type=jnp.float32
    )


def iota_of(shape, axis):
    return lax.broadcasted_iota(jnp.int32, shape, axis)


def ids_at(places, ends_ref):
    total = jnp.zeros(places.shape, jnp.int32)
    for seq in range(ends_ref.shape[0]):
        total = total + (places >= ends_ref[seq]).astype(jnp.int32)
    return total


def id_at(place, ends_ref):
    total = jnp.int32(0)
    for seq in range(ends_ref.shape[0]):
        total = total + (place >= ends_ref[seq]).astype(jnp.int32)
    return total


class Stretch:
    def __init__(self, start, rows, before, conv_ref, head_ref, ends_ref, channels):
        length = rows.shape[0]
        self.channels = channels
        self.heads = channels // 64
        width = conv_ref.shape[1]
        state = (width - channels) // 2
        places = start + iota_of((length, 1), 0)
        self.ids = ids_at(places, ends_ref)
        self.ids_row = ids_at(start + iota_of((1, length), 1), ends_ref)
        inputs = rows[:, :width]
        joined = jnp.concatenate([before[:, :width], inputs], axis=0)
        self.shifted = [inputs]
        value = conv_ref[4:5, :] + inputs * conv_ref[3:4, :]
        for offset in range(1, 4):
            same = (ids_at(places - offset, ends_ref) == self.ids) & (places >= offset)
            moved = pltpu.roll(joined, offset, 0)[8:, :]
            moved = jnp.where(same, moved, 0.0)
            self.shifted.append(moved)
            value = value + moved * conv_ref[3 - offset : 4 - offset, :]
        self.value = value
        self.sig = jax.nn.sigmoid(value)
        act = value * self.sig
        self.x = act[:, :channels]
        self.b = act[:, channels : channels + state]
        self.c = act[:, channels + state :]
        self.b_low = to_low(self.b)
        self.c_low = to_low(self.c)
        self.dt_in = rows[:, width:] + head_ref[0:1, :]
        self.dt = jnp.maximum(self.dt_in, 0.0) + jnp.log1p(jnp.exp(-jnp.abs(self.dt_in)))
        self.rate = head_ref[1:2, :]
        rows_at = iota_of((length, length), 0)
        columns_at = iota_of((length, length), 1)
        lower = (rows_at >= columns_at).astype(jnp.float32)
        self.cum = dot_full(lower, self.dt * self.rate, HIGHEST)
        self.cum_rows = self.cum.T[:8, :]
        self.dt_rows = self.dt.T[:8, :]
        self.causal = (self.ids == self.ids_row) & (rows_at >= columns_at)
        self.scores = dot_lanes(self.c_low, self.b_low)
        last_id = jnp.where(start > 0, id_at(start - 1, ends_ref), -1)
        end_id = id_at(start + length - 1, ends_ref)
        self.enter = jnp.where(self.ids == last_id, jnp.exp(self.cum), 0.0)
        end_cum = self.cum[length - 1 : length, :]
        self.tail = jnp.where(self.ids == end_id, jnp.exp(end_cum - self.cum), 0.0)
        self.tail_weight = self.tail * self.dt
        self.keep = jnp.where(last_id == end_id, jnp.exp(end_cum), 0.0)

    def decay(self, head):
        spread = self.cum[:, head : head + 1] - self.cum_rows[head : head + 1, :]
        return jnp.where(self.causal, jnp.exp(jnp.minimum(spread, 0.0)), 0.0)

    def per_channel(self, by_head):
        return jnp.concatenate(
            [
                jnp.broadcast_to(by_head[:, head : head + 1], (by_head.shape[0], 64))
                for head in range(self.heads)
            ],
            axis=1,
        )

    def state_keep(self):
        return jnp.concatenate(
            [
                jnp.broadcast_to(self.keep[:, head : head + 1], (64, LANES))
                for head in range(self.heads)
            ],
            axis=0,
        )


def head_lanes(channels):
    return (iota_of((channels, LANES), 0) // 64 == iota_of((channels, LANES), 1)).astype(
        jnp.float32
    )


def pick_rows(deal_ref, start, length):
    places = start + iota_of((length, 1), 0)
    return jnp.where(deal_ref[...] == places, 1.0, 0.0).astype(jnp.bfloat16)


def scan_forward_kernel(
    ends_ref, deal_ref, rows_ref, conv_ref, head_ref, y_ref, seq_ref, states_ref, before, state, total
):
    step = pl.program_id(0)
    length = seq_ref.shape[0]
    channels = y_ref.shape[1]
    start = step * length

    @pl.when(step == 0)
    def _():
        before[...] = jnp.zeros_like(before)
        state[...] = jnp.zeros_like(state)
        total[...] = jnp.zeros_like(total)

    picks = pick_rows(deal_ref, start, length)
    rows = dot_full(picks, rows_ref[...])
    seq_ref[...] = to_low(rows)
    part = Stretch(start, rows, before[...], conv_ref, head_ref, ends_ref, channels)
    before[...] = rows[length - 8 :, :]
    state_now = state[...]
    states_ref[0] = state_now
    x_low = to_low(part.x)
    outs = []
    lane = iota_of((length, LANES), 1)
    for pair in range(channels // LANES):
        x_pair = x_low[:, pair * LANES : (pair + 1) * LANES]
        halves = []
        for head in (2 * pair, 2 * pair + 1):
            weights = part.decay(head) * part.scores * part.dt_rows[head : head + 1, :]
            halves.append(dot_full(to_low(weights), x_pair))
        outs.append(jnp.where(lane < 64, halves[0], halves[1]))
    earlier = dot_lanes(part.c_low, to_low(state_now))
    skip = part.per_channel(head_ref[2:3, :])
    y = jnp.concatenate(outs, axis=1) + part.per_channel(part.enter) * earlier + skip * part.x
    state[...] = part.state_keep() * state_now + dot_rows(
        to_low(part.per_channel(part.tail_weight) * part.x), part.b_low
    )
    total[...] += dot_rows(picks, to_low(y))

    @pl.when(step == pl.num_programs(0) - 1)
    def _():
        y_ref[...] = to_low(total[...])


def scan_forward(ends, deal_row, rows, conv_table, head_table, channels, freight):
    group_rows, width = rows.shape
    steps = group_rows // STRETCH
    state_rows = (channels, LANES)
    return run(
        scan_forward_kernel,
        (ends, deal_row, rows, conv_table, head_table),
        grid=(steps,),
        in_specs=[
            pl.BlockSpec(memory_space=pltpu.SMEM),
            whole(deal_row.shape),
            whole(rows.shape),
            whole(conv_table.shape),
            whole(head_table.shape),
        ],
        out_specs=[
            whole((group_rows, channels)),
            pl.BlockSpec((STRETCH, width), lambda step: (step, 0)),
            pl.BlockSpec((1,) + state_rows, lambda step: (step, 0, 0)),
        ],
        out_shape=[
            jax.ShapeDtypeStruct((group_rows, channels), jnp.bfloat16),
            jax.ShapeDtypeStruct((group_rows, width), jnp.bfloat16),
            jax.ShapeDtypeStruct((steps,) + state_rows, jnp.float32),
        ],
        scratch=[
            pltpu.VMEM((8, width), jnp.float32),
            pltpu.VMEM(state_rows, jnp.float32),
            pltpu.VMEM((group_rows, channels), jnp.float32),
        ],
        freight=freight,
        micros=25,
        name="scan_forward",
    )


def scan_backward_kernel(
    ends_ref,
    deal_ref,
    seq_ref,
    states_ref,
    dy_ref,
    conv_ref,
    head_ref,
    other_ref,
    drows_ref,
    conv_grad_ref,
    head_grad_ref,
    other_sum_ref,
    after,
    state_grad,
    *other_scratch,
):
    order = pl.program_id(0)
    steps = pl.num_programs(0)
    reducer = Reducer(other_ref.shape[0], other_ref, other_sum_ref, other_scratch)

    @pl.when(order == 0)
    def _():
        reducer.begin()

    step = steps - 1 - order
    length = STRETCH
    channels = dy_ref.shape[1]
    width = conv_ref.shape[1]
    state_width = (width - channels) // 2
    start = pl.multiple_of(step * length, length)

    @pl.when(order == 0)
    def _():
        after[...] = jnp.zeros_like(after)
        state_grad[...] = jnp.zeros_like(state_grad)
        drows_ref[...] = jnp.zeros_like(drows_ref)
        conv_grad_ref[...] = jnp.zeros_like(conv_grad_ref)
        head_grad_ref[...] = jnp.zeros_like(head_grad_ref)

    picks = pick_rows(deal_ref, start, length)
    dy = dot_full(picks, dy_ref[...])
    rows = seq_ref[pl.ds(start, length), :].astype(jnp.float32)
    place = pl.multiple_of(jnp.maximum(start - 16, 0), 16)
    before = seq_ref[pl.ds(place, 16), :].astype(jnp.float32)[8:, :]
    part = Stretch(start, rows, before, conv_ref, head_ref, ends_ref, channels)
    state_now = states_ref[0]
    state_low = to_low(state_now)
    next_grad = state_grad[...]
    next_low = to_low(next_grad)
    lanes_of = head_lanes(channels)
    x_low = to_low(part.x)
    dy_low = to_low(dy)
    lane = iota_of((length, LANES), 1)

    enter = part.per_channel(part.enter)
    tail_weight = part.per_channel(part.tail_weight)
    earlier = dot_lanes(part.c_low, state_low)
    enter_grad = dot_full(dy * earlier, lanes_of, HIGHEST)
    entered = to_low(enter * dy)
    c_grad = dot_full(entered, state_low)
    state_grad[...] = part.state_keep() * next_grad + dot_rows(entered, part.c_low)
    onward = dot_lanes(part.b_low, next_low)
    x_grad = part.per_channel(head_ref[2:3, :]) * dy + tail_weight * onward
    tail_grad = dot_full(part.x * onward, lanes_of, HIGHEST)
    b_grad = dot_full(to_low(tail_weight * part.x), next_low)
    tail_part = tail_grad * part.tail_weight
    cum_grad = enter_grad * part.enter - tail_part
    dt_grad = tail_grad * part.tail
    kept = dot_lanes(jnp.ones((8, LANES), jnp.float32), next_grad * state_now, HIGHEST)
    keep_grad = dot_full(kept, lanes_of, HIGHEST)[:1, :]
    end_grad = jnp.sum(tail_part, axis=0, keepdims=True) + keep_grad * part.keep

    score_grad = jnp.zeros((length, length), jnp.float32)
    cum_columns, cum_rows, dt_rows, outs = [], [], [], []
    for pair in range(channels // LANES):
        x_pair = x_low[:, pair * LANES : (pair + 1) * LANES]
        dy_pair = dy_low[:, pair * LANES : (pair + 1) * LANES]
        halves = []
        for half, head in enumerate((2 * pair, 2 * pair + 1)):
            mine = (lane < 64) if half == 0 else (lane >= 64)
            weight_grad = dot_lanes(jnp.where(mine, dy_pair, jnp.zeros_like(dy_pair)), x_pair)
            decay = part.decay(head)
            dt_row = part.dt_rows[head : head + 1, :]
            by_decay = weight_grad * decay
            by_dt = by_decay * part.scores
            by_spread = by_dt * dt_row
            dt_rows.append(jnp.sum(by_dt, axis=0, keepdims=True))
            cum_rows.append(jnp.sum(by_spread, axis=0, keepdims=True))
            cum_columns.append(jnp.sum(by_spread, axis=1, keepdims=True))
            score_grad = score_grad + by_decay * dt_row
            halves.append(dot_rows(to_low(decay * part.scores * dt_row), dy_pair))
        outs.append(jnp.where(lane < 64, halves[0], halves[1]))
    x_grad = x_grad + jnp.concatenate(outs, axis=1)
    score_low = to_low(score_grad)
    c_grad = c_grad + dot_full(score_low, part.b_low)
    b_grad = b_grad + dot_rows(score_low, part.c_low)

    heads = len(dt_rows)
    blank = jnp.zeros((LANES - heads, length), jnp.float32)
    dt_grad = dt_grad + jnp.concatenate(dt_rows + [blank], axis=0).T
    cum_grad = cum_grad - jnp.concatenate(cum_rows + [blank], axis=0).T
    for head in range(heads):
        cum_grad = cum_grad + jnp.where(lane == head, cum_columns[head], 0.0)
    at_end = iota_of((length, 1), 0) == length - 1
    cum_grad = cum_grad + jnp.where(at_end, end_grad, 0.0)
    upper = (iota_of((length, length), 1) >= iota_of((length, length), 0)).astype(jnp.float32)
    log_grad = dot_full(upper, cum_grad, HIGHEST)
    dt_grad = dt_grad + log_grad * part.rate
    dt_in_grad = dt_grad * jax.nn.sigmoid(part.dt_in)
    dt_in_grad = jnp.where(lane < heads, dt_in_grad, 0.0)
    head_grad_ref[0:1, :] += jnp.sum(dt_in_grad, axis=0, keepdims=True)
    head_grad_ref[1:2, :] += jnp.sum(log_grad * part.dt, axis=0, keepdims=True) * part.rate
    skip_sum = jnp.broadcast_to(jnp.sum(dy * part.x, axis=0, keepdims=True), (8, channels))
    head_grad_ref[2:3, :] += dot_full(skip_sum, lanes_of, HIGHEST)[:1, :]

    act_grad = jnp.concatenate([x_grad, b_grad, c_grad], axis=1)
    value_grad = act_grad * part.sig * (1.0 + part.value * (1.0 - part.sig))
    conv_grad_ref[4:5, :] += jnp.sum(value_grad, axis=0, keepdims=True)
    for offset in range(4):
        conv_grad_ref[3 - offset : 4 - offset, :] += jnp.sum(
            value_grad * part.shifted[offset], axis=0, keepdims=True
        )
    joined = jnp.concatenate([value_grad, after[...]], axis=0)
    places = start + iota_of((length, 1), 0)
    rows_grad = value_grad * conv_ref[3:4, :]
    for offset in range(1, 4):
        moved = pltpu.roll(joined, length + 8 - offset, 0)[:length, :]
        same = (ids_at(places + offset, ends_ref) == part.ids) & (
            places + offset < steps * length
        )
        rows_grad = rows_grad + jnp.where(same, moved, 0.0) * conv_ref[3 - offset : 4 - offset, :]
    after[...] = value_grad[:8, :]
    drows_ref[...] += to_low(
        dot_rows(picks, to_low(jnp.concatenate([rows_grad, dt_in_grad], axis=1)))
    )

    stages = reducer.inner + 3
    last = dy_ref.shape[0] // length - 1
    for count in range(stages):

        @pl.when(order == min(count, last))
        def _():
            reducer.step(count)

    @pl.when(order == steps - 1)
    def _():
        reducer.finish()


def scan_backward(
    ends, deal_row, seq_rows, states, dy, conv_table, head_table, other, freight
):
    group_rows, width = seq_rows.shape
    channels = dy.shape[1]
    steps = group_rows // STRETCH
    return run(
        scan_backward_kernel,
        (ends, deal_row, seq_rows, states, dy, conv_table, head_table, other),
        grid=(steps,),
        in_specs=[
            pl.BlockSpec(memory_space=pltpu.SMEM),
            whole(deal_row.shape),
            once(seq_rows.shape),
            pl.BlockSpec((1, channels, LANES), lambda step: (steps - 1 - step, 0, 0)),
            once(dy.shape),
            whole(conv_table.shape),
            whole(head_table.shape),
            pl.BlockSpec(memory_space=pl.ANY),
        ],
        out_specs=[
            whole((group_rows, width)),
            whole(conv_table.shape),
            whole(head_table.shape),
            whole(other.shape[2:]),
        ],
        out_shape=[
            jax.ShapeDtypeStruct((group_rows, width), jnp.bfloat16),
            jax.ShapeDtypeStruct(conv_table.shape, jnp.float32),
            jax.ShapeDtypeStruct(head_table.shape, jnp.float32),
            jax.ShapeDtypeStruct(other.shape[2:], jnp.float32),
        ],
        scratch=[
            pltpu.VMEM((8, conv_table.shape[1]), jnp.float32),
            pltpu.VMEM((channels, LANES), jnp.float32),
        ]
        + Reducer.scratch(other.shape[0], *other.shape[2:]),
        freight=freight,
        flips=FLIPS,
        inner=other.shape[0],
        micros=40,
        name="scan_backward",
    )


def whole(shape):
    return pl.BlockSpec(shape, lambda *steps: (0,) * len(shape))


def once(shape):
    return pl.BlockSpec(
        shape, lambda *steps: (0,) * len(shape), pipeline_mode=pl.Buffered(buffer_count=1)
    )


MESH = pl.DeviceIdType.MESH
FLIPS = (1, 2, 4)


def flipped(place, flip):
    result = place
    for bit in FLIPS:
        if flip & bit:
            result = result + bit - 2 * bit * lax.rem(lax.div(place, bit), 2)
    return result


def own_shard_group(inner):
    shard = lax.axis_index("shard")
    place = lax.rem(shard, inner)
    return place, shard - place


def peers_in_order(place, inner):
    if inner == 1:
        return []
    if inner == 4:
        half = lax.div(place, 2)
        return [flipped(place, 1), 2 - half, 3 - 3 * half]
    return [lax.rem(place + shift, inner) for shift in range(1, inner)]


def greet(flips, inner):
    barrier = pltpu.get_barrier_semaphore()
    part = lax.axis_index("seq")
    place, first = own_shard_group(inner)
    for flip in flips:
        pl.semaphore_signal(
            barrier, inc=1, device_id={"seq": flipped(part, flip)}, device_id_type=MESH
        )
    for peer in peers_in_order(place, inner):
        pl.semaphore_signal(
            barrier, inc=1, device_id={"shard": first + peer}, device_id_type=MESH
        )
    pl.semaphore_wait(barrier, len(flips) + inner - 1)


class Parcel:
    flips = ()
    sems = 1

    def __init__(self, array, shift, inner, index=None, output=None):
        self.array, self.shift, self.inner, self.index = array, shift, inner, index
        self.shape = array.shape if index is None else array.shape[1:]
        self.output = output

    def moves(self, source, target):
        place, first = own_shard_group(self.inner)
        to = lax.rem(place + self.shift, self.inner)
        if self.index is not None:
            source = source.at[self.index(to)]
        return [(source, target, target, {"shard": first + to})]

    def stays(self, source, target):
        return []


class PlaneSwap:
    flips = (1, 2, 3, 4, 5, 6, 7)
    inner = 1
    sems = 8

    output = None

    def __init__(self, array):
        self.array, self.shape = array, array.shape

    def moves(self, source, target):
        part = lax.axis_index("seq")
        return [
            (
                source.at[flipped(part, flip)],
                target.at[part],
                target.at[flipped(part, flip)],
                {"seq": flipped(part, flip)},
            )
            for flip in self.flips
        ]

    def stays(self, source, target):
        part = lax.axis_index("seq")
        return [(source.at[part], target.at[part])]


COLLECTIVES = []


def run(
    kernel,
    args,
    *,
    in_specs,
    out_specs,
    out_shape,
    name,
    micros,
    grid=(),
    scratch=(),
    freight=(),
    flips=(),
    inner=1,
    late=False,
):
    freight = list(freight)
    flips = tuple(sorted(set(flips).union(*[item.flips for item in freight])))
    inner = max([inner] + [item.inner for item in freight])
    talks = bool(flips) or inner > 1
    count_in, count_out, count_scratch = len(args), len(out_shape), len(scratch)
    count = len(freight)
    loaded = [item for item in freight if item.output is None]

    def wrapped(*refs):
        ins, refs = refs[:count_in], refs[count_in:]
        sources, refs = list(refs[: len(loaded)]), refs[len(loaded) :]
        outs, refs = refs[:count_out], refs[count_out:]
        sources = [
            sources.pop(0) if item.output is None else outs[item.output] for item in freight
        ]
        targets, refs = refs[:count], refs[count:]
        own, refs = refs[:count_scratch], refs[count_scratch:]

        def remote(item, place, order, source, target, device):
            send, recv = refs[3 * place : 3 * place + 2]
            return pltpu.make_async_remote_copy(
                src_ref=source,
                dst_ref=target,
                send_sem=send.at[order],
                recv_sem=recv.at[order],
                device_id=device,
                device_id_type=MESH,
            )

        def moves(chosen):
            for place, item in enumerate(freight):
                if not chosen(item):
                    continue
                for order, move in enumerate(item.moves(sources[place], targets[place])):
                    yield item, place, order, move

        def stays(chosen):
            for place, item in enumerate(freight):
                if not chosen(item):
                    continue
                for source, target in item.stays(sources[place], targets[place]):
                    yield pltpu.make_async_copy(source, target, refs[3 * place + 2])

        def depart(chosen=lambda item: True):
            for item, place, order, (source, target, _, device) in moves(chosen):
                remote(item, place, order, source, target, device).start()
            for copy in stays(chosen):
                copy.start()

        def arrive(chosen=lambda item: True):
            for item, place, order, (source, target, arrival, device) in moves(chosen):
                remote(item, place, order, source, arrival, device).wait_recv()
                remote(item, place, order, source, target, device).wait_send()
            for copy in stays(chosen):
                copy.wait()

        if grid:
            at = [pl.program_id(axis) for axis in range(len(grid))]
            first, last = at[0] == 0, at[0] == grid[0] - 1
            for axis in range(1, len(grid)):
                first = first & (at[axis] == 0)
                last = last & (at[axis] == grid[axis] - 1)
            if talks:

                @pl.when(first)
                def _():
                    greet(flips, inner)
                    if not late:
                        depart()

            if late:
                kernel(depart, arrive, targets, *ins, *outs, *own)
            else:
                kernel(*ins, *outs, *own)
            if talks and not late:
                pl.when(last)(arrive)
        else:
            if talks:
                greet(flips, inner)
            if late:
                kernel(depart, *ins, *outs, *own)
            else:
                depart()
                kernel(*ins, *outs, *own)
            arrive()

    anywhere = pl.BlockSpec(memory_space=pl.ANY)
    extra = {}
    if talks:
        COLLECTIVES.append(name)
        extra = dict(collective_id=len(COLLECTIVES), has_side_effects=True)
    sems = []
    for item in freight:
        sems += [
            pltpu.SemaphoreType.DMA((item.sems,)),
            pltpu.SemaphoreType.DMA((item.sems,)),
            pltpu.SemaphoreType.DMA(()),
        ]
    results = pl.pallas_call(
        wrapped,
        grid=grid,
        in_specs=list(in_specs) + [anywhere] * len(loaded),
        out_specs=list(out_specs) + [anywhere] * count,
        out_shape=list(out_shape)
        + [jax.ShapeDtypeStruct(item.shape, item.array.dtype) for item in freight],
        scratch_shapes=list(scratch) + sems,
        compiler_params=pltpu.CompilerParams(vmem_limit_bytes=VMEM_BYTES, **extra),
        cost_estimate=cost_of(micros),
        name=name,
    )(*args, *[item.array for item in loaded])
    results = list(results)
    if freight:
        return results[:count_out] + [results[count_out:]]
    return results


class LineSum:
    def __init__(self, inner, sums, from_below, from_above, send, below_recv, above_recv):
        self.inner = inner
        self.sums, self.from_below, self.from_above = sums, from_below, from_above
        self.send, self.below_recv, self.above_recv = send, below_recv, above_recv
        self.place, self.first = own_shard_group(inner)
        self.targets = list(reversed(peers_in_order(self.place, inner))) + [self.place]

    def copy(self, order, up):
        target = self.targets[order]
        inbox = self.from_below if up else self.from_above
        recv = self.below_recv if up else self.above_recv
        return pltpu.make_async_remote_copy(
            src_ref=self.sums.at[order],
            dst_ref=inbox.at[target],
            send_sem=self.send.at[order],
            recv_sem=recv.at[target],
            device_id={"shard": self.first + self.place + (1 if up else -1)},
            device_id_type=MESH,
        )

    def arrived(self, target, up):
        inbox = self.from_below if up else self.from_above
        recv = self.below_recv if up else self.above_recv
        pltpu.make_async_remote_copy(
            src_ref=inbox.at[target],
            dst_ref=inbox.at[target],
            send_sem=self.send.at[0],
            recv_sem=recv.at[target],
            device_id={"shard": self.first + self.place + (-1 if up else 1)},
            device_id_type=MESH,
        ).wait_recv()
        return to_full(inbox[target])

    def ways(self):
        return ((True, self.place > 0), (False, self.place < self.inner - 1))

    def push(self, order):
        target = self.targets[order]
        for up, comes in self.ways():
            heads = (target > self.place) if up else (target < self.place)

            @pl.when(heads & comes)
            def _():
                self.sums[order] = to_low(
                    to_full(self.sums[order]) + self.arrived(target, up)
                )

            @pl.when(heads)
            def _():
                self.copy(order, up).start()

    def add_own(self, total):
        for up, comes in self.ways():

            @pl.when(comes)
            def _():
                total[...] += self.arrived(self.place, up)

    def finish(self):
        for order in range(self.inner - 1):
            for up in (True, False):
                target = self.targets[order]

                @pl.when((target > self.place) if up else (target < self.place))
                def _():
                    self.copy(order, up).wait_send()

    @staticmethod
    def scratch(inner, rows, width):
        sems = lambda *shape: pltpu.SemaphoreType.DMA(shape)
        return [
            pltpu.VMEM((max(1, inner - 1), rows, width), jnp.bfloat16),
            pltpu.VMEM((inner, rows, width), jnp.bfloat16),
            pltpu.VMEM((inner, rows, width), jnp.bfloat16),
            sems(max(1, inner - 1)),
            sems(inner),
            sems(inner),
        ]


class Reducer:
    def __init__(self, inner, p_ref, total, refs):
        self.inner, self.p_ref, self.total = inner, p_ref, total
        self.held, self.paired, self.turned, self.crossed = refs[:4]
        self.load, self.core_send, self.core_recv = refs[4:7]
        self.turn_send, self.turn_recv, self.cross_send, self.cross_recv = refs[7:11]
        self.line = LineSum(inner, *refs[11:])
        self.part = lax.axis_index("seq")
        half = self.held.shape[2] // 2
        self.spans = [pl.ds(0, half), pl.ds(half, half)]

    @staticmethod
    def scratch(inner, rows, width):
        low = jnp.bfloat16
        sems = lambda *shape: pltpu.SemaphoreType.DMA(shape)
        return [
            pltpu.VMEM((inner, 4, rows, width), low),
            pltpu.VMEM((inner, 4, rows, width), low),
            pltpu.VMEM((inner, 2, rows // 2, width), low),
            pltpu.VMEM((inner, 4, rows // 2, width), low),
            sems(inner, 4),
            sems(inner, 4),
            sems(inner, 4),
            sems(inner, 2),
            sems(inner, 2),
            sems(inner, 4),
            sems(inner, 4),
        ] + LineSum.scratch(inner, rows, width)

    EVENS = (6, 2, 4, 0)

    def to_core(self, order, slot):
        return pltpu.make_async_remote_copy(
            src_ref=self.p_ref.at[
                self.line.targets[order], flipped(self.part, self.EVENS[slot] + 1)
            ],
            dst_ref=self.paired.at[order, slot],
            send_sem=self.core_send.at[order, slot],
            recv_sem=self.core_recv.at[order, slot],
            device_id={"seq": flipped(self.part, 1)},
            device_id_type=MESH,
        )

    def loading(self, order, slot):
        return pltpu.make_async_copy(
            self.p_ref.at[self.line.targets[order], flipped(self.part, self.EVENS[slot])],
            self.held.at[order, slot],
            self.load.at[order, slot],
        )

    def turn(self, order, span):
        return pltpu.make_async_remote_copy(
            src_ref=self.held.at[order, 0, self.spans[span]],
            dst_ref=self.turned.at[order, span],
            send_sem=self.turn_send.at[order, span],
            recv_sem=self.turn_recv.at[order, span],
            device_id={"seq": flipped(self.part, (2, 4)[span])},
            device_id_type=MESH,
        )

    CROSSINGS = ((1, 2, 0), (2, 4, 1), (2, 4, 0), (1, 2, 1))

    def cross(self, order, kind):
        slot, flip, span = self.CROSSINGS[kind]
        return pltpu.make_async_remote_copy(
            src_ref=self.held.at[order, slot, self.spans[span]],
            dst_ref=self.crossed.at[order, kind],
            send_sem=self.cross_send.at[order, kind],
            recv_sem=self.cross_recv.at[order, kind],
            device_id={"seq": flipped(self.part, flip)},
            device_id_type=MESH,
        )

    def begin(self):
        for order in range(self.inner):
            for slot in range(4):
                self.to_core(order, slot).start()
                self.loading(order, slot).start()

    def total_of(self, order, slot):
        self.loading(order, slot).wait()
        self.to_core(order, slot).wait_recv()
        return to_full(self.held[order, slot]) + to_full(self.paired[order, slot])

    def stage_a(self, order):
        self.held[order, 0] = to_low(self.total_of(order, 0))
        for span in range(2):
            self.turn(order, span).start()
        for slot in (1, 2):
            self.held[order, slot] = to_low(self.total_of(order, slot))
            self.cross(order, slot - 1).start()

    def stage_b(self, order):
        for kind in (2, 3):
            slot, _, span = self.CROSSINGS[kind]
            self.turn(order, span).wait_recv()
            at = self.spans[span]
            self.held[order, slot, at] = to_low(
                to_full(self.held[order, slot, at]) + to_full(self.turned[order, span])
            )
            self.cross(order, kind).start()

    def stage_c(self, order):
        total = self.total_of(order, 3)
        for kind in range(4):
            self.cross(order, kind).wait_recv()
        crossed = [to_full(self.crossed[order, kind]) for kind in range(4)]
        total = total + jnp.concatenate(
            [crossed[0] + crossed[2], crossed[1] + crossed[3]], axis=0
        )
        if order == self.inner - 1:
            self.total[...] = total
        else:
            self.line.sums[order] = to_low(total)

    def stage_d(self, order):
        if order == self.inner - 1:
            self.line.add_own(self.total)
        else:
            self.line.push(order)

    def step(self, count):
        for stage, late in (
            (self.stage_a, 0),
            (self.stage_b, 1),
            (self.stage_c, 2),
            (self.stage_d, 3),
        ):
            if 0 <= count - late < self.inner:
                stage(count - late)

    def finish(self):
        for order in range(self.inner):
            for slot in range(4):
                self.to_core(order, slot).wait_send()
            for span in range(2):
                self.turn(order, span).wait_send()
            for kind in range(4):
                self.cross(order, kind).wait_send()
        self.line.finish()

    def whole(self):
        self.begin()
        for count in range(self.inner + 3):
            self.step(count)
        self.finish()


def reduce_kernel(inner, p_ref, out_ref, *scratch):
    Reducer(inner, p_ref, out_ref, scratch).whole()


def reduce_rows(partial, freight=()):
    inner, _, rows, width = partial.shape
    return run(
        functools.partial(reduce_kernel, inner),
        (partial,),
        in_specs=[pl.BlockSpec(memory_space=pl.ANY)],
        out_specs=[pl.BlockSpec(memory_space=pltpu.VMEM)],
        out_shape=[jax.ShapeDtypeStruct((rows, width), jnp.float32)],
        scratch=Reducer.scratch(inner, rows, width),
        freight=freight,
        flips=FLIPS,
        inner=inner,
        micros=25 * inner,
        name="reduce_rows",
    )


def plane_gather(own, target, send, recv):
    part = lax.axis_index("seq")
    half = own.shape[0] // 2
    spans = [pl.ds(0, half), pl.ds(half, half)]
    started = []

    def copy_of(kind, block, span, flip, from_own=False):
        place = target(block).at[spans[span]]
        return pltpu.make_async_remote_copy(
            src_ref=own.at[spans[span]] if from_own else place,
            dst_ref=place,
            send_sem=send.at[kind],
            recv_sem=recv.at[kind],
            device_id={"seq": flipped(part, flip)},
            device_id_type=MESH,
        )

    def push(kind, block, span, flip, from_own=False):
        copy = copy_of(kind, block, span, flip, from_own)
        copy.start()
        started.append(copy)

    def arrived(kind, block, span, flip):
        copy_of(kind, block, span, flip).wait_recv()

    def first():
        for kind, span, flip in (
            (3, 1, 2), (4, 0, 4), (2, 0, 2), (5, 1, 4), (0, 0, 1), (1, 1, 1)
        ):
            push(kind, part, span, flip, True)

    def second():
        side, over = flipped(part, 2), flipped(part, 4)
        arrived(3, side, 1, 2)
        push(6, side, 1, 4)
        arrived(4, over, 0, 4)
        push(7, over, 0, 2)
        push(9, side, 1, 1)
        push(10, over, 0, 1)
        arrived(2, side, 0, 2)
        push(8, side, 0, 1)
        arrived(5, over, 1, 4)
        push(11, over, 1, 1)

    def third():
        far = flipped(part, 6)
        arrived(6, far, 1, 4)
        push(13, far, 1, 1)
        arrived(7, far, 0, 2)
        push(12, far, 0, 1)

    def last():
        for kind, flip, span in (
            (0, 1, 0), (1, 1, 1), (9, 3, 1), (10, 5, 0), (8, 3, 0), (11, 5, 1), (13, 7, 1), (12, 7, 0)
        ):
            arrived(kind, flipped(part, flip), span, 1)
        for copy in started:
            copy.wait_send()

    return first, second, third, last


def line_gather(inner, own, target, send, recv):
    place, first = own_shard_group(inner)
    half = own.shape[0] // 2
    spans = [pl.ds(0, half), pl.ds(half, half)]

    def copy_of(way, step, span):
        block = place - step if way == 0 else place + step
        to = place + 1 if way == 0 else place - 1
        spot = target(block).at[spans[span]]
        return pltpu.make_async_remote_copy(
            src_ref=own.at[spans[span]] if step == 0 else spot,
            dst_ref=spot,
            send_sem=send.at[way, step, span],
            recv_sem=recv.at[way, step, span],
            device_id={"shard": first + to},
            device_id_type=MESH,
        )

    def sends(way, step):
        if way == 0:
            return (place < inner - 1) & (place >= step)
        return (place > 0) & (place + step < inner)

    def receives(way, step):
        return place >= step if way == 0 else place + step < inner

    def start(step, span):
        for way in range(2):

            @pl.when(sends(way, step))
            def _():
                copy_of(way, step, span).start()

    def begin():
        for span in range(2):
            start(0, span)

    def onward(step):
        for span in range(2):
            for way in range(2):

                @pl.when(receives(way, step))
                def _():
                    block = place - step if way == 0 else place + step
                    spot = target(block).at[spans[span]]
                    pltpu.make_async_remote_copy(
                        src_ref=spot,
                        dst_ref=spot,
                        send_sem=send.at[way, step - 1, span],
                        recv_sem=recv.at[way, step - 1, span],
                        device_id={"shard": block + first},
                        device_id_type=MESH,
                    ).wait_recv()

            if step < inner - 1:
                start(step, span)

    def finish():
        for step in range(inner - 1):
            for span in range(2):
                for way in range(2):

                    @pl.when(sends(way, step))
                    def _():
                        copy_of(way, step, span).wait_send()

    return begin, onward, finish


def group_gather(inner, own, target, sems):
    part = lax.axis_index("seq")
    place, _ = own_shard_group(inner)
    sources = [place] + peers_in_order(place, inner)
    line_send, line_recv, send, recv = sems
    line = line_gather(inner, own, lambda p: target(p, part), line_send, line_recv)
    planes = [
        plane_gather(
            own if order == 0 else target(source, part),
            lambda b, source=source: target(source, b),
            send.at[order],
            recv.at[order],
        )
        for order, source in enumerate(sources)
    ]
    return line, planes


def group_sems(inner):
    sems = lambda *shape: pltpu.SemaphoreType.DMA(shape)
    steps = max(1, inner - 1)
    return [sems(2, steps, 2), sems(2, steps, 2), sems(inner, 14), sems(inner, 14)]


def gather_kernel(inner, depart, x_ref, out_ref, own_sem, *sems):
    part = lax.axis_index("seq")
    place, _ = own_shard_group(inner)
    own = pltpu.make_async_copy(x_ref, out_ref.at[place, part], own_sem)
    (begin, onward, finish), planes = group_gather(
        inner, x_ref, lambda p, b: out_ref.at[p, b], sems
    )
    if inner > 1:
        begin()
    planes[0][0]()
    own.start()
    planes[0][1]()
    for order in range(1, inner):
        onward(order)
        if order == inner - 1:
            depart()
        planes[order][0]()
        planes[order - 1][2]()
        planes[order][1]()
    if inner == 1:
        depart()
    planes[inner - 1][2]()
    for stages in planes:
        stages[3]()
    if inner > 1:
        finish()
    own.wait()


def gather_rows(x, inner, freight=()):
    rows, width = x.shape
    seq_devices = lax.axis_size("seq")
    return run(
        functools.partial(gather_kernel, inner),
        (x,),
        in_specs=[pl.BlockSpec(memory_space=pl.ANY)],
        out_specs=[pl.BlockSpec(memory_space=pl.ANY)],
        out_shape=[jax.ShapeDtypeStruct((inner, seq_devices, rows, width), x.dtype)],
        scratch=[pltpu.SemaphoreType.DMA(())] + group_sems(inner),
        freight=freight,
        flips=FLIPS,
        inner=inner,
        late=True,
        micros=25 * inner,
        name="gather_rows",
    )


def begin_kernel(
    inner, x_ref, g_ref, w_ref, s_ref, r_ref, x_out, g_out, w_out, s_out, r_out, own_sems, *sems
):
    part = lax.axis_index("seq")
    place, _ = own_shard_group(inner)
    rows = w_ref.shape[0]
    targets = [
        lambda p: s_out.at[p],
        lambda p: w_out.at[pl.ds(p * rows, rows)],
        lambda p: r_out.at[p],
    ]
    sources = [s_ref, w_ref, r_ref]
    lines = [
        line_gather(inner, source, target, sems[2 * order], sems[2 * order + 1])
        for order, (source, target) in enumerate(zip(sources, targets))
    ]
    line, planes = group_gather(inner, g_ref, lambda p, b: g_out.at[p, b], sems[6:10])
    lines.append(line)
    x_plane = plane_gather(x_ref, lambda b: x_out.at[b], sems[10], sems[11])
    rows_line = lines.pop(2)
    for begin_line, _, _ in lines:
        begin_line()
    x_plane[0]()
    planes[0][0]()
    owns = [
        pltpu.make_async_copy(source, target(place), own_sems.at[order])
        for order, (source, target) in enumerate(zip(sources, targets))
    ]
    owns.append(pltpu.make_async_copy(x_ref, x_out.at[part], own_sems.at[3]))
    owns.append(pltpu.make_async_copy(g_ref, g_out.at[place, part], own_sems.at[4]))
    for copy in owns:
        copy.start()
    x_plane[1]()
    planes[0][1]()
    x_plane[2]()
    planes[0][2]()
    for step in range(1, inner):
        for _, onward, _ in reversed(lines):
            onward(step)
        if step == max(1, inner - 2):
            rows_line[0]()
        planes[step][0]()
        if step > 1:
            planes[step - 1][2]()
        planes[step][1]()
    rows_line[1](1)
    planes[inner - 1][2]()
    for step in range(2, inner):
        rows_line[1](step)
    x_plane[3]()
    for stages in planes:
        stages[3]()
    for _, _, finish in lines + [rows_line]:
        finish()
    for copy in owns:
        copy.wait()


def begin(x, grad, weights, small, rows, inner):
    seq_devices = lax.axis_size("seq")
    anywhere = pl.BlockSpec(memory_space=pl.ANY)
    sems = lambda *shape: pltpu.SemaphoreType.DMA(shape)
    line_sems = [sems(2, inner - 1, 2)] * 6
    return run(
        functools.partial(begin_kernel, inner),
        (x, grad, weights, small, rows),
        in_specs=[anywhere] * 5,
        out_specs=[anywhere] * 5,
        out_shape=[
            jax.ShapeDtypeStruct((seq_devices,) + x.shape, x.dtype),
            jax.ShapeDtypeStruct((inner, seq_devices) + grad.shape, grad.dtype),
            jax.ShapeDtypeStruct((inner * weights.shape[0], weights.shape[1]), weights.dtype),
            jax.ShapeDtypeStruct((inner,) + small.shape, small.dtype),
            jax.ShapeDtypeStruct((inner,) + rows.shape, rows.dtype),
        ],
        scratch=[sems(5)] + line_sems + group_sems(inner) + [sems(14), sems(14)],
        flips=FLIPS,
        inner=inner,
        micros=130,
        name="begin",
    )


def settle_kernel(
    inner,
    counts,
    spot,
    hidden_ref,
    small_ref,
    x_ref,
    mix_ref,
    gain_ref,
    *refs,
):
    part = lax.axis_index("seq")
    place, _ = own_shard_group(inner)
    parts, refs = refs[:counts], refs[counts:]
    tokens_out, refs = refs[0], refs[1:]
    outs, refs = refs[: counts + 1], refs[counts + 1 :]
    hidden_sum, small_held, small_sum, small_load = refs[:4]
    refs = refs[4:]
    take = len(Reducer.scratch(1, 16, LANES))
    hidden = Reducer(1, hidden_ref, hidden_sum, refs[:take])
    small = Reducer(inner, small_held, small_sum, refs[take : 2 * take])
    refs = refs[2 * take :]
    lines, totals, planes, owns = [], [], [], []
    for index in range(counts + 1):
        low, gsend, grecv, here = refs[:4]
        refs = refs[4:]
        out = outs[index]
        planes.append(plane_gather(low, lambda b, out=out: out.at[b], gsend, grecv))
        owns.append((low, pltpu.make_async_copy(low, out.at[part], here)))
    loads = []
    for index in range(counts):
        total, load = refs[:2]
        line = LineSum(inner, *refs[2:8])
        refs = refs[8:]
        lines.append(line)
        totals.append(total)
        for order in range(inner - 1):
            loads.append(
                pltpu.make_async_copy(
                    parts[index].at[line.targets[order]], line.sums.at[order], load.at[order]
                )
            )
        loads.append(
            pltpu.make_async_copy(parts[index].at[place], owns[index][0], load.at[inner - 1])
        )
    small_loading = pltpu.make_async_copy(small_ref, small_held, small_load)
    for copy in loads:
        copy.start()
    small_loading.start()
    hidden.begin()

    def send_part(index):
        for copy in loads[index * inner : (index + 1) * inner]:
            copy.wait()
        totals[index][...] = to_full(owns[index][0][...])
        for order in range(inner - 1):
            lines[index].push(order)

    def gather_part(index):
        lines[index].add_own(totals[index])
        owns[index][0][...] = to_low(totals[index][...])
        planes[index][0]()
        owns[index][1].start()

    hidden.step(0)
    send_part(0)
    for count in range(1, 4):
        hidden.step(count)
    x = to_full(x_ref[...])
    scale = norm_scale(x)
    unit = x * scale
    grad = hidden_sum[...]
    gain_grad = jnp.sum(grad * unit, axis=0, keepdims=True)
    scaled = grad * gain_ref[...]
    mean = jnp.mean(scaled * unit, axis=1, keepdims=True)
    tokens_out[...] = to_low(mix_ref[...] + scale * (scaled - unit * mean))
    small_loading.wait()
    wide = small_held.shape[3]
    depth = gain_grad.shape[1] // inner
    rows16 = pl.ds(spot // 16 * 16, 16)
    at_row = iota_of((16, wide), 0) == spot % 16
    for shard in range(inner):
        row = gain_grad[:, shard * depth : (shard + 1) * depth]
        if depth < wide:
            row = jnp.concatenate([row, jnp.zeros((1, wide - depth), jnp.float32)], axis=1)
        old = to_full(small_held[shard, 0, rows16])
        small_held[shard, 0, rows16] = to_low(jnp.where(at_row, old + row, old))
    small.begin()
    small.step(0)
    for index in range(1, counts):
        send_part(index)
        small.step(index)
        gather_part(index - 1)
        if index > 1:
            planes[index - 2][1]()
    for count in range(counts, inner + 3):
        small.step(count)
    owns[counts][0][...] = to_low(small_sum[...])
    planes[counts][0]()
    owns[counts][1].start()
    if counts > 1:
        planes[counts - 2][1]()
        planes[counts - 2][2]()
    gather_part(counts - 1)
    planes[counts][1]()
    planes[counts][2]()
    planes[counts - 1][1]()
    for index in range(counts - 2):
        planes[index][2]()
    planes[counts - 1][2]()
    for plane in planes:
        plane[3]()
    hidden.finish()
    small.finish()
    for line in lines:
        line.finish()
    for _, copy in owns:
        copy.wait()


def settle(hidden, small, x, mix, gain, parts, spot, inner):
    _, _, rows, width = hidden.shape
    seq_devices = lax.axis_size("seq")
    anywhere = pl.BlockSpec(memory_space=pl.ANY)
    inside = pl.BlockSpec(memory_space=pltpu.VMEM)
    low = jnp.bfloat16
    sems = lambda *shape: pltpu.SemaphoreType.DMA(shape)
    small_rows, small_wide = small.shape[2:]
    shapes = [part.shape[1:] for part in parts] + [(small_rows, small_wide)]
    scratch = [
        pltpu.VMEM((rows, width), jnp.float32),
        pltpu.VMEM(small.shape, low),
        pltpu.VMEM((small_rows, small_wide), jnp.float32),
        sems(),
    ]
    scratch += Reducer.scratch(1, rows, width)
    scratch += Reducer.scratch(inner, small_rows, small_wide)
    for shape in shapes:
        scratch += [pltpu.VMEM(shape, low), sems(14), sems(14), sems()]
    for shape in shapes[:-1]:
        scratch += [pltpu.VMEM(shape, jnp.float32), sems(inner)]
        scratch += LineSum.scratch(inner, *shape)
    return run(
        functools.partial(settle_kernel, inner, len(parts), spot),
        (hidden, small, x, mix, gain) + tuple(parts),
        in_specs=[anywhere] * 2 + [inside] * 3 + [anywhere] * len(parts),
        out_specs=[inside] + [anywhere] * len(shapes),
        out_shape=[jax.ShapeDtypeStruct((rows, width), low)]
        + [jax.ShapeDtypeStruct((seq_devices,) + shape, low) for shape in shapes],
        scratch=scratch,
        flips=FLIPS,
        inner=inner,
        micros=90,
        name="settle",
    )


def params_of(limit=VMEM_BYTES):
    return pltpu.CompilerParams(vmem_limit_bytes=limit)


def project_kernel(x_ref, gain_ref, w_ref, dt_ref, hidden_ref, gate_ref, rows_ref):
    x = to_full(x_ref[...])
    hidden = to_low(x * norm_scale(x) * gain_ref[...])
    hidden_ref[...] = hidden
    gate_width = gate_ref.shape[1]
    used = gate_width + rows_ref.shape[1] - LANES
    projected = dot_full(hidden, w_ref[:, :used])
    gate_ref[...] = projected[:, :gate_width]
    rest = used - gate_width
    rows_ref[:, :rest] = to_low(projected[:, gate_width:])
    rows_ref[:, rest:] = to_low(dot_full(hidden, dt_ref[...]))


def project(x, gain, weights, dt_weights, gate_width, columns, freight=()):
    rows, width = x.shape
    columns = columns + LANES
    tile = 256
    block = lambda extent: pl.BlockSpec((tile, extent), lambda step: (step, 0))
    return run(
        project_kernel,
        (x, gain, weights, dt_weights,),
        grid=(rows // tile,),
        in_specs=[
            block(width), whole(gain.shape), whole(weights.shape), whole(dt_weights.shape)
        ],
        out_specs=[block(width), block(gate_width), block(columns - gate_width)],
        out_shape=[
            jax.ShapeDtypeStruct((rows, width), jnp.bfloat16),
            jax.ShapeDtypeStruct((rows, gate_width), jnp.float32),
            jax.ShapeDtypeStruct((rows, columns - gate_width), jnp.bfloat16),
        ],
        freight=freight,
        micros=11,
        name="project",
    )


def put_split(columns, rows):
    lane = iota_of((rows, LANES), 1)
    result = jnp.zeros((rows, LANES), jnp.float32)
    for place, column in enumerate(columns):
        high = to_full(to_low(column))
        result = jnp.where(lane == 2 * place, high, result)
        result = jnp.where(lane == 2 * place + 1, column - high, result)
    return to_low(result)


def mix_out_kernel(y_ref, gate_ref, gain_ref, packed_ref, part_ref, w_ref):
    width = w_ref.shape[1]

    @pl.when(pl.program_id(0) == 0)
    def _():
        unpack_rows(packed_ref, w_ref, True)

    gated = to_full(y_ref[...]) * jax.nn.silu(gate_ref[...])
    part_ref[0, :, :width] = to_low(dot_full(to_low(gated * gain_ref[...]), w_ref[...]))
    squares = jnp.sum(gated * gated, axis=1, keepdims=True)
    part_ref[0, :, width:] = put_split([squares], y_ref.shape[0])


def mix_out(y, gate, gain, weights, blocks, freight=()):
    rows, channels = y.shape
    width = weights.shape[2]
    tile = rows // blocks
    block = pl.BlockSpec((tile, channels), lambda step: (step, 0))
    return run(
        mix_out_kernel,
        (y, gate, gain, weights),
        grid=(blocks,),
        in_specs=[block, block, whole(gain.shape), whole(weights.shape)],
        out_specs=[pl.BlockSpec((1, tile, width + LANES), lambda step: (step, 0, 0))],
        out_shape=[jax.ShapeDtypeStruct((blocks, tile, width + LANES), jnp.bfloat16)],
        scratch=[pltpu.VMEM((channels, width), jnp.bfloat16)],
        freight=freight,
        micros=9,
        name="mix_out",
    )


def mix_back_kernel(
    mix_ref,
    y_ref,
    gate_ref,
    gain_ref,
    packed_ref,
    dy_ref,
    dgate_ref,
    w_grad_ref,
    gain_grad_ref,
    total,
    w_ref,
):
    step = pl.program_id(0)
    width = w_ref.shape[1]

    @pl.when(step == 0)
    def _():
        unpack_rows(packed_ref, w_ref, True)
        total[...] = jnp.zeros_like(total)
        gain_grad_ref[...] = jnp.zeros_like(gain_grad_ref)

    mix = mix_ref[0, :, :width]
    extra = to_full(mix_ref[0, :, width:])
    share = extra[:, 0:1] + extra[:, 1:2]
    scale = extra[:, 2:3] + extra[:, 3:4]
    normed_grad = dot_lanes(mix, w_ref[...])
    y = to_full(y_ref[...])
    gate = gate_ref[...]
    sig = jax.nn.sigmoid(gate)
    act = gate * sig
    unit = y * act * scale
    gain = gain_ref[...]
    gain_grad_ref[0:1, :] += jnp.sum(normed_grad * unit, axis=0, keepdims=True)
    gated_grad = scale * (normed_grad * gain - unit * share)
    dy_ref[...] = to_low(gated_grad * act)
    dgate_ref[...] = to_low(gated_grad * y * sig * (1.0 + gate * (1.0 - sig)))
    total[...] += dot_rows(to_low(unit * gain), mix)

    @pl.when(step == pl.num_programs(0) - 1)
    def _():
        w_grad_ref[...] = to_low(total[...])


def mix_back(mix, y, gate, gain, weights, freight=()):
    blocks, tile, wide = mix.shape
    rows, channels = y.shape
    shape = (channels, weights.shape[2])
    block = pl.BlockSpec((tile, channels), lambda step: (step, 0))
    return run(
        mix_back_kernel,
        (mix, y, gate, gain, weights,),
        grid=(blocks,),
        in_specs=[
            pl.BlockSpec((1, tile, wide), lambda step: (step, 0, 0)),
            block,
            block,
            whole(gain.shape),
            whole(weights.shape),
        ],
        out_specs=[block, block, whole(shape), whole((8, channels))],
        out_shape=[
            jax.ShapeDtypeStruct((rows, channels), jnp.bfloat16),
            jax.ShapeDtypeStruct((rows, channels), jnp.bfloat16),
            jax.ShapeDtypeStruct(shape, jnp.bfloat16),
            jax.ShapeDtypeStruct((8, channels), jnp.float32),
        ],
        scratch=[pltpu.VMEM(shape, jnp.float32), pltpu.VMEM(shape, jnp.bfloat16)],
        freight=freight,
        micros=12,
        name="mix_back",
    )


def project_back_kernel(
    dgate_ref, drows_ref, hidden_ref, w_ref, dt_ref, part_ref, main_grad_ref, rest_grad_ref, total
):
    step = pl.program_id(0)

    @pl.when(step == 0)
    def _():
        total[...] = jnp.zeros_like(total)

    grads = jnp.concatenate([dgate_ref[...], drows_ref[...]], axis=1)
    columns = grads.shape[1] - LANES
    part_ref[0] = to_low(
        dot_lanes(grads[:, :columns], w_ref[:, :columns])
        + dot_lanes(grads[:, columns:], dt_ref[...])
    )
    total[...] += dot_rows(hidden_ref[...], grads)

    @pl.when(step == pl.num_programs(0) - 1)
    def _():
        main = main_grad_ref.shape[1]
        main_grad_ref[...] = to_low(total[:, :main])
        rest_grad_ref[...] = to_low(total[:, main:])


def project_back(dgate, drows, hidden, weights, dt_weights, blocks, freight=()):
    rows, width = hidden.shape
    tile = rows // blocks
    main = 2 * dgate.shape[1]
    rest = dgate.shape[1] + drows.shape[1] - main
    block = lambda extent: pl.BlockSpec((tile, extent), lambda step: (step, 0))
    return run(
        project_back_kernel,
        (dgate, drows, hidden, weights, dt_weights,),
        grid=(blocks,),
        in_specs=[
            block(dgate.shape[1]),
            block(drows.shape[1]),
            block(width),
            whole(weights.shape),
            whole(dt_weights.shape),
        ],
        out_specs=[
            pl.BlockSpec((1, tile, width), lambda step: (step, 0, 0)),
            whole((width, main)),
            whole((width, rest)),
        ],
        out_shape=[
            jax.ShapeDtypeStruct((blocks, tile, width), jnp.bfloat16),
            jax.ShapeDtypeStruct((width, main), jnp.bfloat16),
            jax.ShapeDtypeStruct((width, rest), jnp.bfloat16),
        ],
        scratch=[pltpu.VMEM((width, main + rest), jnp.float32)],
        freight=freight,
        micros=25,
        name="project_back",
    )


def unpack_rows(packed_ref, held_ref, first):
    blocks, both, _ = packed_ref.shape
    fine = held_ref.shape[0] // blocks
    start = 0 if first else both - fine
    for block in range(blocks):
        held_ref[block * fine : (block + 1) * fine] = packed_ref[block, start : start + fine]


def shared_kernel(
    rows_ref,
    grad_ref,
    up_ref,
    down_ref,
    res_ref,
    back_ref,
    up_grad_ref,
    down_grad_ref,
    up_sum,
    down_sum,
    down_held,
):
    step = pl.program_id(0)

    @pl.when(step == 0)
    def _():
        up_sum[...] = jnp.zeros_like(up_sum)
        down_sum[...] = jnp.zeros_like(down_sum)
        unpack_rows(down_ref, down_held, False)

    hidden, width = down_held.shape
    rows = rows_ref[0, :, :width]
    grad = grad_ref[0]
    joined = dot_full(rows, up_ref[...])
    gate, up = joined[:, :hidden], joined[:, hidden:]
    sig = jax.nn.sigmoid(gate)
    act = gate * sig
    acted = to_low(act * up)
    res_ref[0] = to_low(dot_full(acted, down_held[...]))
    down_sum[...] += dot_rows(acted, grad)
    act_grad = dot_lanes(grad, down_held[...])
    joined_grad = to_low(
        jnp.concatenate(
            [act_grad * up * sig * (1.0 + gate * (1.0 - sig)), act_grad * act], axis=1
        )
    )
    up_sum[...] += dot_rows(rows, joined_grad)
    back_ref[0] = to_low(dot_lanes(joined_grad, up_ref[...]))

    @pl.when(step == pl.num_programs(0) - 1)
    def _():
        up_grad_ref[...] = to_low(up_sum[...])
        down_grad_ref[...] = to_low(down_sum[...])


def shared_expert(rows, grad, up, down, hidden, blocks, inner, freight=()):
    _, tile, wide = rows.shape
    width = down.shape[2]
    down_shape = (hidden, width)
    up_shape = (width, 2 * hidden)
    block = pl.BlockSpec((1, tile, width), lambda step: (step, 0, 0))
    low = jnp.bfloat16
    own = lambda extent: pl.BlockSpec(
        (1, tile, extent), lambda step: (own_shard_group(inner)[0] * blocks + step, 0, 0)
    )
    return run(
        shared_kernel,
        (rows, grad, up, down),
        grid=(blocks,),
        in_specs=[
            own(wide),
            own(width),
            pl.BlockSpec((width, up_shape[1]), lambda step: (0, up.shape[1] // up_shape[1] - 1)),
            whole(down.shape),
        ],
        out_specs=[block, block, whole(up_shape), whole(down_shape)],
        out_shape=[
            jax.ShapeDtypeStruct((blocks, tile, width), low),
            jax.ShapeDtypeStruct((blocks, tile, width), low),
            jax.ShapeDtypeStruct(up_shape, low),
            jax.ShapeDtypeStruct(down_shape, low),
        ],
        scratch=[
            pltpu.VMEM(up_shape, jnp.float32),
            pltpu.VMEM(down_shape, jnp.float32),
            pltpu.VMEM(down_shape, low),
        ],
        freight=freight,
        micros=18,
        name="shared_expert",
    )


def dispatch_kernel(
    rows_ref, grad_ref, x_ref, g_ref, picks_ref, *, top_count, slots, own_first
):
    per_device = x_ref.shape[0]
    together, tok_rows, _ = rows_ref.shape
    width = g_ref.shape[2]
    wide = width + LANES
    taken = per_device * slots
    lane = iota_of((tok_rows, LANES), 1)
    named = (lane >= 2 * top_count) & (lane < 3 * top_count)
    before = iota_of((tok_rows, tok_rows), 0) > iota_of((tok_rows, tok_rows), 1)
    before = to_low(jnp.where(before, 1.0, 0.0))
    first = own_first()
    for index in range(together):
        extra = to_full(rows_ref[index, :, width:wide])
        member = jnp.zeros((tok_rows, LANES), jnp.float32)
        for expert in range(per_device):
            own = (first + expert).astype(jnp.float32)
            hit = jnp.sum(jnp.where(named & (extra == own), 1.0, 0.0), axis=1, keepdims=True)
            member = jnp.where(lane // slots == expert, hit, member)
        ranks = dot_full(before, to_low(member))
        picks = jnp.where(
            (ranks == to_full(lane % slots)) & (member > 0.0), 1.0, 0.0
        ).astype(jnp.bfloat16)
        picks_ref[index] = picks
        rows = to_low(dot_rows(picks[:, :taken], rows_ref[index]))
        grads = to_low(dot_rows(picks[:, :taken], grad_ref[index]))
        start = index * slots
        for expert in range(per_device):
            span = slice(expert * slots, (expert + 1) * slots)
            x_ref[expert, start : start + slots] = rows[span]
            g_ref[expert, start : start + slots] = grads[span]


def dispatch(rows, grad, per_device, top_count, slots, own_first, freight=()):
    blocks, tok_rows, wide = rows.shape
    width = grad.shape[2]
    together = 4
    block = lambda extent: pl.BlockSpec((together, tok_rows, extent), lambda step: (step, 0, 0))
    taken = lambda extent: pl.BlockSpec(
        (per_device, together * slots, extent), lambda step: (0, step, 0)
    )
    return run(
        functools.partial(
            dispatch_kernel, top_count=top_count, slots=slots, own_first=own_first
        ),
        (rows, grad),
        grid=(blocks // together,),
        in_specs=[block(wide), block(width)],
        out_specs=[taken(width + LANES), taken(width), block(LANES)],
        out_shape=[
            jax.ShapeDtypeStruct((per_device, blocks * slots, width + LANES), jnp.bfloat16),
            jax.ShapeDtypeStruct((per_device, blocks * slots, width), jnp.bfloat16),
            jax.ShapeDtypeStruct((blocks, tok_rows, LANES), jnp.bfloat16),
        ],
        freight=freight,
        micros=30,
        name="dispatch",
    )


def experts_kernel(
    depart, arrive, targets, *refs, count, per_device, top_count, own_first, inner, incoming, outgoing
):
    x_ref, g_ref = refs[:2]
    total = 2 * count * per_device
    given = total - len(incoming)
    pieces, refs = list(refs[2 : 2 + given]), refs[2 + given :]
    for order, key in enumerate(incoming):
        pieces.insert(key, targets[order])
    res_ref, dx_ref = refs[:2]
    outs = refs[2 : 2 + total]
    up_held, down_held, up_sum, down_sum, up_low, down_low, sems = refs[2 + total :]
    own_place, _ = own_shard_group(inner)
    is_incoming = lambda item: item.output is None
    is_outgoing = lambda item: item.output is not None
    expert, step = pl.program_id(0), pl.program_id(1)
    steps = pl.num_programs(1)
    slot = lax.rem(expert, 2)
    width, double = up_held.shape[1:]
    hidden = double // 2
    tile = x_ref.shape[1]

    def parts(refs_of, which, up, down):
        result = []
        for shift in range(count):
            from_place = lax.rem(own_place + count - shift, count)
            for kind, held in enumerate((up, down)):
                extent = held.shape[0] // count
                start = pl.multiple_of(from_place * extent, extent)
                piece = refs_of[(shift * per_device + which) * 2 + kind]
                if len(piece.shape) == 3:
                    piece = piece.at[own_place * per_device + which]
                result.append((piece, held.at[pl.ds(start, extent)], (shift, kind)))
        return result

    def fetch(which):
        half = which % 2
        return [
            pltpu.make_async_copy(piece, held, sems.at[half, at[0], at[1]])
            for piece, held, at in parts(pieces, which, up_held.at[half], down_held.at[half])
        ]

    for which in range(per_device):

        @pl.when((step == 0) & (expert == which))
        def _():
            if which == 0:
                for copy in fetch(0):
                    copy.start()
                depart(is_incoming)
            if which == 1:
                arrive(is_incoming)
                depart(is_outgoing)
                for copy in fetch(1):
                    copy.start()
            for copy in fetch(which):
                copy.wait()
            if 1 <= which < per_device - 1:
                for copy in fetch(which + 1):
                    copy.start()

    @pl.when(step == 0)
    def _():
        up_sum[...] = jnp.zeros_like(up_sum)
        down_sum[...] = jnp.zeros_like(down_sum)

    up, down = up_held.at[slot], down_held.at[slot]
    rows = x_ref[0, :, :width]
    extra = to_full(x_ref[0, :, width:])
    lane = iota_of((tile, LANES), 1)
    own = own_first() + expert
    hits = jnp.where((lane < 3 * top_count) & (extra == own.astype(jnp.float32)), 1.0, 0.0)
    gate_slot = jnp.zeros((tile, 1), jnp.float32)
    for route in range(top_count):
        place = 2 * top_count + route
        value = extra[:, 2 * route : 2 * route + 1] + extra[:, 2 * route + 1 : 2 * route + 2]
        gate_slot = gate_slot + hits[:, place : place + 1] * value
    joined = dot_full(rows, up[...])
    gate, lift = joined[:, :hidden], joined[:, hidden:]
    sig = jax.nn.sigmoid(gate)
    act = gate * sig
    acted = to_low(act * lift)
    res = to_low(dot_full(acted, down[...]))
    grads = g_ref[0]
    wide_grads = to_full(grads)
    wide_res = to_full(res)
    gate_grad = jnp.sum(wide_res * wide_grads, axis=1, keepdims=True)
    res_ref[0] = to_low(wide_res * gate_slot)
    weighted = to_low(wide_grads * gate_slot)
    act_grad = dot_lanes(weighted, down[...])
    down_sum[...] += dot_rows(acted, weighted)
    joined_grad = to_low(
        jnp.concatenate(
            [act_grad * lift * sig * (1.0 + gate * (1.0 - sig)), act_grad * act], axis=1
        )
    )
    dx_ref[0, :, :width] = to_low(dot_lanes(joined_grad, up[...]))
    high = to_full(to_low(gate_grad))
    half = LANES // 2
    dx_ref[0, :, width:] = to_low(
        jnp.where(lane == own, high, 0.0) + jnp.where(lane == own + half, gate_grad - high, 0.0)
    )
    up_sum[...] += dot_rows(rows, joined_grad)

    for which in range(per_device):

        @pl.when((step == steps - 1) & (expert == which))
        def _():
            up_low[...] = to_low(up_sum[...])
            down_low[...] = to_low(down_sum[...])
            copies = [
                pltpu.make_async_copy(held, piece, sems.at[2, at[0], at[1]])
                for piece, held, at in parts(outs, which, up_low, down_low)
            ]
            for copy in copies:
                copy.start()
            for copy in copies:
                copy.wait()

    if outgoing:

        @pl.when((step == steps - 1) & (expert == per_device - 1))
        def _():
            arrive(is_outgoing)


def experts(x, g, pieces, hidden, top_count, own_first, inner, incoming=(), outgoing=()):
    per_device, rows, wide = x.shape
    width = g.shape[2]
    count = (len(pieces) + len(incoming)) // per_device // 2
    incoming = sorted(incoming, key=lambda entry: entry[0])
    full_list = list(pieces)
    for key, item in incoming:
        full_list.insert(key, jax.ShapeDtypeStruct(item.shape, item.array.dtype))
    low = jnp.bfloat16
    shapes = [jax.ShapeDtypeStruct(piece.shape[-2:], low) for piece in full_list]
    freight = [item for _, item in incoming] + [
        Parcel(shapes[key], shift, inner, output=2 + key) for key, shift in outgoing
    ]
    double = 2 * hidden
    tile = min(rows, 256)
    block = lambda extent: pl.BlockSpec((1, tile, extent), lambda e, step: (e, step, 0))
    anywhere = pl.BlockSpec(memory_space=pl.ANY)
    low = jnp.bfloat16
    outs = run(
        functools.partial(
            experts_kernel,
            count=count,
            per_device=per_device,
            top_count=top_count,
            own_first=own_first,
            inner=inner,
            incoming=[key for key, _ in incoming],
            outgoing=outgoing,
        ),
        (x, g) + tuple(pieces),
        grid=(per_device, rows // tile),
        in_specs=[block(wide), block(width)] + [anywhere] * len(pieces),
        out_specs=[block(width), block(wide)] + [anywhere] * len(shapes),
        out_shape=[
            jax.ShapeDtypeStruct((per_device, rows, width), low),
            jax.ShapeDtypeStruct((per_device, rows, wide), low),
        ]
        + shapes,
        scratch=[
            pltpu.VMEM((2, width, double), low),
            pltpu.VMEM((2, hidden, width), low),
            pltpu.VMEM((width, double), jnp.float32),
            pltpu.VMEM((hidden, width), jnp.float32),
            pltpu.VMEM((width, double), low),
            pltpu.VMEM((hidden, width), low),
            pltpu.SemaphoreType.DMA((3, count, 2)),
        ],
        freight=freight,
        inner=inner if freight else 1,
        late=True,
        micros=45,
        name="experts",
    )
    sent = outs.pop()[len(incoming) :] if freight else []
    return outs[0], outs[1], outs[2:], sent


def combine_kernel(
    picks_ref, res_ref, dx_ref, sres_ref, sback_ref, out_ref, back_ref, *, slots, inner
):
    step = pl.program_id(0)
    together, _, width = out_ref.shape
    per_device = res_ref.shape[0]
    blocks = sres_ref.shape[0]
    place, _ = own_shard_group(inner)
    for index in range(together):
        picks = picks_ref[index, :, : per_device * slots]
        start = index * slots
        stacked = lambda ref: jnp.concatenate(
            [ref[expert, start : start + slots] for expert in range(per_device)], axis=0
        )
        out_ref[index] = to_low(dot_full(picks, stacked(res_ref)))
        back_ref[index] = to_low(dot_full(picks, stacked(dx_ref)))

    @pl.when(lax.div(step * together, blocks) == place)
    def _():
        first = lax.rem(step * together, blocks)
        for index in range(together):
            out_ref[index] = to_low(to_full(out_ref[index]) + to_full(sres_ref[first + index]))
            back_ref[index, :, :width] = to_low(
                to_full(back_ref[index, :, :width]) + to_full(sback_ref[first + index])
            )


def combine(picks, res, dx, shared_res, shared_back, inner, freight=()):
    blocks, tok_rows, _ = picks.shape
    per_device, rows, width = res.shape
    slots = rows // blocks
    together = 4
    block = lambda extent: pl.BlockSpec((together, tok_rows, extent), lambda step: (step, 0, 0))
    taken = lambda extent: pl.BlockSpec(
        (per_device, together * slots, extent), lambda step: (0, step, 0)
    )
    return run(
        functools.partial(combine_kernel, slots=slots, inner=inner),
        (picks, res, dx, shared_res, shared_back),
        grid=(blocks // together,),
        in_specs=[
            block(LANES),
            taken(width),
            taken(width + LANES),
            whole(shared_res.shape),
            whole(shared_back.shape),
        ],
        out_specs=[block(width), block(width + LANES)],
        out_shape=[
            jax.ShapeDtypeStruct((blocks, tok_rows, width), jnp.bfloat16),
            jax.ShapeDtypeStruct((blocks, tok_rows, width + LANES), jnp.bfloat16),
        ],
        freight=freight,
        micros=30,
        name="combine",
    )


def assemble_kernel(
    main_ref, shared_in_ref, small_ref, rows_ref, w_in_ref, shared_ref, out_ref, down_ref
):
    seq_devices, rows, double = main_ref.shape
    channels = double // 2
    for device in range(seq_devices):
        for target, source in ((w_in_ref, main_ref), (shared_ref, shared_in_ref)):
            extent = source.shape[2] // 2
            for side in range(2):
                start = (side * seq_devices + device) * extent
                target[:, start : start + extent] = to_full(
                    source[device, :, side * extent : (side + 1) * extent]
                )
    start = 2 * seq_devices * channels
    w_in_ref[:, start:] = to_full(small_ref[0, :rows, : w_in_ref.shape[1] - start])
    halves, _, out_rows, _ = out_ref.shape
    down_rows = down_ref.shape[2]
    for half in range(halves):
        at = half * (out_rows + down_rows)
        out_ref[half, 0] = to_full(rows_ref[0, at : at + out_rows])
        down_ref[half, 0] = to_full(rows_ref[0, at + out_rows : at + out_rows + down_rows])


def assemble(main, shared, small, rows, columns, shared_columns, out_rows, down_rows, halves):
    seq_devices, depth_rows, _ = main.shape
    tile = depth_rows // seq_devices
    width = rows.shape[2]
    out_fine = out_rows // halves // seq_devices
    down_fine = down_rows // halves // seq_devices
    flat = lambda extent: pl.BlockSpec((tile, extent), lambda step: (step, 0))
    fine = lambda extent: pl.BlockSpec(
        (halves, 1, extent, width), lambda step: (0, step, 0, 0)
    )
    full = jnp.float32
    results = pl.pallas_call(
        assemble_kernel,
        grid=(seq_devices,),
        in_specs=[
            pl.BlockSpec((seq_devices, tile, main.shape[2]), lambda step: (0, step, 0)),
            pl.BlockSpec((seq_devices, tile, shared.shape[2]), lambda step: (0, step, 0)),
            pl.BlockSpec((1,) + small.shape[1:], lambda step: (step, 0, 0)),
            pl.BlockSpec((1,) + rows.shape[1:], lambda step: (step, 0, 0)),
        ],
        out_specs=[flat(columns), flat(shared_columns), fine(out_fine), fine(down_fine)],
        out_shape=[
            jax.ShapeDtypeStruct((depth_rows, columns), full),
            jax.ShapeDtypeStruct((depth_rows, shared_columns), full),
            jax.ShapeDtypeStruct((halves, seq_devices, out_fine, width), full),
            jax.ShapeDtypeStruct((halves, seq_devices, down_fine, width), full),
        ],
        compiler_params=params_of(),
        cost_estimate=cost_of(10),
        name="assemble",
    )(main, shared, small, rows)
    return results[0], results[1], results[2].reshape(-1, width), results[3].reshape(-1, width)


def collect_kernel(place_ref, *refs):
    del place_ref
    step = pl.program_id(0)
    up_ref, down_ref = refs[-2:]
    for order in range(len(refs) // 2 - 1):

        @pl.when(step == order)
        def _():
            up_ref[0] = to_full(refs[2 * order][...])
            down_ref[0] = to_full(refs[2 * order + 1][...])


def collect(place, pieces, per_device):
    count = len(pieces) // 2
    up, down = pieces[0].shape, pieces[1].shape

    def here(step, place):
        shift, expert = lax.div(step, per_device), lax.rem(step, per_device)
        return (
            lax.rem(place[0] + shift, count // per_device) * per_device + expert, 0, 0
        )

    still = lambda shape: pl.BlockSpec(shape, lambda step, place: (0, 0))
    return pl.pallas_call(
        collect_kernel,
        grid_spec=pltpu.PrefetchScalarGridSpec(
            num_scalar_prefetch=1,
            grid=(count,),
            in_specs=[still(up), still(down)] * count,
            out_specs=[pl.BlockSpec((1,) + up, here), pl.BlockSpec((1,) + down, here)],
        ),
        out_shape=[
            jax.ShapeDtypeStruct((count,) + up, jnp.float32),
            jax.ShapeDtypeStruct((count,) + down, jnp.float32),
        ],
        compiler_params=params_of(),
        cost_estimate=cost_of(12),
        name="collect",
    )(place, *pieces)


def route_hits(routes, route, lane):
    return lane == routes[:, route : route + 1]


def token_forward_kernel(
    mixed_ref, x_ref, gain_ref, router_ref, routes_ref, after_ref, wide_ref, gates_ref, *, inner_width, top_count
):
    width = x_ref.shape[1]
    rows = x_ref.shape[0]
    squares = mixed_ref[:, width : width + 1] + mixed_ref[:, width + 1 : width + 2]
    scale = lax.rsqrt(squares / inner_width + EPSILON)
    after = to_full(x_ref[...]) + mixed_ref[:, :width] * scale
    after_ref[...] = after
    moe_in = to_low(after * norm_scale(after) * gain_ref[...])
    wide_ref[:, :width] = moe_in
    logits = dot_full(moe_in, router_ref[...])
    lane = iota_of((rows, LANES), 1)
    routes = routes_ref[...]
    picked = [
        jnp.sum(jnp.where(route_hits(routes, k, lane), logits, 0.0), axis=1, keepdims=True)
        for k in range(top_count)
    ]
    largest = functools.reduce(jnp.maximum, picked)
    powers = [jnp.exp(value - largest) for value in picked]
    total = sum(powers)
    gates = jnp.zeros((rows, LANES), jnp.float32)
    extra = jnp.zeros((rows, LANES), jnp.float32)
    for k in range(top_count):
        value = powers[k] / total
        high = to_full(to_low(value))
        gates = jnp.where(lane == k, value, gates)
        extra = jnp.where(lane == 2 * k, high, extra)
        extra = jnp.where(lane == 2 * k + 1, value - high, extra)
        extra = jnp.where(lane == 2 * top_count + k, to_full(routes[:, k : k + 1]), extra)
    gates_ref[...] = jnp.where(lane == top_count, scale, gates)
    wide_ref[:, width:] = to_low(extra)


def token_forward(mixed, x, gain, router, routes, inner_width, top_count):
    rows, width = x.shape
    arrays = (mixed, x, gain, router, routes)
    return pl.pallas_call(
        functools.partial(
            token_forward_kernel, inner_width=inner_width, top_count=top_count
        ),
        in_specs=[whole(array.shape) for array in arrays],
        out_specs=[whole((rows, width)), whole((rows, width + LANES)), whole((rows, LANES))],
        out_shape=[
            jax.ShapeDtypeStruct((rows, width), jnp.float32),
            jax.ShapeDtypeStruct((rows, width + LANES), jnp.bfloat16),
            jax.ShapeDtypeStruct((rows, LANES), jnp.float32),
        ],
        compiler_params=params_of(),
        cost_estimate=cost_of(5),
        name="token_forward",
    )(*arrays)


def token_back_kernel(
    back_ref,
    mixed_ref,
    after_ref,
    wide_ref,
    gates_ref,
    grad_ref,
    gain_ref,
    router_ref,
    routes_ref,
    mix_ref,
    mix_wide_ref,
    router_grad_ref,
    gain_grad_ref,
    *,
    inner_width,
    top_count,
):
    rows, width = grad_ref.shape
    lane = iota_of((rows, LANES), 1)
    half = LANES // 2
    routes = routes_ref[...]
    gates = gates_ref[...]
    all_grads = back_ref[:, width:]
    values = [gates[:, k : k + 1] for k in range(top_count)]
    grads = [
        jnp.sum(
            jnp.where(
                route_hits(routes, k, lane) | route_hits(routes, k, lane - half), all_grads, 0.0
            ),
            axis=1,
            keepdims=True,
        )
        for k in range(top_count)
    ]
    common = sum(value * grad for value, grad in zip(values, grads))
    logit_grad = jnp.zeros((rows, LANES), jnp.float32)
    for k in range(top_count):
        logit_grad = jnp.where(
            route_hits(routes, k, lane), values[k] * (grads[k] - common), logit_grad
        )
    logit_grad = to_low(logit_grad)
    router_grad_ref[...] = to_low(dot_rows(wide_ref[:, :width], logit_grad))
    moe_grad = back_ref[:, :width] + dot_lanes(logit_grad, router_ref[...])
    after = after_ref[...]
    scale = norm_scale(after)
    unit = after * scale
    gain_grad_ref[...] = jnp.broadcast_to(
        jnp.sum(moe_grad * unit, axis=0, keepdims=True), (8, width)
    )
    scaled = moe_grad * gain_ref[...]
    mean = jnp.mean(scaled * unit, axis=1, keepdims=True)
    mix = to_full(grad_ref[...]) + scale * (scaled - unit * mean)
    mix_ref[...] = mix
    mix_low = to_low(mix)
    mix_wide_ref[:, :width] = mix_low
    mix_scale = gates[:, top_count : top_count + 1]
    share = jnp.sum(to_full(mix_low) * mixed_ref[:, :width], axis=1, keepdims=True)
    mix_wide_ref[:, width:] = put_split([share * mix_scale / inner_width, mix_scale], rows)


def token_back(back, mixed, after, wide, gates, grad, gain, router, routes, inner_width, top_count):
    rows, width = grad.shape
    arrays = (back, mixed, after, wide, gates, grad, gain, router, routes)
    return pl.pallas_call(
        functools.partial(token_back_kernel, inner_width=inner_width, top_count=top_count),
        in_specs=[whole(array.shape) for array in arrays],
        out_specs=[
            whole((rows, width)),
            whole((rows, width + LANES)),
            whole((width, LANES)),
            whole((8, width)),
        ],
        out_shape=[
            jax.ShapeDtypeStruct((rows, width), jnp.float32),
            jax.ShapeDtypeStruct((rows, width + LANES), jnp.bfloat16),
            jax.ShapeDtypeStruct((width, LANES), jnp.bfloat16),
            jax.ShapeDtypeStruct((8, width), jnp.float32),
        ],
        compiler_params=params_of(),
        cost_estimate=cost_of(6),
        name="token_back",
    )(*arrays)


def split_small(joined, arrays):
    results, start = [], 0
    for piece in arrays:
        part = joined[:, start : start + piece.size]
        results.append(part.reshape((-1,) + piece.shape[1:]))
        start += piece.size
    return results


def flat_of(arrays):
    return jnp.concatenate([piece.reshape(-1) for piece in arrays])


def rows_to_send(weights, part):
    seq_devices = lax.axis_size("seq")
    halves = max(1, seq_devices // lax.axis_size("shard"))
    mine = []
    for weight in weights:
        view = weight.reshape(halves, seq_devices, -1, weight.shape[1])
        mine.append(lax.dynamic_index_in_dim(view, part, 1, keepdims=False))
    return jnp.concatenate(mine, axis=1).reshape(-1, weights[0].shape[1])


def rows_by_owner(joined):
    seq_devices = lax.axis_size("seq")
    return joined.reshape(seq_devices, -1, joined.shape[2])


def rows_of_owner(taken, weights):
    seq_devices = lax.axis_size("seq")
    halves = max(1, seq_devices // lax.axis_size("shard"))
    fine_rows = [weight.shape[0] // halves // seq_devices for weight in weights]
    width = taken.shape[2]
    taken = taken.reshape(seq_devices, -1, sum(fine_rows), width).transpose(1, 0, 2, 3)
    results, start = [], 0
    for fine in fine_rows:
        results.append(taken[:, :, start : start + fine].reshape(-1, width))
        start += fine
    return results


def rows_from_owner(grads):
    seq_devices = lax.axis_size("seq")
    shard_devices = lax.axis_size("shard")
    width = grads[0].shape[1]
    turns = shard_devices * max(1, seq_devices // shard_devices) // seq_devices
    pieces = [
        grad.reshape(turns, seq_devices, -1, width).transpose(1, 0, 2, 3) for grad in grads
    ]
    return jnp.concatenate(pieces, axis=2).reshape(seq_devices, -1, width)


def rows_of_shard(joined, weights):
    seq_devices = lax.axis_size("seq")
    halves = max(1, seq_devices // lax.axis_size("shard"))
    fine_rows = [weight.shape[0] // halves // seq_devices for weight in weights]
    width = joined.shape[2]
    spread = joined.reshape(seq_devices, halves, -1, width).transpose(1, 0, 2, 3)
    results, start = [], 0
    for fine in fine_rows:
        results.append(to_full(spread[:, :, start : start + fine]).reshape(-1, width))
        start += fine
    return results


def inner_groups(inner):
    count = lax.axis_size("shard")
    return [list(range(start, start + inner)) for start in range(0, count, inner)]


def outer_groups(inner):
    count = lax.axis_size("shard")
    return [list(range(start, count, inner)) for start in range(inner)]


def carry(array, freight):
    result, arrays = run(
        lambda source, target: None,
        (array,),
        in_specs=[pl.BlockSpec(memory_space=pl.ANY)],
        out_specs=[pl.BlockSpec(memory_space=pl.ANY)],
        out_shape=[jax.ShapeDtypeStruct((8, LANES), jnp.float32)],
        freight=freight,
        micros=30,
        name="carry",
    )
    del result
    return array, arrays


def stacked_pieces(received, place, inner):
    own = jnp.stack(received)[lax.rem(place + inner - jnp.arange(inner), inner)]
    joined = lax.all_gather(own, "shard", axis_index_groups=outer_groups(inner))
    return joined.reshape(-1, joined.shape[-1])


def split_piece(grad, shift, place, inner):
    outer = lax.axis_size("shard") // inner
    rows = grad.reshape(outer, inner, -1, grad.shape[1])
    here = lax.rem(place + inner - shift, inner)
    return lax.psum_scatter(
        lax.dynamic_index_in_dim(rows, here, 1, keepdims=False),
        "shard",
        axis_index_groups=outer_groups(inner),
    )


def local(
    tokens,
    out_grad,
    deal_order,
    lengths,
    routes,
    norm_in,
    w_in,
    w_dt,
    conv_w,
    conv_b,
    dt_bias,
    a_log,
    d_skip,
    norm_gate,
    w_out,
    norm_moe,
    w_router,
    w_shared,
    w_shared_down,
    w_experts,
    w_experts_down,
):
    seq_devices = lax.axis_size("seq")
    shard_devices = lax.axis_size("shard")
    part = lax.axis_index("seq")
    shard = lax.axis_index("shard")
    inner = min(shard_devices, INNER)
    outer = shard_devices // inner
    place = lax.rem(shard, inner)
    _, tok_rows, width = tokens.shape
    group_rows = tok_rows * seq_devices
    inner_width = w_out.shape[0] * shard_devices
    channels = inner_width // seq_devices
    head_total = w_dt.shape[1]
    heads = head_total // seq_devices
    shared_width = w_shared_down.shape[0] * shard_devices
    shared_part = shared_width // seq_devices
    depth_rows = w_in.shape[0]
    expert_total = w_router.shape[1]
    local_experts, _, double = w_experts.shape
    hidden = double // 2
    hidden_rows = w_experts_down.shape[1]
    top_count = routes.shape[2]
    per_device = local_experts // inner
    blocks = inner * seq_devices
    COLLECTIVES.clear()

    def own_columns(array, start, extent):
        return lax.dynamic_slice_in_dim(array, start + part * extent, extent, 1)

    def own_rows(array, extent):
        return lax.dynamic_slice_in_dim(array, part * extent, extent, 0)

    small_weights = [
        norm_in, own_columns(w_dt, 0, heads), conv_w, conv_b, dt_bias, a_log, d_skip, norm_gate, norm_moe, w_router
    ]
    in_columns = jnp.concatenate(
        [
            own_columns(w_in, 0, channels),
            own_columns(w_in, inner_width, channels),
            w_in[:, 2 * inner_width :],
            own_columns(w_shared, 0, shared_part),
            own_columns(w_shared, shared_width, shared_part),
        ],
        axis=1,
    )
    flat = flat_of(small_weights)
    rows_sent = rows_to_send([w_out, w_shared_down], part)
    if outer == 1:
        wide = in_columns.shape[1]
        flat_rows = -(-flat.size // (wide * 32)) * 32
        flat = jnp.pad(flat, (0, flat_rows * wide - flat.size)).reshape(flat_rows, wide)
        x_group, grad_all, proj_in, joined, rows_joined = begin(
            tokens[0], out_grad[0], in_columns, flat, rows_sent, inner
        )
        joined = joined.reshape(inner, -1)
        x_group = x_group.reshape(group_rows, width)
    else:
        x_group = gather_rows(tokens[0], 1)[0].reshape(group_rows, width)
        grad_all = gather_rows(out_grad[0], inner)[0]
        proj_in = lax.all_gather(in_columns, "shard", tiled=True)
        joined = lax.all_gather(flat, "shard")
        rows_joined = lax.all_gather(rows_sent, "shard")
    (
        gain_in,
        dt_columns,
        conv_weight,
        conv_bias,
        step_bias,
        decay_log,
        skip_gain,
        gain_gate,
        gain_moe,
        router,
    ) = split_small(joined, small_weights)
    dt_columns = jnp.pad(dt_columns, ((0, 0), (0, LANES - heads)))
    grad_all = grad_all.reshape(blocks, tok_rows, width)

    weights_of = (w_experts, w_experts_down)

    def own_first():
        here, _ = own_shard_group(inner)
        return lax.axis_index("seq") * local_experts + here * per_device

    pieces = {
        (0, expert, kind): weights_of[kind] for expert in range(per_device) for kind in range(2)
    }

    def parcels(*keys):
        return [
            Parcel(
                weights_of[kind],
                shift,
                inner,
                lambda to, expert=expert: to * per_device + expert,
            )
            for shift, expert, kind in keys
        ]

    def unpack(keys, arrays):
        pieces.update(zip(keys, arrays))

    last = inner - 1

    gain_row = to_full(gain_in)[None]
    in_width = in_columns.shape[1] - 2 * shared_part
    keys = [(1, 0, DOWN)]
    hidden_in, gate_in, rows_in, arrays = project(
        x_group, gain_row, proj_in, dt_columns, channels, in_width, parcels(*keys)
    )
    unpack(keys, arrays)
    ends = jnp.cumsum(lengths[0]).astype(jnp.int32)
    conv_part = jnp.concatenate(
        [own_rows(conv_weight, channels), conv_weight[inner_width:]], axis=0
    )
    bias_part = jnp.concatenate([own_rows(conv_bias, channels), conv_bias[inner_width:]], axis=0)
    conv_table = to_full(
        jnp.pad(jnp.concatenate([conv_part.T, bias_part[None]], axis=0), ((0, 3), (0, 0)))
    )
    head_table = jnp.pad(
        jnp.stack(
            [
                to_full(own_rows(step_bias, heads)),
                -jnp.exp(to_full(own_rows(decay_log, heads))),
                to_full(own_rows(skip_gain, heads)),
            ]
        ),
        ((0, 5), (0, LANES - heads)),
    )
    keys = [(1, 0, UP), (last, 0, DOWN)]
    y, seq_rows, states, (taken, *arrays) = scan_forward(
        ends,
        deal_order,
        rows_in,
        conv_table,
        head_table,
        channels,
        [PlaneSwap(rows_by_owner(rows_joined))] + parcels(*keys),
    )
    unpack(keys, arrays)
    if outer > 1:
        out_rows, down_rows = rows_of_owner(taken, [w_out, w_shared_down])
        taken = jnp.concatenate(
            [
                out_rows.reshape(seq_devices, -1, width),
                down_rows.reshape(seq_devices, -1, width),
            ],
            axis=1,
        )
    own_weights = taken
    gate_gain = to_full(own_rows(gain_gate, channels))[None]
    keys = [(1, 1, DOWN)]
    mix_part, arrays = mix_out(y, gate_in, gate_gain, own_weights, seq_devices, parcels(*keys))
    unpack(keys, arrays)
    keys = [(last, 0, UP), (last, 1, DOWN)]
    mixed, arrays = reduce_rows(mix_part[None], parcels(*keys))
    unpack(keys, arrays)

    moe_row = to_full(gain_moe)[None]
    router_wide = jnp.pad(router, ((0, 0), (0, LANES - expert_total)))
    route_ids = jnp.pad(routes[0], ((0, 0), (0, LANES - top_count)))
    after_mix, moe_wide, gates = token_forward(
        mixed, tokens[0], moe_row, router_wide, route_ids, inner_width, top_count
    )
    keys = [(2, 0, UP), (2, 0, DOWN), (last, 1, UP)]
    moe_all, arrays = gather_rows(moe_wide, inner, parcels(*keys))
    unpack(keys, arrays)
    moe_all = moe_all.reshape(blocks, tok_rows, width + LANES)
    capacity = min(tok_rows, max(2, tok_rows * top_count * 5 // (expert_total * 3)))
    slots = -(-capacity // 16) * 16
    keys = [(2, 1, UP)]
    expert_rows, grad_rows, picks, arrays = dispatch(
        moe_all, grad_all, per_device, top_count, slots, own_first, parcels(*keys)
    )
    unpack(keys, arrays)
    keys = [(2, 1, DOWN)]
    shared_res, shared_back, shared_up_grad, shared_down_grad, arrays = shared_expert(
        moe_all,
        grad_all,
        proj_in,
        own_weights,
        shared_part,
        seq_devices,
        inner,
        parcels(*keys),
    )
    unpack(keys, arrays)
    order = [
        (shift, expert, kind)
        for shift in range(inner)
        for expert in range(per_device)
        for kind in range(2)
    ]
    if outer == 1:
        late_keys = [(1, 1, UP)]
        early_keys = [(1, 0, UP), (last, 0, DOWN)]
        expert_res, expert_back, grads, sent = experts(
            expert_rows,
            grad_rows,
            [pieces[key] for key in order if key not in late_keys],
            hidden,
            top_count,
            own_first,
            inner,
            [(order.index(key), parcels(key)[0]) for key in late_keys],
            [(order.index(key), inner - key[0]) for key in early_keys],
        )
    else:
        for expert in range(per_device):
            for kind in range(2):
                pieces[0, expert, kind] = lax.dynamic_index_in_dim(
                    weights_of[kind], place * per_device + expert, 0, keepdims=False
                )
        keys = [(1, 1, UP)]
        moe_all, arrays = carry(moe_all, parcels(*keys))
        unpack(keys, arrays)
        early_keys, sent = [], []
        held = [
            stacked_pieces([pieces[shift, expert, kind] for shift in range(inner)], place, inner)
            for expert in range(per_device)
            for kind in range(2)
        ]
        expert_res, expert_back, grads, _ = experts(
            expert_rows, grad_rows, held, hidden, top_count, own_first, inner
        )
        grads = [
            split_piece(grads[expert * 2 + kind], shift, place, inner)
            for shift, expert, kind in order
        ]
    grads = dict(zip(order, grads))
    returned = {key: grads[key] for key in order if key[0] == 0}
    returned.update(zip(early_keys, sent))

    def back_parcels(*keys):
        keys = [key for key in keys if key not in early_keys]
        return [Parcel(grads[key], inner - key[0], inner) for key in keys]

    def unpack_back(keys, arrays):
        keys = [key for key in keys if key not in early_keys]
        returned.update(zip(keys, arrays))

    keys = [(1, 0, UP), (last, 0, DOWN), (last, 0, UP), (1, 0, DOWN), (1, 1, DOWN)]
    out_part, back_part, arrays = combine(
        picks, expert_res, expert_back, shared_res, shared_back, inner, back_parcels(*keys)
    )
    unpack_back(keys, arrays)
    keys = [(2, 0, UP), (last, 1, UP)]
    back, arrays = reduce_rows(
        back_part.reshape(inner, seq_devices, tok_rows, -1), back_parcels(*keys)
    )
    unpack_back(keys, arrays)
    mix_grad, mix_wide, router_grad, gain_moe_grad = token_back(
        back,
        mixed,
        after_mix,
        moe_wide,
        gates,
        out_grad[0],
        moe_row,
        router_wide,
        route_ids,
        inner_width,
        top_count,
    )

    keys = [(1, 1, UP), (last, 1, DOWN)]
    mix_group, arrays = gather_rows(mix_wide, 1, back_parcels(*keys))
    unpack_back(keys, arrays)
    keys = [(2, 0, DOWN)]
    dy, gate_in_grad, proj_out_grad, gain_gate_grad, arrays = mix_back(
        mix_group[0], y, gate_in, gate_gain, own_weights, back_parcels(*keys)
    )
    unpack_back(keys, arrays)
    keys = [(2, 1, UP)]
    rows_grad, conv_grad, head_grad, out_sum, (taken, *arrays) = scan_backward(
        ends,
        deal_order,
        seq_rows,
        states,
        dy,
        conv_table,
        head_table,
        out_part.reshape(inner, seq_devices, tok_rows, -1),
        [PlaneSwap(rows_from_owner([proj_out_grad, shared_down_grad]))] + back_parcels(*keys),
    )
    unpack_back(keys, arrays)
    layer_out = to_low(after_mix + out_sum)
    keys = [(2, 1, DOWN)]
    hidden_part, main_grad, rest_grad, arrays = project_back(
        gate_in_grad, rows_grad, hidden_in, proj_in, dt_columns, seq_devices, back_parcels(*keys)
    )
    unpack_back(keys, arrays)
    experts_grad, experts_down_grad = collect(
        place[None], [returned[key] for key in order], per_device
    )
    def spread(values, length, axis=0):
        shape = values.shape[:axis] + (length,) + values.shape[axis + 1 :]
        return lax.dynamic_update_slice_in_dim(
            jnp.zeros(shape, values.dtype), values, part * values.shape[axis], axis
        )

    state_columns = rest_grad.shape[1] - LANES
    conv_rows_grad = conv_grad[:5].T
    conv_full = jnp.concatenate(
        [spread(conv_rows_grad[:channels], inner_width), conv_rows_grad[channels:]], axis=0
    )
    by_depth = [
        rest_grad[:, :state_columns],
        router_grad[:, :expert_total],
        spread(rest_grad[:, state_columns : state_columns + heads], head_total, 1),
        to_low(gain_moe_grad[0])[:, None],
    ]
    by_shard = [
        conv_full[:, :4],
        conv_full[:, 4],
        spread(head_grad[0, :heads], head_total),
        spread(head_grad[1, :heads], head_total),
        spread(head_grad[2, :heads], head_total),
        spread(gain_gate_grad[0], inner_width),
    ]
    shapes = [(piece.shape[0] // shard_devices,) + piece.shape[1:] for piece in by_shard]
    by_shard = jnp.concatenate(
        [to_low(piece).reshape(shard_devices, -1) for piece in by_shard], axis=1
    )
    extents = [piece.shape[1] for piece in by_depth]
    used = sum(extents)
    if outer == 1:
        wide = -(-max(used, depth_rows) // LANES) * LANES
        by_depth.append(jnp.zeros((width, wide - used), jnp.bfloat16))
        by_depth = jnp.concatenate(by_depth, axis=1).reshape(inner, seq_devices, -1, wide)
        depth_each = by_depth.shape[2]
        size = by_shard.shape[1]
        each = -(-size // (seq_devices * wide))
        padded = -(-each // 16) * 16
        by_shard = jnp.pad(by_shard, ((0, 0), (0, each * seq_devices * wide - size)))
        by_shard = by_shard.reshape(inner, seq_devices, each, wide)
        by_shard = jnp.pad(by_shard, ((0, 0), (0, 0), (0, padded - each), (0, 0)))
        tokens_grad, rows_all, shared_all, main_all, small_all = settle(
            hidden_part[None],
            jnp.concatenate([by_depth, by_shard], axis=2),
            tokens[0],
            mix_grad,
            gain_row,
            [
                taken.reshape(inner, -1, width),
                shared_up_grad.reshape(inner, depth_rows, -1),
                main_grad.reshape(inner, depth_rows, -1),
            ],
            depth_each + each,
            inner,
        )
        w_in_grad, w_shared_grad, w_out_grad, w_shared_down_grad = assemble(
            main_all,
            shared_all,
            small_all,
            rows_all,
            w_in.shape[1],
            2 * shared_width,
            w_out.shape[0],
            w_shared_down.shape[0],
            max(1, seq_devices // shard_devices),
        )
        depth_sum = to_full(small_all[:, :depth_each].reshape(depth_rows, wide))
        shard_sum = small_all[:, depth_each : depth_each + each].reshape(-1)
        norm_in_grad = to_full(small_all[0, depth_each + each, :depth_rows])
    else:
        hidden_grad = reduce_rows(hidden_part[None])[0]
        residual = to_full(tokens[0])
        own_scale = norm_scale(residual)
        own_unit = residual * own_scale
        scaled = hidden_grad * gain_row
        tokens_grad = to_low(
            mix_grad
            + own_scale
            * (scaled - own_unit * jnp.mean(scaled * own_unit, axis=1, keepdims=True))
        )
        by_depth.append(to_low(jnp.sum(hidden_grad * own_unit, axis=0))[:, None])
        by_depth = jnp.concatenate(by_depth, axis=1).reshape(shard_devices, -1)
        packed = jnp.concatenate([by_depth, by_shard], axis=1)
        summed = lax.psum(lax.psum_scatter(packed, "shard", tiled=True), "seq").reshape(-1)
        count = depth_rows * (used + 1)
        depth_sum = to_full(summed[:count]).reshape(depth_rows, used + 1)
        shard_sum = summed[count:]
        norm_in_grad = depth_sum[:, used]

        def from_line(part, rows):
            own = lax.psum_scatter(part.reshape(shard_devices, rows, -1), "shard")
            return lax.all_gather(own, "seq")

        def columns_of(joined, extent):
            joined = joined.reshape(seq_devices, depth_rows, 2, extent).transpose(1, 2, 0, 3)
            return to_full(joined.reshape(depth_rows, -1))

        w_in_main = columns_of(from_line(main_grad, depth_rows), channels)
        w_in_grad = jnp.concatenate([w_in_main, depth_sum[:, :state_columns]], axis=1)
        w_shared_grad = columns_of(from_line(shared_up_grad, depth_rows), shared_part)
        rows_each = taken.shape[0] * taken.shape[1] // shard_devices
        w_out_grad, w_shared_down_grad = rows_of_shard(
            from_line(taken, rows_each), [w_out, w_shared_down]
        )
    results, start = [], 0
    for shape in shapes:
        size = 1
        for extent in shape:
            size *= extent
        results.append(to_full(shard_sum[start : start + size]).reshape(shape))
        start += size
    conv_w_grad, conv_b_grad, dt_bias_grad, a_log_grad, d_skip_grad, norm_gate_grad = results
    start = state_columns
    w_router_grad = depth_sum[:, start : start + expert_total]
    start += expert_total
    w_dt_grad = depth_sum[:, start : start + head_total]
    start += head_total
    norm_moe_grad = depth_sum[:, start]
    return (
        layer_out[None],
        tokens_grad[None],
        norm_in_grad,
        w_in_grad,
        w_dt_grad,
        conv_w_grad,
        conv_b_grad,
        dt_bias_grad,
        a_log_grad,
        d_skip_grad,
        norm_gate_grad,
        w_out_grad,
        norm_moe_grad,
        w_router_grad,
        w_shared_grad,
        w_shared_down_grad,
        experts_grad,
        experts_down_grad,
    )


def solution(mesh):
    placed = (
        P("shard", "seq", None),
        P("shard", "seq", None),
        P("shard", None),
        P("shard", None),
        P("shard", "seq", None),
        P("shard"),
        P("shard", None),
        P("shard", None),
        P("shard", None),
        P("shard"),
        P("shard"),
        P("shard"),
        P("shard"),
        P("shard"),
        P("shard", None),
        P("shard"),
        P("shard", None),
        P("shard", None),
        P("shard", None),
        P("seq", "shard", None),
        P("seq", "shard", None),
    )
    return jax.shard_map(
        local,
        mesh=mesh,
        in_specs=placed,
        out_specs=(
            P("shard", "seq", None),
            P("shard", "seq", None),
            P("shard"),
            P("shard", None),
            P("shard", None),
            P("shard", None),
            P("shard"),
            P("shard"),
            P("shard"),
            P("shard"),
            P("shard"),
            P("shard", None),
            P("shard"),
            P("shard", None),
            P("shard", None),
            P("shard", None),
            P("seq", "shard", None),
            P("seq", "shard", None),
        ),
        check_vma=False,
    )
```

```python
import functools

import jax
import jax.numpy as jnp
from jax import lax
from jax.experimental import pallas as pl
from jax.experimental.pallas import tpu as pltpu
from jax.sharding import PartitionSpec as P

STRETCH = 256
INNER = 4
UP, DOWN = 0, 1
EPSILON = 1e-05
HIGHEST = lax.Precision.HIGHEST


def matmul(left_side, right_side):
    return jnp.dot(left_side, right_side, preferred_element_type=jnp.float32)


def left_contract(left_side, right_side):
    return lax.dot_general(
        left_side, right_side, (((0,), (0,)), ((), ())), preferred_element_type=jnp.float32
    )


def right_contract(left_side, right_side):
    return lax.dot_general(
        left_side, right_side, (((1,), (1,)), ((), ())), preferred_element_type=jnp.float32
    )


def to_low(values):
    return values.astype(jnp.bfloat16)


def to_full(values):
    return values.astype(jnp.float32)


def norm_scale(values):
    return lax.rsqrt(jnp.mean(values * values, axis=-1, keepdims=True) + EPSILON)


LANES = 128
VMEM_BYTES = 56 * 1024 * 1024


def cost_of(micros):
    return pl.CostEstimate(flops=0, transcendentals=0, bytes_accessed=int(micros * 3.6e6))


def dot_rows(left_side, right_side, precision=None):
    return lax.dot_general(
        left_side,
        right_side,
        (((0,), (0,)), ((), ())),
        precision=precision,
        preferred_element_type=jnp.float32,
    )


def dot_lanes(left_side, right_side, precision=None):
    return lax.dot_general(
        left_side,
        right_side,
        (((1,), (1,)), ((), ())),
        precision=precision,
        preferred_element_type=jnp.float32,
    )


def dot_full(left_side, right_side, precision=None):
    return jnp.dot(
        left_side, right_side, precision=precision, preferred_element_type=jnp.float32
    )


def iota_of(shape, axis):
    return lax.broadcasted_iota(jnp.int32, shape, axis)


def ids_at(places, lengths_ref):
    total, end = jnp.zeros(places.shape, jnp.int32), 0
    for seq in range(lengths_ref.shape[0]):
        end = end + lengths_ref[seq]
        total = total + (places >= end).astype(jnp.int32)
    return total


def id_at(place, lengths_ref):
    total, end = jnp.int32(0), 0
    for seq in range(lengths_ref.shape[0]):
        end = end + lengths_ref[seq]
        total = total + (place >= end).astype(jnp.int32)
    return total


class Stretch:
    def __init__(self, start, rows, before, conv_ref, head_ref, lengths_ref, channels):
        length = rows.shape[0]
        self.channels = channels
        self.heads = channels // 64
        width = conv_ref.shape[1]
        state = (width - channels) // 2
        places = start + iota_of((length, 1), 0)
        self.ids = ids_at(places, lengths_ref)
        self.ids_row = ids_at(start + iota_of((1, length), 1), lengths_ref)
        inputs = rows[:, :width]
        joined = jnp.concatenate([before[:, :width], inputs], axis=0)
        self.shifted = [inputs]
        value = conv_ref[4:5, :] + inputs * conv_ref[3:4, :]
        for offset in range(1, 4):
            same = (ids_at(places - offset, lengths_ref) == self.ids) & (places >= offset)
            moved = pltpu.roll(joined, offset, 0)[8:, :]
            moved = jnp.where(same, moved, 0.0)
            self.shifted.append(moved)
            value = value + moved * conv_ref[3 - offset : 4 - offset, :]
        self.value = value
        self.sig = jax.nn.sigmoid(value)
        act = value * self.sig
        self.x = act[:, :channels]
        self.b = act[:, channels : channels + state]
        self.c = act[:, channels + state :]
        self.b_low = to_low(self.b)
        self.c_low = to_low(self.c)
        self.dt_in = rows[:, width:] + head_ref[0:1, :]
        self.dt = jnp.maximum(self.dt_in, 0.0) + jnp.log1p(jnp.exp(-jnp.abs(self.dt_in)))
        self.rate = head_ref[1:2, :]
        rows_at = iota_of((length, length), 0)
        columns_at = iota_of((length, length), 1)
        lower = (rows_at >= columns_at).astype(jnp.float32)
        self.cum = dot_full(lower, self.dt * self.rate, HIGHEST)
        self.cum_rows = self.cum.T[:8, :]
        self.dt_rows = self.dt.T[:8, :]
        self.causal = (self.ids == self.ids_row) & (rows_at >= columns_at)
        self.scores = dot_lanes(self.c_low, self.b_low)
        last_id = jnp.where(start > 0, id_at(start - 1, lengths_ref), -1)
        end_id = id_at(start + length - 1, lengths_ref)
        self.enter = jnp.where(self.ids == last_id, jnp.exp(self.cum), 0.0)
        end_cum = self.cum[length - 1 : length, :]
        self.tail = jnp.where(self.ids == end_id, jnp.exp(end_cum - self.cum), 0.0)
        self.tail_weight = self.tail * self.dt
        self.keep = jnp.where(last_id == end_id, jnp.exp(end_cum), 0.0)

    def decay(self, head):
        spread = self.cum[:, head : head + 1] - self.cum_rows[head : head + 1, :]
        return jnp.where(self.causal, jnp.exp(jnp.minimum(spread, 0.0)), 0.0)

    def per_channel(self, by_head):
        return jnp.concatenate(
            [
                jnp.broadcast_to(by_head[:, head : head + 1], (by_head.shape[0], 64))
                for head in range(self.heads)
            ],
            axis=1,
        )

    def state_keep(self):
        return jnp.concatenate(
            [
                jnp.broadcast_to(self.keep[:, head : head + 1], (64, LANES))
                for head in range(self.heads)
            ],
            axis=0,
        )


def head_lanes(channels):
    return (iota_of((channels, LANES), 0) // 64 == iota_of((channels, LANES), 1)).astype(
        jnp.float32
    )


def pick_rows(deal_ref, start, length):
    places = start + iota_of((length, 1), 0)
    return jnp.where(deal_ref[...] == places, 1.0, 0.0).astype(jnp.bfloat16)


def scan_forward_kernel(
    lengths_ref, deal_ref, rows_ref, conv_ref, head_ref, y_ref, seq_ref, states_ref, before, state, total
):
    step = pl.program_id(0)
    length = seq_ref.shape[0]
    channels = y_ref.shape[1]
    start = step * length

    @pl.when(step == 0)
    def _():
        before[...] = jnp.zeros_like(before)
        state[...] = jnp.zeros_like(state)
        total[...] = jnp.zeros_like(total)

    picks = pick_rows(deal_ref, start, length)
    rows = dot_full(picks, rows_ref[...])
    seq_ref[...] = to_low(rows)
    part = Stretch(start, rows, before[...], conv_ref, head_ref, lengths_ref, channels)
    before[...] = rows[length - 8 :, :]
    state_now = state[...]
    states_ref[0] = state_now
    x_low = to_low(part.x)
    outs = []
    lane = iota_of((length, LANES), 1)
    for pair in range(channels // LANES):
        x_pair = x_low[:, pair * LANES : (pair + 1) * LANES]
        halves = []
        for head in (2 * pair, 2 * pair + 1):
            weights = part.decay(head) * part.scores * part.dt_rows[head : head + 1, :]
            halves.append(dot_full(to_low(weights), x_pair))
        outs.append(jnp.where(lane < 64, halves[0], halves[1]))
    earlier = dot_lanes(part.c_low, to_low(state_now))
    skip = part.per_channel(head_ref[2:3, :])
    y = jnp.concatenate(outs, axis=1) + part.per_channel(part.enter) * earlier + skip * part.x
    state[...] = part.state_keep() * state_now + dot_rows(
        to_low(part.per_channel(part.tail_weight) * part.x), part.b_low
    )
    total[...] += dot_rows(picks, to_low(y))

    @pl.when(step == pl.num_programs(0) - 1)
    def _():
        y_ref[...] = to_low(total[...])


def scan_forward(lengths, deal_row, rows, conv_table, head_table, channels, freight):
    group_rows, width = rows.shape
    steps = group_rows // STRETCH
    state_rows = (channels, LANES)
    return run(
        scan_forward_kernel,
        (lengths, deal_row, rows, conv_table, head_table),
        grid=(steps,),
        in_specs=[
            pl.BlockSpec(memory_space=pltpu.SMEM),
            whole(deal_row.shape),
            whole(rows.shape),
            whole(conv_table.shape),
            whole(head_table.shape),
        ],
        out_specs=[
            whole((group_rows, channels)),
            pl.BlockSpec((STRETCH, width), lambda step: (step, 0)),
            pl.BlockSpec((1,) + state_rows, lambda step: (step, 0, 0)),
        ],
        out_shape=[
            jax.ShapeDtypeStruct((group_rows, channels), jnp.bfloat16),
            jax.ShapeDtypeStruct((group_rows, width), jnp.bfloat16),
            jax.ShapeDtypeStruct((steps,) + state_rows, jnp.float32),
        ],
        scratch=[
            pltpu.VMEM((8, width), jnp.float32),
            pltpu.VMEM(state_rows, jnp.float32),
            pltpu.VMEM((group_rows, channels), jnp.float32),
        ],
        freight=freight,
        micros=25,
        name="scan_forward",
    )


def scan_backward_kernel(
    lengths_ref,
    deal_ref,
    seq_ref,
    states_ref,
    dy_ref,
    conv_ref,
    head_ref,
    other_ref,
    drows_ref,
    conv_grad_ref,
    head_grad_ref,
    other_sum_ref,
    after,
    state_grad,
    *other_scratch,
):
    order = pl.program_id(0)
    steps = pl.num_programs(0)
    reducer = Reducer(other_ref.shape[0], other_ref, other_sum_ref, other_scratch)

    last = dy_ref.shape[0] // STRETCH - 1

    @pl.when(order == 0)
    def _():
        reducer.begin()

    for count in range(min(last + 1, reducer.inner + 3)):

        @pl.when(order == count)
        def _():
            reducer.step(count)

    step = steps - 1 - order
    length = STRETCH
    channels = dy_ref.shape[1]
    width = conv_ref.shape[1]
    state_width = (width - channels) // 2
    start = pl.multiple_of(step * length, length)

    @pl.when(order == 0)
    def _():
        after[...] = jnp.zeros_like(after)
        state_grad[...] = jnp.zeros_like(state_grad)
        drows_ref[...] = jnp.zeros_like(drows_ref)
        conv_grad_ref[...] = jnp.zeros_like(conv_grad_ref)
        head_grad_ref[...] = jnp.zeros_like(head_grad_ref)

    picks = pick_rows(deal_ref, start, length)
    dy = dot_full(picks, dy_ref[...])
    rows = seq_ref[pl.ds(start, length), :].astype(jnp.float32)
    place = pl.multiple_of(jnp.maximum(start - 16, 0), 16)
    before = seq_ref[pl.ds(place, 16), :].astype(jnp.float32)[8:, :]
    part = Stretch(start, rows, before, conv_ref, head_ref, lengths_ref, channels)
    state_now = states_ref[0]
    state_low = to_low(state_now)
    next_grad = state_grad[...]
    next_low = to_low(next_grad)
    lanes_of = head_lanes(channels)
    x_low = to_low(part.x)
    dy_low = to_low(dy)
    lane = iota_of((length, LANES), 1)

    enter = part.per_channel(part.enter)
    tail_weight = part.per_channel(part.tail_weight)
    earlier = dot_lanes(part.c_low, state_low)
    enter_grad = dot_full(dy * earlier, lanes_of, HIGHEST)
    entered = to_low(enter * dy)
    c_grad = dot_full(entered, state_low)
    state_grad[...] = part.state_keep() * next_grad + dot_rows(entered, part.c_low)
    onward = dot_lanes(part.b_low, next_low)
    x_grad = part.per_channel(head_ref[2:3, :]) * dy + tail_weight * onward
    tail_grad = dot_full(part.x * onward, lanes_of, HIGHEST)
    b_grad = dot_full(to_low(tail_weight * part.x), next_low)
    tail_part = tail_grad * part.tail_weight
    cum_grad = enter_grad * part.enter - tail_part
    dt_grad = tail_grad * part.tail
    kept = dot_lanes(jnp.ones((8, LANES), jnp.float32), next_grad * state_now, HIGHEST)
    keep_grad = dot_full(kept, lanes_of, HIGHEST)[:1, :]
    end_grad = jnp.sum(tail_part, axis=0, keepdims=True) + keep_grad * part.keep

    score_grad = jnp.zeros((length, length), jnp.float32)
    cum_columns, cum_rows, dt_rows, outs = [], [], [], []
    for pair in range(channels // LANES):
        x_pair = x_low[:, pair * LANES : (pair + 1) * LANES]
        dy_pair = dy_low[:, pair * LANES : (pair + 1) * LANES]
        halves = []
        for half, head in enumerate((2 * pair, 2 * pair + 1)):
            mine = (lane < 64) if half == 0 else (lane >= 64)
            weight_grad = dot_lanes(jnp.where(mine, dy_pair, jnp.zeros_like(dy_pair)), x_pair)
            decay = part.decay(head)
            dt_row = part.dt_rows[head : head + 1, :]
            by_decay = weight_grad * decay
            by_dt = by_decay * part.scores
            by_spread = by_dt * dt_row
            dt_rows.append(jnp.sum(by_dt, axis=0, keepdims=True))
            cum_rows.append(jnp.sum(by_spread, axis=0, keepdims=True))
            cum_columns.append(jnp.sum(by_spread, axis=1, keepdims=True))
            score_grad = score_grad + by_decay * dt_row
            halves.append(dot_rows(to_low(decay * part.scores * dt_row), dy_pair))
        outs.append(jnp.where(lane < 64, halves[0], halves[1]))
    x_grad = x_grad + jnp.concatenate(outs, axis=1)
    score_low = to_low(score_grad)
    c_grad = c_grad + dot_full(score_low, part.b_low)
    b_grad = b_grad + dot_rows(score_low, part.c_low)

    heads = len(dt_rows)
    blank = jnp.zeros((LANES - heads, length), jnp.float32)
    dt_grad = dt_grad + jnp.concatenate(dt_rows + [blank], axis=0).T
    cum_grad = cum_grad - jnp.concatenate(cum_rows + [blank], axis=0).T
    for head in range(heads):
        cum_grad = cum_grad + jnp.where(lane == head, cum_columns[head], 0.0)
    at_end = iota_of((length, 1), 0) == length - 1
    cum_grad = cum_grad + jnp.where(at_end, end_grad, 0.0)
    upper = (iota_of((length, length), 1) >= iota_of((length, length), 0)).astype(jnp.float32)
    log_grad = dot_full(upper, cum_grad, HIGHEST)
    dt_grad = dt_grad + log_grad * part.rate
    dt_in_grad = dt_grad * jax.nn.sigmoid(part.dt_in)
    dt_in_grad = jnp.where(lane < heads, dt_in_grad, 0.0)
    head_grad_ref[0:1, :] += jnp.sum(dt_in_grad, axis=0, keepdims=True)
    head_grad_ref[1:2, :] += jnp.sum(log_grad * part.dt, axis=0, keepdims=True) * part.rate
    skip_sum = jnp.broadcast_to(jnp.sum(dy * part.x, axis=0, keepdims=True), (8, channels))
    head_grad_ref[2:3, :] += dot_full(skip_sum, lanes_of, HIGHEST)[:1, :]

    act_grad = jnp.concatenate([x_grad, b_grad, c_grad], axis=1)
    value_grad = act_grad * part.sig * (1.0 + part.value * (1.0 - part.sig))
    conv_grad_ref[4:5, :] += jnp.sum(value_grad, axis=0, keepdims=True)
    for offset in range(4):
        conv_grad_ref[3 - offset : 4 - offset, :] += jnp.sum(
            value_grad * part.shifted[offset], axis=0, keepdims=True
        )
    joined = jnp.concatenate([value_grad, after[...]], axis=0)
    places = start + iota_of((length, 1), 0)
    rows_grad = value_grad * conv_ref[3:4, :]
    for offset in range(1, 4):
        moved = pltpu.roll(joined, length + 8 - offset, 0)[:length, :]
        same = (ids_at(places + offset, lengths_ref) == part.ids) & (
            places + offset < steps * length
        )
        rows_grad = rows_grad + jnp.where(same, moved, 0.0) * conv_ref[3 - offset : 4 - offset, :]
    after[...] = value_grad[:8, :]
    drows_ref[...] += to_low(
        dot_rows(picks, to_low(jnp.concatenate([rows_grad, dt_in_grad], axis=1)))
    )

    for count in range(last + 1, reducer.inner + 3):

        @pl.when(order == last)
        def _():
            reducer.step(count)

    @pl.when(order == steps - 1)
    def _():
        reducer.finish()


def scan_backward(
    lengths, deal_row, seq_rows, states, dy, conv_table, head_table, other, freight
):
    group_rows, width = seq_rows.shape
    channels = dy.shape[1]
    steps = group_rows // STRETCH
    return run(
        scan_backward_kernel,
        (lengths, deal_row, seq_rows, states, dy, conv_table, head_table, other),
        grid=(steps,),
        in_specs=[
            pl.BlockSpec(memory_space=pltpu.SMEM),
            whole(deal_row.shape),
            once(seq_rows.shape),
            pl.BlockSpec((1, channels, LANES), lambda step: (steps - 1 - step, 0, 0)),
            once(dy.shape),
            whole(conv_table.shape),
            whole(head_table.shape),
            pl.BlockSpec(memory_space=pl.ANY),
        ],
        out_specs=[
            whole((group_rows, width)),
            whole(conv_table.shape),
            whole(head_table.shape),
            whole(other.shape[2:]),
        ],
        out_shape=[
            jax.ShapeDtypeStruct((group_rows, width), jnp.bfloat16),
            jax.ShapeDtypeStruct(conv_table.shape, jnp.float32),
            jax.ShapeDtypeStruct(head_table.shape, jnp.float32),
            jax.ShapeDtypeStruct(other.shape[2:], jnp.float32),
        ],
        scratch=[
            pltpu.VMEM((8, conv_table.shape[1]), jnp.float32),
            pltpu.VMEM((channels, LANES), jnp.float32),
        ]
        + Reducer.scratch(other.shape[0], *other.shape[2:]),
        freight=freight,
        flips=FLIPS,
        inner=other.shape[0],
        micros=40,
        name="scan_backward",
    )


def whole(shape):
    return pl.BlockSpec(shape, lambda *steps: (0,) * len(shape))


def once(shape):
    return pl.BlockSpec(
        shape, lambda *steps: (0,) * len(shape), pipeline_mode=pl.Buffered(buffer_count=1)
    )


MESH = pl.DeviceIdType.MESH
FLIPS = (1, 2, 4)


def flipped(place, flip):
    result = place
    for bit in FLIPS:
        if flip & bit:
            result = result + bit - 2 * bit * lax.rem(lax.div(place, bit), 2)
    return result


def own_shard_group(inner):
    shard = lax.axis_index("shard")
    place = lax.rem(shard, inner)
    return place, shard - place


def peers_in_order(place, inner):
    if inner == 1:
        return []
    if inner == 4:
        half = lax.div(place, 2)
        return [flipped(place, 1), 2 - half, 3 - 3 * half]
    return [lax.rem(place + shift, inner) for shift in range(1, inner)]


def greet(flips, inner):
    barrier = pltpu.get_barrier_semaphore()
    part = lax.axis_index("seq")
    place, first = own_shard_group(inner)
    for flip in flips:
        pl.semaphore_signal(
            barrier, inc=1, device_id={"seq": flipped(part, flip)}, device_id_type=MESH
        )
    for peer in peers_in_order(place, inner):
        pl.semaphore_signal(
            barrier, inc=1, device_id={"shard": first + peer}, device_id_type=MESH
        )
    pl.semaphore_wait(barrier, len(flips) + inner - 1)


class Parcel:
    flips = ()
    sems = 1

    def __init__(self, array, shift, inner, index=None, output=None):
        self.array, self.shift, self.inner, self.index = array, shift, inner, index
        self.shape = array.shape if index is None else array.shape[1:]
        self.output = output

    def moves(self, source, target):
        place, first = own_shard_group(self.inner)
        to = lax.rem(place + self.shift, self.inner)
        if self.index is not None:
            source = source.at[self.index(to)]
        return [(source, target, target, {"shard": first + to})]

    def stays(self, source, target):
        return []


class PlaneSwap:
    flips = (1, 2, 3, 4, 5, 6, 7)
    inner = 1
    sems = 8

    output = None

    def __init__(self, array):
        self.array, self.shape = array, array.shape

    def moves(self, source, target):
        part = lax.axis_index("seq")
        return [
            (
                source.at[flipped(part, flip)],
                target.at[part],
                target.at[flipped(part, flip)],
                {"seq": flipped(part, flip)},
            )
            for flip in self.flips
        ]

    def stays(self, source, target):
        part = lax.axis_index("seq")
        return [(source.at[part], target.at[part])]


COLLECTIVES = []


def run(
    kernel,
    args,
    *,
    in_specs,
    out_specs,
    out_shape,
    name,
    micros,
    grid=(),
    scratch=(),
    freight=(),
    flips=(),
    inner=1,
    late=False,
):
    freight = list(freight)
    for place, item in enumerate(freight):
        item.rank = place
    flips = tuple(sorted(set(flips).union(*[item.flips for item in freight])))
    inner = max([inner] + [item.inner for item in freight])
    talks = bool(flips) or inner > 1
    count_in, count_out, count_scratch = len(args), len(out_shape), len(scratch)
    count = len(freight)
    loaded = [item for item in freight if item.output is None]

    def wrapped(*refs):
        ins, refs = refs[:count_in], refs[count_in:]
        sources, refs = list(refs[: len(loaded)]), refs[len(loaded) :]
        outs, refs = refs[:count_out], refs[count_out:]
        sources = [
            sources.pop(0) if item.output is None else outs[item.output] for item in freight
        ]
        targets, refs = refs[:count], refs[count:]
        own, refs = refs[:count_scratch], refs[count_scratch:]

        def remote(item, place, order, source, target, device):
            send, recv = refs[3 * place : 3 * place + 2]
            return pltpu.make_async_remote_copy(
                src_ref=source,
                dst_ref=target,
                send_sem=send.at[order],
                recv_sem=recv.at[order],
                device_id=device,
                device_id_type=MESH,
            )

        def moves(chosen):
            for place, item in enumerate(freight):
                if not chosen(item):
                    continue
                for order, move in enumerate(item.moves(sources[place], targets[place])):
                    yield item, place, order, move

        def stays(chosen):
            for place, item in enumerate(freight):
                if not chosen(item):
                    continue
                for source, target in item.stays(sources[place], targets[place]):
                    yield pltpu.make_async_copy(source, target, refs[3 * place + 2])

        def depart(chosen=lambda item: True):
            for item, place, order, (source, target, _, device) in moves(chosen):
                remote(item, place, order, source, target, device).start()
            for copy in stays(chosen):
                copy.start()

        def arrive(chosen=lambda item: True):
            for item, place, order, (source, target, arrival, device) in moves(chosen):
                remote(item, place, order, source, arrival, device).wait_recv()
                remote(item, place, order, source, target, device).wait_send()
            for copy in stays(chosen):
                copy.wait()

        if grid:
            at = [pl.program_id(axis) for axis in range(len(grid))]
            first, last = at[0] == 0, at[0] == grid[0] - 1
            for axis in range(1, len(grid)):
                first = first & (at[axis] == 0)
                last = last & (at[axis] == grid[axis] - 1)
            if talks:

                @pl.when(first)
                def _():
                    greet(flips, inner)
                    if not late:
                        depart()

            if late:
                kernel(depart, arrive, targets, *ins, *outs, *own)
            else:
                kernel(*ins, *outs, *own)
            if talks and not late:
                pl.when(last)(arrive)
        else:
            if talks:
                greet(flips, inner)
            if late:
                kernel(depart, *ins, *outs, *own)
            else:
                depart()
                kernel(*ins, *outs, *own)
            arrive()

    anywhere = pl.BlockSpec(memory_space=pl.ANY)
    extra = {}
    if talks:
        COLLECTIVES.append(name)
        extra = dict(collective_id=len(COLLECTIVES), has_side_effects=True)
    sems = []
    for item in freight:
        sems += [
            pltpu.SemaphoreType.DMA((item.sems,)),
            pltpu.SemaphoreType.DMA((item.sems,)),
            pltpu.SemaphoreType.DMA(()),
        ]
    results = pl.pallas_call(
        wrapped,
        grid=grid,
        in_specs=list(in_specs) + [anywhere] * len(loaded),
        out_specs=list(out_specs) + [anywhere] * count,
        out_shape=list(out_shape)
        + [jax.ShapeDtypeStruct(item.shape, item.array.dtype) for item in freight],
        scratch_shapes=list(scratch) + sems,
        compiler_params=pltpu.CompilerParams(vmem_limit_bytes=VMEM_BYTES, **extra),
        cost_estimate=cost_of(micros),
        name=name,
    )(*args, *[item.array for item in loaded])
    results = list(results)
    if freight:
        return results[:count_out] + [results[count_out:]]
    return results


class LineSum:
    def __init__(self, inner, sums, from_below, from_above, send, below_recv, above_recv):
        self.inner = inner
        self.sums, self.from_below, self.from_above = sums, from_below, from_above
        self.send, self.below_recv, self.above_recv = send, below_recv, above_recv
        self.place, self.first = own_shard_group(inner)
        self.targets = list(reversed(peers_in_order(self.place, inner))) + [self.place]

    def copy(self, order, up):
        target = self.targets[order]
        inbox = self.from_below if up else self.from_above
        recv = self.below_recv if up else self.above_recv
        return pltpu.make_async_remote_copy(
            src_ref=self.sums.at[order],
            dst_ref=inbox.at[target],
            send_sem=self.send.at[order],
            recv_sem=recv.at[target],
            device_id={"shard": self.first + self.place + (1 if up else -1)},
            device_id_type=MESH,
        )

    def arrived(self, target, up):
        inbox = self.from_below if up else self.from_above
        recv = self.below_recv if up else self.above_recv
        pltpu.make_async_remote_copy(
            src_ref=inbox.at[target],
            dst_ref=inbox.at[target],
            send_sem=self.send.at[0],
            recv_sem=recv.at[target],
            device_id={"shard": self.first + self.place + (-1 if up else 1)},
            device_id_type=MESH,
        ).wait_recv()
        return to_full(inbox[target])

    def ways(self):
        return ((True, self.place > 0), (False, self.place < self.inner - 1))

    def push_free(self, order):
        target = self.targets[order]
        for up, comes in self.ways():
            heads = (target > self.place) if up else (target < self.place)

            @pl.when(heads & jnp.logical_not(comes))
            def _():
                self.copy(order, up).start()

    def push_rest(self, order):
        target = self.targets[order]
        for up, comes in self.ways():
            heads = (target > self.place) if up else (target < self.place)

            @pl.when(heads & comes)
            def _():
                self.sums[order] = to_low(
                    to_full(self.sums[order]) + self.arrived(target, up)
                )
                self.copy(order, up).start()

    def add_own(self, total):
        for up, comes in self.ways():

            @pl.when(comes)
            def _():
                total[...] += self.arrived(self.place, up)

    def finish(self):
        for order in range(self.inner - 1):
            for up in (True, False):
                target = self.targets[order]

                @pl.when((target > self.place) if up else (target < self.place))
                def _():
                    self.copy(order, up).wait_send()

    @staticmethod
    def scratch(inner, rows, width):
        sems = lambda *shape: pltpu.SemaphoreType.DMA(shape)
        return [
            pltpu.VMEM((max(1, inner - 1), rows, width), jnp.bfloat16),
            pltpu.VMEM((inner, rows, width), jnp.bfloat16),
            pltpu.VMEM((inner, rows, width), jnp.bfloat16),
            sems(max(1, inner - 1)),
            sems(inner),
            sems(inner),
        ]


class Reducer:
    def __init__(self, inner, p_ref, total, refs):
        self.inner, self.p_ref, self.total = inner, p_ref, total
        self.held, self.paired, self.turned, self.crossed = refs[:4]
        self.load, self.core_send, self.core_recv = refs[4:7]
        self.turn_send, self.turn_recv, self.cross_send, self.cross_recv = refs[7:11]
        self.line = LineSum(inner, *refs[11:])
        self.part = lax.axis_index("seq")
        half = self.held.shape[2] // 2
        self.spans = [pl.ds(0, half), pl.ds(half, half)]

    @staticmethod
    def scratch(inner, rows, width):
        low = jnp.bfloat16
        sems = lambda *shape: pltpu.SemaphoreType.DMA(shape)
        return [
            pltpu.VMEM((inner, 4, rows, width), low),
            pltpu.VMEM((inner, 4, rows, width), low),
            pltpu.VMEM((inner, 2, rows // 2, width), low),
            pltpu.VMEM((inner, 4, rows // 2, width), low),
            sems(inner, 4),
            sems(inner, 4),
            sems(inner, 4),
            sems(inner, 2),
            sems(inner, 2),
            sems(inner, 4),
            sems(inner, 4),
        ] + LineSum.scratch(inner, rows, width)

    EVENS = (6, 2, 4, 0)

    def to_core(self, order, slot):
        return pltpu.make_async_remote_copy(
            src_ref=self.p_ref.at[
                self.line.targets[order], flipped(self.part, self.EVENS[slot] + 1)
            ],
            dst_ref=self.paired.at[order, slot],
            send_sem=self.core_send.at[order, slot],
            recv_sem=self.core_recv.at[order, slot],
            device_id={"seq": flipped(self.part, 1)},
            device_id_type=MESH,
        )

    def loading(self, order, slot):
        return pltpu.make_async_copy(
            self.p_ref.at[self.line.targets[order], flipped(self.part, self.EVENS[slot])],
            self.held.at[order, slot],
            self.load.at[order, slot],
        )

    def turn(self, order, span):
        return pltpu.make_async_remote_copy(
            src_ref=self.held.at[order, 0, self.spans[span]],
            dst_ref=self.turned.at[order, span],
            send_sem=self.turn_send.at[order, span],
            recv_sem=self.turn_recv.at[order, span],
            device_id={"seq": flipped(self.part, (2, 4)[span])},
            device_id_type=MESH,
        )

    CROSSINGS = ((1, 2, 0), (2, 4, 1), (2, 4, 0), (1, 2, 1))

    def cross(self, order, kind):
        slot, flip, span = self.CROSSINGS[kind]
        return pltpu.make_async_remote_copy(
            src_ref=self.held.at[order, slot, self.spans[span]],
            dst_ref=self.crossed.at[order, kind],
            send_sem=self.cross_send.at[order, kind],
            recv_sem=self.cross_recv.at[order, kind],
            device_id={"seq": flipped(self.part, flip)},
            device_id_type=MESH,
        )

    def begin(self):
        for order in range(self.inner):
            for slot in range(4):
                self.to_core(order, slot).start()
                self.loading(order, slot).start()

    def total_of(self, order, slot):
        self.loading(order, slot).wait()
        self.to_core(order, slot).wait_recv()
        return to_full(self.held[order, slot]) + to_full(self.paired[order, slot])

    def stage_a(self, order):
        self.held[order, 0] = to_low(self.total_of(order, 0))
        for span in range(2):
            self.turn(order, span).start()
        for slot in (1, 2):
            self.held[order, slot] = to_low(self.total_of(order, slot))
            self.cross(order, slot - 1).start()

    def stage_b(self, order):
        for kind in (2, 3):
            slot, _, span = self.CROSSINGS[kind]
            self.turn(order, span).wait_recv()
            at = self.spans[span]
            self.held[order, slot, at] = to_low(
                to_full(self.held[order, slot, at]) + to_full(self.turned[order, span])
            )
            self.cross(order, kind).start()

    def stage_c(self, order):
        total = self.total_of(order, 3)
        for kind in range(4):
            self.cross(order, kind).wait_recv()
        crossed = [to_full(self.crossed[order, kind]) for kind in range(4)]
        total = total + jnp.concatenate(
            [crossed[0] + crossed[2], crossed[1] + crossed[3]], axis=0
        )
        if order == self.inner - 1:
            self.total[...] = total
        else:
            self.line.sums[order] = to_low(total)
            self.line.push_free(order)

    def stage_d(self, order):
        if order == self.inner - 1:
            self.line.add_own(self.total)
        else:
            self.line.push_rest(order)

    def step(self, count):
        for stage, late in (
            (self.stage_b, 1),
            (self.stage_a, 0),
            (self.stage_c, 2),
            (self.stage_d, 3),
        ):
            if 0 <= count - late < self.inner:
                stage(count - late)

    def steps(self):
        return self.inner + 3

    def finish(self):
        for order in range(self.inner):
            for slot in range(4):
                self.to_core(order, slot).wait_send()
            for span in range(2):
                self.turn(order, span).wait_send()
            for kind in range(4):
                self.cross(order, kind).wait_send()
        self.line.finish()

    def whole(self, depart):
        self.begin()
        depart(0)
        for count in range(self.inner + 3):
            self.step(count)
            if count >= 2:
                depart(count - 1)
        self.finish()


def reduce_kernel(inner, staged, depart, p_ref, out_ref, *scratch):
    def leave(number):
        if staged:
            depart(lambda item: item.rank == number)

    if not staged:
        depart()
    Reducer(inner, p_ref, out_ref, scratch).whole(leave)


def reduce_rows(partial, freight=()):
    inner, _, rows, width = partial.shape
    return run(
        functools.partial(reduce_kernel, inner, inner > 1),
        (partial,),
        in_specs=[pl.BlockSpec(memory_space=pl.ANY)],
        out_specs=[pl.BlockSpec(memory_space=pltpu.VMEM)],
        out_shape=[jax.ShapeDtypeStruct((rows, width), jnp.float32)],
        scratch=Reducer.scratch(inner, rows, width),
        freight=freight,
        flips=FLIPS,
        inner=inner,
        late=True,
        micros=25 * inner,
        name="reduce_rows",
    )


def plane_gather(own, target, send, recv):
    part = lax.axis_index("seq")
    half = own.shape[0] // 2
    spans = [pl.ds(0, half), pl.ds(half, half)]
    started = []

    def copy_of(kind, block, span, flip, from_own=False):
        place = target(block).at[spans[span]]
        return pltpu.make_async_remote_copy(
            src_ref=own.at[spans[span]] if from_own else place,
            dst_ref=place,
            send_sem=send.at[kind],
            recv_sem=recv.at[kind],
            device_id={"seq": flipped(part, flip)},
            device_id_type=MESH,
        )

    def push(kind, block, span, flip, from_own=False):
        copy = copy_of(kind, block, span, flip, from_own)
        copy.start()
        started.append(copy)

    def arrived(kind, block, span, flip):
        copy_of(kind, block, span, flip).wait_recv()

    def first():
        for kind, span, flip in (
            (3, 1, 2), (4, 0, 4), (2, 0, 2), (5, 1, 4), (0, 0, 1), (1, 1, 1)
        ):
            push(kind, part, span, flip, True)

    def second():
        side, over = flipped(part, 2), flipped(part, 4)
        arrived(3, side, 1, 2)
        push(6, side, 1, 4)
        arrived(4, over, 0, 4)
        push(7, over, 0, 2)
        push(9, side, 1, 1)
        push(10, over, 0, 1)
        arrived(2, side, 0, 2)
        push(8, side, 0, 1)
        arrived(5, over, 1, 4)
        push(11, over, 1, 1)

    def third():
        far = flipped(part, 6)
        arrived(6, far, 1, 4)
        push(13, far, 1, 1)
        arrived(7, far, 0, 2)
        push(12, far, 0, 1)

    def last():
        for kind, flip, span in (
            (0, 1, 0), (1, 1, 1), (9, 3, 1), (10, 5, 0), (8, 3, 0), (11, 5, 1), (13, 7, 1), (12, 7, 0)
        ):
            arrived(kind, flipped(part, flip), span, 1)
        for copy in started:
            copy.wait_send()

    return first, second, third, last


def line_gather(inner, own, target, send, recv):
    place, first = own_shard_group(inner)
    half = own.shape[0] // 2
    spans = [pl.ds(0, half), pl.ds(half, half)]

    def copy_of(way, step, span):
        block = place - step if way == 0 else place + step
        to = place + 1 if way == 0 else place - 1
        spot = target(block).at[spans[span]]
        return pltpu.make_async_remote_copy(
            src_ref=own.at[spans[span]] if step == 0 else spot,
            dst_ref=spot,
            send_sem=send.at[way, step, span],
            recv_sem=recv.at[way, step, span],
            device_id={"shard": first + to},
            device_id_type=MESH,
        )

    def sends(way, step):
        if way == 0:
            return (place < inner - 1) & (place >= step)
        return (place > 0) & (place + step < inner)

    def receives(way, step):
        return place >= step if way == 0 else place + step < inner

    def start(step, span):
        for way in range(2):

            @pl.when(sends(way, step))
            def _():
                copy_of(way, step, span).start()

    def begin():
        for span in range(2):
            start(0, span)

    def onward(step):
        for span in range(2):
            for way in range(2):

                @pl.when(receives(way, step))
                def _():
                    block = place - step if way == 0 else place + step
                    spot = target(block).at[spans[span]]
                    pltpu.make_async_remote_copy(
                        src_ref=spot,
                        dst_ref=spot,
                        send_sem=send.at[way, step - 1, span],
                        recv_sem=recv.at[way, step - 1, span],
                        device_id={"shard": block + first},
                        device_id_type=MESH,
                    ).wait_recv()

            if step < inner - 1:
                start(step, span)

    def finish():
        for step in range(inner - 1):
            for span in range(2):
                for way in range(2):

                    @pl.when(sends(way, step))
                    def _():
                        copy_of(way, step, span).wait_send()

    return begin, onward, finish


def group_gather(inner, own, target, sems):
    part = lax.axis_index("seq")
    place, _ = own_shard_group(inner)
    sources = [place] + peers_in_order(place, inner)
    line_send, line_recv, send, recv = sems
    line = line_gather(inner, own, lambda p: target(p, part), line_send, line_recv)
    planes = [
        plane_gather(
            own if order == 0 else target(source, part),
            lambda b, source=source: target(source, b),
            send.at[order],
            recv.at[order],
        )
        for order, source in enumerate(sources)
    ]
    return line, planes


def group_sems(inner):
    sems = lambda *shape: pltpu.SemaphoreType.DMA(shape)
    steps = max(1, inner - 1)
    return [sems(2, steps, 2), sems(2, steps, 2), sems(inner, 14), sems(inner, 14)]


def gather_kernel(inner, depart, x_ref, out_ref, own_sem, *sems):
    part = lax.axis_index("seq")
    place, _ = own_shard_group(inner)
    own = pltpu.make_async_copy(x_ref, out_ref.at[place, part], own_sem)
    (begin, onward, finish), planes = group_gather(
        inner, x_ref, lambda p, b: out_ref.at[p, b], sems
    )
    if inner > 1:
        begin()
    else:
        depart()
    planes[0][0]()
    own.start()
    planes[0][1]()
    for order in range(1, inner):
        onward(order)
        if order == inner - 1:
            depart()
        planes[order][0]()
        planes[order - 1][2]()
        planes[order][1]()
    planes[inner - 1][2]()
    for stages in planes:
        stages[3]()
    if inner > 1:
        finish()
    own.wait()


def gather_rows(x, inner, freight=()):
    rows, width = x.shape
    seq_devices = lax.axis_size("seq")
    return run(
        functools.partial(gather_kernel, inner),
        (x,),
        in_specs=[pl.BlockSpec(memory_space=pl.ANY)],
        out_specs=[pl.BlockSpec(memory_space=pl.ANY)],
        out_shape=[jax.ShapeDtypeStruct((inner, seq_devices, rows, width), x.dtype)],
        scratch=[pltpu.SemaphoreType.DMA(())] + group_sems(inner),
        freight=freight,
        flips=FLIPS,
        inner=inner,
        late=True,
        micros=25 * inner,
        name="gather_rows",
    )


def begin_kernel(
    inner,
    x_ref,
    g_ref,
    s_ref,
    d_ref,
    in_ref,
    shared_ref,
    out_ref,
    down_ref,
    x_out,
    g_out,
    w_out,
    s_out,
    d_out,
    r_out,
    w_ref,
    r_ref,
    own_sems,
    pick_sems,
    *sems,
):
    part = lax.axis_index("seq")
    place, _ = own_shard_group(inner)
    rows = w_ref.shape[0]
    seq_devices = x_out.shape[0]
    picks = []

    def pick(source, target):
        picks.append(pltpu.make_async_copy(source, target, pick_sems.at[len(picks)]))

    shared = shared_ref.shape[1] // seq_devices // 2
    state = w_ref.shape[1] - 2 * shared
    channels = (in_ref.shape[1] - state) // (2 * seq_devices - 2)
    state -= 2 * channels
    at = 0
    for source, extent in ((in_ref, channels), (shared_ref, shared)):
        for side in range(2):
            start = pl.multiple_of((side * seq_devices + part) * extent, extent)
            pick(source.at[:, pl.ds(start, extent)], w_ref.at[:, pl.ds(at, extent)])
            at += extent
        if source is in_ref:
            pick(
                source.at[:, pl.ds(in_ref.shape[1] - state, state)],
                w_ref.at[:, pl.ds(at, state)],
            )
            at += state
    halves = seq_devices // inner
    at = 0
    for half in range(halves):
        for source in (out_ref, down_ref):
            fine = source.shape[0] // halves // seq_devices
            start = pl.multiple_of((half * seq_devices + part) * fine, fine)
            pick(source.at[pl.ds(start, fine)], r_ref.at[pl.ds(at, fine)])
            at += fine
    for copy in picks:
        copy.start()
    targets = [
        lambda p: s_out.at[p],
        lambda p: w_out.at[pl.ds(p * rows, rows)],
        lambda p: r_out.at[p],
        lambda p: d_out.at[p],
    ]
    sources = [s_ref, w_ref, r_ref, d_ref]
    lines = [
        line_gather(inner, source, target, sems[2 * order], sems[2 * order + 1])
        for order, (source, target) in enumerate(zip(sources, targets))
    ]
    line, planes = group_gather(inner, g_ref, lambda p, b: g_out.at[p, b], sems[8:12])
    lines.append(line)
    x_plane = plane_gather(x_ref, lambda b: x_out.at[b], sems[12], sems[13])
    rows_line = lines.pop(2)
    lines[0][0]()
    lines[2][0]()
    lines[3][0]()
    x_plane[0]()
    planes[0][0]()
    for copy in picks:
        copy.wait()
    lines[1][0]()
    owns = [
        pltpu.make_async_copy(source, target(place), own_sems.at[order])
        for order, (source, target) in enumerate(zip(sources, targets))
    ]
    owns.append(pltpu.make_async_copy(x_ref, x_out.at[part], own_sems.at[4]))
    owns.append(pltpu.make_async_copy(g_ref, g_out.at[place, part], own_sems.at[5]))
    for copy in owns:
        copy.start()
    x_plane[1]()
    planes[0][1]()
    x_plane[2]()
    planes[0][2]()
    for step in range(1, inner):
        for _, onward, _ in reversed(lines):
            onward(step)
        if step == max(1, inner - 2):
            rows_line[0]()
        planes[step][0]()
        if step > 1:
            planes[step - 1][2]()
        planes[step][1]()
    rows_line[1](1)
    planes[inner - 1][2]()
    for step in range(2, inner):
        rows_line[1](step)
    x_plane[3]()
    for stages in planes:
        stages[3]()
    for _, _, finish in lines + [rows_line]:
        finish()
    for copy in owns:
        copy.wait()


def begin(x, grad, small, by_depth, w_in, w_shared, w_out, w_down, in_width, shared_part, inner):
    seq_devices = lax.axis_size("seq")
    low = jnp.bfloat16
    depth, width = w_in.shape[0], w_out.shape[1]
    columns = in_width + 2 * shared_part
    rows = (w_out.shape[0] + w_down.shape[0]) // seq_devices
    anywhere = pl.BlockSpec(memory_space=pl.ANY)
    sems = lambda *shape: pltpu.SemaphoreType.DMA(shape)
    line_sems = [sems(2, inner - 1, 2)] * 8
    return run(
        functools.partial(begin_kernel, inner),
        (x, grad, small, by_depth, w_in, w_shared, w_out, w_down),
        in_specs=[anywhere] * 8,
        out_specs=[anywhere] * 6,
        out_shape=[
            jax.ShapeDtypeStruct((seq_devices,) + x.shape, x.dtype),
            jax.ShapeDtypeStruct((inner, seq_devices) + grad.shape, grad.dtype),
            jax.ShapeDtypeStruct((inner * depth, columns), low),
            jax.ShapeDtypeStruct((inner,) + small.shape, small.dtype),
            jax.ShapeDtypeStruct((inner,) + by_depth.shape, low),
            jax.ShapeDtypeStruct((inner, rows, width), low),
        ],
        scratch=[pltpu.VMEM((depth, columns), low), pltpu.VMEM((rows, width), low)]
        + [sems(6), sems(5 + 2 * (seq_devices // inner))]
        + line_sems + group_sems(inner) + [sems(14), sems(14)],
        flips=FLIPS,
        inner=inner,
        micros=130,
        name="begin",
    )


def settle_kernel(
    inner,
    counts,
    hidden_ref,
    small_ref,
    x_ref,
    mix_ref,
    gain_ref,
    *refs,
):
    part = lax.axis_index("seq")
    place, _ = own_shard_group(inner)
    parts, refs = refs[:counts], refs[counts:]
    tokens_out, refs = refs[0], refs[1:]
    outs, refs = refs[: counts + 1], refs[counts + 1 :]
    hidden_sum, small_sum = refs[:2]
    refs = refs[2:]
    take = len(Reducer.scratch(1, 16, LANES))
    hidden = Reducer(1, hidden_ref, hidden_sum, refs[:take])
    small = Reducer(inner, small_ref, small_sum, refs[take : 2 * take])
    refs = refs[2 * take :]
    lines, totals, planes, owns = [], [], [], []
    for index in range(counts + 1):
        low, gsend, grecv, here = refs[:4]
        refs = refs[4:]
        out = outs[index]
        planes.append(plane_gather(low, lambda b, out=out: out.at[b], gsend, grecv))
        owns.append((low, pltpu.make_async_copy(low, out.at[part], here)))
    loads = []
    for index in range(counts):
        total, load = refs[:2]
        line = LineSum(inner, *refs[2:8])
        refs = refs[8:]
        lines.append(line)
        totals.append(total)
        for order in range(inner - 1):
            loads.append(
                pltpu.make_async_copy(
                    parts[index].at[line.targets[order]], line.sums.at[order], load.at[order]
                )
            )
        loads.append(
            pltpu.make_async_copy(parts[index].at[place], owns[index][0], load.at[inner - 1])
        )
    for copy in loads:
        copy.start()
    small.begin()
    hidden.begin()

    def load(index):
        for copy in loads[index * inner : (index + 1) * inner]:
            copy.wait()
        totals[index][...] = to_full(owns[index][0][...])

    def push_free(index, orders):
        for order in orders:
            lines[index].push_free(order)

    def push_rest(index, orders):
        for order in orders:
            lines[index].push_rest(order)

    def gather_part(index):
        lines[index].add_own(totals[index])
        owns[index][0][...] = to_low(totals[index][...])
        planes[index][0]()
        owns[index][1].start()

    every = range(inner - 1)
    small.step(0)
    small.step(1)
    load(0)
    push_free(0, every[:1])
    for count in range(2, small.steps() - 2):
        small.step(count)
    hidden.step(0)
    push_free(0, every[1:])
    for index in range(1, counts):
        load(index)
        push_free(index, every)
    push_rest(0, every[:1])
    for count in range(small.steps() - 2, small.steps()):
        small.step(count)
    owns[counts][0][...] = to_low(small_sum[...])
    planes[counts][0]()
    owns[counts][1].start()
    hidden.step(1)
    push_rest(0, every[1:])
    planes[counts][1]()
    hidden.step(2)
    hidden.step(3)
    planes[counts][2]()
    x = to_full(x_ref[...])
    scale = norm_scale(x)
    unit = x * scale
    scaled = hidden_sum[...] * gain_ref[...]
    mean = jnp.mean(scaled * unit, axis=1, keepdims=True)
    tokens_out[...] = to_low(mix_ref[...] + scale * (scaled - unit * mean))
    if counts > 1:
        push_rest(1, every[:1])
    gather_part(0)
    if counts > 1:
        push_rest(1, every[1:])
    for index in range(1, counts):
        planes[index - 1][1]()
        if index > 1:
            planes[index - 2][2]()
        gather_part(index)
        if index + 1 < counts:
            push_rest(index + 1, every)
    if counts > 1:
        planes[counts - 2][2]()
    planes[counts - 1][1]()
    planes[counts - 1][2]()
    for plane in planes:
        plane[3]()
    hidden.finish()
    small.finish()
    for line in lines:
        line.finish()
    for _, copy in owns:
        copy.wait()


def settle(hidden, small, x, mix, gain, parts, inner):
    _, _, rows, width = hidden.shape
    seq_devices = lax.axis_size("seq")
    anywhere = pl.BlockSpec(memory_space=pl.ANY)
    inside = pl.BlockSpec(memory_space=pltpu.VMEM)
    low = jnp.bfloat16
    sems = lambda *shape: pltpu.SemaphoreType.DMA(shape)
    small_rows, small_wide = small.shape[2:]
    shapes = [part.shape[1:] for part in parts] + [(small_rows, small_wide)]
    scratch = [
        pltpu.VMEM((rows, width), jnp.float32),
        pltpu.VMEM((small_rows, small_wide), jnp.float32),
    ]
    scratch += Reducer.scratch(1, rows, width)
    scratch += Reducer.scratch(inner, small_rows, small_wide)
    for shape in shapes:
        scratch += [pltpu.VMEM(shape, low), sems(14), sems(14), sems()]
    for shape in shapes[:-1]:
        scratch += [pltpu.VMEM(shape, jnp.float32), sems(inner)]
        scratch += LineSum.scratch(inner, *shape)
    return run(
        functools.partial(settle_kernel, inner, len(parts)),
        (hidden, small, x, mix, gain) + tuple(parts),
        in_specs=[anywhere] * 2 + [inside] * 3 + [anywhere] * len(parts),
        out_specs=[inside] + [anywhere] * len(shapes),
        out_shape=[jax.ShapeDtypeStruct((rows, width), low)]
        + [jax.ShapeDtypeStruct((seq_devices,) + shape, low) for shape in shapes],
        scratch=scratch,
        flips=FLIPS,
        inner=inner,
        micros=90,
        name="settle",
    )


def params_of(limit=VMEM_BYTES):
    return pltpu.CompilerParams(vmem_limit_bytes=limit)


def project_kernel(x_ref, gain_ref, w_ref, dt_ref, hidden_ref, gate_ref, rows_ref):
    x = to_full(x_ref[...])
    hidden = to_low(x * norm_scale(x) * gain_ref[...])
    hidden_ref[...] = hidden
    gate_width = gate_ref.shape[1]
    used = gate_width + rows_ref.shape[1] - LANES
    projected = dot_full(hidden, w_ref[:, :used])
    gate_ref[...] = projected[:, :gate_width]
    rest = used - gate_width
    rows_ref[:, :rest] = to_low(projected[:, gate_width:])
    rows_ref[:, rest:] = to_low(dot_full(hidden, dt_ref[...]))


def project(x, gain, weights, dt_weights, gate_width, columns, freight=()):
    rows, width = x.shape
    columns = columns + LANES
    tile = 256
    block = lambda extent: pl.BlockSpec((tile, extent), lambda step: (step, 0))
    return run(
        project_kernel,
        (x, gain, weights, dt_weights,),
        grid=(rows // tile,),
        in_specs=[
            block(width), whole(gain.shape), whole(weights.shape), whole(dt_weights.shape)
        ],
        out_specs=[block(width), block(gate_width), block(columns - gate_width)],
        out_shape=[
            jax.ShapeDtypeStruct((rows, width), jnp.bfloat16),
            jax.ShapeDtypeStruct((rows, gate_width), jnp.float32),
            jax.ShapeDtypeStruct((rows, columns - gate_width), jnp.bfloat16),
        ],
        freight=freight,
        micros=11,
        name="project",
    )


def put_split(columns, rows):
    lane = iota_of((rows, LANES), 1)
    result = jnp.zeros((rows, LANES), jnp.float32)
    for place, column in enumerate(columns):
        high = to_full(to_low(column))
        result = jnp.where(lane == 2 * place, high, result)
        result = jnp.where(lane == 2 * place + 1, column - high, result)
    return to_low(result)


def mix_out_kernel(y_ref, gate_ref, gain_ref, packed_ref, part_ref, w_ref):
    width = w_ref.shape[1]

    @pl.when(pl.program_id(0) == 0)
    def _():
        unpack_rows(packed_ref, w_ref, True)

    gated = to_full(y_ref[...]) * jax.nn.silu(gate_ref[...])
    part_ref[0, :, :width] = to_low(dot_full(to_low(gated * gain_ref[...]), w_ref[...]))
    squares = jnp.sum(gated * gated, axis=1, keepdims=True)
    part_ref[0, :, width:] = put_split([squares], y_ref.shape[0])


def mix_out(y, gate, gain, weights, blocks, freight=()):
    rows, channels = y.shape
    width = weights.shape[2]
    tile = rows // blocks
    block = pl.BlockSpec((tile, channels), lambda step: (step, 0))
    return run(
        mix_out_kernel,
        (y, gate, gain, weights),
        grid=(blocks,),
        in_specs=[block, block, whole(gain.shape), whole(weights.shape)],
        out_specs=[pl.BlockSpec((1, tile, width + LANES), lambda step: (step, 0, 0))],
        out_shape=[jax.ShapeDtypeStruct((blocks, tile, width + LANES), jnp.bfloat16)],
        scratch=[pltpu.VMEM((channels, width), jnp.bfloat16)],
        freight=freight,
        micros=9,
        name="mix_out",
    )


def mix_back_kernel(
    mix_ref,
    y_ref,
    gate_ref,
    gain_ref,
    packed_ref,
    dy_ref,
    dgate_ref,
    w_grad_ref,
    gain_grad_ref,
    total,
    w_ref,
):
    step = pl.program_id(0)
    width = w_ref.shape[1]

    @pl.when(step == 0)
    def _():
        unpack_rows(packed_ref, w_ref, True)
        total[...] = jnp.zeros_like(total)
        gain_grad_ref[...] = jnp.zeros_like(gain_grad_ref)

    mix = mix_ref[0, :, :width]
    extra = to_full(mix_ref[0, :, width:])
    share = extra[:, 0:1] + extra[:, 1:2]
    scale = extra[:, 2:3] + extra[:, 3:4]
    normed_grad = dot_lanes(mix, w_ref[...])
    y = to_full(y_ref[...])
    gate = gate_ref[...]
    sig = jax.nn.sigmoid(gate)
    act = gate * sig
    unit = y * act * scale
    gain = gain_ref[...]
    gain_grad_ref[0:1, :] += jnp.sum(normed_grad * unit, axis=0, keepdims=True)
    gated_grad = scale * (normed_grad * gain - unit * share)
    dy_ref[...] = to_low(gated_grad * act)
    dgate_ref[...] = to_low(gated_grad * y * sig * (1.0 + gate * (1.0 - sig)))
    total[...] += dot_rows(to_low(unit * gain), mix)

    @pl.when(step == pl.num_programs(0) - 1)
    def _():
        w_grad_ref[...] = to_low(total[...])


def mix_back(mix, y, gate, gain, weights, freight=()):
    blocks, tile, wide = mix.shape
    rows, channels = y.shape
    shape = (channels, weights.shape[2])
    block = pl.BlockSpec((tile, channels), lambda step: (step, 0))
    return run(
        mix_back_kernel,
        (mix, y, gate, gain, weights,),
        grid=(blocks,),
        in_specs=[
            pl.BlockSpec((1, tile, wide), lambda step: (step, 0, 0)),
            block,
            block,
            whole(gain.shape),
            whole(weights.shape),
        ],
        out_specs=[block, block, whole(shape), whole((8, channels))],
        out_shape=[
            jax.ShapeDtypeStruct((rows, channels), jnp.bfloat16),
            jax.ShapeDtypeStruct((rows, channels), jnp.bfloat16),
            jax.ShapeDtypeStruct(shape, jnp.bfloat16),
            jax.ShapeDtypeStruct((8, channels), jnp.float32),
        ],
        scratch=[pltpu.VMEM(shape, jnp.float32), pltpu.VMEM(shape, jnp.bfloat16)],
        freight=freight,
        micros=12,
        name="mix_back",
    )


def project_back_kernel(
    dgate_ref, drows_ref, hidden_ref, w_ref, dt_ref, part_ref, main_grad_ref, rest_grad_ref, total
):
    step = pl.program_id(0)

    @pl.when(step == 0)
    def _():
        total[...] = jnp.zeros_like(total)

    grads = jnp.concatenate([dgate_ref[...], drows_ref[...]], axis=1)
    columns = grads.shape[1] - LANES
    part_ref[0] = to_low(
        dot_lanes(grads[:, :columns], w_ref[:, :columns])
        + dot_lanes(grads[:, columns:], dt_ref[...])
    )
    total[...] += dot_rows(hidden_ref[...], grads)

    @pl.when(step == pl.num_programs(0) - 1)
    def _():
        main = main_grad_ref.shape[1]
        main_grad_ref[...] = to_low(total[:, :main])
        rest_grad_ref[...] = to_low(total[:, main:])
        by_gain = jnp.sum(total[:, :columns] * to_full(w_ref[:, :columns]), axis=1, keepdims=True)
        by_gain += jnp.sum(total[:, columns:] * to_full(dt_ref[...]), axis=1, keepdims=True)
        rest = rest_grad_ref.shape[1]
        lane = iota_of((rest_grad_ref.shape[0], LANES), 1)
        rest_grad_ref[:, rest - LANES :] = to_low(
            jnp.where(lane == LANES - 1, by_gain, total[:, columns:])
        )


def project_back(dgate, drows, hidden, weights, dt_weights, blocks, freight=()):
    rows, width = hidden.shape
    tile = rows // blocks
    main = 2 * dgate.shape[1]
    rest = dgate.shape[1] + drows.shape[1] - main
    block = lambda extent: pl.BlockSpec((tile, extent), lambda step: (step, 0))
    return run(
        project_back_kernel,
        (dgate, drows, hidden, weights, dt_weights,),
        grid=(blocks,),
        in_specs=[
            block(dgate.shape[1]),
            block(drows.shape[1]),
            block(width),
            whole(weights.shape),
            whole(dt_weights.shape),
        ],
        out_specs=[
            pl.BlockSpec((1, tile, width), lambda step: (step, 0, 0)),
            whole((width, main)),
            whole((width, rest)),
        ],
        out_shape=[
            jax.ShapeDtypeStruct((blocks, tile, width), jnp.bfloat16),
            jax.ShapeDtypeStruct((width, main), jnp.bfloat16),
            jax.ShapeDtypeStruct((width, rest), jnp.bfloat16),
        ],
        scratch=[pltpu.VMEM((width, main + rest), jnp.float32)],
        freight=freight,
        micros=25,
        name="project_back",
    )


def unpack_rows(packed_ref, held_ref, first):
    blocks, both, _ = packed_ref.shape
    fine = held_ref.shape[0] // blocks
    start = 0 if first else both - fine
    for block in range(blocks):
        held_ref[block * fine : (block + 1) * fine] = packed_ref[block, start : start + fine]


def shared_kernel(
    rows_ref,
    grad_ref,
    up_ref,
    down_ref,
    res_ref,
    back_ref,
    up_grad_ref,
    down_grad_ref,
    up_sum,
    down_sum,
    down_held,
):
    step = pl.program_id(0)

    @pl.when(step == 0)
    def _():
        up_sum[...] = jnp.zeros_like(up_sum)
        down_sum[...] = jnp.zeros_like(down_sum)
        unpack_rows(down_ref, down_held, False)

    hidden, width = down_held.shape
    rows = rows_ref[0, :, :width]
    grad = grad_ref[0]
    joined = dot_full(rows, up_ref[...])
    gate, up = joined[:, :hidden], joined[:, hidden:]
    sig = jax.nn.sigmoid(gate)
    act = gate * sig
    acted = to_low(act * up)
    res_ref[0] = to_low(dot_full(acted, down_held[...]))
    down_sum[...] += dot_rows(acted, grad)
    act_grad = dot_lanes(grad, down_held[...])
    joined_grad = to_low(
        jnp.concatenate(
            [act_grad * up * sig * (1.0 + gate * (1.0 - sig)), act_grad * act], axis=1
        )
    )
    up_sum[...] += dot_rows(rows, joined_grad)
    back_ref[0] = to_low(dot_lanes(joined_grad, up_ref[...]))

    @pl.when(step == pl.num_programs(0) - 1)
    def _():
        up_grad_ref[...] = to_low(up_sum[...])
        down_grad_ref[...] = to_low(down_sum[...])


def shared_expert(rows, grad, up, down, hidden, blocks, inner, freight=()):
    _, tile, wide = rows.shape
    width = down.shape[2]
    down_shape = (hidden, width)
    up_shape = (width, 2 * hidden)
    block = pl.BlockSpec((1, tile, width), lambda step: (step, 0, 0))
    low = jnp.bfloat16
    own = lambda extent: pl.BlockSpec(
        (1, tile, extent), lambda step: (own_shard_group(inner)[0] * blocks + step, 0, 0)
    )
    return run(
        shared_kernel,
        (rows, grad, up, down),
        grid=(blocks,),
        in_specs=[
            own(wide),
            own(width),
            pl.BlockSpec((width, up_shape[1]), lambda step: (0, up.shape[1] // up_shape[1] - 1)),
            whole(down.shape),
        ],
        out_specs=[block, block, whole(up_shape), whole(down_shape)],
        out_shape=[
            jax.ShapeDtypeStruct((blocks, tile, width), low),
            jax.ShapeDtypeStruct((blocks, tile, width), low),
            jax.ShapeDtypeStruct(up_shape, low),
            jax.ShapeDtypeStruct(down_shape, low),
        ],
        scratch=[
            pltpu.VMEM(up_shape, jnp.float32),
            pltpu.VMEM(down_shape, jnp.float32),
            pltpu.VMEM(down_shape, low),
        ],
        freight=freight,
        micros=18,
        name="shared_expert",
    )


def dispatch_kernel(
    rows_ref, grad_ref, x_ref, g_ref, picks_ref, *, top_count, slots, own_first
):
    per_device = x_ref.shape[0]
    together, tok_rows, _ = rows_ref.shape
    width = g_ref.shape[2]
    wide = width + LANES
    taken = per_device * slots
    lane = iota_of((tok_rows, LANES), 1)
    named = (lane >= 2 * top_count) & (lane < 3 * top_count)
    before = iota_of((tok_rows, tok_rows), 0) > iota_of((tok_rows, tok_rows), 1)
    before = to_low(jnp.where(before, 1.0, 0.0))
    first = own_first()
    for index in range(together):
        extra = to_full(rows_ref[index, :, width:wide])
        member = jnp.zeros((tok_rows, LANES), jnp.float32)
        for expert in range(per_device):
            own = (first + expert).astype(jnp.float32)
            hit = jnp.sum(jnp.where(named & (extra == own), 1.0, 0.0), axis=1, keepdims=True)
            member = jnp.where(lane // slots == expert, hit, member)
        ranks = dot_full(before, to_low(member))
        picks = jnp.where(
            (ranks == to_full(lane % slots)) & (member > 0.0), 1.0, 0.0
        ).astype(jnp.bfloat16)
        picks_ref[index] = picks
        rows = to_low(dot_rows(picks[:, :taken], rows_ref[index]))
        grads = to_low(dot_rows(picks[:, :taken], grad_ref[index]))
        start = index * slots
        for expert in range(per_device):
            span = slice(expert * slots, (expert + 1) * slots)
            x_ref[expert, start : start + slots] = rows[span]
            g_ref[expert, start : start + slots] = grads[span]


def dispatch(rows, grad, per_device, top_count, slots, own_first, freight=()):
    blocks, tok_rows, wide = rows.shape
    width = grad.shape[2]
    together = 4
    block = lambda extent: pl.BlockSpec((together, tok_rows, extent), lambda step: (step, 0, 0))
    taken = lambda extent: pl.BlockSpec(
        (per_device, together * slots, extent), lambda step: (0, step, 0)
    )
    return run(
        functools.partial(
            dispatch_kernel, top_count=top_count, slots=slots, own_first=own_first
        ),
        (rows, grad),
        grid=(blocks // together,),
        in_specs=[block(wide), block(width)],
        out_specs=[taken(width + LANES), taken(width), block(LANES)],
        out_shape=[
            jax.ShapeDtypeStruct((per_device, blocks * slots, width + LANES), jnp.bfloat16),
            jax.ShapeDtypeStruct((per_device, blocks * slots, width), jnp.bfloat16),
            jax.ShapeDtypeStruct((blocks, tok_rows, LANES), jnp.bfloat16),
        ],
        freight=freight,
        micros=30,
        name="dispatch",
    )


def experts_kernel(
    depart, arrive, targets, *refs, count, per_device, top_count, own_first, inner, incoming, outgoing
):
    x_ref, g_ref = refs[:2]
    total = 2 * count * per_device
    given = total - len(incoming)
    pieces, refs = list(refs[2 : 2 + given]), refs[2 + given :]
    for order, key in enumerate(incoming):
        pieces.insert(key, targets[order])
    res_ref, dx_ref = refs[:2]
    outs = refs[2 : 2 + total]
    up_held, down_held, up_sum, down_sum, up_low, down_low, sems = refs[2 + total :]
    own_place, _ = own_shard_group(inner)
    is_incoming = lambda item: item.output is None
    is_outgoing = lambda item: item.output is not None
    expert, step = pl.program_id(0), pl.program_id(1)
    steps = pl.num_programs(1)
    slot = lax.rem(expert, 2)
    width, double = up_held.shape[1:]
    hidden = double // 2
    tile = x_ref.shape[1]

    def parts(refs_of, which, up, down):
        result = []
        for shift in range(count):
            from_place = lax.rem(own_place + count - shift, count)
            for kind, held in enumerate((up, down)):
                extent = held.shape[0] // count
                start = pl.multiple_of(from_place * extent, extent)
                piece = refs_of[(shift * per_device + which) * 2 + kind]
                if len(piece.shape) == 3:
                    piece = piece.at[own_place * per_device + which]
                result.append((piece, held.at[pl.ds(start, extent)], (shift, kind)))
        return result

    def fetch(which):
        half = which % 2
        return [
            pltpu.make_async_copy(piece, held, sems.at[half, at[0], at[1]])
            for piece, held, at in parts(pieces, which, up_held.at[half], down_held.at[half])
        ]

    for which in range(per_device):

        @pl.when((step == 0) & (expert == which))
        def _():
            if which == 0:
                for copy in fetch(0):
                    copy.start()
                depart(is_incoming)
            if which == 1:
                arrive(is_incoming)
                depart(is_outgoing)
                for copy in fetch(1):
                    copy.start()
            for copy in fetch(which):
                copy.wait()
            if 1 <= which < per_device - 1:
                for copy in fetch(which + 1):
                    copy.start()

    @pl.when(step == 0)
    def _():
        up_sum[...] = jnp.zeros_like(up_sum)
        down_sum[...] = jnp.zeros_like(down_sum)

    up, down = up_held.at[slot], down_held.at[slot]
    rows = x_ref[0, :, :width]
    extra = to_full(x_ref[0, :, width:])
    lane = iota_of((tile, LANES), 1)
    own = own_first() + expert
    hits = jnp.where((lane < 3 * top_count) & (extra == own.astype(jnp.float32)), 1.0, 0.0)
    gate_slot = jnp.zeros((tile, 1), jnp.float32)
    for route in range(top_count):
        place = 2 * top_count + route
        value = extra[:, 2 * route : 2 * route + 1] + extra[:, 2 * route + 1 : 2 * route + 2]
        gate_slot = gate_slot + hits[:, place : place + 1] * value
    joined = dot_full(rows, up[...])
    gate, lift = joined[:, :hidden], joined[:, hidden:]
    sig = jax.nn.sigmoid(gate)
    act = gate * sig
    acted = to_low(act * lift)
    res = to_low(dot_full(acted, down[...]))
    grads = g_ref[0]
    wide_grads = to_full(grads)
    wide_res = to_full(res)
    gate_grad = jnp.sum(wide_res * wide_grads, axis=1, keepdims=True)
    res_ref[0] = to_low(wide_res * gate_slot)
    weighted = to_low(wide_grads * gate_slot)
    act_grad = dot_lanes(weighted, down[...])
    down_sum[...] += dot_rows(acted, weighted)
    joined_grad = to_low(
        jnp.concatenate(
            [act_grad * lift * sig * (1.0 + gate * (1.0 - sig)), act_grad * act], axis=1
        )
    )
    dx_ref[0, :, :width] = to_low(dot_lanes(joined_grad, up[...]))
    high = to_full(to_low(gate_grad))
    half = LANES // 2
    dx_ref[0, :, width:] = to_low(
        jnp.where(lane == own, high, 0.0) + jnp.where(lane == own + half, gate_grad - high, 0.0)
    )
    up_sum[...] += dot_rows(rows, joined_grad)

    for which in range(per_device):

        @pl.when((step == steps - 1) & (expert == which))
        def _():
            up_low[...] = to_low(up_sum[...])
            down_low[...] = to_low(down_sum[...])
            copies = [
                pltpu.make_async_copy(held, piece, sems.at[2, at[0], at[1]])
                for piece, held, at in parts(outs, which, up_low, down_low)
            ]
            for copy in copies:
                copy.start()
            for copy in copies:
                copy.wait()

    if outgoing:

        @pl.when((step == steps - 1) & (expert == per_device - 1))
        def _():
            arrive(is_outgoing)


def experts(x, g, pieces, hidden, top_count, own_first, inner, incoming=(), outgoing=()):
    per_device, rows, wide = x.shape
    width = g.shape[2]
    count = (len(pieces) + len(incoming)) // per_device // 2
    incoming = sorted(incoming, key=lambda entry: entry[0])
    full_list = list(pieces)
    for key, item in incoming:
        full_list.insert(key, jax.ShapeDtypeStruct(item.shape, item.array.dtype))
    low = jnp.bfloat16
    shapes = [jax.ShapeDtypeStruct(piece.shape[-2:], low) for piece in full_list]
    freight = [item for _, item in incoming] + [
        Parcel(shapes[key], shift, inner, output=2 + key) for key, shift in outgoing
    ]
    double = 2 * hidden
    tile = min(rows, 256)
    block = lambda extent: pl.BlockSpec((1, tile, extent), lambda e, step: (e, step, 0))
    anywhere = pl.BlockSpec(memory_space=pl.ANY)
    low = jnp.bfloat16
    outs = run(
        functools.partial(
            experts_kernel,
            count=count,
            per_device=per_device,
            top_count=top_count,
            own_first=own_first,
            inner=inner,
            incoming=[key for key, _ in incoming],
            outgoing=outgoing,
        ),
        (x, g) + tuple(pieces),
        grid=(per_device, rows // tile),
        in_specs=[block(wide), block(width)] + [anywhere] * len(pieces),
        out_specs=[block(width), block(wide)] + [anywhere] * len(shapes),
        out_shape=[
            jax.ShapeDtypeStruct((per_device, rows, width), low),
            jax.ShapeDtypeStruct((per_device, rows, wide), low),
        ]
        + shapes,
        scratch=[
            pltpu.VMEM((2, width, double), low),
            pltpu.VMEM((2, hidden, width), low),
            pltpu.VMEM((width, double), jnp.float32),
            pltpu.VMEM((hidden, width), jnp.float32),
            pltpu.VMEM((width, double), low),
            pltpu.VMEM((hidden, width), low),
            pltpu.SemaphoreType.DMA((3, count, 2)),
        ],
        freight=freight,
        inner=inner if freight else 1,
        late=True,
        micros=45,
        name="experts",
    )
    sent = outs.pop()[len(incoming) :] if freight else []
    return outs[0], outs[1], outs[2:], sent


def combine_kernel(
    picks_ref, res_ref, dx_ref, sres_ref, sback_ref, out_ref, back_ref, *, slots, inner
):
    step = pl.program_id(0)
    together, _, width = out_ref.shape
    per_device = res_ref.shape[0]
    blocks = sres_ref.shape[0]
    place, _ = own_shard_group(inner)
    for index in range(together):
        picks = picks_ref[index, :, : per_device * slots]
        start = index * slots
        stacked = lambda ref: jnp.concatenate(
            [ref[expert, start : start + slots] for expert in range(per_device)], axis=0
        )
        out_ref[index] = to_low(dot_full(picks, stacked(res_ref)))
        back_ref[index] = to_low(dot_full(picks, stacked(dx_ref)))

    @pl.when(lax.div(step * together, blocks) == place)
    def _():
        first = lax.rem(step * together, blocks)
        for index in range(together):
            out_ref[index] = to_low(to_full(out_ref[index]) + to_full(sres_ref[first + index]))
            back_ref[index, :, :width] = to_low(
                to_full(back_ref[index, :, :width]) + to_full(sback_ref[first + index])
            )


def combine(picks, res, dx, shared_res, shared_back, inner, freight=()):
    blocks, tok_rows, _ = picks.shape
    per_device, rows, width = res.shape
    slots = rows // blocks
    together = 4
    block = lambda extent: pl.BlockSpec((together, tok_rows, extent), lambda step: (step, 0, 0))
    taken = lambda extent: pl.BlockSpec(
        (per_device, together * slots, extent), lambda step: (0, step, 0)
    )
    return run(
        functools.partial(combine_kernel, slots=slots, inner=inner),
        (picks, res, dx, shared_res, shared_back),
        grid=(blocks // together,),
        in_specs=[
            block(LANES),
            taken(width),
            taken(width + LANES),
            whole(shared_res.shape),
            whole(shared_back.shape),
        ],
        out_specs=[block(width), block(width + LANES)],
        out_shape=[
            jax.ShapeDtypeStruct((blocks, tok_rows, width), jnp.bfloat16),
            jax.ShapeDtypeStruct((blocks, tok_rows, width + LANES), jnp.bfloat16),
        ],
        freight=freight,
        micros=30,
        name="combine",
    )


def assemble_kernel(
    main_ref, shared_in_ref, small_ref, rows_ref, w_in_ref, shared_ref, out_ref, down_ref
):
    seq_devices, rows, double = main_ref.shape
    channels = double // 2
    for device in range(seq_devices):
        for target, source in ((w_in_ref, main_ref), (shared_ref, shared_in_ref)):
            extent = source.shape[2] // 2
            for side in range(2):
                start = (side * seq_devices + device) * extent
                target[:, start : start + extent] = to_full(
                    source[device, :, side * extent : (side + 1) * extent]
                )
    start = 2 * seq_devices * channels
    w_in_ref[:, start:] = to_full(small_ref[0, :rows, : w_in_ref.shape[1] - start])
    halves, _, out_rows, _ = out_ref.shape
    down_rows = down_ref.shape[2]
    for half in range(halves):
        at = half * (out_rows + down_rows)
        out_ref[half, 0] = to_full(rows_ref[0, at : at + out_rows])
        down_ref[half, 0] = to_full(rows_ref[0, at + out_rows : at + out_rows + down_rows])


def assemble(main, shared, small, rows, columns, shared_columns, out_rows, down_rows, halves):
    seq_devices, depth_rows, _ = main.shape
    tile = depth_rows // seq_devices
    width = rows.shape[2]
    out_fine = out_rows // halves // seq_devices
    down_fine = down_rows // halves // seq_devices
    flat = lambda extent: pl.BlockSpec((tile, extent), lambda step: (step, 0))
    fine = lambda extent: pl.BlockSpec(
        (halves, 1, extent, width), lambda step: (0, step, 0, 0)
    )
    full = jnp.float32
    results = pl.pallas_call(
        assemble_kernel,
        grid=(seq_devices,),
        in_specs=[
            pl.BlockSpec((seq_devices, tile, main.shape[2]), lambda step: (0, step, 0)),
            pl.BlockSpec((seq_devices, tile, shared.shape[2]), lambda step: (0, step, 0)),
            pl.BlockSpec((1,) + small.shape[1:], lambda step: (step, 0, 0)),
            pl.BlockSpec((1,) + rows.shape[1:], lambda step: (step, 0, 0)),
        ],
        out_specs=[flat(columns), flat(shared_columns), fine(out_fine), fine(down_fine)],
        out_shape=[
            jax.ShapeDtypeStruct((depth_rows, columns), full),
            jax.ShapeDtypeStruct((depth_rows, shared_columns), full),
            jax.ShapeDtypeStruct((halves, seq_devices, out_fine, width), full),
            jax.ShapeDtypeStruct((halves, seq_devices, down_fine, width), full),
        ],
        compiler_params=params_of(),
        cost_estimate=cost_of(10),
        name="assemble",
    )(main, shared, small, rows)
    return results[0], results[1], results[2].reshape(-1, width), results[3].reshape(-1, width)


def collect_kernel(place_ref, *refs):
    del place_ref
    step = pl.program_id(0)
    up_ref, down_ref = refs[-2:]
    for order in range(len(refs) // 2 - 1):

        @pl.when(step == order)
        def _():
            up_ref[0] = to_full(refs[2 * order][...])
            down_ref[0] = to_full(refs[2 * order + 1][...])


def collect(place, pieces, per_device):
    count = len(pieces) // 2
    up, down = pieces[0].shape, pieces[1].shape

    def here(step, place):
        shift, expert = lax.div(step, per_device), lax.rem(step, per_device)
        return (
            lax.rem(place[0] + shift, count // per_device) * per_device + expert, 0, 0
        )

    still = lambda shape: pl.BlockSpec(shape, lambda step, place: (0, 0))
    return pl.pallas_call(
        collect_kernel,
        grid_spec=pltpu.PrefetchScalarGridSpec(
            num_scalar_prefetch=1,
            grid=(count,),
            in_specs=[still(up), still(down)] * count,
            out_specs=[pl.BlockSpec((1,) + up, here), pl.BlockSpec((1,) + down, here)],
        ),
        out_shape=[
            jax.ShapeDtypeStruct((count,) + up, jnp.float32),
            jax.ShapeDtypeStruct((count,) + down, jnp.float32),
        ],
        compiler_params=params_of(),
        cost_estimate=cost_of(12),
        name="collect",
    )(place, *pieces)


def route_hits(routes, route, lane):
    return lane == routes[:, route : route + 1]


def token_forward_kernel(
    mixed_ref, x_ref, gain_ref, router_ref, routes_ref, after_ref, wide_ref, gates_ref, *, inner_width, top_count
):
    width = x_ref.shape[1]
    rows = x_ref.shape[0]
    squares = mixed_ref[:, width : width + 1] + mixed_ref[:, width + 1 : width + 2]
    scale = lax.rsqrt(squares / inner_width + EPSILON)
    after = to_full(x_ref[...]) + mixed_ref[:, :width] * scale
    after_ref[...] = after
    moe_in = to_low(after * norm_scale(after) * gain_ref[...])
    wide_ref[:, :width] = moe_in
    logits = dot_full(moe_in, router_ref[...])
    lane = iota_of((rows, LANES), 1)
    routes = routes_ref[...]
    picked = [
        jnp.sum(jnp.where(route_hits(routes, k, lane), logits, 0.0), axis=1, keepdims=True)
        for k in range(top_count)
    ]
    largest = functools.reduce(jnp.maximum, picked)
    powers = [jnp.exp(value - largest) for value in picked]
    total = sum(powers)
    gates = jnp.zeros((rows, LANES), jnp.float32)
    extra = jnp.zeros((rows, LANES), jnp.float32)
    for k in range(top_count):
        value = powers[k] / total
        high = to_full(to_low(value))
        gates = jnp.where(lane == k, value, gates)
        extra = jnp.where(lane == 2 * k, high, extra)
        extra = jnp.where(lane == 2 * k + 1, value - high, extra)
        extra = jnp.where(lane == 2 * top_count + k, to_full(routes[:, k : k + 1]), extra)
    gates_ref[...] = jnp.where(lane == top_count, scale, gates)
    wide_ref[:, width:] = to_low(extra)


def token_forward(mixed, x, gain, router, routes, inner_width, top_count):
    rows, width = x.shape
    arrays = (mixed, x, gain, router, routes)
    return pl.pallas_call(
        functools.partial(
            token_forward_kernel, inner_width=inner_width, top_count=top_count
        ),
        in_specs=[whole(array.shape) for array in arrays],
        out_specs=[whole((rows, width)), whole((rows, width + LANES)), whole((rows, LANES))],
        out_shape=[
            jax.ShapeDtypeStruct((rows, width), jnp.float32),
            jax.ShapeDtypeStruct((rows, width + LANES), jnp.bfloat16),
            jax.ShapeDtypeStruct((rows, LANES), jnp.float32),
        ],
        compiler_params=params_of(),
        cost_estimate=cost_of(5),
        name="token_forward",
    )(*arrays)


def token_back_kernel(
    back_ref,
    mixed_ref,
    after_ref,
    wide_ref,
    gates_ref,
    grad_ref,
    gain_ref,
    router_ref,
    routes_ref,
    mix_ref,
    mix_wide_ref,
    router_grad_ref,
    gain_grad_ref,
    *,
    inner_width,
    top_count,
):
    rows, width = grad_ref.shape
    lane = iota_of((rows, LANES), 1)
    half = LANES // 2
    routes = routes_ref[...]
    gates = gates_ref[...]
    all_grads = back_ref[:, width:]
    values = [gates[:, k : k + 1] for k in range(top_count)]
    grads = [
        jnp.sum(
            jnp.where(
                route_hits(routes, k, lane) | route_hits(routes, k, lane - half), all_grads, 0.0
            ),
            axis=1,
            keepdims=True,
        )
        for k in range(top_count)
    ]
    common = sum(value * grad for value, grad in zip(values, grads))
    logit_grad = jnp.zeros((rows, LANES), jnp.float32)
    for k in range(top_count):
        logit_grad = jnp.where(
            route_hits(routes, k, lane), values[k] * (grads[k] - common), logit_grad
        )
    logit_grad = to_low(logit_grad)
    router_grad_ref[...] = to_low(dot_rows(wide_ref[:, :width], logit_grad))
    moe_grad = back_ref[:, :width] + dot_lanes(logit_grad, router_ref[...])
    after = after_ref[...]
    scale = norm_scale(after)
    unit = after * scale
    gain_grad_ref[...] = jnp.broadcast_to(
        jnp.sum(moe_grad * unit, axis=0, keepdims=True), (8, width)
    )
    scaled = moe_grad * gain_ref[...]
    mean = jnp.mean(scaled * unit, axis=1, keepdims=True)
    mix = to_full(grad_ref[...]) + scale * (scaled - unit * mean)
    mix_ref[...] = mix
    mix_low = to_low(mix)
    mix_wide_ref[:, :width] = mix_low
    mix_scale = gates[:, top_count : top_count + 1]
    share = jnp.sum(to_full(mix_low) * mixed_ref[:, :width], axis=1, keepdims=True)
    mix_wide_ref[:, width:] = put_split([share * mix_scale / inner_width, mix_scale], rows)


def token_back(back, mixed, after, wide, gates, grad, gain, router, routes, inner_width, top_count):
    rows, width = grad.shape
    arrays = (back, mixed, after, wide, gates, grad, gain, router, routes)
    return pl.pallas_call(
        functools.partial(token_back_kernel, inner_width=inner_width, top_count=top_count),
        in_specs=[whole(array.shape) for array in arrays],
        out_specs=[
            whole((rows, width)),
            whole((rows, width + LANES)),
            whole((width, LANES)),
            whole((8, width)),
        ],
        out_shape=[
            jax.ShapeDtypeStruct((rows, width), jnp.float32),
            jax.ShapeDtypeStruct((rows, width + LANES), jnp.bfloat16),
            jax.ShapeDtypeStruct((width, LANES), jnp.bfloat16),
            jax.ShapeDtypeStruct((8, width), jnp.float32),
        ],
        compiler_params=params_of(),
        cost_estimate=cost_of(6),
        name="token_back",
    )(*arrays)


def split_small(joined, arrays):
    results, start = [], 0
    for piece in arrays:
        part = joined[:, start : start + piece.size]
        results.append(part.reshape((-1,) + piece.shape[1:]))
        start += piece.size
    return results


def flat_of(arrays):
    return jnp.concatenate([piece.reshape(-1) for piece in arrays])


def rows_to_send(weights, part):
    seq_devices = lax.axis_size("seq")
    halves = max(1, seq_devices // lax.axis_size("shard"))
    mine = []
    for weight in weights:
        view = weight.reshape(halves, seq_devices, -1, weight.shape[1])
        mine.append(lax.dynamic_index_in_dim(view, part, 1, keepdims=False))
    return jnp.concatenate(mine, axis=1).reshape(-1, weights[0].shape[1])


def rows_by_owner(joined):
    seq_devices = lax.axis_size("seq")
    return joined.reshape(seq_devices, -1, joined.shape[2])


def rows_of_owner(taken, weights):
    seq_devices = lax.axis_size("seq")
    halves = max(1, seq_devices // lax.axis_size("shard"))
    fine_rows = [weight.shape[0] // halves // seq_devices for weight in weights]
    width = taken.shape[2]
    taken = taken.reshape(seq_devices, -1, sum(fine_rows), width).transpose(1, 0, 2, 3)
    results, start = [], 0
    for fine in fine_rows:
        results.append(taken[:, :, start : start + fine].reshape(-1, width))
        start += fine
    return results


def rows_from_owner(grads):
    seq_devices = lax.axis_size("seq")
    shard_devices = lax.axis_size("shard")
    width = grads[0].shape[1]
    turns = shard_devices * max(1, seq_devices // shard_devices) // seq_devices
    pieces = [
        grad.reshape(turns, seq_devices, -1, width).transpose(1, 0, 2, 3) for grad in grads
    ]
    return jnp.concatenate(pieces, axis=2).reshape(seq_devices, -1, width)


def rows_of_shard(joined, weights):
    seq_devices = lax.axis_size("seq")
    halves = max(1, seq_devices // lax.axis_size("shard"))
    fine_rows = [weight.shape[0] // halves // seq_devices for weight in weights]
    width = joined.shape[2]
    spread = joined.reshape(seq_devices, halves, -1, width).transpose(1, 0, 2, 3)
    results, start = [], 0
    for fine in fine_rows:
        results.append(to_full(spread[:, :, start : start + fine]).reshape(-1, width))
        start += fine
    return results


def inner_groups(inner):
    count = lax.axis_size("shard")
    return [list(range(start, start + inner)) for start in range(0, count, inner)]


def outer_groups(inner):
    count = lax.axis_size("shard")
    return [list(range(start, count, inner)) for start in range(inner)]


def carry(array, freight):
    result, arrays = run(
        lambda source, target: None,
        (array,),
        in_specs=[pl.BlockSpec(memory_space=pl.ANY)],
        out_specs=[pl.BlockSpec(memory_space=pl.ANY)],
        out_shape=[jax.ShapeDtypeStruct((8, LANES), jnp.float32)],
        freight=freight,
        micros=30,
        name="carry",
    )
    del result
    return array, arrays


def stacked_pieces(received, place, inner):
    own = jnp.stack(received)[lax.rem(place + inner - jnp.arange(inner), inner)]
    joined = lax.all_gather(own, "shard", axis_index_groups=outer_groups(inner))
    return joined.reshape(-1, joined.shape[-1])


def split_piece(grad, shift, place, inner):
    outer = lax.axis_size("shard") // inner
    rows = grad.reshape(outer, inner, -1, grad.shape[1])
    here = lax.rem(place + inner - shift, inner)
    return lax.psum_scatter(
        lax.dynamic_index_in_dim(rows, here, 1, keepdims=False),
        "shard",
        axis_index_groups=outer_groups(inner),
    )


def local(
    tokens,
    out_grad,
    deal_order,
    lengths,
    routes,
    norm_in,
    w_in,
    w_dt,
    conv_w,
    conv_b,
    dt_bias,
    a_log,
    d_skip,
    norm_gate,
    w_out,
    norm_moe,
    w_router,
    w_shared,
    w_shared_down,
    w_experts,
    w_experts_down,
):
    seq_devices = lax.axis_size("seq")
    shard_devices = lax.axis_size("shard")
    part = lax.axis_index("seq")
    shard = lax.axis_index("shard")
    inner = min(shard_devices, INNER)
    outer = shard_devices // inner
    place = lax.rem(shard, inner)
    _, tok_rows, width = tokens.shape
    group_rows = tok_rows * seq_devices
    inner_width = w_out.shape[0] * shard_devices
    channels = inner_width // seq_devices
    head_total = w_dt.shape[1]
    heads = head_total // seq_devices
    shared_width = w_shared_down.shape[0] * shard_devices
    shared_part = shared_width // seq_devices
    depth_rows = w_in.shape[0]
    expert_total = w_router.shape[1]
    local_experts, _, double = w_experts.shape
    hidden = double // 2
    hidden_rows = w_experts_down.shape[1]
    top_count = routes.shape[2]
    per_device = local_experts // inner
    blocks = inner * seq_devices
    COLLECTIVES.clear()

    def own_columns(array, start, extent):
        return lax.dynamic_slice_in_dim(array, start + part * extent, extent, 1)

    def own_rows(array, extent):
        return lax.dynamic_slice_in_dim(array, part * extent, extent, 0)

    small_weights = [norm_in, conv_w, conv_b, dt_bias, a_log, d_skip, norm_gate, norm_moe]
    by_depth = jnp.concatenate(
        [
            w_router,
            own_columns(w_dt, 0, heads),
            jnp.zeros((depth_rows, LANES - expert_total - heads), jnp.bfloat16),
        ],
        axis=1,
    )
    in_width = 2 * channels + w_in.shape[1] - 2 * inner_width
    flat = flat_of(small_weights)
    if outer == 1:
        flat_rows = -(-flat.size // (LANES * 32)) * 32
        flat = jnp.pad(flat, (0, flat_rows * LANES - flat.size)).reshape(flat_rows, LANES)
        x_group, grad_all, proj_in, joined, depth_joined, rows_joined = begin(
            tokens[0],
            out_grad[0],
            flat,
            by_depth,
            w_in,
            w_shared,
            w_out,
            w_shared_down,
            in_width,
            shared_part,
            inner,
        )
        joined = joined.reshape(inner, -1)
        x_group = x_group.reshape(group_rows, width)
    else:
        x_group = gather_rows(tokens[0], 1)[0].reshape(group_rows, width)
        grad_all = gather_rows(out_grad[0], inner)[0]
        in_columns = jnp.concatenate(
            [
                own_columns(w_in, 0, channels),
                own_columns(w_in, inner_width, channels),
                w_in[:, 2 * inner_width :],
                own_columns(w_shared, 0, shared_part),
                own_columns(w_shared, shared_width, shared_part),
            ],
            axis=1,
        )
        proj_in = lax.all_gather(in_columns, "shard", tiled=True)
        joined = lax.all_gather(flat, "shard")
        depth_joined = lax.all_gather(by_depth, "shard")
        rows_joined = lax.all_gather(rows_to_send([w_out, w_shared_down], part), "shard")
    (
        gain_in,
        conv_weight,
        conv_bias,
        step_bias,
        decay_log,
        skip_gain,
        gain_gate,
        gain_moe,
    ) = split_small(joined, small_weights)
    depth_joined = depth_joined.reshape(width, LANES)
    lane = jnp.arange(LANES)[None]
    router_wide = jnp.where(lane < expert_total, depth_joined, 0)
    dt_columns = jnp.where(lane < heads, jnp.roll(depth_joined, -expert_total, axis=1), 0)
    grad_all = grad_all.reshape(blocks, tok_rows, width)

    weights_of = (w_experts, w_experts_down)

    def own_first():
        here, _ = own_shard_group(inner)
        return lax.axis_index("seq") * local_experts + here * per_device

    pieces = {
        (0, expert, kind): weights_of[kind] for expert in range(per_device) for kind in range(2)
    }

    def parcels(*keys):
        return [
            Parcel(
                weights_of[kind],
                shift,
                inner,
                lambda to, expert=expert: to * per_device + expert,
            )
            for shift, expert, kind in keys
        ]

    def unpack(keys, arrays):
        pieces.update(zip(keys, arrays))

    last = inner - 1

    gain_row = to_full(gain_in)[None]
    keys = [(1, 0, DOWN)]
    hidden_in, gate_in, rows_in, arrays = project(
        x_group, gain_row, proj_in, dt_columns, channels, in_width, parcels(*keys)
    )
    unpack(keys, arrays)
    conv_part = jnp.concatenate(
        [own_rows(conv_weight, channels), conv_weight[inner_width:]], axis=0
    )
    bias_part = jnp.concatenate([own_rows(conv_bias, channels), conv_bias[inner_width:]], axis=0)
    conv_table = to_full(
        jnp.pad(jnp.concatenate([conv_part.T, bias_part[None]], axis=0), ((0, 3), (0, 0)))
    )
    head_table = jnp.pad(
        jnp.stack(
            [
                to_full(own_rows(step_bias, heads)),
                -jnp.exp(to_full(own_rows(decay_log, heads))),
                to_full(own_rows(skip_gain, heads)),
            ]
        ),
        ((0, 5), (0, LANES - heads)),
    )
    keys = [(1, 0, UP), (last, 0, DOWN)]
    y, seq_rows, states, (taken, *arrays) = scan_forward(
        lengths[0],
        deal_order,
        rows_in,
        conv_table,
        head_table,
        channels,
        [PlaneSwap(rows_by_owner(rows_joined))] + parcels(*keys),
    )
    unpack(keys, arrays)
    if outer > 1:
        out_rows, down_rows = rows_of_owner(taken, [w_out, w_shared_down])
        taken = jnp.concatenate(
            [
                out_rows.reshape(seq_devices, -1, width),
                down_rows.reshape(seq_devices, -1, width),
            ],
            axis=1,
        )
    own_weights = taken
    gate_gain = to_full(own_rows(gain_gate, channels))[None]
    (mix_part,) = mix_out(y, gate_in, gate_gain, own_weights, seq_devices)
    keys = [(last, 0, UP), (last, 1, DOWN)]
    mixed, arrays = reduce_rows(mix_part[None], parcels(*keys))
    unpack(keys, arrays)

    moe_row = to_full(gain_moe)[None]
    route_ids = jnp.pad(routes[0], ((0, 0), (0, LANES - top_count)))
    after_mix, moe_wide, gates = token_forward(
        mixed, tokens[0], moe_row, router_wide, route_ids, inner_width, top_count
    )
    keys = [(2, 0, UP), (2, 0, DOWN), (last, 1, UP)]
    moe_all, arrays = gather_rows(moe_wide, inner, parcels(*keys))
    unpack(keys, arrays)
    moe_all = moe_all.reshape(blocks, tok_rows, width + LANES)
    capacity = min(tok_rows, max(2, tok_rows * top_count * 5 // (expert_total * 3)))
    slots = -(-capacity // 16) * 16
    keys = [(2, 1, UP)]
    expert_rows, grad_rows, picks, arrays = dispatch(
        moe_all, grad_all, per_device, top_count, slots, own_first, parcels(*keys)
    )
    unpack(keys, arrays)
    keys = [(2, 1, DOWN)]
    shared_res, shared_back, shared_up_grad, shared_down_grad, arrays = shared_expert(
        moe_all,
        grad_all,
        proj_in,
        own_weights,
        shared_part,
        seq_devices,
        inner,
        parcels(*keys),
    )
    unpack(keys, arrays)
    order = [
        (shift, expert, kind)
        for shift in range(inner)
        for expert in range(per_device)
        for kind in range(2)
    ]
    if outer == 1:
        late_keys = [(1, 1, UP), (1, 1, DOWN)]
        early_keys = [(1, 0, UP), (last, 0, DOWN)]
        expert_res, expert_back, grads, sent = experts(
            expert_rows,
            grad_rows,
            [pieces[key] for key in order if key not in late_keys],
            hidden,
            top_count,
            own_first,
            inner,
            [(order.index(key), parcels(key)[0]) for key in late_keys],
            [(order.index(key), inner - key[0]) for key in early_keys],
        )
    else:
        for expert in range(per_device):
            for kind in range(2):
                pieces[0, expert, kind] = lax.dynamic_index_in_dim(
                    weights_of[kind], place * per_device + expert, 0, keepdims=False
                )
        keys = [(1, 1, UP), (1, 1, DOWN)]
        moe_all, arrays = carry(moe_all, parcels(*keys))
        unpack(keys, arrays)
        early_keys, sent = [], []
        held = [
            stacked_pieces([pieces[shift, expert, kind] for shift in range(inner)], place, inner)
            for expert in range(per_device)
            for kind in range(2)
        ]
        expert_res, expert_back, grads, _ = experts(
            expert_rows, grad_rows, held, hidden, top_count, own_first, inner
        )
        grads = [
            split_piece(grads[expert * 2 + kind], shift, place, inner)
            for shift, expert, kind in order
        ]
    grads = dict(zip(order, grads))
    returned = {key: grads[key] for key in order if key[0] == 0}
    returned.update(zip(early_keys, sent))

    def back_parcels(*keys):
        keys = [key for key in keys if key not in early_keys]
        return [Parcel(grads[key], inner - key[0], inner) for key in keys]

    def unpack_back(keys, arrays):
        keys = [key for key in keys if key not in early_keys]
        returned.update(zip(keys, arrays))

    keys = [(1, 0, UP), (last, 0, DOWN), (last, 0, UP), (1, 0, DOWN)]
    out_part, back_part, arrays = combine(
        picks, expert_res, expert_back, shared_res, shared_back, inner, back_parcels(*keys)
    )
    unpack_back(keys, arrays)
    keys = [(last, 1, UP), (2, 0, DOWN), (1, 1, UP)]
    back, arrays = reduce_rows(
        back_part.reshape(inner, seq_devices, tok_rows, -1), back_parcels(*keys)
    )
    unpack_back(keys, arrays)
    mix_grad, mix_wide, router_grad, gain_moe_grad = token_back(
        back,
        mixed,
        after_mix,
        moe_wide,
        gates,
        out_grad[0],
        moe_row,
        router_wide,
        route_ids,
        inner_width,
        top_count,
    )

    keys = [(2, 0, UP)]
    mix_group, arrays = gather_rows(mix_wide, 1, back_parcels(*keys))
    unpack_back(keys, arrays)
    keys = [(last, 1, DOWN)]
    dy, gate_in_grad, proj_out_grad, gain_gate_grad, arrays = mix_back(
        mix_group[0], y, gate_in, gate_gain, own_weights, back_parcels(*keys)
    )
    unpack_back(keys, arrays)
    keys = [(2, 1, UP), (1, 1, DOWN)]
    rows_grad, conv_grad, head_grad, out_sum, arrays = scan_backward(
        lengths[0],
        deal_order,
        seq_rows,
        states,
        dy,
        conv_table,
        head_table,
        out_part.reshape(inner, seq_devices, tok_rows, -1),
        back_parcels(*keys),
    )
    unpack_back(keys, arrays)
    layer_out = to_low(after_mix + out_sum)
    keys = [(2, 1, DOWN)]
    swap = [PlaneSwap(rows_from_owner([proj_out_grad, shared_down_grad]))]
    hidden_part, main_grad, rest_grad, (taken, *arrays) = project_back(
        gate_in_grad, rows_grad, hidden_in, proj_in, dt_columns, seq_devices, swap + back_parcels(*keys)
    )
    unpack_back(keys, arrays)
    experts_grad, experts_down_grad = collect(
        place[None], [returned[key] for key in order], per_device
    )
    def spread(values, length, axis=0):
        shape = values.shape[:axis] + (length,) + values.shape[axis + 1 :]
        return lax.dynamic_update_slice_in_dim(
            jnp.zeros(shape, values.dtype), values, part * values.shape[axis], axis
        )

    state_columns = rest_grad.shape[1] - LANES
    conv_rows_grad = conv_grad[:5].T
    conv_full = jnp.concatenate(
        [spread(conv_rows_grad[:channels], inner_width), conv_rows_grad[channels:]], axis=0
    )
    by_depth = [
        rest_grad[:, :state_columns],
        router_grad[:, :expert_total],
        spread(rest_grad[:, state_columns : state_columns + heads], head_total, 1),
        rest_grad[:, -1:],
        to_low(gain_moe_grad[0])[:, None],
    ]
    by_shard = [
        conv_full[:, :4],
        conv_full[:, 4],
        spread(head_grad[0, :heads], head_total),
        spread(head_grad[1, :heads], head_total),
        spread(head_grad[2, :heads], head_total),
        spread(gain_gate_grad[0], inner_width),
    ]
    shapes = [(piece.shape[0] // shard_devices,) + piece.shape[1:] for piece in by_shard]
    by_shard = jnp.concatenate(
        [to_low(piece).reshape(shard_devices, -1) for piece in by_shard], axis=1
    )
    extents = [piece.shape[1] for piece in by_depth]
    used = sum(extents)
    if outer == 1:
        wide = -(-used // LANES) * LANES
        by_depth.append(jnp.zeros((width, wide - used), jnp.bfloat16))
        by_depth = jnp.concatenate(by_depth, axis=1).reshape(inner, seq_devices, -1, wide)
        depth_each = by_depth.shape[2]
        size = by_shard.shape[1]
        each = -(-size // (seq_devices * wide))
        padded = -(-each // 16) * 16
        by_shard = jnp.pad(by_shard, ((0, 0), (0, each * seq_devices * wide - size)))
        by_shard = by_shard.reshape(inner, seq_devices, each, wide)
        by_shard = jnp.pad(by_shard, ((0, 0), (0, 0), (0, padded - each), (0, 0)))
        tokens_grad, main_all, rows_all, shared_all, small_all = settle(
            hidden_part[None],
            jnp.concatenate([by_depth, by_shard], axis=2),
            tokens[0],
            mix_grad,
            gain_row,
            [
                main_grad.reshape(inner, depth_rows, -1),
                taken.reshape(inner, -1, width),
                shared_up_grad.reshape(inner, depth_rows, -1),
            ],
            inner,
        )
        w_in_grad, w_shared_grad, w_out_grad, w_shared_down_grad = assemble(
            main_all,
            shared_all,
            small_all,
            rows_all,
            w_in.shape[1],
            2 * shared_width,
            w_out.shape[0],
            w_shared_down.shape[0],
            max(1, seq_devices // shard_devices),
        )
        depth_sum = to_full(small_all[:, :depth_each].reshape(depth_rows, wide))
        shard_sum = small_all[:, depth_each : depth_each + each].reshape(-1)
    else:
        hidden_grad = reduce_rows(hidden_part[None])[0]
        residual = to_full(tokens[0])
        own_scale = norm_scale(residual)
        own_unit = residual * own_scale
        scaled = hidden_grad * gain_row
        tokens_grad = to_low(
            mix_grad
            + own_scale
            * (scaled - own_unit * jnp.mean(scaled * own_unit, axis=1, keepdims=True))
        )
        by_depth = jnp.concatenate(by_depth, axis=1).reshape(shard_devices, -1)
        packed = jnp.concatenate([by_depth, by_shard], axis=1)
        summed = lax.psum(lax.psum_scatter(packed, "shard", tiled=True), "seq").reshape(-1)
        count = depth_rows * used
        depth_sum = to_full(summed[:count]).reshape(depth_rows, used)
        shard_sum = summed[count:]

        def from_line(part, rows):
            own = lax.psum_scatter(part.reshape(shard_devices, rows, -1), "shard")
            return lax.all_gather(own, "seq")

        def columns_of(joined, extent):
            joined = joined.reshape(seq_devices, depth_rows, 2, extent).transpose(1, 2, 0, 3)
            return to_full(joined.reshape(depth_rows, -1))

        w_in_main = columns_of(from_line(main_grad, depth_rows), channels)
        w_in_grad = jnp.concatenate([w_in_main, depth_sum[:, :state_columns]], axis=1)
        w_shared_grad = columns_of(from_line(shared_up_grad, depth_rows), shared_part)
        rows_each = taken.shape[0] * taken.shape[1] // shard_devices
        w_out_grad, w_shared_down_grad = rows_of_shard(
            from_line(taken, rows_each), [w_out, w_shared_down]
        )
    results, start = [], 0
    for shape in shapes:
        size = 1
        for extent in shape:
            size *= extent
        results.append(to_full(shard_sum[start : start + size]).reshape(shape))
        start += size
    conv_w_grad, conv_b_grad, dt_bias_grad, a_log_grad, d_skip_grad, norm_gate_grad = results
    start = state_columns
    w_router_grad = depth_sum[:, start : start + expert_total]
    start += expert_total
    w_dt_grad = depth_sum[:, start : start + head_total]
    start += head_total
    norm_in_grad = depth_sum[:, start] / to_full(norm_in)
    norm_moe_grad = depth_sum[:, start + 1]
    return (
        layer_out[None],
        tokens_grad[None],
        norm_in_grad,
        w_in_grad,
        w_dt_grad,
        conv_w_grad,
        conv_b_grad,
        dt_bias_grad,
        a_log_grad,
        d_skip_grad,
        norm_gate_grad,
        w_out_grad,
        norm_moe_grad,
        w_router_grad,
        w_shared_grad,
        w_shared_down_grad,
        experts_grad,
        experts_down_grad,
    )


def solution(mesh):
    placed = (
        P("shard", "seq", None),
        P("shard", "seq", None),
        P("shard", None),
        P("shard", None),
        P("shard", "seq", None),
        P("shard"),
        P("shard", None),
        P("shard", None),
        P("shard", None),
        P("shard"),
        P("shard"),
        P("shard"),
        P("shard"),
        P("shard"),
        P("shard", None),
        P("shard"),
        P("shard", None),
        P("shard", None),
        P("shard", None),
        P("seq", "shard", None),
        P("seq", "shard", None),
    )
    return jax.shard_map(
        local,
        mesh=mesh,
        in_specs=placed,
        out_specs=(
            P("shard", "seq", None),
            P("shard", "seq", None),
            P("shard"),
            P("shard", None),
            P("shard", None),
            P("shard", None),
            P("shard"),
            P("shard"),
            P("shard"),
            P("shard"),
            P("shard"),
            P("shard", None),
            P("shard"),
            P("shard", None),
            P("shard", None),
            P("shard", None),
            P("seq", "shard", None),
            P("seq", "shard", None),
        ),
        check_vma=False,
    )
```

```python
import functools

import jax
import jax.numpy as jnp
from jax import lax
from jax.experimental import pallas as pl
from jax.experimental.pallas import tpu as pltpu
from jax.sharding import PartitionSpec as P

STRETCH = 256
INNER = 4
UP, DOWN = 0, 1
EPSILON = 1e-05
HIGHEST = lax.Precision.HIGHEST


def matmul(left_side, right_side):
    return jnp.dot(left_side, right_side, preferred_element_type=jnp.float32)


def left_contract(left_side, right_side):
    return lax.dot_general(
        left_side, right_side, (((0,), (0,)), ((), ())), preferred_element_type=jnp.float32
    )


def right_contract(left_side, right_side):
    return lax.dot_general(
        left_side, right_side, (((1,), (1,)), ((), ())), preferred_element_type=jnp.float32
    )


def to_low(values):
    return values.astype(jnp.bfloat16)


def to_full(values):
    return values.astype(jnp.float32)


def norm_scale(values):
    return lax.rsqrt(jnp.mean(values * values, axis=-1, keepdims=True) + EPSILON)


LANES = 128
VMEM_BYTES = 56 * 1024 * 1024


def cost_of(micros):
    return pl.CostEstimate(flops=0, transcendentals=0, bytes_accessed=int(micros * 3.6e6))


def dot_rows(left_side, right_side, precision=None):
    return lax.dot_general(
        left_side,
        right_side,
        (((0,), (0,)), ((), ())),
        precision=precision,
        preferred_element_type=jnp.float32,
    )


def dot_lanes(left_side, right_side, precision=None):
    return lax.dot_general(
        left_side,
        right_side,
        (((1,), (1,)), ((), ())),
        precision=precision,
        preferred_element_type=jnp.float32,
    )


def dot_full(left_side, right_side, precision=None):
    return jnp.dot(
        left_side, right_side, precision=precision, preferred_element_type=jnp.float32
    )


def iota_of(shape, axis):
    return lax.broadcasted_iota(jnp.int32, shape, axis)


def ids_at(places, lengths_ref):
    total, end = jnp.zeros(places.shape, jnp.int32), 0
    for seq in range(lengths_ref.shape[0]):
        end = end + lengths_ref[seq]
        total = total + (places >= end).astype(jnp.int32)
    return total


def id_at(place, lengths_ref):
    total, end = jnp.int32(0), 0
    for seq in range(lengths_ref.shape[0]):
        end = end + lengths_ref[seq]
        total = total + (place >= end).astype(jnp.int32)
    return total


class Stretch:
    def __init__(self, start, rows, before, conv_ref, head_ref, lengths_ref, channels):
        length = rows.shape[0]
        self.channels = channels
        self.heads = channels // 64
        width = conv_ref.shape[1]
        state = (width - channels) // 2
        places = start + iota_of((length, 1), 0)
        self.ids = ids_at(places, lengths_ref)
        self.ids_row = ids_at(start + iota_of((1, length), 1), lengths_ref)
        inputs = rows[:, :width]
        joined = jnp.concatenate([before[:, :width], inputs], axis=0)
        self.shifted = [inputs]
        value = conv_ref[4:5, :] + inputs * conv_ref[3:4, :]
        for offset in range(1, 4):
            same = (ids_at(places - offset, lengths_ref) == self.ids) & (places >= offset)
            moved = pltpu.roll(joined, offset, 0)[8:, :]
            moved = jnp.where(same, moved, 0.0)
            self.shifted.append(moved)
            value = value + moved * conv_ref[3 - offset : 4 - offset, :]
        self.value = value
        self.sig = jax.nn.sigmoid(value)
        act = value * self.sig
        self.x = act[:, :channels]
        self.b = act[:, channels : channels + state]
        self.c = act[:, channels + state :]
        self.b_low = to_low(self.b)
        self.c_low = to_low(self.c)
        self.dt_in = rows[:, width:] + head_ref[0:1, :]
        self.dt = jnp.maximum(self.dt_in, 0.0) + jnp.log1p(jnp.exp(-jnp.abs(self.dt_in)))
        self.rate = head_ref[1:2, :]
        rows_at = iota_of((length, length), 0)
        columns_at = iota_of((length, length), 1)
        lower = (rows_at >= columns_at).astype(jnp.float32)
        self.cum = dot_full(lower, self.dt * self.rate, HIGHEST)
        self.cum_rows = self.cum.T[:8, :]
        self.dt_rows = self.dt.T[:8, :]
        self.causal = (self.ids == self.ids_row) & (rows_at >= columns_at)
        self.scores = dot_lanes(self.c_low, self.b_low)
        last_id = jnp.where(start > 0, id_at(start - 1, lengths_ref), -1)
        end_id = id_at(start + length - 1, lengths_ref)
        self.enter = jnp.where(self.ids == last_id, jnp.exp(self.cum), 0.0)
        end_cum = self.cum[length - 1 : length, :]
        self.tail = jnp.where(self.ids == end_id, jnp.exp(end_cum - self.cum), 0.0)
        self.tail_weight = self.tail * self.dt
        self.keep = jnp.where(last_id == end_id, jnp.exp(end_cum), 0.0)

    def decay(self, head):
        spread = self.cum[:, head : head + 1] - self.cum_rows[head : head + 1, :]
        return jnp.where(self.causal, jnp.exp(jnp.minimum(spread, 0.0)), 0.0)

    def per_channel(self, by_head):
        return jnp.concatenate(
            [
                jnp.broadcast_to(by_head[:, head : head + 1], (by_head.shape[0], 64))
                for head in range(self.heads)
            ],
            axis=1,
        )

    def state_keep(self):
        return jnp.concatenate(
            [
                jnp.broadcast_to(self.keep[:, head : head + 1], (64, LANES))
                for head in range(self.heads)
            ],
            axis=0,
        )


def head_lanes(channels):
    return (iota_of((channels, LANES), 0) // 64 == iota_of((channels, LANES), 1)).astype(
        jnp.float32
    )


def pick_rows(deal_ref, start, length):
    places = start + iota_of((length, 1), 0)
    return jnp.where(deal_ref[...] == places, 1.0, 0.0).astype(jnp.bfloat16)


def scan_forward_kernel(
    lengths_ref, deal_ref, rows_ref, conv_ref, head_ref, y_ref, seq_ref, states_ref, before, state, total
):
    step = pl.program_id(0)
    length = seq_ref.shape[0]
    channels = y_ref.shape[1]
    start = step * length

    @pl.when(step == 0)
    def _():
        before[...] = jnp.zeros_like(before)
        state[...] = jnp.zeros_like(state)
        total[...] = jnp.zeros_like(total)

    picks = pick_rows(deal_ref, start, length)
    rows = dot_full(picks, rows_ref[...])
    seq_ref[...] = to_low(rows)
    part = Stretch(start, rows, before[...], conv_ref, head_ref, lengths_ref, channels)
    before[...] = rows[length - 8 :, :]
    state_now = state[...]
    states_ref[0] = state_now
    x_low = to_low(part.x)
    outs = []
    lane = iota_of((length, LANES), 1)
    for pair in range(channels // LANES):
        x_pair = x_low[:, pair * LANES : (pair + 1) * LANES]
        halves = []
        for head in (2 * pair, 2 * pair + 1):
            weights = part.decay(head) * part.scores * part.dt_rows[head : head + 1, :]
            halves.append(dot_full(to_low(weights), x_pair))
        outs.append(jnp.where(lane < 64, halves[0], halves[1]))
    earlier = dot_lanes(part.c_low, to_low(state_now))
    skip = part.per_channel(head_ref[2:3, :])
    y = jnp.concatenate(outs, axis=1) + part.per_channel(part.enter) * earlier + skip * part.x
    state[...] = part.state_keep() * state_now + dot_rows(
        to_low(part.per_channel(part.tail_weight) * part.x), part.b_low
    )
    total[...] += dot_rows(picks, to_low(y))

    @pl.when(step == pl.num_programs(0) - 1)
    def _():
        y_ref[...] = to_low(total[...])


def scan_forward(lengths, deal_row, rows, conv_table, head_table, channels, freight):
    group_rows, width = rows.shape
    steps = group_rows // STRETCH
    state_rows = (channels, LANES)
    return run(
        scan_forward_kernel,
        (lengths, deal_row, rows, conv_table, head_table),
        grid=(steps,),
        in_specs=[
            pl.BlockSpec(memory_space=pltpu.SMEM),
            whole(deal_row.shape),
            whole(rows.shape),
            whole(conv_table.shape),
            whole(head_table.shape),
        ],
        out_specs=[
            whole((group_rows, channels)),
            pl.BlockSpec((STRETCH, width), lambda step: (step, 0)),
            pl.BlockSpec((1,) + state_rows, lambda step: (step, 0, 0)),
        ],
        out_shape=[
            jax.ShapeDtypeStruct((group_rows, channels), jnp.bfloat16),
            jax.ShapeDtypeStruct((group_rows, width), jnp.bfloat16),
            jax.ShapeDtypeStruct((steps,) + state_rows, jnp.float32),
        ],
        scratch=[
            pltpu.VMEM((8, width), jnp.float32),
            pltpu.VMEM(state_rows, jnp.float32),
            pltpu.VMEM((group_rows, channels), jnp.float32),
        ],
        freight=freight,
        micros=25,
        name="scan_forward",
    )


def scan_backward_kernel(
    lengths_ref,
    deal_ref,
    seq_ref,
    states_ref,
    dy_ref,
    conv_ref,
    head_ref,
    other_ref,
    drows_ref,
    conv_grad_ref,
    head_grad_ref,
    other_sum_ref,
    after,
    state_grad,
    *other_scratch,
):
    order = pl.program_id(0)
    steps = pl.num_programs(0)
    reducer = Reducer(other_ref.shape[0], other_ref, other_sum_ref, other_scratch)

    last = dy_ref.shape[0] // STRETCH - 1

    @pl.when(order == 0)
    def _():
        reducer.begin()

    for count in range(min(last + 1, reducer.inner + 3)):

        @pl.when(order == count)
        def _():
            reducer.step(count)

    step = steps - 1 - order
    length = STRETCH
    channels = dy_ref.shape[1]
    width = conv_ref.shape[1]
    state_width = (width - channels) // 2
    start = pl.multiple_of(step * length, length)

    @pl.when(order == 0)
    def _():
        after[...] = jnp.zeros_like(after)
        state_grad[...] = jnp.zeros_like(state_grad)
        drows_ref[...] = jnp.zeros_like(drows_ref)
        conv_grad_ref[...] = jnp.zeros_like(conv_grad_ref)
        head_grad_ref[...] = jnp.zeros_like(head_grad_ref)

    picks = pick_rows(deal_ref, start, length)
    dy = dot_full(picks, dy_ref[...])
    rows = seq_ref[pl.ds(start, length), :].astype(jnp.float32)
    place = pl.multiple_of(jnp.maximum(start - 16, 0), 16)
    before = seq_ref[pl.ds(place, 16), :].astype(jnp.float32)[8:, :]
    part = Stretch(start, rows, before, conv_ref, head_ref, lengths_ref, channels)
    state_now = states_ref[0]
    state_low = to_low(state_now)
    next_grad = state_grad[...]
    next_low = to_low(next_grad)
    lanes_of = head_lanes(channels)
    x_low = to_low(part.x)
    dy_low = to_low(dy)
    lane = iota_of((length, LANES), 1)

    enter = part.per_channel(part.enter)
    tail_weight = part.per_channel(part.tail_weight)
    earlier = dot_lanes(part.c_low, state_low)
    enter_grad = dot_full(dy * earlier, lanes_of, HIGHEST)
    entered = to_low(enter * dy)
    c_grad = dot_full(entered, state_low)
    state_grad[...] = part.state_keep() * next_grad + dot_rows(entered, part.c_low)
    onward = dot_lanes(part.b_low, next_low)
    x_grad = part.per_channel(head_ref[2:3, :]) * dy + tail_weight * onward
    tail_grad = dot_full(part.x * onward, lanes_of, HIGHEST)
    b_grad = dot_full(to_low(tail_weight * part.x), next_low)
    tail_part = tail_grad * part.tail_weight
    cum_grad = enter_grad * part.enter - tail_part
    dt_grad = tail_grad * part.tail
    kept = dot_lanes(jnp.ones((8, LANES), jnp.float32), next_grad * state_now, HIGHEST)
    keep_grad = dot_full(kept, lanes_of, HIGHEST)[:1, :]
    end_grad = jnp.sum(tail_part, axis=0, keepdims=True) + keep_grad * part.keep

    score_grad = jnp.zeros((length, length), jnp.float32)
    cum_columns, cum_rows, dt_rows, outs = [], [], [], []
    for pair in range(channels // LANES):
        x_pair = x_low[:, pair * LANES : (pair + 1) * LANES]
        dy_pair = dy_low[:, pair * LANES : (pair + 1) * LANES]
        halves = []
        for half, head in enumerate((2 * pair, 2 * pair + 1)):
            mine = (lane < 64) if half == 0 else (lane >= 64)
            weight_grad = dot_lanes(jnp.where(mine, dy_pair, jnp.zeros_like(dy_pair)), x_pair)
            decay = part.decay(head)
            dt_row = part.dt_rows[head : head + 1, :]
            by_decay = weight_grad * decay
            by_dt = by_decay * part.scores
            by_spread = by_dt * dt_row
            dt_rows.append(jnp.sum(by_dt, axis=0, keepdims=True))
            cum_rows.append(jnp.sum(by_spread, axis=0, keepdims=True))
            cum_columns.append(jnp.sum(by_spread, axis=1, keepdims=True))
            score_grad = score_grad + by_decay * dt_row
            halves.append(dot_rows(to_low(decay * part.scores * dt_row), dy_pair))
        outs.append(jnp.where(lane < 64, halves[0], halves[1]))
    x_grad = x_grad + jnp.concatenate(outs, axis=1)
    score_low = to_low(score_grad)
    c_grad = c_grad + dot_full(score_low, part.b_low)
    b_grad = b_grad + dot_rows(score_low, part.c_low)

    heads = len(dt_rows)
    blank = jnp.zeros((LANES - heads, length), jnp.float32)
    dt_grad = dt_grad + jnp.concatenate(dt_rows + [blank], axis=0).T
    cum_grad = cum_grad - jnp.concatenate(cum_rows + [blank], axis=0).T
    for head in range(heads):
        cum_grad = cum_grad + jnp.where(lane == head, cum_columns[head], 0.0)
    at_end = iota_of((length, 1), 0) == length - 1
    cum_grad = cum_grad + jnp.where(at_end, end_grad, 0.0)
    upper = (iota_of((length, length), 1) >= iota_of((length, length), 0)).astype(jnp.float32)
    log_grad = dot_full(upper, cum_grad, HIGHEST)
    dt_grad = dt_grad + log_grad * part.rate
    dt_in_grad = dt_grad * jax.nn.sigmoid(part.dt_in)
    dt_in_grad = jnp.where(lane < heads, dt_in_grad, 0.0)
    head_grad_ref[0:1, :] += jnp.sum(dt_in_grad, axis=0, keepdims=True)
    head_grad_ref[1:2, :] += jnp.sum(log_grad * part.dt, axis=0, keepdims=True) * part.rate
    skip_sum = jnp.broadcast_to(jnp.sum(dy * part.x, axis=0, keepdims=True), (8, channels))
    head_grad_ref[2:3, :] += dot_full(skip_sum, lanes_of, HIGHEST)[:1, :]

    act_grad = jnp.concatenate([x_grad, b_grad, c_grad], axis=1)
    value_grad = act_grad * part.sig * (1.0 + part.value * (1.0 - part.sig))
    conv_grad_ref[4:5, :] += jnp.sum(value_grad, axis=0, keepdims=True)
    for offset in range(4):
        conv_grad_ref[3 - offset : 4 - offset, :] += jnp.sum(
            value_grad * part.shifted[offset], axis=0, keepdims=True
        )
    joined = jnp.concatenate([value_grad, after[...]], axis=0)
    places = start + iota_of((length, 1), 0)
    rows_grad = value_grad * conv_ref[3:4, :]
    for offset in range(1, 4):
        moved = pltpu.roll(joined, length + 8 - offset, 0)[:length, :]
        same = (ids_at(places + offset, lengths_ref) == part.ids) & (
            places + offset < steps * length
        )
        rows_grad = rows_grad + jnp.where(same, moved, 0.0) * conv_ref[3 - offset : 4 - offset, :]
    after[...] = value_grad[:8, :]
    drows_ref[...] += to_low(
        dot_rows(picks, to_low(jnp.concatenate([rows_grad, dt_in_grad], axis=1)))
    )

    for count in range(last + 1, reducer.inner + 3):

        @pl.when(order == last)
        def _():
            reducer.step(count)

    @pl.when(order == steps - 1)
    def _():
        reducer.finish()


def scan_backward(
    lengths, deal_row, seq_rows, states, dy, conv_table, head_table, other, freight
):
    group_rows, width = seq_rows.shape
    channels = dy.shape[1]
    steps = group_rows // STRETCH
    return run(
        scan_backward_kernel,
        (lengths, deal_row, seq_rows, states, dy, conv_table, head_table, other),
        grid=(steps,),
        in_specs=[
            pl.BlockSpec(memory_space=pltpu.SMEM),
            whole(deal_row.shape),
            once(seq_rows.shape),
            pl.BlockSpec((1, channels, LANES), lambda step: (steps - 1 - step, 0, 0)),
            once(dy.shape),
            whole(conv_table.shape),
            whole(head_table.shape),
            pl.BlockSpec(memory_space=pl.ANY),
        ],
        out_specs=[
            whole((group_rows, width)),
            whole(conv_table.shape),
            whole(head_table.shape),
            whole(other.shape[2:]),
        ],
        out_shape=[
            jax.ShapeDtypeStruct((group_rows, width), jnp.bfloat16),
            jax.ShapeDtypeStruct(conv_table.shape, jnp.float32),
            jax.ShapeDtypeStruct(head_table.shape, jnp.float32),
            jax.ShapeDtypeStruct(other.shape[2:], jnp.float32),
        ],
        scratch=[
            pltpu.VMEM((8, conv_table.shape[1]), jnp.float32),
            pltpu.VMEM((channels, LANES), jnp.float32),
        ]
        + Reducer.scratch(other.shape[0], *other.shape[2:]),
        freight=freight,
        flips=FLIPS,
        inner=other.shape[0],
        micros=40,
        name="scan_backward",
    )


def whole(shape):
    return pl.BlockSpec(shape, lambda *steps: (0,) * len(shape))


def once(shape):
    return pl.BlockSpec(
        shape, lambda *steps: (0,) * len(shape), pipeline_mode=pl.Buffered(buffer_count=1)
    )


MESH = pl.DeviceIdType.MESH
FLIPS = (1, 2, 4)


def flipped(place, flip):
    result = place
    for bit in FLIPS:
        if flip & bit:
            result = result + bit - 2 * bit * lax.rem(lax.div(place, bit), 2)
    return result


def own_shard_group(inner):
    shard = lax.axis_index("shard")
    place = lax.rem(shard, inner)
    return place, shard - place


def peers_in_order(place, inner):
    if inner == 1:
        return []
    if inner == 4:
        half = lax.div(place, 2)
        return [flipped(place, 1), 2 - half, 3 - 3 * half]
    return [lax.rem(place + shift, inner) for shift in range(1, inner)]


def greet(flips, inner):
    barrier = pltpu.get_barrier_semaphore()
    part = lax.axis_index("seq")
    place, first = own_shard_group(inner)
    for flip in flips:
        pl.semaphore_signal(
            barrier, inc=1, device_id={"seq": flipped(part, flip)}, device_id_type=MESH
        )
    for peer in peers_in_order(place, inner):
        pl.semaphore_signal(
            barrier, inc=1, device_id={"shard": first + peer}, device_id_type=MESH
        )
    pl.semaphore_wait(barrier, len(flips) + inner - 1)


def among(place, places):
    if places is None:
        return None
    return functools.reduce(jnp.logical_or, [place == one for one in places])


def do_if(condition, action):
    if condition is None:
        action()
    else:
        pl.when(condition)(action)


class Parcel:
    flips = ()
    sems = 1

    def __init__(self, array, shift, inner, index=None, output=None, senders=None):
        self.array, self.shift, self.inner, self.index = array, shift, inner, index
        self.senders = senders
        self.shape = array.shape if index is None else array.shape[1:]
        self.output = output

    def moves(self, source, target):
        place, first = own_shard_group(self.inner)
        to = lax.rem(place + self.shift, self.inner)
        if self.index is not None:
            source = source.at[self.index(to)]
        return [(source, target, target, {"shard": first + to})]

    def sends(self):
        return among(own_shard_group(self.inner)[0], self.senders)

    def comes(self):
        place, _ = own_shard_group(self.inner)
        return among(lax.rem(place + self.inner - self.shift, self.inner), self.senders)

    def stays(self, source, target):
        return []


class PlaneSwap:
    flips = (1, 2, 3, 4, 5, 6, 7)
    inner = 1
    sems = 8

    output = None

    def __init__(self, array):
        self.array, self.shape = array, array.shape

    def sends(self):
        return None

    def comes(self):
        return None

    def moves(self, source, target):
        part = lax.axis_index("seq")
        return [
            (
                source.at[flipped(part, flip)],
                target.at[part],
                target.at[flipped(part, flip)],
                {"seq": flipped(part, flip)},
            )
            for flip in self.flips
        ]

    def stays(self, source, target):
        part = lax.axis_index("seq")
        return [(source.at[part], target.at[part])]


COLLECTIVES = []


def run(
    kernel,
    args,
    *,
    in_specs,
    out_specs,
    out_shape,
    name,
    micros,
    grid=(),
    scratch=(),
    freight=(),
    flips=(),
    inner=1,
    late=False,
):
    freight = list(freight)
    for place, item in enumerate(freight):
        item.rank = place
    flips = tuple(sorted(set(flips).union(*[item.flips for item in freight])))
    inner = max([inner] + [item.inner for item in freight])
    talks = bool(flips) or inner > 1
    count_in, count_out, count_scratch = len(args), len(out_shape), len(scratch)
    count = len(freight)
    loaded = [item for item in freight if item.output is None]

    def wrapped(*refs):
        ins, refs = refs[:count_in], refs[count_in:]
        sources, refs = list(refs[: len(loaded)]), refs[len(loaded) :]
        outs, refs = refs[:count_out], refs[count_out:]
        sources = [
            sources.pop(0) if item.output is None else outs[item.output] for item in freight
        ]
        targets, refs = refs[:count], refs[count:]
        own, refs = refs[:count_scratch], refs[count_scratch:]

        def remote(item, place, order, source, target, device):
            send, recv = refs[3 * place : 3 * place + 2]
            return pltpu.make_async_remote_copy(
                src_ref=source,
                dst_ref=target,
                send_sem=send.at[order],
                recv_sem=recv.at[order],
                device_id=device,
                device_id_type=MESH,
            )

        def moves(chosen):
            for place, item in enumerate(freight):
                if not chosen(item):
                    continue
                for order, move in enumerate(item.moves(sources[place], targets[place])):
                    yield item, place, order, move

        def stays(chosen):
            for place, item in enumerate(freight):
                if not chosen(item):
                    continue
                for source, target in item.stays(sources[place], targets[place]):
                    yield pltpu.make_async_copy(source, target, refs[3 * place + 2])

        def depart(chosen=lambda item: True, gate=None):
            for item, place, order, (source, target, _, device) in moves(chosen):
                allowed = item.sends()
                if gate is not None:
                    allowed = gate if allowed is None else allowed & gate
                do_if(
                    allowed,
                    lambda: remote(item, place, order, source, target, device).start(),
                )
            for copy in stays(chosen):
                copy.start()

        def arrive(chosen=lambda item: True):
            for item, place, order, (source, target, arrival, device) in moves(chosen):
                do_if(
                    item.comes(),
                    lambda: remote(item, place, order, source, arrival, device).wait_recv(),
                )
                do_if(
                    item.sends(),
                    lambda: remote(item, place, order, source, target, device).wait_send(),
                )
            for copy in stays(chosen):
                copy.wait()

        if grid:
            at = [pl.program_id(axis) for axis in range(len(grid))]
            first, last = at[0] == 0, at[0] == grid[0] - 1
            for axis in range(1, len(grid)):
                first = first & (at[axis] == 0)
                last = last & (at[axis] == grid[axis] - 1)
            if talks:

                @pl.when(first)
                def _():
                    greet(flips, inner)
                    if not late:
                        depart()

            if late:
                kernel(depart, arrive, targets, *ins, *outs, *own)
            else:
                kernel(*ins, *outs, *own)
            if talks and not late:
                pl.when(last)(arrive)
        else:
            if talks:
                greet(flips, inner)
            if late:
                kernel(depart, *ins, *outs, *own)
            else:
                depart()
                kernel(*ins, *outs, *own)
            arrive()

    anywhere = pl.BlockSpec(memory_space=pl.ANY)
    extra = {}
    if talks:
        COLLECTIVES.append(name)
        extra = dict(collective_id=len(COLLECTIVES), has_side_effects=True)
    sems = []
    for item in freight:
        sems += [
            pltpu.SemaphoreType.DMA((item.sems,)),
            pltpu.SemaphoreType.DMA((item.sems,)),
            pltpu.SemaphoreType.DMA(()),
        ]
    results = pl.pallas_call(
        wrapped,
        grid=grid,
        in_specs=list(in_specs) + [anywhere] * len(loaded),
        out_specs=list(out_specs) + [anywhere] * count,
        out_shape=list(out_shape)
        + [jax.ShapeDtypeStruct(item.shape, item.array.dtype) for item in freight],
        scratch_shapes=list(scratch) + sems,
        compiler_params=pltpu.CompilerParams(vmem_limit_bytes=VMEM_BYTES, **extra),
        cost_estimate=cost_of(micros),
        name=name,
    )(*args, *[item.array for item in loaded])
    results = list(results)
    if freight:
        return results[:count_out] + [results[count_out:]]
    return results


class LineSum:
    def __init__(self, inner, sums, from_below, from_above, send, below_recv, above_recv):
        self.inner = inner
        self.sums, self.from_below, self.from_above = sums, from_below, from_above
        self.send, self.below_recv, self.above_recv = send, below_recv, above_recv
        self.place, self.first = own_shard_group(inner)
        self.targets = list(reversed(peers_in_order(self.place, inner))) + [self.place]

    def copy(self, order, up):
        target = self.targets[order]
        inbox = self.from_below if up else self.from_above
        recv = self.below_recv if up else self.above_recv
        return pltpu.make_async_remote_copy(
            src_ref=self.sums.at[order],
            dst_ref=inbox.at[target],
            send_sem=self.send.at[order],
            recv_sem=recv.at[target],
            device_id={"shard": self.first + self.place + (1 if up else -1)},
            device_id_type=MESH,
        )

    def arrived(self, target, up):
        inbox = self.from_below if up else self.from_above
        recv = self.below_recv if up else self.above_recv
        pltpu.make_async_remote_copy(
            src_ref=inbox.at[target],
            dst_ref=inbox.at[target],
            send_sem=self.send.at[0],
            recv_sem=recv.at[target],
            device_id={"shard": self.first + self.place + (-1 if up else 1)},
            device_id_type=MESH,
        ).wait_recv()
        return to_full(inbox[target])

    def ways(self):
        return ((True, self.place > 0), (False, self.place < self.inner - 1))

    def push_free(self, order):
        target = self.targets[order]
        for up, comes in self.ways():
            heads = (target > self.place) if up else (target < self.place)

            @pl.when(heads & jnp.logical_not(comes))
            def _():
                self.copy(order, up).start()

    def push_rest(self, order):
        target = self.targets[order]
        for up, comes in self.ways():
            heads = (target > self.place) if up else (target < self.place)

            @pl.when(heads & comes)
            def _():
                self.sums[order] = to_low(
                    to_full(self.sums[order]) + self.arrived(target, up)
                )
                self.copy(order, up).start()

    def add_own(self, total):
        for up, comes in self.ways():

            @pl.when(comes)
            def _():
                total[...] += self.arrived(self.place, up)

    def finish(self):
        for order in range(self.inner - 1):
            for up in (True, False):
                target = self.targets[order]

                @pl.when((target > self.place) if up else (target < self.place))
                def _():
                    self.copy(order, up).wait_send()

    @staticmethod
    def scratch(inner, rows, width):
        sems = lambda *shape: pltpu.SemaphoreType.DMA(shape)
        return [
            pltpu.VMEM((max(1, inner - 1), rows, width), jnp.bfloat16),
            pltpu.VMEM((inner, rows, width), jnp.bfloat16),
            pltpu.VMEM((inner, rows, width), jnp.bfloat16),
            sems(max(1, inner - 1)),
            sems(inner),
            sems(inner),
        ]


class Reducer:
    def __init__(self, inner, p_ref, total, refs, make=None):
        self.inner, self.p_ref, self.total, self.make = inner, p_ref, total, make
        self.held, self.paired, self.turned, self.crossed = refs[:4]
        self.load, self.core_send, self.core_recv = refs[4:7]
        self.turn_send, self.turn_recv, self.cross_send, self.cross_recv = refs[7:11]
        self.line = LineSum(inner, *refs[11:])
        self.part = lax.axis_index("seq")
        half = self.held.shape[2] // 2
        self.spans = [pl.ds(0, half), pl.ds(half, half)]

    @staticmethod
    def scratch(inner, rows, width):
        low = jnp.bfloat16
        sems = lambda *shape: pltpu.SemaphoreType.DMA(shape)
        return [
            pltpu.VMEM((inner, 4, rows, width), low),
            pltpu.VMEM((inner, 4, rows, width), low),
            pltpu.VMEM((inner, 2, rows // 2, width), low),
            pltpu.VMEM((inner, 4, rows // 2, width), low),
            sems(inner, 4),
            sems(inner, 4),
            sems(inner, 4),
            sems(inner, 2),
            sems(inner, 2),
            sems(inner, 4),
            sems(inner, 4),
        ] + LineSum.scratch(inner, rows, width)

    EVENS = (6, 2, 4, 0)

    def to_core(self, order, slot):
        return pltpu.make_async_remote_copy(
            src_ref=self.p_ref.at[order, slot]
            if self.make
            else self.p_ref.at[
                self.line.targets[order], flipped(self.part, self.EVENS[slot] + 1)
            ],
            dst_ref=self.paired.at[order, slot],
            send_sem=self.core_send.at[order, slot],
            recv_sem=self.core_recv.at[order, slot],
            device_id={"seq": flipped(self.part, 1)},
            device_id_type=MESH,
        )

    def loading(self, order, slot):
        return pltpu.make_async_copy(
            self.p_ref.at[self.line.targets[order], flipped(self.part, self.EVENS[slot])],
            self.held.at[order, slot],
            self.load.at[order, slot],
        )

    def turn(self, order, span):
        return pltpu.make_async_remote_copy(
            src_ref=self.held.at[order, 0, self.spans[span]],
            dst_ref=self.turned.at[order, span],
            send_sem=self.turn_send.at[order, span],
            recv_sem=self.turn_recv.at[order, span],
            device_id={"seq": flipped(self.part, (2, 4)[span])},
            device_id_type=MESH,
        )

    CROSSINGS = ((1, 2, 0), (2, 4, 1), (2, 4, 0), (1, 2, 1))

    def cross(self, order, kind):
        slot, flip, span = self.CROSSINGS[kind]
        return pltpu.make_async_remote_copy(
            src_ref=self.held.at[order, slot, self.spans[span]],
            dst_ref=self.crossed.at[order, kind],
            send_sem=self.cross_send.at[order, kind],
            recv_sem=self.cross_recv.at[order, kind],
            device_id={"seq": flipped(self.part, flip)},
            device_id_type=MESH,
        )

    def begin(self):
        for order in range(self.inner):
            for slot in range(4):
                if self.make:
                    target = self.line.targets[order]
                    block = flipped(self.part, self.EVENS[slot] + 1)
                    self.make(target, block, self.p_ref.at[order, slot])
                self.to_core(order, slot).start()
                if not self.make:
                    self.loading(order, slot).start()
            if self.make:
                for slot in range(4):
                    block = flipped(self.part, self.EVENS[slot])
                    self.make(self.line.targets[order], block, self.held.at[order, slot])

    def total_of(self, order, slot):
        if not self.make:
            self.loading(order, slot).wait()
        self.to_core(order, slot).wait_recv()
        return to_full(self.held[order, slot]) + to_full(self.paired[order, slot])

    def stage_a(self, order):
        self.held[order, 0] = to_low(self.total_of(order, 0))
        for span in range(2):
            self.turn(order, span).start()
        for slot in (1, 2):
            self.held[order, slot] = to_low(self.total_of(order, slot))
            self.cross(order, slot - 1).start()

    def stage_b(self, order):
        for kind in (2, 3):
            slot, _, span = self.CROSSINGS[kind]
            self.turn(order, span).wait_recv()
            at = self.spans[span]
            self.held[order, slot, at] = to_low(
                to_full(self.held[order, slot, at]) + to_full(self.turned[order, span])
            )
            self.cross(order, kind).start()

    def stage_c(self, order):
        total = self.total_of(order, 3)
        for kind in range(4):
            self.cross(order, kind).wait_recv()
        crossed = [to_full(self.crossed[order, kind]) for kind in range(4)]
        total = total + jnp.concatenate(
            [crossed[0] + crossed[2], crossed[1] + crossed[3]], axis=0
        )
        if order == self.inner - 1:
            self.total[...] = total
        else:
            self.line.sums[order] = to_low(total)
            self.line.push_free(order)

    def stage_d(self, order):
        if order == self.inner - 1:
            self.line.add_own(self.total)
        else:
            self.line.push_rest(order)

    def step(self, count):
        for stage, late in (
            (self.stage_b, 1),
            (self.stage_a, 0),
            (self.stage_c, 2),
            (self.stage_d, 3),
        ):
            if 0 <= count - late < self.inner:
                stage(count - late)

    def steps(self):
        return self.inner + 3

    def finish(self):
        for order in range(self.inner):
            for slot in range(4):
                self.to_core(order, slot).wait_send()
            for span in range(2):
                self.turn(order, span).wait_send()
            for kind in range(4):
                self.cross(order, kind).wait_send()
        self.line.finish()

    def whole(self, depart):
        self.begin()
        depart(0)
        for count in range(self.inner + 3):
            self.step(count)
            if count >= 2:
                depart(count - 1)
        self.finish()


def reduce_kernel(inner, staged, depart, p_ref, out_ref, *scratch):
    def leave(number):
        if staged:
            depart(lambda item: item.rank == number)

    if not staged:
        depart()
    Reducer(inner, p_ref, out_ref, scratch).whole(leave)


def reduce_rows(partial, freight=()):
    inner, _, rows, width = partial.shape
    return run(
        functools.partial(reduce_kernel, inner, inner > 1),
        (partial,),
        in_specs=[pl.BlockSpec(memory_space=pl.ANY)],
        out_specs=[pl.BlockSpec(memory_space=pltpu.VMEM)],
        out_shape=[jax.ShapeDtypeStruct((rows, width), jnp.float32)],
        scratch=Reducer.scratch(inner, rows, width),
        freight=freight,
        flips=FLIPS,
        inner=inner,
        late=True,
        micros=25 * inner,
        name="reduce_rows",
    )


def plane_gather(own, target, send, recv):
    part = lax.axis_index("seq")
    half = own.shape[0] // 2
    spans = [pl.ds(0, half), pl.ds(half, half)]
    started = []

    def copy_of(kind, block, span, flip, from_own=False):
        place = target(block).at[spans[span]]
        return pltpu.make_async_remote_copy(
            src_ref=own.at[spans[span]] if from_own else place,
            dst_ref=place,
            send_sem=send.at[kind],
            recv_sem=recv.at[kind],
            device_id={"seq": flipped(part, flip)},
            device_id_type=MESH,
        )

    def push(kind, block, span, flip, from_own=False):
        copy = copy_of(kind, block, span, flip, from_own)
        copy.start()
        started.append(copy)

    def arrived(kind, block, span, flip):
        copy_of(kind, block, span, flip).wait_recv()

    def first():
        for kind, span, flip in (
            (3, 1, 2), (4, 0, 4), (2, 0, 2), (5, 1, 4), (0, 0, 1), (1, 1, 1)
        ):
            push(kind, part, span, flip, True)

    def second():
        side, over = flipped(part, 2), flipped(part, 4)
        arrived(3, side, 1, 2)
        push(6, side, 1, 4)
        arrived(4, over, 0, 4)
        push(7, over, 0, 2)
        push(9, side, 1, 1)
        push(10, over, 0, 1)
        arrived(2, side, 0, 2)
        push(8, side, 0, 1)
        arrived(5, over, 1, 4)
        push(11, over, 1, 1)

    def third():
        far = flipped(part, 6)
        arrived(6, far, 1, 4)
        push(13, far, 1, 1)
        arrived(7, far, 0, 2)
        push(12, far, 0, 1)

    def last():
        for kind, flip, span in (
            (0, 1, 0), (1, 1, 1), (9, 3, 1), (10, 5, 0), (8, 3, 0), (11, 5, 1), (13, 7, 1), (12, 7, 0)
        ):
            arrived(kind, flipped(part, flip), span, 1)
        for copy in started:
            copy.wait_send()

    return first, second, third, last


def line_gather(inner, own, target, send, recv, split=2):
    place, first = own_shard_group(inner)
    half = own.shape[0] // split
    spans = [pl.ds(span * half, half) for span in range(split)]

    def copy_of(way, step, span):
        block = place - step if way == 0 else place + step
        to = place + 1 if way == 0 else place - 1
        spot = target(block).at[spans[span]]
        return pltpu.make_async_remote_copy(
            src_ref=own.at[spans[span]] if step == 0 else spot,
            dst_ref=spot,
            send_sem=send.at[way, step, span],
            recv_sem=recv.at[way, step, span],
            device_id={"shard": first + to},
            device_id_type=MESH,
        )

    def sends(way, step):
        if way == 0:
            return (place < inner - 1) & (place >= step)
        return (place > 0) & (place + step < inner)

    def receives(way, step):
        return place >= step if way == 0 else place + step < inner

    def start(step, span):
        for way in range(2):

            @pl.when(sends(way, step))
            def _():
                copy_of(way, step, span).start()

    def begin():
        for span in range(split):
            start(0, span)

    def onward(step):
        for span in range(split):
            for way in range(2):

                @pl.when(receives(way, step))
                def _():
                    block = place - step if way == 0 else place + step
                    spot = target(block).at[spans[span]]
                    pltpu.make_async_remote_copy(
                        src_ref=spot,
                        dst_ref=spot,
                        send_sem=send.at[way, step - 1, span],
                        recv_sem=recv.at[way, step - 1, span],
                        device_id={"shard": block + first},
                        device_id_type=MESH,
                    ).wait_recv()

            if step < inner - 1:
                start(step, span)

    def finish():
        for step in range(inner - 1):
            for span in range(split):
                for way in range(2):

                    @pl.when(sends(way, step))
                    def _():
                        copy_of(way, step, span).wait_send()

    return begin, onward, finish


def group_gather(inner, own, target, sems):
    part = lax.axis_index("seq")
    place, _ = own_shard_group(inner)
    sources = [place] + peers_in_order(place, inner)
    line_send, line_recv, send, recv = sems
    line = line_gather(inner, own, lambda p: target(p, part), line_send, line_recv)
    planes = [
        plane_gather(
            own if order == 0 else target(source, part),
            lambda b, source=source: target(source, b),
            send.at[order],
            recv.at[order],
        )
        for order, source in enumerate(sources)
    ]
    return line, planes


def group_sems(inner):
    sems = lambda *shape: pltpu.SemaphoreType.DMA(shape)
    steps = max(1, inner - 1)
    return [sems(2, steps, 2), sems(2, steps, 2), sems(inner, 14), sems(inner, 14)]


def gather_kernel(inner, depart, x_ref, out_ref, own_sem, *sems):
    part = lax.axis_index("seq")
    place, _ = own_shard_group(inner)
    own = pltpu.make_async_copy(x_ref, out_ref.at[place, part], own_sem)
    (begin, onward, finish), planes = group_gather(
        inner, x_ref, lambda p, b: out_ref.at[p, b], sems
    )
    if inner > 1:
        begin()
    else:
        depart()
    planes[0][0]()
    own.start()
    planes[0][1]()
    for order in range(1, inner):
        onward(order)
        if order < inner - 1:
            depart(lambda item: item.rank == order - 1)
        else:
            depart(lambda item: item.rank >= order - 1)
        planes[order][0]()
        planes[order - 1][2]()
        planes[order][1]()
    planes[inner - 1][2]()
    for stages in planes:
        stages[3]()
    if inner > 1:
        finish()
    own.wait()


def gather_rows(x, inner, freight=()):
    rows, width = x.shape
    seq_devices = lax.axis_size("seq")
    return run(
        functools.partial(gather_kernel, inner),
        (x,),
        in_specs=[pl.BlockSpec(memory_space=pl.ANY)],
        out_specs=[pl.BlockSpec(memory_space=pl.ANY)],
        out_shape=[jax.ShapeDtypeStruct((inner, seq_devices, rows, width), x.dtype)],
        scratch=[pltpu.SemaphoreType.DMA(())] + group_sems(inner),
        freight=freight,
        flips=FLIPS,
        inner=inner,
        late=True,
        micros=25 * inner,
        name="gather_rows",
    )


def begin_kernel(
    inner,
    depart,
    x_ref,
    g_ref,
    s_ref,
    d_ref,
    in_ref,
    shared_ref,
    out_ref,
    down_ref,
    x_out,
    g_out,
    w_out,
    s_out,
    d_out,
    r_out,
    w_ref,
    r_ref,
    b_ref,
    b_line,
    b_all,
    own_sems,
    pick_sems,
    place_sems,
    *sems,
):
    part = lax.axis_index("seq")
    place, _ = own_shard_group(inner)
    rows = w_ref.shape[0]
    seq_devices = x_out.shape[0]
    picks = []

    def pick(source, target):
        picks.append(pltpu.make_async_copy(source, target, pick_sems.at[len(picks)]))

    shared = shared_ref.shape[1] // seq_devices // 2
    channels = w_ref.shape[1] // 2 - shared
    share, state = b_ref.shape
    at = 0
    for source, extent in ((in_ref, channels), (shared_ref, shared)):
        for side in range(2):
            start = pl.multiple_of((side * seq_devices + part) * extent, extent)
            pick(source.at[:, pl.ds(start, extent)], w_ref.at[:, pl.ds(at, extent)])
            at += extent
    start = pl.multiple_of(part * share, share)
    pick(in_ref.at[pl.ds(start, share), pl.ds(in_ref.shape[1] - state, state)], b_ref)
    halves = seq_devices // inner
    at = 0
    for half in range(halves):
        for source in (out_ref, down_ref):
            fine = source.shape[0] // halves // seq_devices
            start = pl.multiple_of((half * seq_devices + part) * fine, fine)
            pick(source.at[pl.ds(start, fine)], r_ref.at[pl.ds(at, fine)])
            at += fine
    for copy in picks:
        copy.start()
    targets = [
        lambda p: s_out.at[p],
        lambda p: w_out.at[pl.ds(p * rows, rows), pl.ds(0, w_ref.shape[1])],
        lambda p: r_out.at[p],
        lambda p: d_out.at[p],
        lambda p: b_line.at[pl.ds(p * share, share)],
    ]
    sources = [s_ref, w_ref, r_ref, d_ref, b_ref]
    lines = [
        line_gather(
            inner, source, target, sems[2 * order], sems[2 * order + 1], 1 if order == 4 else 2
        )
        for order, (source, target) in enumerate(zip(sources, targets))
    ]
    b_plane = plane_gather(b_line, lambda b: b_all.at[b], sems[16], sems[17])
    line, planes = group_gather(inner, g_ref, lambda p, b: g_out.at[p, b], sems[10:14])
    lines.append(line)
    x_plane = plane_gather(x_ref, lambda b: x_out.at[b], sems[14], sems[15])
    rows_line = lines.pop(2)
    lines[0][0]()
    lines[2][0]()
    lines[4][0]()
    x_plane[0]()
    planes[0][0]()
    for copy in picks:
        copy.wait()
    lines[3][0]()
    lines[1][0]()
    rows_line[0]()
    at_end = (place == 0) | (place == inner - 1)
    depart(gate=at_end)
    owns = [
        pltpu.make_async_copy(source, target(place), own_sems.at[order])
        for order, (source, target) in enumerate(zip(sources, targets))
    ]
    owns.append(pltpu.make_async_copy(x_ref, x_out.at[part], own_sems.at[5]))
    owns.append(pltpu.make_async_copy(g_ref, g_out.at[place, part], own_sems.at[6]))
    for copy in owns:
        copy.start()
    x_plane[1]()
    planes[0][1]()
    x_plane[2]()
    planes[0][2]()
    *other_lines, g_line = lines
    for step in range(1, inner):
        g_line[1](step)
        planes[step][0]()
        if step > 1:
            planes[step - 1][2]()
        planes[step][1]()
        for _, onward, _ in reversed(other_lines):
            onward(step)
        if step == 1:
            rows_line[1](1)
            depart(gate=jnp.logical_not(at_end))
    planes[inner - 1][2]()
    owns[4].wait()
    b_plane[0]()
    for step in range(2, inner):
        rows_line[1](step)
    b_plane[1]()
    b_plane[2]()
    x_plane[3]()
    for stages in planes:
        stages[3]()
    b_plane[3]()
    own_b = pltpu.make_async_copy(b_line, b_all.at[part], own_sems.at[7])
    own_b.start()
    own_b.wait()
    spread = []
    for device in range(seq_devices):
        for shard in range(inner):
            spread.append(
                pltpu.make_async_copy(
                    b_all.at[device, pl.ds(shard * share, share)],
                    w_out.at[
                        pl.ds(shard * rows + device * share, share), pl.ds(w_ref.shape[1], state)
                    ],
                    place_sems.at[device, shard],
                )
            )
    for copy in spread:
        copy.start()
    for _, _, finish in lines + [rows_line]:
        finish()
    for order, copy in enumerate(owns):
        if order != 4:
            copy.wait()
    for copy in spread:
        copy.wait()


def begin(
    x, grad, small, by_depth, w_in, w_shared, w_out, w_down, in_width, shared_part, inner, freight
):
    seq_devices = lax.axis_size("seq")
    low = jnp.bfloat16
    depth, width = w_in.shape[0], w_out.shape[1]
    columns = in_width + 2 * shared_part
    w_columns = 2 * w_out.shape[0] * inner // seq_devices + 2 * shared_part
    rows = (w_out.shape[0] + w_down.shape[0]) // seq_devices
    anywhere = pl.BlockSpec(memory_space=pl.ANY)
    sems = lambda *shape: pltpu.SemaphoreType.DMA(shape)
    line_sems = [sems(2, inner - 1, 2)] * 10
    state = in_width + 2 * shared_part - w_columns
    fine = depth // seq_devices
    return run(
        functools.partial(begin_kernel, inner),
        (x, grad, small, by_depth, w_in, w_shared, w_out, w_down),
        in_specs=[anywhere] * 8,
        out_specs=[anywhere] * 6,
        out_shape=[
            jax.ShapeDtypeStruct((seq_devices,) + x.shape, x.dtype),
            jax.ShapeDtypeStruct((inner, seq_devices) + grad.shape, grad.dtype),
            jax.ShapeDtypeStruct((inner * depth, columns), low),
            jax.ShapeDtypeStruct((inner,) + small.shape, small.dtype),
            jax.ShapeDtypeStruct((inner,) + by_depth.shape, low),
            jax.ShapeDtypeStruct((inner, rows, width), low),
        ],
        scratch=[
            pltpu.VMEM((depth, w_columns), low),
            pltpu.VMEM((rows, width), low),
            pltpu.VMEM((fine, state), low),
            pltpu.VMEM((inner * fine, state), low),
            pltpu.VMEM((seq_devices, inner * fine, state), low),
            sems(8),
            sems(5 + 2 * (seq_devices // inner)),
            sems(seq_devices, inner),
        ]
        + line_sems
        + group_sems(inner)
        + [sems(14)] * 4,
        freight=freight,
        flips=FLIPS,
        inner=inner,
        late=True,
        micros=130,
        name="begin",
    )


def settle_kernel(
    inner,
    counts,
    hidden_ref,
    small_ref,
    x_ref,
    mix_ref,
    gain_ref,
    *refs,
):
    part = lax.axis_index("seq")
    place, _ = own_shard_group(inner)
    parts, refs = refs[:counts], refs[counts:]
    tokens_out, refs = refs[0], refs[1:]
    outs, refs = refs[: counts + 1], refs[counts + 1 :]
    hidden_sum, small_sum = refs[:2]
    refs = refs[2:]
    take = len(Reducer.scratch(1, 16, LANES))
    hidden = Reducer(1, hidden_ref, hidden_sum, refs[:take])
    small = Reducer(inner, small_ref, small_sum, refs[take : 2 * take])
    refs = refs[2 * take :]
    lines, totals, planes, owns = [], [], [], []
    for index in range(counts + 1):
        low, gsend, grecv, here = refs[:4]
        refs = refs[4:]
        out = outs[index]
        planes.append(plane_gather(low, lambda b, out=out: out.at[b], gsend, grecv))
        owns.append((low, pltpu.make_async_copy(low, out.at[part], here)))
    loads = []
    for index in range(counts):
        total, load = refs[:2]
        line = LineSum(inner, *refs[2:8])
        refs = refs[8:]
        lines.append(line)
        totals.append(total)
        for order in range(inner - 1):
            loads.append(
                pltpu.make_async_copy(
                    parts[index].at[line.targets[order]], line.sums.at[order], load.at[order]
                )
            )
        loads.append(
            pltpu.make_async_copy(parts[index].at[place], owns[index][0], load.at[inner - 1])
        )
    for copy in loads:
        copy.start()
    small.begin()
    hidden.begin()

    def load(index):
        for copy in loads[index * inner : (index + 1) * inner]:
            copy.wait()
        totals[index][...] = to_full(owns[index][0][...])

    def push_free(index, orders):
        for order in orders:
            lines[index].push_free(order)

    def push_rest(index, orders):
        for order in orders:
            lines[index].push_rest(order)

    def gather_part(index):
        lines[index].add_own(totals[index])
        owns[index][0][...] = to_low(totals[index][...])
        planes[index][0]()
        owns[index][1].start()

    every = range(inner - 1)
    small.step(0)
    small.step(1)
    load(0)
    push_free(0, every[:1])
    for count in range(2, small.steps() - 2):
        small.step(count)
    hidden.step(0)
    push_free(0, every[1:])
    for index in range(1, counts):
        load(index)
        push_free(index, every)
    push_rest(0, every[:1])
    for count in range(small.steps() - 2, small.steps()):
        small.step(count)
    owns[counts][0][...] = to_low(small_sum[...])
    planes[counts][0]()
    owns[counts][1].start()
    hidden.step(1)
    push_rest(0, every[1:])
    planes[counts][1]()
    hidden.step(2)
    hidden.step(3)
    planes[counts][2]()
    x = to_full(x_ref[...])
    scale = norm_scale(x)
    unit = x * scale
    scaled = hidden_sum[...] * gain_ref[...]
    mean = jnp.mean(scaled * unit, axis=1, keepdims=True)
    tokens_out[...] = to_low(mix_ref[...] + scale * (scaled - unit * mean))
    if counts > 1:
        push_rest(1, every[:1])
    gather_part(0)
    if counts > 1:
        push_rest(1, every[1:])
    for index in range(1, counts):
        planes[index - 1][1]()
        if index > 1:
            planes[index - 2][2]()
        gather_part(index)
        if index + 1 < counts:
            push_rest(index + 1, every)
    if counts > 1:
        planes[counts - 2][2]()
    planes[counts - 1][1]()
    planes[counts - 1][2]()
    for plane in planes:
        plane[3]()
    hidden.finish()
    small.finish()
    for line in lines:
        line.finish()
    for _, copy in owns:
        copy.wait()


def settle(hidden, small, x, mix, gain, parts, inner):
    _, _, rows, width = hidden.shape
    seq_devices = lax.axis_size("seq")
    anywhere = pl.BlockSpec(memory_space=pl.ANY)
    inside = pl.BlockSpec(memory_space=pltpu.VMEM)
    low = jnp.bfloat16
    sems = lambda *shape: pltpu.SemaphoreType.DMA(shape)
    small_rows, small_wide = small.shape[2:]
    shapes = [part.shape[1:] for part in parts] + [(small_rows, small_wide)]
    scratch = [
        pltpu.VMEM((rows, width), jnp.float32),
        pltpu.VMEM((small_rows, small_wide), jnp.float32),
    ]
    scratch += Reducer.scratch(1, rows, width)
    scratch += Reducer.scratch(inner, small_rows, small_wide)
    for shape in shapes:
        scratch += [pltpu.VMEM(shape, low), sems(14), sems(14), sems()]
    for shape in shapes[:-1]:
        scratch += [pltpu.VMEM(shape, jnp.float32), sems(inner)]
        scratch += LineSum.scratch(inner, *shape)
    return run(
        functools.partial(settle_kernel, inner, len(parts)),
        (hidden, small, x, mix, gain) + tuple(parts),
        in_specs=[anywhere] * 2 + [inside] * 3 + [anywhere] * len(parts),
        out_specs=[inside] + [anywhere] * len(shapes),
        out_shape=[jax.ShapeDtypeStruct((rows, width), low)]
        + [jax.ShapeDtypeStruct((seq_devices,) + shape, low) for shape in shapes],
        scratch=scratch,
        flips=FLIPS,
        inner=inner,
        micros=90,
        name="settle",
    )


def params_of(limit=VMEM_BYTES):
    return pltpu.CompilerParams(vmem_limit_bytes=limit)


def project_kernel(x_ref, gain_ref, w_ref, dt_ref, hidden_ref, gate_ref, rows_ref):
    x = to_full(x_ref[...])
    hidden = to_low(x * norm_scale(x) * gain_ref[...])
    hidden_ref[...] = hidden
    gate_width = gate_ref.shape[1]
    used = 2 * gate_width
    state = rows_ref.shape[1] - LANES - gate_width
    projected = dot_full(hidden, w_ref[:, :used])
    gate_ref[...] = projected[:, :gate_width]
    rows_ref[:, :gate_width] = to_low(projected[:, gate_width:])
    rows_ref[:, gate_width : gate_width + state] = to_low(
        dot_full(hidden, w_ref[:, w_ref.shape[1] - state :])
    )
    rows_ref[:, gate_width + state :] = to_low(dot_full(hidden, dt_ref[...]))


def project(x, gain, weights, dt_weights, gate_width, columns, freight=()):
    rows, width = x.shape
    columns = columns + LANES
    tile = 256
    block = lambda extent: pl.BlockSpec((tile, extent), lambda step: (step, 0))
    return run(
        project_kernel,
        (x, gain, weights, dt_weights,),
        grid=(rows // tile,),
        in_specs=[
            block(width), whole(gain.shape), whole(weights.shape), whole(dt_weights.shape)
        ],
        out_specs=[block(width), block(gate_width), block(columns - gate_width)],
        out_shape=[
            jax.ShapeDtypeStruct((rows, width), jnp.bfloat16),
            jax.ShapeDtypeStruct((rows, gate_width), jnp.float32),
            jax.ShapeDtypeStruct((rows, columns - gate_width), jnp.bfloat16),
        ],
        freight=freight,
        micros=11,
        name="project",
    )


def put_split(columns, rows):
    lane = iota_of((rows, LANES), 1)
    result = jnp.zeros((rows, LANES), jnp.float32)
    for place, column in enumerate(columns):
        high = to_full(to_low(column))
        result = jnp.where(lane == 2 * place, high, result)
        result = jnp.where(lane == 2 * place + 1, column - high, result)
    return to_low(result)


def mix_out_kernel(y_ref, gate_ref, gain_ref, packed_ref, out_ref, w_ref, sent, *scratch):
    width = w_ref.shape[1]
    rows = out_ref.shape[0]
    unpack_rows(packed_ref, w_ref, True)

    def make(_, block, place):
        at = pl.ds(pl.multiple_of(block * rows, rows), rows)
        gated = to_full(y_ref[at, :]) * jax.nn.silu(gate_ref[at, :])
        place[:, :width] = to_low(dot_full(to_low(gated * gain_ref[...]), w_ref[...]))
        squares = jnp.sum(gated * gated, axis=1, keepdims=True)
        place[:, width:] = put_split([squares], rows)

    Reducer(1, sent, out_ref, scratch, make).whole(lambda number: None)


def mix_out(y, gate, gain, weights, blocks, freight=()):
    rows, channels = y.shape
    width = weights.shape[2]
    tile = rows // blocks
    inside = pl.BlockSpec(memory_space=pltpu.VMEM)
    return run(
        mix_out_kernel,
        (y, gate, gain, weights),
        in_specs=[inside] * 4,
        out_specs=[inside],
        out_shape=[jax.ShapeDtypeStruct((tile, width + LANES), jnp.float32)],
        scratch=[
            pltpu.VMEM((channels, width), jnp.bfloat16),
            pltpu.VMEM((1, 4, tile, width + LANES), jnp.bfloat16),
        ]
        + Reducer.scratch(1, tile, width + LANES),
        freight=freight,
        flips=FLIPS,
        micros=35,
        name="mix_out",
    )


def mix_back_kernel(
    mix_ref,
    y_ref,
    gate_ref,
    gain_ref,
    packed_ref,
    dy_ref,
    dgate_ref,
    w_grad_ref,
    gain_grad_ref,
    total,
    w_ref,
):
    step = pl.program_id(0)
    width = w_ref.shape[1]

    @pl.when(step == 0)
    def _():
        unpack_rows(packed_ref, w_ref, True)
        total[...] = jnp.zeros_like(total)
        gain_grad_ref[...] = jnp.zeros_like(gain_grad_ref)

    mix = mix_ref[0, :, :width]
    extra = to_full(mix_ref[0, :, width:])
    share = extra[:, 0:1] + extra[:, 1:2]
    scale = extra[:, 2:3] + extra[:, 3:4]
    normed_grad = dot_lanes(mix, w_ref[...])
    y = to_full(y_ref[...])
    gate = gate_ref[...]
    sig = jax.nn.sigmoid(gate)
    act = gate * sig
    unit = y * act * scale
    gain = gain_ref[...]
    gain_grad_ref[0:1, :] += jnp.sum(normed_grad * unit, axis=0, keepdims=True)
    gated_grad = scale * (normed_grad * gain - unit * share)
    dy_ref[...] = to_low(gated_grad * act)
    dgate_ref[...] = to_low(gated_grad * y * sig * (1.0 + gate * (1.0 - sig)))
    total[...] += dot_rows(to_low(unit * gain), mix)

    @pl.when(step == pl.num_programs(0) - 1)
    def _():
        w_grad_ref[...] = to_low(total[...])


def mix_back(mix, y, gate, gain, weights, freight=()):
    blocks, tile, wide = mix.shape
    rows, channels = y.shape
    shape = (channels, weights.shape[2])
    block = pl.BlockSpec((tile, channels), lambda step: (step, 0))
    return run(
        mix_back_kernel,
        (mix, y, gate, gain, weights,),
        grid=(blocks,),
        in_specs=[
            pl.BlockSpec((1, tile, wide), lambda step: (step, 0, 0)),
            block,
            block,
            whole(gain.shape),
            whole(weights.shape),
        ],
        out_specs=[block, block, whole(shape), whole((8, channels))],
        out_shape=[
            jax.ShapeDtypeStruct((rows, channels), jnp.bfloat16),
            jax.ShapeDtypeStruct((rows, channels), jnp.bfloat16),
            jax.ShapeDtypeStruct(shape, jnp.bfloat16),
            jax.ShapeDtypeStruct((8, channels), jnp.float32),
        ],
        scratch=[pltpu.VMEM(shape, jnp.float32), pltpu.VMEM(shape, jnp.bfloat16)],
        freight=freight,
        micros=12,
        name="mix_back",
    )


def project_back_kernel(
    dgate_ref, drows_ref, hidden_ref, w_ref, dt_ref, part_ref, main_grad_ref, rest_grad_ref, total
):
    step = pl.program_id(0)

    @pl.when(step == 0)
    def _():
        total[...] = jnp.zeros_like(total)

    grads = jnp.concatenate([dgate_ref[...], drows_ref[...]], axis=1)
    main = 2 * dgate_ref.shape[1]
    columns = grads.shape[1] - LANES
    state_at = w_ref.shape[1] - (columns - main)
    part_ref[0] = to_low(
        dot_lanes(grads[:, :main], w_ref[:, :main])
        + dot_lanes(grads[:, main:columns], w_ref[:, state_at:])
        + dot_lanes(grads[:, columns:], dt_ref[...])
    )
    total[...] += dot_rows(hidden_ref[...], grads)

    @pl.when(step == pl.num_programs(0) - 1)
    def _():
        main_grad_ref[...] = to_low(total[:, :main])
        rest_grad_ref[...] = to_low(total[:, main:])
        by_gain = jnp.sum(total[:, :main] * to_full(w_ref[:, :main]), axis=1, keepdims=True)
        by_gain += jnp.sum(
            total[:, main:columns] * to_full(w_ref[:, state_at:]), axis=1, keepdims=True
        )
        by_gain += jnp.sum(total[:, columns:] * to_full(dt_ref[...]), axis=1, keepdims=True)
        rest = rest_grad_ref.shape[1]
        lane = iota_of((rest_grad_ref.shape[0], LANES), 1)
        rest_grad_ref[:, rest - LANES :] = to_low(
            jnp.where(lane == LANES - 1, by_gain, total[:, columns:])
        )


def project_back(dgate, drows, hidden, weights, dt_weights, blocks, freight=()):
    rows, width = hidden.shape
    tile = rows // blocks
    main = 2 * dgate.shape[1]
    rest = dgate.shape[1] + drows.shape[1] - main
    block = lambda extent: pl.BlockSpec((tile, extent), lambda step: (step, 0))
    return run(
        project_back_kernel,
        (dgate, drows, hidden, weights, dt_weights,),
        grid=(blocks,),
        in_specs=[
            block(dgate.shape[1]),
            block(drows.shape[1]),
            block(width),
            whole(weights.shape),
            whole(dt_weights.shape),
        ],
        out_specs=[
            pl.BlockSpec((1, tile, width), lambda step: (step, 0, 0)),
            whole((width, main)),
            whole((width, rest)),
        ],
        out_shape=[
            jax.ShapeDtypeStruct((blocks, tile, width), jnp.bfloat16),
            jax.ShapeDtypeStruct((width, main), jnp.bfloat16),
            jax.ShapeDtypeStruct((width, rest), jnp.bfloat16),
        ],
        scratch=[pltpu.VMEM((width, main + rest), jnp.float32)],
        freight=freight,
        micros=25,
        name="project_back",
    )


def unpack_rows(packed_ref, held_ref, first):
    blocks, both, _ = packed_ref.shape
    fine = held_ref.shape[0] // blocks
    start = 0 if first else both - fine
    for block in range(blocks):
        held_ref[block * fine : (block + 1) * fine] = packed_ref[block, start : start + fine]


def shared_kernel(
    rows_ref,
    grad_ref,
    up_ref,
    down_ref,
    res_ref,
    back_ref,
    up_grad_ref,
    down_grad_ref,
    up_sum,
    down_sum,
    down_held,
):
    step = pl.program_id(0)

    @pl.when(step == 0)
    def _():
        up_sum[...] = jnp.zeros_like(up_sum)
        down_sum[...] = jnp.zeros_like(down_sum)
        unpack_rows(down_ref, down_held, False)

    hidden, width = down_held.shape
    rows = rows_ref[0, :, :width]
    grad = grad_ref[0]
    joined = dot_full(rows, up_ref[...])
    gate, up = joined[:, :hidden], joined[:, hidden:]
    sig = jax.nn.sigmoid(gate)
    act = gate * sig
    acted = to_low(act * up)
    res_ref[0] = to_low(dot_full(acted, down_held[...]))
    down_sum[...] += dot_rows(acted, grad)
    act_grad = dot_lanes(grad, down_held[...])
    joined_grad = to_low(
        jnp.concatenate(
            [act_grad * up * sig * (1.0 + gate * (1.0 - sig)), act_grad * act], axis=1
        )
    )
    up_sum[...] += dot_rows(rows, joined_grad)
    back_ref[0] = to_low(dot_lanes(joined_grad, up_ref[...]))

    @pl.when(step == pl.num_programs(0) - 1)
    def _():
        up_grad_ref[...] = to_low(up_sum[...])
        down_grad_ref[...] = to_low(down_sum[...])


def shared_expert(rows, grad, up, up_at, down, hidden, blocks, inner, freight=()):
    _, tile, wide = rows.shape
    width = down.shape[2]
    down_shape = (hidden, width)
    up_shape = (width, 2 * hidden)
    block = pl.BlockSpec((1, tile, width), lambda step: (step, 0, 0))
    low = jnp.bfloat16
    own = lambda extent: pl.BlockSpec(
        (1, tile, extent), lambda step: (own_shard_group(inner)[0] * blocks + step, 0, 0)
    )
    return run(
        shared_kernel,
        (rows, grad, up, down),
        grid=(blocks,),
        in_specs=[
            own(wide),
            own(width),
            pl.BlockSpec((width, up_shape[1]), lambda step: (0, up_at // up_shape[1])),
            whole(down.shape),
        ],
        out_specs=[block, block, whole(up_shape), whole(down_shape)],
        out_shape=[
            jax.ShapeDtypeStruct((blocks, tile, width), low),
            jax.ShapeDtypeStruct((blocks, tile, width), low),
            jax.ShapeDtypeStruct(up_shape, low),
            jax.ShapeDtypeStruct(down_shape, low),
        ],
        scratch=[
            pltpu.VMEM(up_shape, jnp.float32),
            pltpu.VMEM(down_shape, jnp.float32),
            pltpu.VMEM(down_shape, low),
        ],
        freight=freight,
        micros=18,
        name="shared_expert",
    )


def dispatch_kernel(
    rows_ref, grad_ref, x_ref, g_ref, picks_ref, *, top_count, slots, own_first
):
    per_device = x_ref.shape[0]
    together, tok_rows, _ = rows_ref.shape
    width = g_ref.shape[2]
    wide = width + LANES
    taken = per_device * slots
    lane = iota_of((tok_rows, LANES), 1)
    named = (lane >= 2 * top_count) & (lane < 3 * top_count)
    before = iota_of((tok_rows, tok_rows), 0) > iota_of((tok_rows, tok_rows), 1)
    before = to_low(jnp.where(before, 1.0, 0.0))
    first = own_first()
    for index in range(together):
        extra = to_full(rows_ref[index, :, width:wide])
        member = jnp.zeros((tok_rows, LANES), jnp.float32)
        for expert in range(per_device):
            own = (first + expert).astype(jnp.float32)
            hit = jnp.sum(jnp.where(named & (extra == own), 1.0, 0.0), axis=1, keepdims=True)
            member = jnp.where(lane // slots == expert, hit, member)
        ranks = dot_full(before, to_low(member))
        picks = jnp.where(
            (ranks == to_full(lane % slots)) & (member > 0.0), 1.0, 0.0
        ).astype(jnp.bfloat16)
        picks_ref[index] = picks
        rows = to_low(dot_rows(picks[:, :taken], rows_ref[index]))
        grads = to_low(dot_rows(picks[:, :taken], grad_ref[index]))
        start = index * slots
        for expert in range(per_device):
            span = slice(expert * slots, (expert + 1) * slots)
            x_ref[expert, start : start + slots] = rows[span]
            g_ref[expert, start : start + slots] = grads[span]


def dispatch(rows, grad, per_device, top_count, slots, own_first, freight=()):
    blocks, tok_rows, wide = rows.shape
    width = grad.shape[2]
    together = 4
    block = lambda extent: pl.BlockSpec((together, tok_rows, extent), lambda step: (step, 0, 0))
    taken = lambda extent: pl.BlockSpec(
        (per_device, together * slots, extent), lambda step: (0, step, 0)
    )
    return run(
        functools.partial(
            dispatch_kernel, top_count=top_count, slots=slots, own_first=own_first
        ),
        (rows, grad),
        grid=(blocks // together,),
        in_specs=[block(wide), block(width)],
        out_specs=[taken(width + LANES), taken(width), block(LANES)],
        out_shape=[
            jax.ShapeDtypeStruct((per_device, blocks * slots, width + LANES), jnp.bfloat16),
            jax.ShapeDtypeStruct((per_device, blocks * slots, width), jnp.bfloat16),
            jax.ShapeDtypeStruct((blocks, tok_rows, LANES), jnp.bfloat16),
        ],
        freight=freight,
        micros=30,
        name="dispatch",
    )


def experts_kernel(
    depart, arrive, targets, *refs, count, per_device, top_count, own_first, inner, doubles, outgoing
):
    x_ref, g_ref = refs[:2]
    total = 2 * count * per_device
    pieces, refs = refs[2 : 2 + total], refs[2 + total :]
    seconds, refs = dict(zip(doubles, refs[: len(doubles)])), refs[len(doubles) :]
    res_ref, dx_ref = refs[:2]
    outs = refs[2 : 2 + total]
    up_held, down_held, up_sum, down_sum, up_low, down_low, sems = refs[2 + total :]
    own_place, _ = own_shard_group(inner)
    expert, step = pl.program_id(0), pl.program_id(1)
    steps = pl.num_programs(1)
    slot = lax.rem(expert, 2)
    width, double = up_held.shape[1:]
    hidden = double // 2
    tile = x_ref.shape[1]

    def parts(which, up, down):
        result = []
        for shift in range(count):
            from_place = lax.rem(own_place + count - shift, count)
            for kind, held in enumerate((up, down)):
                extent = held.shape[0] // count
                start = pl.multiple_of(from_place * extent, extent)
                number = (shift * per_device + which) * 2 + kind
                result.append((number, held.at[pl.ds(start, extent)], (shift, kind)))
        return result

    def fetch(which, action):
        half = which % 2
        for number, held, at in parts(which, up_held.at[half], down_held.at[half]):
            sem = sems.at[half, at[0], at[1]]
            piece = pieces[number]
            if len(piece.shape) == 3:
                piece = piece.at[own_place * per_device + which]
            if number in seconds:
                early = among(own_place, doubles[number])
                pl.when(early)(
                    lambda: action(pltpu.make_async_copy(piece, held, sem))
                )
                pl.when(jnp.logical_not(early))(
                    lambda: action(pltpu.make_async_copy(seconds[number], held, sem))
                )
            else:
                action(pltpu.make_async_copy(piece, held, sem))

    begin_copy = lambda copy: copy.start()
    end_copy = lambda copy: copy.wait()

    for which in range(per_device):

        @pl.when((step == 0) & (expert == which))
        def _():
            if which == 0:
                fetch(0, begin_copy)
            if which == 1:
                depart()
            fetch(which, end_copy)
            if which + 1 < per_device:
                fetch(which + 1, begin_copy)

    @pl.when(step == 0)
    def _():
        up_sum[...] = jnp.zeros_like(up_sum)
        down_sum[...] = jnp.zeros_like(down_sum)

    up, down = up_held.at[slot], down_held.at[slot]
    rows = x_ref[0, :, :width]
    extra = to_full(x_ref[0, :, width:])
    lane = iota_of((tile, LANES), 1)
    own = own_first() + expert
    hits = jnp.where((lane < 3 * top_count) & (extra == own.astype(jnp.float32)), 1.0, 0.0)
    gate_slot = jnp.zeros((tile, 1), jnp.float32)
    for route in range(top_count):
        place = 2 * top_count + route
        value = extra[:, 2 * route : 2 * route + 1] + extra[:, 2 * route + 1 : 2 * route + 2]
        gate_slot = gate_slot + hits[:, place : place + 1] * value
    joined = dot_full(rows, up[...])
    gate, lift = joined[:, :hidden], joined[:, hidden:]
    sig = jax.nn.sigmoid(gate)
    act = gate * sig
    acted = to_low(act * lift)
    res = to_low(dot_full(acted, down[...]))
    grads = g_ref[0]
    wide_grads = to_full(grads)
    wide_res = to_full(res)
    gate_grad = jnp.sum(wide_res * wide_grads, axis=1, keepdims=True)
    res_ref[0] = to_low(wide_res * gate_slot)
    weighted = to_low(wide_grads * gate_slot)
    act_grad = dot_lanes(weighted, down[...])
    down_sum[...] += dot_rows(acted, weighted)
    joined_grad = to_low(
        jnp.concatenate(
            [act_grad * lift * sig * (1.0 + gate * (1.0 - sig)), act_grad * act], axis=1
        )
    )
    dx_ref[0, :, :width] = to_low(dot_lanes(joined_grad, up[...]))
    high = to_full(to_low(gate_grad))
    half = LANES // 2
    dx_ref[0, :, width:] = to_low(
        jnp.where(lane == own, high, 0.0) + jnp.where(lane == own + half, gate_grad - high, 0.0)
    )
    up_sum[...] += dot_rows(rows, joined_grad)

    for which in range(per_device):

        @pl.when((step == steps - 1) & (expert == which))
        def _():
            up_low[...] = to_low(up_sum[...])
            down_low[...] = to_low(down_sum[...])
            copies = [
                pltpu.make_async_copy(held, outs[number], sems.at[2, at[0], at[1]])
                for number, held, at in parts(which, up_low, down_low)
            ]
            for copy in copies:
                copy.start()
            for copy in copies:
                copy.wait()

    if outgoing:

        @pl.when((step == steps - 1) & (expert == per_device - 1))
        def _():
            arrive()


def experts(x, g, pieces, hidden, top_count, own_first, inner, doubles=(), outgoing=()):
    per_device, rows, wide = x.shape
    width = g.shape[2]
    count = len(pieces) // per_device // 2
    low = jnp.bfloat16
    shapes = [jax.ShapeDtypeStruct(piece.shape[-2:], low) for piece in pieces]
    freight = [Parcel(shapes[key], shift, inner, output=2 + key) for key, shift in outgoing]
    others = [other for _, other, _ in doubles]
    double = 2 * hidden
    tile = min(rows, 256)
    block = lambda extent: pl.BlockSpec((1, tile, extent), lambda e, step: (e, step, 0))
    anywhere = pl.BlockSpec(memory_space=pl.ANY)
    low = jnp.bfloat16
    outs = run(
        functools.partial(
            experts_kernel,
            count=count,
            per_device=per_device,
            top_count=top_count,
            own_first=own_first,
            inner=inner,
            doubles={number: places for number, _, places in doubles},
            outgoing=outgoing,
        ),
        (x, g) + tuple(pieces) + tuple(others),
        grid=(per_device, rows // tile),
        in_specs=[block(wide), block(width)] + [anywhere] * (len(pieces) + len(others)),
        out_specs=[block(width), block(wide)] + [anywhere] * len(shapes),
        out_shape=[
            jax.ShapeDtypeStruct((per_device, rows, width), low),
            jax.ShapeDtypeStruct((per_device, rows, wide), low),
        ]
        + shapes,
        scratch=[
            pltpu.VMEM((2, width, double), low),
            pltpu.VMEM((2, hidden, width), low),
            pltpu.VMEM((width, double), jnp.float32),
            pltpu.VMEM((hidden, width), jnp.float32),
            pltpu.VMEM((width, double), low),
            pltpu.VMEM((hidden, width), low),
            pltpu.SemaphoreType.DMA((3, count, 2)),
        ],
        freight=freight,
        inner=inner if freight else 1,
        late=True,
        micros=45,
        name="experts",
    )
    sent = outs.pop() if freight else []
    return outs[0], outs[1], outs[2:], sent


def combine_kernel(
    picks_ref, res_ref, dx_ref, sres_ref, sback_ref, out_ref, back_ref, *, slots, inner
):
    step = pl.program_id(0)
    together, _, width = out_ref.shape
    per_device = res_ref.shape[0]
    blocks = sres_ref.shape[0]
    place, _ = own_shard_group(inner)
    for index in range(together):
        picks = picks_ref[index, :, : per_device * slots]
        start = index * slots
        stacked = lambda ref: jnp.concatenate(
            [ref[expert, start : start + slots] for expert in range(per_device)], axis=0
        )
        out_ref[index] = to_low(dot_full(picks, stacked(res_ref)))
        back_ref[index] = to_low(dot_full(picks, stacked(dx_ref)))

    @pl.when(lax.div(step * together, blocks) == place)
    def _():
        first = lax.rem(step * together, blocks)
        for index in range(together):
            out_ref[index] = to_low(to_full(out_ref[index]) + to_full(sres_ref[first + index]))
            back_ref[index, :, :width] = to_low(
                to_full(back_ref[index, :, :width]) + to_full(sback_ref[first + index])
            )


def combine(picks, res, dx, shared_res, shared_back, inner, freight=()):
    blocks, tok_rows, _ = picks.shape
    per_device, rows, width = res.shape
    slots = rows // blocks
    together = 4
    block = lambda extent: pl.BlockSpec((together, tok_rows, extent), lambda step: (step, 0, 0))
    taken = lambda extent: pl.BlockSpec(
        (per_device, together * slots, extent), lambda step: (0, step, 0)
    )
    return run(
        functools.partial(combine_kernel, slots=slots, inner=inner),
        (picks, res, dx, shared_res, shared_back),
        grid=(blocks // together,),
        in_specs=[
            block(LANES),
            taken(width),
            taken(width + LANES),
            whole(shared_res.shape),
            whole(shared_back.shape),
        ],
        out_specs=[block(width), block(width + LANES)],
        out_shape=[
            jax.ShapeDtypeStruct((blocks, tok_rows, width), jnp.bfloat16),
            jax.ShapeDtypeStruct((blocks, tok_rows, width + LANES), jnp.bfloat16),
        ],
        freight=freight,
        micros=30,
        name="combine",
    )


def assemble_kernel(
    main_ref, shared_in_ref, small_ref, rows_ref, w_in_ref, shared_ref, out_ref, down_ref
):
    seq_devices, rows, double = main_ref.shape
    channels = double // 2
    for device in range(seq_devices):
        for target, source in ((w_in_ref, main_ref), (shared_ref, shared_in_ref)):
            extent = source.shape[2] // 2
            for side in range(2):
                start = (side * seq_devices + device) * extent
                target[:, start : start + extent] = to_full(
                    source[device, :, side * extent : (side + 1) * extent]
                )
    start = 2 * seq_devices * channels
    w_in_ref[:, start:] = to_full(small_ref[0, :rows, : w_in_ref.shape[1] - start])
    halves, _, out_rows, _ = out_ref.shape
    down_rows = down_ref.shape[2]
    for half in range(halves):
        at = half * (out_rows + down_rows)
        out_ref[half, 0] = to_full(rows_ref[0, at : at + out_rows])
        down_ref[half, 0] = to_full(rows_ref[0, at + out_rows : at + out_rows + down_rows])


def assemble(main, shared, small, rows, columns, shared_columns, out_rows, down_rows, halves):
    seq_devices, depth_rows, _ = main.shape
    tile = depth_rows // seq_devices
    width = rows.shape[2]
    out_fine = out_rows // halves // seq_devices
    down_fine = down_rows // halves // seq_devices
    flat = lambda extent: pl.BlockSpec((tile, extent), lambda step: (step, 0))
    fine = lambda extent: pl.BlockSpec(
        (halves, 1, extent, width), lambda step: (0, step, 0, 0)
    )
    full = jnp.float32
    results = pl.pallas_call(
        assemble_kernel,
        grid=(seq_devices,),
        in_specs=[
            pl.BlockSpec((seq_devices, tile, main.shape[2]), lambda step: (0, step, 0)),
            pl.BlockSpec((seq_devices, tile, shared.shape[2]), lambda step: (0, step, 0)),
            pl.BlockSpec((1,) + small.shape[1:], lambda step: (step, 0, 0)),
            pl.BlockSpec((1,) + rows.shape[1:], lambda step: (step, 0, 0)),
        ],
        out_specs=[flat(columns), flat(shared_columns), fine(out_fine), fine(down_fine)],
        out_shape=[
            jax.ShapeDtypeStruct((depth_rows, columns), full),
            jax.ShapeDtypeStruct((depth_rows, shared_columns), full),
            jax.ShapeDtypeStruct((halves, seq_devices, out_fine, width), full),
            jax.ShapeDtypeStruct((halves, seq_devices, down_fine, width), full),
        ],
        compiler_params=params_of(),
        cost_estimate=cost_of(10),
        name="assemble",
    )(main, shared, small, rows)
    return results[0], results[1], results[2].reshape(-1, width), results[3].reshape(-1, width)


def collect_kernel(place_ref, *refs):
    del place_ref
    step = pl.program_id(0)
    up_ref, down_ref = refs[-2:]
    for order in range(len(refs) // 2 - 1):

        @pl.when(step == order)
        def _():
            up_ref[0] = to_full(refs[2 * order][...])
            down_ref[0] = to_full(refs[2 * order + 1][...])


def collect(place, pieces, per_device):
    count = len(pieces) // 2
    up, down = pieces[0].shape, pieces[1].shape

    def here(step, place):
        shift, expert = lax.div(step, per_device), lax.rem(step, per_device)
        return (
            lax.rem(place[0] + shift, count // per_device) * per_device + expert, 0, 0
        )

    still = lambda shape: pl.BlockSpec(shape, lambda step, place: (0, 0))
    return pl.pallas_call(
        collect_kernel,
        grid_spec=pltpu.PrefetchScalarGridSpec(
            num_scalar_prefetch=1,
            grid=(count,),
            in_specs=[still(up), still(down)] * count,
            out_specs=[pl.BlockSpec((1,) + up, here), pl.BlockSpec((1,) + down, here)],
        ),
        out_shape=[
            jax.ShapeDtypeStruct((count,) + up, jnp.float32),
            jax.ShapeDtypeStruct((count,) + down, jnp.float32),
        ],
        compiler_params=params_of(),
        cost_estimate=cost_of(12),
        name="collect",
    )(place, *pieces)


def route_hits(routes, route, lane):
    return lane == routes[:, route : route + 1]


def token_forward_kernel(
    mixed_ref, x_ref, gain_ref, router_ref, routes_ref, after_ref, wide_ref, gates_ref, *, inner_width, top_count
):
    width = x_ref.shape[1]
    rows = x_ref.shape[0]
    squares = mixed_ref[:, width : width + 1] + mixed_ref[:, width + 1 : width + 2]
    scale = lax.rsqrt(squares / inner_width + EPSILON)
    after = to_full(x_ref[...]) + mixed_ref[:, :width] * scale
    after_ref[...] = after
    moe_in = to_low(after * norm_scale(after) * gain_ref[...])
    wide_ref[:, :width] = moe_in
    logits = dot_full(moe_in, router_ref[...])
    lane = iota_of((rows, LANES), 1)
    routes = routes_ref[...]
    picked = [
        jnp.sum(jnp.where(route_hits(routes, k, lane), logits, 0.0), axis=1, keepdims=True)
        for k in range(top_count)
    ]
    largest = functools.reduce(jnp.maximum, picked)
    powers = [jnp.exp(value - largest) for value in picked]
    total = sum(powers)
    gates = jnp.zeros((rows, LANES), jnp.float32)
    extra = jnp.zeros((rows, LANES), jnp.float32)
    for k in range(top_count):
        value = powers[k] / total
        high = to_full(to_low(value))
        gates = jnp.where(lane == k, value, gates)
        extra = jnp.where(lane == 2 * k, high, extra)
        extra = jnp.where(lane == 2 * k + 1, value - high, extra)
        extra = jnp.where(lane == 2 * top_count + k, to_full(routes[:, k : k + 1]), extra)
    gates_ref[...] = jnp.where(lane == top_count, scale, gates)
    wide_ref[:, width:] = to_low(extra)


def token_forward(mixed, x, gain, router, routes, inner_width, top_count):
    rows, width = x.shape
    arrays = (mixed, x, gain, router, routes)
    return pl.pallas_call(
        functools.partial(
            token_forward_kernel, inner_width=inner_width, top_count=top_count
        ),
        in_specs=[whole(array.shape) for array in arrays],
        out_specs=[whole((rows, width)), whole((rows, width + LANES)), whole((rows, LANES))],
        out_shape=[
            jax.ShapeDtypeStruct((rows, width), jnp.float32),
            jax.ShapeDtypeStruct((rows, width + LANES), jnp.bfloat16),
            jax.ShapeDtypeStruct((rows, LANES), jnp.float32),
        ],
        compiler_params=params_of(),
        cost_estimate=cost_of(5),
        name="token_forward",
    )(*arrays)


def token_back_kernel(
    back_ref,
    mixed_ref,
    after_ref,
    wide_ref,
    gates_ref,
    grad_ref,
    gain_ref,
    router_ref,
    routes_ref,
    mix_ref,
    mix_wide_ref,
    router_grad_ref,
    gain_grad_ref,
    *,
    inner_width,
    top_count,
):
    rows, width = grad_ref.shape
    lane = iota_of((rows, LANES), 1)
    half = LANES // 2
    routes = routes_ref[...]
    gates = gates_ref[...]
    all_grads = back_ref[:, width:]
    values = [gates[:, k : k + 1] for k in range(top_count)]
    grads = [
        jnp.sum(
            jnp.where(
                route_hits(routes, k, lane) | route_hits(routes, k, lane - half), all_grads, 0.0
            ),
            axis=1,
            keepdims=True,
        )
        for k in range(top_count)
    ]
    common = sum(value * grad for value, grad in zip(values, grads))
    logit_grad = jnp.zeros((rows, LANES), jnp.float32)
    for k in range(top_count):
        logit_grad = jnp.where(
            route_hits(routes, k, lane), values[k] * (grads[k] - common), logit_grad
        )
    logit_grad = to_low(logit_grad)
    router_grad_ref[...] = to_low(dot_rows(wide_ref[:, :width], logit_grad))
    moe_grad = back_ref[:, :width] + dot_lanes(logit_grad, router_ref[...])
    after = after_ref[...]
    scale = norm_scale(after)
    unit = after * scale
    gain_grad_ref[...] = jnp.broadcast_to(
        jnp.sum(moe_grad * unit, axis=0, keepdims=True), (8, width)
    )
    scaled = moe_grad * gain_ref[...]
    mean = jnp.mean(scaled * unit, axis=1, keepdims=True)
    mix = to_full(grad_ref[...]) + scale * (scaled - unit * mean)
    mix_ref[...] = mix
    mix_low = to_low(mix)
    mix_wide_ref[:, :width] = mix_low
    mix_scale = gates[:, top_count : top_count + 1]
    share = jnp.sum(to_full(mix_low) * mixed_ref[:, :width], axis=1, keepdims=True)
    mix_wide_ref[:, width:] = put_split([share * mix_scale / inner_width, mix_scale], rows)


def token_back(back, mixed, after, wide, gates, grad, gain, router, routes, inner_width, top_count):
    rows, width = grad.shape
    arrays = (back, mixed, after, wide, gates, grad, gain, router, routes)
    return pl.pallas_call(
        functools.partial(token_back_kernel, inner_width=inner_width, top_count=top_count),
        in_specs=[whole(array.shape) for array in arrays],
        out_specs=[
            whole((rows, width)),
            whole((rows, width + LANES)),
            whole((width, LANES)),
            whole((8, width)),
        ],
        out_shape=[
            jax.ShapeDtypeStruct((rows, width), jnp.float32),
            jax.ShapeDtypeStruct((rows, width + LANES), jnp.bfloat16),
            jax.ShapeDtypeStruct((width, LANES), jnp.bfloat16),
            jax.ShapeDtypeStruct((8, width), jnp.float32),
        ],
        compiler_params=params_of(),
        cost_estimate=cost_of(6),
        name="token_back",
    )(*arrays)


ROWS_AFTER = 16


def pack_kernel(
    rest_ref, router_ref, conv_ref, head_ref, gate_ref, moe_ref, out_ref, wide, *, inner_width, experts, heads
):
    part = lax.axis_index("seq")
    inner, seq_devices, block_rows, columns = out_ref.shape
    depth = block_rows - ROWS_AFTER
    state = columns - LANES
    lane = iota_of((rest_ref.shape[0], LANES), 1)
    last = to_full(rest_ref[:, state:])
    steps = jnp.where(lane < heads, last, 0.0)
    extra = to_full(router_ref[...]) + pltpu.roll(steps, experts + heads * part, 1)
    extra = to_low(jnp.where(lane == LANES - 1, last, extra))
    for shard in range(inner):
        for device in range(seq_devices):
            start = (shard * seq_devices + device) * depth
            out_ref[shard, device, :depth, :state] = rest_ref[start : start + depth, :state]
            out_ref[shard, device, :depth, state:] = extra[start : start + depth]
    channels = gate_ref.shape[1]
    others = conv_ref.shape[1] - channels
    wide[...] = jnp.zeros_like(wide)
    own = pl.ds(pl.multiple_of(part * channels, channels), channels)
    wide[:8, own] = conv_ref[:, :channels]
    wide[:8, inner_width : inner_width + others] = conv_ref[:, channels:]
    wide[8:, own] = gate_ref[...]
    convs = wide[:8, :]
    gates = wide[8:, :]
    per_conv = (inner_width + others) // inner
    per_gate = inner_width // inner
    width = moe_ref.shape[1] // inner
    row = iota_of((ROWS_AFTER, columns), 0)
    blank = jnp.zeros((1, columns), jnp.float32)
    head_lane = iota_of((8, LANES), 1)
    values = jnp.where(head_lane < heads, head_ref[...], 0.0)
    values = [
        jnp.concatenate([pltpu.roll(values, heads * part, 1)[k : k + 1], blank[:, LANES:]], axis=1)
        for k in range(3)
    ]
    moe = moe_ref[...]

    def pieces(rows, at, start, extent):
        count = -(-extent // columns)
        return [rows[at : at + 1, start + k * columns : start + (k + 1) * columns] for k in range(count)]

    for shard in range(inner):
        for device in range(seq_devices):
            if device < 5:
                lines = pieces(convs, device, shard * per_conv, per_conv)
            elif device == 5:
                lines = pieces(gates, 0, shard * per_gate, per_gate)
            elif device == 6:
                lines = values
            else:
                lines = [moe[:1, shard * width : (shard + 1) * width]]
                lines = [jnp.concatenate([lines[0], blank[:, width:]], axis=1) if width < columns else lines[0]]
            tile = jnp.zeros((ROWS_AFTER, columns), jnp.float32)
            for k, line in enumerate(lines):
                tile = jnp.where(row == k, line, tile)
            out_ref[shard, device, depth:] = to_low(tile)


def pack(rest, router, conv, head, gate, moe, inner, seq_devices, inner_width, experts, heads):
    depth = rest.shape[0] // inner // seq_devices
    columns = rest.shape[1]
    arrays = (rest, router, conv, head, gate, moe)
    reach = inner_width + conv.shape[1] - gate.shape[1] + columns
    return pl.pallas_call(
        functools.partial(pack_kernel, inner_width=inner_width, experts=experts, heads=heads),
        in_specs=[whole(array.shape) for array in arrays],
        out_specs=whole((inner, seq_devices, depth + ROWS_AFTER, columns)),
        out_shape=jax.ShapeDtypeStruct(
            (inner, seq_devices, depth + ROWS_AFTER, columns), jnp.bfloat16
        ),
        scratch_shapes=[pltpu.VMEM((16, -(-reach // LANES) * LANES), jnp.float32)],
        compiler_params=params_of(),
        cost_estimate=cost_of(3),
        name="pack",
    )(*arrays)


def rows_to_send(weights, part):
    seq_devices = lax.axis_size("seq")
    halves = max(1, seq_devices // lax.axis_size("shard"))
    mine = []
    for weight in weights:
        view = weight.reshape(halves, seq_devices, -1, weight.shape[1])
        mine.append(lax.dynamic_index_in_dim(view, part, 1, keepdims=False))
    return jnp.concatenate(mine, axis=1).reshape(-1, weights[0].shape[1])


def rows_by_owner(joined):
    seq_devices = lax.axis_size("seq")
    return joined.reshape(seq_devices, -1, joined.shape[2])


def rows_of_owner(taken, weights):
    seq_devices = lax.axis_size("seq")
    halves = max(1, seq_devices // lax.axis_size("shard"))
    fine_rows = [weight.shape[0] // halves // seq_devices for weight in weights]
    width = taken.shape[2]
    taken = taken.reshape(seq_devices, -1, sum(fine_rows), width).transpose(1, 0, 2, 3)
    results, start = [], 0
    for fine in fine_rows:
        results.append(taken[:, :, start : start + fine].reshape(-1, width))
        start += fine
    return results


def rows_from_owner(grads):
    seq_devices = lax.axis_size("seq")
    shard_devices = lax.axis_size("shard")
    width = grads[0].shape[1]
    turns = shard_devices * max(1, seq_devices // shard_devices) // seq_devices
    pieces = [
        grad.reshape(turns, seq_devices, -1, width).transpose(1, 0, 2, 3) for grad in grads
    ]
    return jnp.concatenate(pieces, axis=2).reshape(seq_devices, -1, width)


def rows_of_shard(joined, weights):
    seq_devices = lax.axis_size("seq")
    halves = max(1, seq_devices // lax.axis_size("shard"))
    fine_rows = [weight.shape[0] // halves // seq_devices for weight in weights]
    width = joined.shape[2]
    spread = joined.reshape(seq_devices, halves, -1, width).transpose(1, 0, 2, 3)
    results, start = [], 0
    for fine in fine_rows:
        results.append(to_full(spread[:, :, start : start + fine]).reshape(-1, width))
        start += fine
    return results


def inner_groups(inner):
    count = lax.axis_size("shard")
    return [list(range(start, start + inner)) for start in range(0, count, inner)]


def outer_groups(inner):
    count = lax.axis_size("shard")
    return [list(range(start, count, inner)) for start in range(inner)]


def stacked_pieces(received, place, inner):
    own = jnp.stack(received)[lax.rem(place + inner - jnp.arange(inner), inner)]
    joined = lax.all_gather(own, "shard", axis_index_groups=outer_groups(inner))
    return joined.reshape(-1, joined.shape[-1])


def split_piece(grad, shift, place, inner):
    outer = lax.axis_size("shard") // inner
    rows = grad.reshape(outer, inner, -1, grad.shape[1])
    here = lax.rem(place + inner - shift, inner)
    return lax.psum_scatter(
        lax.dynamic_index_in_dim(rows, here, 1, keepdims=False),
        "shard",
        axis_index_groups=outer_groups(inner),
    )


def local(
    tokens,
    out_grad,
    deal_order,
    lengths,
    routes,
    norm_in,
    w_in,
    w_dt,
    conv_w,
    conv_b,
    dt_bias,
    a_log,
    d_skip,
    norm_gate,
    w_out,
    norm_moe,
    w_router,
    w_shared,
    w_shared_down,
    w_experts,
    w_experts_down,
):
    seq_devices = lax.axis_size("seq")
    shard_devices = lax.axis_size("shard")
    part = lax.axis_index("seq")
    shard = lax.axis_index("shard")
    inner = min(shard_devices, INNER)
    outer = shard_devices // inner
    place = lax.rem(shard, inner)
    _, tok_rows, width = tokens.shape
    group_rows = tok_rows * seq_devices
    inner_width = w_out.shape[0] * shard_devices
    channels = inner_width // seq_devices
    head_total = w_dt.shape[1]
    heads = head_total // seq_devices
    shared_width = w_shared_down.shape[0] * shard_devices
    shared_part = shared_width // seq_devices
    depth_rows = w_in.shape[0]
    expert_total = w_router.shape[1]
    local_experts, _, double = w_experts.shape
    hidden = double // 2
    hidden_rows = w_experts_down.shape[1]
    top_count = routes.shape[2]
    per_device = local_experts // inner
    blocks = inner * seq_devices
    COLLECTIVES.clear()

    def own_columns(array, start, extent):
        return lax.dynamic_slice_in_dim(array, start + part * extent, extent, 1)

    def own_rows(array, extent):
        return lax.dynamic_slice_in_dim(array, part * extent, extent, 0)

    row_wide = -(-max(conv_w.shape[0], norm_gate.shape[0]) // LANES) * LANES
    row_of = lambda piece: jnp.pad(piece, ((0, 0), (0, row_wide - piece.shape[1])))
    vectors = [conv_b, norm_gate, norm_in, norm_moe, dt_bias, a_log, d_skip]
    flat = jnp.concatenate([row_of(conv_w.T)] + [row_of(vector[None]) for vector in vectors])
    by_depth = jnp.concatenate(
        [
            w_router,
            own_columns(w_dt, 0, heads),
            jnp.zeros((depth_rows, LANES - expert_total - heads), jnp.bfloat16),
        ],
        axis=1,
    )
    weights_of = (w_experts, w_experts_down)

    def own_first():
        here, _ = own_shard_group(inner)
        return lax.axis_index("seq") * local_experts + here * per_device

    pieces = {
        (0, expert, kind): weights_of[kind] for expert in range(per_device) for kind in range(2)
    }

    last = inner - 1
    early_from = {1: range(inner // 2), last: range(inner - inner // 2, inner)} if outer == 1 else {}
    early = {}

    def parcels(*keys, first=False):
        result = []
        for shift, expert, kind in keys:
            senders = None
            if shift in early_from:
                senders = [
                    place for place in range(inner) if (place in early_from[shift]) == first
                ]
            result.append(
                Parcel(
                    weights_of[kind],
                    shift,
                    inner,
                    lambda to, expert=expert: to * per_device + expert,
                    senders=senders,
                )
            )
        return result

    def unpack(keys, arrays):
        pieces.update(zip(keys, arrays))


    in_width = 2 * channels + w_in.shape[1] - 2 * inner_width
    if outer == 1:
        flat = jnp.pad(flat, ((0, -flat.shape[0] % 32), (0, 0)))
        early_keys = [
            (shift, expert, kind)
            for expert in range(per_device)
            for kind in range(2)
            for shift in early_from
        ]
        x_group, grad_all, proj_in, joined, depth_joined, rows_joined, arrays = begin(
            tokens[0],
            out_grad[0],
            flat,
            by_depth,
            w_in,
            w_shared,
            w_out,
            w_shared_down,
            in_width,
            shared_part,
            inner,
            parcels(*early_keys, first=True),
        )
        early.update(zip(early_keys, arrays))
        x_group = x_group.reshape(group_rows, width)
    else:
        x_group = gather_rows(tokens[0], 1)[0].reshape(group_rows, width)
        grad_all = gather_rows(out_grad[0], inner)[0]
        in_columns = jnp.concatenate(
            [
                own_columns(w_in, 0, channels),
                own_columns(w_in, inner_width, channels),
                own_columns(w_shared, 0, shared_part),
                own_columns(w_shared, shared_width, shared_part),
                w_in[:, 2 * inner_width :],
            ],
            axis=1,
        )
        proj_in = lax.all_gather(in_columns, "shard", tiled=True)
        joined = lax.all_gather(flat, "shard")
        depth_joined = lax.all_gather(by_depth, "shard")
        rows_joined = lax.all_gather(rows_to_send([w_out, w_shared_down], part), "shard")
    taps = conv_w.shape[1]
    conv_rows = joined[:, :taps, : conv_w.shape[0]].transpose(1, 0, 2).reshape(taps, -1)
    conv_bias, gain_gate, gain_in, gain_moe, step_bias, decay_log, skip_gain = (
        joined[:, taps + order, : vector.shape[0]].reshape(-1)
        for order, vector in enumerate(vectors)
    )
    depth_joined = depth_joined.reshape(width, LANES)
    lane = jnp.arange(LANES)[None]
    router_wide = jnp.where(lane < expert_total, depth_joined, 0)
    dt_columns = jnp.where(lane < heads, jnp.roll(depth_joined, -expert_total, axis=1), 0)
    grad_all = grad_all.reshape(blocks, tok_rows, width)

    gain_row = to_full(gain_in)[None]
    hidden_in, gate_in, rows_in = project(
        x_group, gain_row, proj_in, dt_columns, channels, in_width
    )
    conv_all = jnp.concatenate([conv_rows, conv_bias[None]], axis=0)
    conv_table = to_full(
        jnp.pad(
            jnp.concatenate([own_columns(conv_all, 0, channels), conv_all[:, inner_width:]], axis=1),
            ((0, 3), (0, 0)),
        )
    )
    head_table = jnp.pad(
        jnp.stack(
            [
                to_full(own_rows(step_bias, heads)),
                -jnp.exp(to_full(own_rows(decay_log, heads))),
                to_full(own_rows(skip_gain, heads)),
            ]
        ),
        ((0, 5), (0, LANES - heads)),
    )
    keys = [(2, 0, DOWN), (1, 0, DOWN), (last, 0, DOWN)]
    y, seq_rows, states, (taken, *arrays) = scan_forward(
        lengths[0],
        deal_order,
        rows_in,
        conv_table,
        head_table,
        channels,
        [PlaneSwap(rows_by_owner(rows_joined))] + parcels(*keys),
    )
    unpack(keys, arrays)
    if outer > 1:
        out_rows, down_rows = rows_of_owner(taken, [w_out, w_shared_down])
        taken = jnp.concatenate(
            [
                out_rows.reshape(seq_devices, -1, width),
                down_rows.reshape(seq_devices, -1, width),
            ],
            axis=1,
        )
    own_weights = taken
    gate_gain = to_full(own_rows(gain_gate, channels))[None]
    keys = [(2, 1, DOWN), (1, 1, DOWN), (last, 1, DOWN)]
    mixed, arrays = mix_out(
        y, gate_in, gate_gain, own_weights, seq_devices, parcels(*keys)
    )
    unpack(keys, arrays)

    moe_row = to_full(gain_moe)[None]
    route_ids = jnp.pad(routes[0], ((0, 0), (0, LANES - top_count)))
    after_mix, moe_wide, gates = token_forward(
        mixed, tokens[0], moe_row, router_wide, route_ids, inner_width, top_count
    )
    keys = [(2, 0, UP), (1, 0, UP), (last, 0, UP)]
    moe_all, arrays = gather_rows(moe_wide, inner, parcels(*keys))
    unpack(keys, arrays)
    moe_all = moe_all.reshape(blocks, tok_rows, width + LANES)
    capacity = min(tok_rows, max(2, tok_rows * top_count * 5 // (expert_total * 3)))
    slots = -(-capacity // 16) * 16
    keys = [(2, 1, UP), (1, 1, UP), (last, 1, UP)]
    expert_rows, grad_rows, picks, arrays = dispatch(
        moe_all, grad_all, per_device, top_count, slots, own_first, parcels(*keys)
    )
    unpack(keys, arrays)
    shared_res, shared_back, shared_up_grad, shared_down_grad = shared_expert(
        moe_all,
        grad_all,
        proj_in,
        2 * channels,
        own_weights,
        shared_part,
        seq_devices,
        inner,
    )
    order = [
        (shift, expert, kind)
        for shift in range(inner)
        for expert in range(per_device)
        for kind in range(2)
    ]
    if outer == 1:
        early_keys = [(1, 0, UP), (last, 0, DOWN)]
        expert_res, expert_back, grads, sent = experts(
            expert_rows,
            grad_rows,
            [early.get(key, pieces[key]) for key in order],
            hidden,
            top_count,
            own_first,
            inner,
            [
                (
                    order.index(key),
                    pieces[key],
                    [(place_of + key[0]) % inner for place_of in early_from[key[0]]],
                )
                for key in order
                if key in early
            ],
            [(order.index(key), inner - key[0]) for key in early_keys],
        )
    else:
        for expert in range(per_device):
            for kind in range(2):
                pieces[0, expert, kind] = lax.dynamic_index_in_dim(
                    weights_of[kind], place * per_device + expert, 0, keepdims=False
                )
        early_keys, sent = [], []
        held = [
            stacked_pieces([pieces[shift, expert, kind] for shift in range(inner)], place, inner)
            for expert in range(per_device)
            for kind in range(2)
        ]
        expert_res, expert_back, grads, _ = experts(
            expert_rows, grad_rows, held, hidden, top_count, own_first, inner
        )
        grads = [
            split_piece(grads[expert * 2 + kind], shift, place, inner)
            for shift, expert, kind in order
        ]
    grads = dict(zip(order, grads))
    returned = {key: grads[key] for key in order if key[0] == 0}
    returned.update(zip(early_keys, sent))

    def back_parcels(*keys):
        keys = [key for key in keys if key not in early_keys]
        return [Parcel(grads[key], inner - key[0], inner) for key in keys]

    def unpack_back(keys, arrays):
        keys = [key for key in keys if key not in early_keys]
        returned.update(zip(keys, arrays))

    keys = [(1, 0, UP), (last, 0, DOWN), (last, 0, UP), (1, 0, DOWN)]
    out_part, back_part, arrays = combine(
        picks, expert_res, expert_back, shared_res, shared_back, inner, back_parcels(*keys)
    )
    unpack_back(keys, arrays)
    keys = [(last, 1, UP), (2, 1, DOWN), (1, 1, UP)]
    back, arrays = reduce_rows(
        back_part.reshape(inner, seq_devices, tok_rows, -1), back_parcels(*keys)
    )
    unpack_back(keys, arrays)
    mix_grad, mix_wide, router_grad, gain_moe_grad = token_back(
        back,
        mixed,
        after_mix,
        moe_wide,
        gates,
        out_grad[0],
        moe_row,
        router_wide,
        route_ids,
        inner_width,
        top_count,
    )

    keys = [(2, 0, DOWN), (last, 1, DOWN)]
    mix_group, arrays = gather_rows(mix_wide, 1, back_parcels(*keys))
    unpack_back(keys, arrays)
    keys = []
    dy, gate_in_grad, proj_out_grad, gain_gate_grad = mix_back(
        mix_group[0], y, gate_in, gate_gain, own_weights
    )
    keys = [(2, 1, UP), (2, 0, UP)]
    rows_grad, conv_grad, head_grad, out_sum, arrays = scan_backward(
        lengths[0],
        deal_order,
        seq_rows,
        states,
        dy,
        conv_table,
        head_table,
        out_part.reshape(inner, seq_devices, tok_rows, -1),
        back_parcels(*keys),
    )
    unpack_back(keys, arrays)
    layer_out = to_low(after_mix + out_sum)
    keys = [(1, 1, DOWN)]
    swap = [PlaneSwap(rows_from_owner([proj_out_grad, shared_down_grad]))]
    hidden_part, main_grad, rest_grad, (taken, *arrays) = project_back(
        gate_in_grad, rows_grad, hidden_in, proj_in, dt_columns, seq_devices, swap + back_parcels(*keys)
    )
    unpack_back(keys, arrays)
    experts_grad, experts_down_grad = collect(
        place[None], [returned[key] for key in order], per_device
    )
    def spread(values, length, axis=0):
        shape = values.shape[:axis] + (length,) + values.shape[axis + 1 :]
        return lax.dynamic_update_slice_in_dim(
            jnp.zeros(shape, values.dtype), values, part * values.shape[axis], axis
        )

    state_columns = rest_grad.shape[1] - LANES
    if outer == 1:
        small = pack(
            rest_grad,
            router_grad,
            conv_grad,
            head_grad,
            gain_gate_grad,
            gain_moe_grad,
            inner,
            seq_devices,
            inner_width,
            expert_total,
            heads,
        )
        tokens_grad, main_all, rows_all, shared_all, small_all = settle(
            hidden_part[None],
            small,
            tokens[0],
            mix_grad,
            gain_row,
            [
                main_grad.reshape(inner, depth_rows, -1),
                taken.reshape(inner, -1, width),
                shared_up_grad.reshape(inner, depth_rows, -1),
            ],
            inner,
        )
        w_in_grad, w_shared_grad, w_out_grad, w_shared_down_grad = assemble(
            main_all,
            shared_all,
            small_all,
            rows_all,
            w_in.shape[1],
            2 * shared_width,
            w_out.shape[0],
            w_shared_down.shape[0],
            max(1, seq_devices // shard_devices),
        )
        depth_each = small_all.shape[1] - ROWS_AFTER
        depth_sum = to_full(small_all[:, :depth_each].reshape(depth_rows, -1))
        after = to_full(small_all[:, depth_each:])
        conv_w_grad = after[:4].reshape(4, -1)[:, : conv_w.shape[0]].T
        conv_b_grad = after[4].reshape(-1)[: conv_b.shape[0]]
        norm_gate_grad = after[5].reshape(-1)[: norm_gate.shape[0]]
        here = shard * dt_bias.shape[0]
        of_heads = lax.dynamic_slice_in_dim(after[6, :3], here, dt_bias.shape[0], 1)
        dt_bias_grad, a_log_grad, d_skip_grad = of_heads[0], of_heads[1], of_heads[2]
        norm_moe_grad = after[7, 0, :depth_rows]
        last_lane = rest_grad.shape[1] - 1
    else:
        conv_rows_grad = conv_grad[:5].T
        conv_full = jnp.concatenate(
            [spread(conv_rows_grad[:channels], inner_width), conv_rows_grad[channels:]], axis=0
        )
        by_depth = [
            rest_grad[:, :state_columns],
            router_grad[:, :expert_total],
            spread(rest_grad[:, state_columns : state_columns + heads], head_total, 1),
            rest_grad[:, -1:],
            to_low(gain_moe_grad[0])[:, None],
        ]
        by_shard = [
            conv_full[:, :4],
            conv_full[:, 4],
            spread(head_grad[0, :heads], head_total),
            spread(head_grad[1, :heads], head_total),
            spread(head_grad[2, :heads], head_total),
            spread(gain_gate_grad[0], inner_width),
        ]
        shapes = [(piece.shape[0] // shard_devices,) + piece.shape[1:] for piece in by_shard]
        by_shard = jnp.concatenate(
            [to_low(piece).reshape(shard_devices, -1) for piece in by_shard], axis=1
        )
        extents = [piece.shape[1] for piece in by_depth]
        used = sum(extents)
        hidden_grad = reduce_rows(hidden_part[None])[0]
        residual = to_full(tokens[0])
        own_scale = norm_scale(residual)
        own_unit = residual * own_scale
        scaled = hidden_grad * gain_row
        tokens_grad = to_low(
            mix_grad
            + own_scale
            * (scaled - own_unit * jnp.mean(scaled * own_unit, axis=1, keepdims=True))
        )
        by_depth = jnp.concatenate(by_depth, axis=1).reshape(shard_devices, -1)
        packed = jnp.concatenate([by_depth, by_shard], axis=1)
        summed = lax.psum(lax.psum_scatter(packed, "shard", tiled=True), "seq").reshape(-1)
        count = depth_rows * used
        depth_sum = to_full(summed[:count]).reshape(depth_rows, used)
        shard_sum = summed[count:]

        def from_line(part, rows):
            own = lax.psum_scatter(part.reshape(shard_devices, rows, -1), "shard")
            return lax.all_gather(own, "seq")

        def columns_of(joined, extent):
            joined = joined.reshape(seq_devices, depth_rows, 2, extent).transpose(1, 2, 0, 3)
            return to_full(joined.reshape(depth_rows, -1))

        w_in_main = columns_of(from_line(main_grad, depth_rows), channels)
        w_in_grad = jnp.concatenate([w_in_main, depth_sum[:, :state_columns]], axis=1)
        w_shared_grad = columns_of(from_line(shared_up_grad, depth_rows), shared_part)
        rows_each = taken.shape[0] * taken.shape[1] // shard_devices
        w_out_grad, w_shared_down_grad = rows_of_shard(
            from_line(taken, rows_each), [w_out, w_shared_down]
        )
        results, start = [], 0
        for shape in shapes:
            size = 1
            for extent in shape:
                size *= extent
            results.append(to_full(shard_sum[start : start + size]).reshape(shape))
            start += size
        conv_w_grad, conv_b_grad, dt_bias_grad, a_log_grad, d_skip_grad, norm_gate_grad = results
        norm_moe_grad = depth_sum[:, used - 1]
        last_lane = used - 2
    start = state_columns
    w_router_grad = depth_sum[:, start : start + expert_total]
    start += expert_total
    w_dt_grad = depth_sum[:, start : start + head_total]
    norm_in_grad = depth_sum[:, last_lane] / to_full(norm_in)
    return (
        layer_out[None],
        tokens_grad[None],
        norm_in_grad,
        w_in_grad,
        w_dt_grad,
        conv_w_grad,
        conv_b_grad,
        dt_bias_grad,
        a_log_grad,
        d_skip_grad,
        norm_gate_grad,
        w_out_grad,
        norm_moe_grad,
        w_router_grad,
        w_shared_grad,
        w_shared_down_grad,
        experts_grad,
        experts_down_grad,
    )


def solution(mesh):
    placed = (
        P("shard", "seq", None),
        P("shard", "seq", None),
        P("shard", None),
        P("shard", None),
        P("shard", "seq", None),
        P("shard"),
        P("shard", None),
        P("shard", None),
        P("shard", None),
        P("shard"),
        P("shard"),
        P("shard"),
        P("shard"),
        P("shard"),
        P("shard", None),
        P("shard"),
        P("shard", None),
        P("shard", None),
        P("shard", None),
        P("seq", "shard", None),
        P("seq", "shard", None),
    )
    return jax.shard_map(
        local,
        mesh=mesh,
        in_specs=placed,
        out_specs=(
            P("shard", "seq", None),
            P("shard", "seq", None),
            P("shard"),
            P("shard", None),
            P("shard", None),
            P("shard", None),
            P("shard"),
            P("shard"),
            P("shard"),
            P("shard"),
            P("shard"),
            P("shard", None),
            P("shard"),
            P("shard", None),
            P("shard", None),
            P("shard", None),
            P("seq", "shard", None),
            P("seq", "shard", None),
        ),
        check_vma=False,
    )
```

```python
import functools

import jax
import jax.numpy as jnp
from jax import lax
from jax.experimental import pallas as pl
from jax.experimental.pallas import tpu as pltpu
from jax.sharding import PartitionSpec as P

STRETCH = 256
INNER = 4
UP, DOWN = 0, 1
EPSILON = 1e-05
HIGHEST = lax.Precision.HIGHEST


def matmul(left_side, right_side):
    return jnp.dot(left_side, right_side, preferred_element_type=jnp.float32)


def left_contract(left_side, right_side):
    return lax.dot_general(
        left_side, right_side, (((0,), (0,)), ((), ())), preferred_element_type=jnp.float32
    )


def right_contract(left_side, right_side):
    return lax.dot_general(
        left_side, right_side, (((1,), (1,)), ((), ())), preferred_element_type=jnp.float32
    )


def to_low(values):
    return values.astype(jnp.bfloat16)


def to_full(values):
    return values.astype(jnp.float32)


def norm_scale(values):
    return lax.rsqrt(jnp.mean(values * values, axis=-1, keepdims=True) + EPSILON)


LANES = 128
VMEM_BYTES = 56 * 1024 * 1024


def cost_of(micros):
    return pl.CostEstimate(flops=0, transcendentals=0, bytes_accessed=int(micros * 3.6e6))


def dot_rows(left_side, right_side, precision=None):
    return lax.dot_general(
        left_side,
        right_side,
        (((0,), (0,)), ((), ())),
        precision=precision,
        preferred_element_type=jnp.float32,
    )


def dot_lanes(left_side, right_side, precision=None):
    return lax.dot_general(
        left_side,
        right_side,
        (((1,), (1,)), ((), ())),
        precision=precision,
        preferred_element_type=jnp.float32,
    )


def dot_full(left_side, right_side, precision=None):
    return jnp.dot(
        left_side, right_side, precision=precision, preferred_element_type=jnp.float32
    )


def iota_of(shape, axis):
    return lax.broadcasted_iota(jnp.int32, shape, axis)


def ids_at(places, lengths_ref):
    total, end = jnp.zeros(places.shape, jnp.int32), 0
    for seq in range(lengths_ref.shape[0]):
        end = end + lengths_ref[seq]
        total = total + (places >= end).astype(jnp.int32)
    return total


def id_at(place, lengths_ref):
    total, end = jnp.int32(0), 0
    for seq in range(lengths_ref.shape[0]):
        end = end + lengths_ref[seq]
        total = total + (place >= end).astype(jnp.int32)
    return total


class Stretch:
    def __init__(self, start, rows, before, conv_ref, head_ref, lengths_ref, channels):
        length = rows.shape[0]
        self.channels = channels
        self.heads = channels // 64
        width = conv_ref.shape[1]
        state = (width - channels) // 2
        places = start + iota_of((length, 1), 0)
        self.ids = ids_at(places, lengths_ref)
        self.ids_row = ids_at(start + iota_of((1, length), 1), lengths_ref)
        inputs = rows[:, :width]
        joined = jnp.concatenate([before[:, :width], inputs], axis=0)
        self.shifted = [inputs]
        value = conv_ref[4:5, :] + inputs * conv_ref[3:4, :]
        for offset in range(1, 4):
            same = (ids_at(places - offset, lengths_ref) == self.ids) & (places >= offset)
            moved = pltpu.roll(joined, offset, 0)[8:, :]
            moved = jnp.where(same, moved, 0.0)
            self.shifted.append(moved)
            value = value + moved * conv_ref[3 - offset : 4 - offset, :]
        self.value = value
        self.sig = jax.nn.sigmoid(value)
        act = value * self.sig
        self.x = act[:, :channels]
        self.b = act[:, channels : channels + state]
        self.c = act[:, channels + state :]
        self.b_low = to_low(self.b)
        self.c_low = to_low(self.c)
        self.dt_in = rows[:, width:] + head_ref[0:1, :]
        self.dt = jnp.maximum(self.dt_in, 0.0) + jnp.log1p(jnp.exp(-jnp.abs(self.dt_in)))
        self.rate = head_ref[1:2, :]
        rows_at = iota_of((length, length), 0)
        columns_at = iota_of((length, length), 1)
        lower = (rows_at >= columns_at).astype(jnp.float32)
        self.cum = dot_full(lower, self.dt * self.rate, HIGHEST)
        self.cum_rows = self.cum.T[:8, :]
        self.dt_rows = self.dt.T[:8, :]
        self.causal = (self.ids == self.ids_row) & (rows_at >= columns_at)
        self.scores = dot_lanes(self.c_low, self.b_low)
        last_id = jnp.where(start > 0, id_at(start - 1, lengths_ref), -1)
        end_id = id_at(start + length - 1, lengths_ref)
        self.enter = jnp.where(self.ids == last_id, jnp.exp(self.cum), 0.0)
        end_cum = self.cum[length - 1 : length, :]
        self.tail = jnp.where(self.ids == end_id, jnp.exp(end_cum - self.cum), 0.0)
        self.tail_weight = self.tail * self.dt
        self.keep = jnp.where(last_id == end_id, jnp.exp(end_cum), 0.0)

    def decay(self, head):
        spread = self.cum[:, head : head + 1] - self.cum_rows[head : head + 1, :]
        return jnp.where(self.causal, jnp.exp(jnp.minimum(spread, 0.0)), 0.0)

    def per_channel(self, by_head):
        return jnp.concatenate(
            [
                jnp.broadcast_to(by_head[:, head : head + 1], (by_head.shape[0], 64))
                for head in range(self.heads)
            ],
            axis=1,
        )

    def state_keep(self):
        return jnp.concatenate(
            [
                jnp.broadcast_to(self.keep[:, head : head + 1], (64, LANES))
                for head in range(self.heads)
            ],
            axis=0,
        )


def head_lanes(channels):
    return (iota_of((channels, LANES), 0) // 64 == iota_of((channels, LANES), 1)).astype(
        jnp.float32
    )


def pick_rows(deal_ref, start, length):
    places = start + iota_of((length, 1), 0)
    return jnp.where(deal_ref[...] == places, 1.0, 0.0).astype(jnp.bfloat16)


def scan_forward_kernel(
    lengths_ref, deal_ref, rows_ref, conv_ref, head_ref, y_ref, seq_ref, states_ref, before, state, total
):
    step = pl.program_id(0)
    length = seq_ref.shape[0]
    channels = y_ref.shape[1]
    start = step * length

    @pl.when(step == 0)
    def _():
        before[...] = jnp.zeros_like(before)
        state[...] = jnp.zeros_like(state)
        total[...] = jnp.zeros_like(total)

    picks = pick_rows(deal_ref, start, length)
    rows = dot_full(picks, rows_ref[...])
    seq_ref[...] = to_low(rows)
    part = Stretch(start, rows, before[...], conv_ref, head_ref, lengths_ref, channels)
    before[...] = rows[length - 8 :, :]
    state_now = state[...]
    states_ref[0] = state_now
    x_low = to_low(part.x)
    outs = []
    lane = iota_of((length, LANES), 1)
    for pair in range(channels // LANES):
        x_pair = x_low[:, pair * LANES : (pair + 1) * LANES]
        halves = []
        for head in (2 * pair, 2 * pair + 1):
            weights = part.decay(head) * part.scores * part.dt_rows[head : head + 1, :]
            halves.append(dot_full(to_low(weights), x_pair))
        outs.append(jnp.where(lane < 64, halves[0], halves[1]))
    earlier = dot_lanes(part.c_low, to_low(state_now))
    skip = part.per_channel(head_ref[2:3, :])
    y = jnp.concatenate(outs, axis=1) + part.per_channel(part.enter) * earlier + skip * part.x
    state[...] = part.state_keep() * state_now + dot_rows(
        to_low(part.per_channel(part.tail_weight) * part.x), part.b_low
    )
    total[...] += dot_rows(picks, to_low(y))

    @pl.when(step == pl.num_programs(0) - 1)
    def _():
        y_ref[...] = to_low(total[...])


def scan_forward(lengths, deal_row, rows, conv_table, head_table, channels, freight):
    group_rows, width = rows.shape
    steps = group_rows // STRETCH
    state_rows = (channels, LANES)
    return run(
        scan_forward_kernel,
        (lengths, deal_row, rows, conv_table, head_table),
        grid=(steps,),
        in_specs=[
            pl.BlockSpec(memory_space=pltpu.SMEM),
            whole(deal_row.shape),
            whole(rows.shape),
            whole(conv_table.shape),
            whole(head_table.shape),
        ],
        out_specs=[
            whole((group_rows, channels)),
            pl.BlockSpec((STRETCH, width), lambda step: (step, 0)),
            pl.BlockSpec((1,) + state_rows, lambda step: (step, 0, 0)),
        ],
        out_shape=[
            jax.ShapeDtypeStruct((group_rows, channels), jnp.bfloat16),
            jax.ShapeDtypeStruct((group_rows, width), jnp.bfloat16),
            jax.ShapeDtypeStruct((steps,) + state_rows, jnp.float32),
        ],
        scratch=[
            pltpu.VMEM((8, width), jnp.float32),
            pltpu.VMEM(state_rows, jnp.float32),
            pltpu.VMEM((group_rows, channels), jnp.float32),
        ],
        freight=freight,
        micros=25,
        name="scan_forward",
    )


def scan_backward_kernel(
    lengths_ref,
    deal_ref,
    seq_ref,
    states_ref,
    dy_ref,
    conv_ref,
    head_ref,
    other_ref,
    drows_ref,
    conv_grad_ref,
    head_grad_ref,
    other_sum_ref,
    after,
    state_grad,
    *other_scratch,
):
    order = pl.program_id(0)
    steps = pl.num_programs(0)
    reducer = Reducer(other_ref.shape[0], other_ref, other_sum_ref, other_scratch)

    last = dy_ref.shape[0] // STRETCH - 1

    @pl.when(order == 0)
    def _():
        reducer.begin()

    for count in range(min(last + 1, reducer.inner + 3)):

        @pl.when(order == count)
        def _():
            reducer.step(count)

    step = steps - 1 - order
    length = STRETCH
    channels = dy_ref.shape[1]
    width = conv_ref.shape[1]
    state_width = (width - channels) // 2
    start = pl.multiple_of(step * length, length)

    @pl.when(order == 0)
    def _():
        after[...] = jnp.zeros_like(after)
        state_grad[...] = jnp.zeros_like(state_grad)
        drows_ref[...] = jnp.zeros_like(drows_ref)
        conv_grad_ref[...] = jnp.zeros_like(conv_grad_ref)
        head_grad_ref[...] = jnp.zeros_like(head_grad_ref)

    picks = pick_rows(deal_ref, start, length)
    dy = dot_full(picks, dy_ref[...])
    rows = seq_ref[pl.ds(start, length), :].astype(jnp.float32)
    place = pl.multiple_of(jnp.maximum(start - 16, 0), 16)
    before = seq_ref[pl.ds(place, 16), :].astype(jnp.float32)[8:, :]
    part = Stretch(start, rows, before, conv_ref, head_ref, lengths_ref, channels)
    state_now = states_ref[0]
    state_low = to_low(state_now)
    next_grad = state_grad[...]
    next_low = to_low(next_grad)
    lanes_of = head_lanes(channels)
    x_low = to_low(part.x)
    dy_low = to_low(dy)
    lane = iota_of((length, LANES), 1)

    enter = part.per_channel(part.enter)
    tail_weight = part.per_channel(part.tail_weight)
    earlier = dot_lanes(part.c_low, state_low)
    enter_grad = dot_full(dy * earlier, lanes_of, HIGHEST)
    entered = to_low(enter * dy)
    c_grad = dot_full(entered, state_low)
    state_grad[...] = part.state_keep() * next_grad + dot_rows(entered, part.c_low)
    onward = dot_lanes(part.b_low, next_low)
    x_grad = part.per_channel(head_ref[2:3, :]) * dy + tail_weight * onward
    tail_grad = dot_full(part.x * onward, lanes_of, HIGHEST)
    b_grad = dot_full(to_low(tail_weight * part.x), next_low)
    tail_part = tail_grad * part.tail_weight
    cum_grad = enter_grad * part.enter - tail_part
    dt_grad = tail_grad * part.tail
    kept = dot_lanes(jnp.ones((8, LANES), jnp.float32), next_grad * state_now, HIGHEST)
    keep_grad = dot_full(kept, lanes_of, HIGHEST)[:1, :]
    end_grad = jnp.sum(tail_part, axis=0, keepdims=True) + keep_grad * part.keep

    score_grad = jnp.zeros((length, length), jnp.float32)
    cum_columns, cum_rows, dt_rows, outs = [], [], [], []
    for pair in range(channels // LANES):
        x_pair = x_low[:, pair * LANES : (pair + 1) * LANES]
        dy_pair = dy_low[:, pair * LANES : (pair + 1) * LANES]
        halves = []
        for half, head in enumerate((2 * pair, 2 * pair + 1)):
            mine = (lane < 64) if half == 0 else (lane >= 64)
            weight_grad = dot_lanes(jnp.where(mine, dy_pair, jnp.zeros_like(dy_pair)), x_pair)
            decay = part.decay(head)
            dt_row = part.dt_rows[head : head + 1, :]
            by_decay = weight_grad * decay
            by_dt = by_decay * part.scores
            by_spread = by_dt * dt_row
            dt_rows.append(jnp.sum(by_dt, axis=0, keepdims=True))
            cum_rows.append(jnp.sum(by_spread, axis=0, keepdims=True))
            cum_columns.append(jnp.sum(by_spread, axis=1, keepdims=True))
            score_grad = score_grad + by_decay * dt_row
            halves.append(dot_rows(to_low(decay * part.scores * dt_row), dy_pair))
        outs.append(jnp.where(lane < 64, halves[0], halves[1]))
    x_grad = x_grad + jnp.concatenate(outs, axis=1)
    score_low = to_low(score_grad)
    c_grad = c_grad + dot_full(score_low, part.b_low)
    b_grad = b_grad + dot_rows(score_low, part.c_low)

    heads = len(dt_rows)
    blank = jnp.zeros((LANES - heads, length), jnp.float32)
    dt_grad = dt_grad + jnp.concatenate(dt_rows + [blank], axis=0).T
    cum_grad = cum_grad - jnp.concatenate(cum_rows + [blank], axis=0).T
    for head in range(heads):
        cum_grad = cum_grad + jnp.where(lane == head, cum_columns[head], 0.0)
    at_end = iota_of((length, 1), 0) == length - 1
    cum_grad = cum_grad + jnp.where(at_end, end_grad, 0.0)
    upper = (iota_of((length, length), 1) >= iota_of((length, length), 0)).astype(jnp.float32)
    log_grad = dot_full(upper, cum_grad, HIGHEST)
    dt_grad = dt_grad + log_grad * part.rate
    dt_in_grad = dt_grad * jax.nn.sigmoid(part.dt_in)
    dt_in_grad = jnp.where(lane < heads, dt_in_grad, 0.0)
    head_grad_ref[0:1, :] += jnp.sum(dt_in_grad, axis=0, keepdims=True)
    head_grad_ref[1:2, :] += jnp.sum(log_grad * part.dt, axis=0, keepdims=True) * part.rate
    skip_sum = jnp.broadcast_to(jnp.sum(dy * part.x, axis=0, keepdims=True), (8, channels))
    head_grad_ref[2:3, :] += dot_full(skip_sum, lanes_of, HIGHEST)[:1, :]

    act_grad = jnp.concatenate([x_grad, b_grad, c_grad], axis=1)
    value_grad = act_grad * part.sig * (1.0 + part.value * (1.0 - part.sig))
    conv_grad_ref[4:5, :] += jnp.sum(value_grad, axis=0, keepdims=True)
    for offset in range(4):
        conv_grad_ref[3 - offset : 4 - offset, :] += jnp.sum(
            value_grad * part.shifted[offset], axis=0, keepdims=True
        )
    joined = jnp.concatenate([value_grad, after[...]], axis=0)
    places = start + iota_of((length, 1), 0)
    rows_grad = value_grad * conv_ref[3:4, :]
    for offset in range(1, 4):
        moved = pltpu.roll(joined, length + 8 - offset, 0)[:length, :]
        same = (ids_at(places + offset, lengths_ref) == part.ids) & (
            places + offset < steps * length
        )
        rows_grad = rows_grad + jnp.where(same, moved, 0.0) * conv_ref[3 - offset : 4 - offset, :]
    after[...] = value_grad[:8, :]
    drows_ref[...] += to_low(
        dot_rows(picks, to_low(jnp.concatenate([rows_grad, dt_in_grad], axis=1)))
    )

    for count in range(last + 1, reducer.inner + 3):

        @pl.when(order == last)
        def _():
            reducer.step(count)

    @pl.when(order == steps - 1)
    def _():
        reducer.finish()


def scan_backward(
    lengths, deal_row, seq_rows, states, dy, conv_table, head_table, other, freight
):
    group_rows, width = seq_rows.shape
    channels = dy.shape[1]
    steps = group_rows // STRETCH
    return run(
        scan_backward_kernel,
        (lengths, deal_row, seq_rows, states, dy, conv_table, head_table, other),
        grid=(steps,),
        in_specs=[
            pl.BlockSpec(memory_space=pltpu.SMEM),
            whole(deal_row.shape),
            once(seq_rows.shape),
            pl.BlockSpec((1, channels, LANES), lambda step: (steps - 1 - step, 0, 0)),
            once(dy.shape),
            whole(conv_table.shape),
            whole(head_table.shape),
            pl.BlockSpec(memory_space=pl.ANY),
        ],
        out_specs=[
            whole((group_rows, width)),
            whole(conv_table.shape),
            whole(head_table.shape),
            whole(other.shape[2:]),
        ],
        out_shape=[
            jax.ShapeDtypeStruct((group_rows, width), jnp.bfloat16),
            jax.ShapeDtypeStruct(conv_table.shape, jnp.float32),
            jax.ShapeDtypeStruct(head_table.shape, jnp.float32),
            jax.ShapeDtypeStruct(other.shape[2:], jnp.float32),
        ],
        scratch=[
            pltpu.VMEM((8, conv_table.shape[1]), jnp.float32),
            pltpu.VMEM((channels, LANES), jnp.float32),
        ]
        + Reducer.scratch(other.shape[0], *other.shape[2:]),
        freight=freight,
        flips=FLIPS,
        inner=other.shape[0],
        micros=40,
        name="scan_backward",
    )


def whole(shape):
    return pl.BlockSpec(shape, lambda *steps: (0,) * len(shape))


def once(shape):
    return pl.BlockSpec(
        shape, lambda *steps: (0,) * len(shape), pipeline_mode=pl.Buffered(buffer_count=1)
    )


MESH = pl.DeviceIdType.MESH
FLIPS = (1, 2, 4)


def flipped(place, flip):
    result = place
    for bit in FLIPS:
        if flip & bit:
            result = result + bit - 2 * bit * lax.rem(lax.div(place, bit), 2)
    return result


def own_shard_group(inner):
    shard = lax.axis_index("shard")
    place = lax.rem(shard, inner)
    return place, shard - place


def peers_in_order(place, inner):
    if inner == 1:
        return []
    if inner == 4:
        half = lax.div(place, 2)
        return [flipped(place, 1), 2 - half, 3 - 3 * half]
    return [lax.rem(place + shift, inner) for shift in range(1, inner)]


def greet(flips, inner):
    barrier = pltpu.get_barrier_semaphore()
    part = lax.axis_index("seq")
    place, first = own_shard_group(inner)
    for flip in flips:
        pl.semaphore_signal(
            barrier, inc=1, device_id={"seq": flipped(part, flip)}, device_id_type=MESH
        )
    for peer in peers_in_order(place, inner):
        pl.semaphore_signal(
            barrier, inc=1, device_id={"shard": first + peer}, device_id_type=MESH
        )
    pl.semaphore_wait(barrier, len(flips) + inner - 1)


def among(place, places):
    if places is None:
        return None
    return functools.reduce(jnp.logical_or, [place == one for one in places])


def do_if(condition, action):
    if condition is None:
        action()
    else:
        pl.when(condition)(action)


class Parcel:
    flips = ()
    sems = 1

    def __init__(self, array, shift, inner, index=None, output=None, senders=None):
        self.array, self.shift, self.inner, self.index = array, shift, inner, index
        self.senders = senders
        self.shape = array.shape if index is None else array.shape[1:]
        self.output = output

    def moves(self, source, target):
        place, first = own_shard_group(self.inner)
        to = lax.rem(place + self.shift, self.inner)
        if self.index is not None:
            source = source.at[self.index(to)]
        return [(source, target, target, {"shard": first + to})]

    def sends(self):
        return among(own_shard_group(self.inner)[0], self.senders)

    def comes(self):
        place, _ = own_shard_group(self.inner)
        return among(lax.rem(place + self.inner - self.shift, self.inner), self.senders)

    def stays(self, source, target):
        return []


class PlaneSwap:
    flips = (1, 2, 3, 4, 5, 6, 7)
    inner = 1
    sems = 8

    output = None

    def __init__(self, array):
        self.array, self.shape = array, array.shape

    def sends(self):
        return None

    def comes(self):
        return None

    def moves(self, source, target):
        part = lax.axis_index("seq")
        return [
            (
                source.at[flipped(part, flip)],
                target.at[part],
                target.at[flipped(part, flip)],
                {"seq": flipped(part, flip)},
            )
            for flip in self.flips
        ]

    def stays(self, source, target):
        part = lax.axis_index("seq")
        return [(source.at[part], target.at[part])]


COLLECTIVES = []


def run(
    kernel,
    args,
    *,
    in_specs,
    out_specs,
    out_shape,
    name,
    micros,
    grid=(),
    scratch=(),
    freight=(),
    flips=(),
    inner=1,
    late=False,
):
    freight = list(freight)
    for place, item in enumerate(freight):
        item.rank = place
    flips = tuple(sorted(set(flips).union(*[item.flips for item in freight])))
    inner = max([inner] + [item.inner for item in freight])
    talks = bool(flips) or inner > 1
    count_in, count_out, count_scratch = len(args), len(out_shape), len(scratch)
    count = len(freight)
    loaded = [item for item in freight if item.output is None]

    def wrapped(*refs):
        ins, refs = refs[:count_in], refs[count_in:]
        sources, refs = list(refs[: len(loaded)]), refs[len(loaded) :]
        outs, refs = refs[:count_out], refs[count_out:]
        sources = [
            sources.pop(0) if item.output is None else outs[item.output] for item in freight
        ]
        targets, refs = refs[:count], refs[count:]
        own, refs = refs[:count_scratch], refs[count_scratch:]

        def remote(item, place, order, source, target, device):
            send, recv = refs[3 * place : 3 * place + 2]
            return pltpu.make_async_remote_copy(
                src_ref=source,
                dst_ref=target,
                send_sem=send.at[order],
                recv_sem=recv.at[order],
                device_id=device,
                device_id_type=MESH,
            )

        def moves(chosen):
            for place, item in enumerate(freight):
                if not chosen(item):
                    continue
                for order, move in enumerate(item.moves(sources[place], targets[place])):
                    yield item, place, order, move

        def stays(chosen):
            for place, item in enumerate(freight):
                if not chosen(item):
                    continue
                for source, target in item.stays(sources[place], targets[place]):
                    yield pltpu.make_async_copy(source, target, refs[3 * place + 2])

        def depart(chosen=lambda item: True, gate=None):
            for item, place, order, (source, target, _, device) in moves(chosen):
                allowed = item.sends()
                if gate is not None:
                    allowed = gate if allowed is None else allowed & gate
                do_if(
                    allowed,
                    lambda: remote(item, place, order, source, target, device).start(),
                )
            for copy in stays(chosen):
                copy.start()

        def arrive(chosen=lambda item: True):
            for item, place, order, (source, target, arrival, device) in moves(chosen):
                do_if(
                    item.comes(),
                    lambda: remote(item, place, order, source, arrival, device).wait_recv(),
                )
                do_if(
                    item.sends(),
                    lambda: remote(item, place, order, source, target, device).wait_send(),
                )
            for copy in stays(chosen):
                copy.wait()

        if grid:
            at = [pl.program_id(axis) for axis in range(len(grid))]
            first, last = at[0] == 0, at[0] == grid[0] - 1
            for axis in range(1, len(grid)):
                first = first & (at[axis] == 0)
                last = last & (at[axis] == grid[axis] - 1)
            if talks:

                @pl.when(first)
                def _():
                    greet(flips, inner)
                    if not late:
                        depart()

            if late:
                kernel(depart, arrive, targets, *ins, *outs, *own)
            else:
                kernel(*ins, *outs, *own)
            if talks and not late:
                pl.when(last)(arrive)
        else:
            if talks:
                greet(flips, inner)
            if late:
                kernel(depart, *ins, *outs, *own)
            else:
                depart()
                kernel(*ins, *outs, *own)
            arrive()

    anywhere = pl.BlockSpec(memory_space=pl.ANY)
    extra = {}
    if talks:
        COLLECTIVES.append(name)
        extra = dict(collective_id=len(COLLECTIVES), has_side_effects=True)
    sems = []
    for item in freight:
        sems += [
            pltpu.SemaphoreType.DMA((item.sems,)),
            pltpu.SemaphoreType.DMA((item.sems,)),
            pltpu.SemaphoreType.DMA(()),
        ]
    results = pl.pallas_call(
        wrapped,
        grid=grid,
        in_specs=list(in_specs) + [anywhere] * len(loaded),
        out_specs=list(out_specs) + [anywhere] * count,
        out_shape=list(out_shape)
        + [jax.ShapeDtypeStruct(item.shape, item.array.dtype) for item in freight],
        scratch_shapes=list(scratch) + sems,
        compiler_params=pltpu.CompilerParams(vmem_limit_bytes=VMEM_BYTES, **extra),
        cost_estimate=cost_of(micros),
        name=name,
    )(*args, *[item.array for item in loaded])
    results = list(results)
    if freight:
        return results[:count_out] + [results[count_out:]]
    return results


class LineSum:
    def __init__(self, inner, sums, from_below, from_above, send, below_recv, above_recv):
        self.inner = inner
        self.sums, self.from_below, self.from_above = sums, from_below, from_above
        self.send, self.below_recv, self.above_recv = send, below_recv, above_recv
        self.place, self.first = own_shard_group(inner)
        self.targets = list(reversed(peers_in_order(self.place, inner))) + [self.place]

    def copy(self, order, up):
        target = self.targets[order]
        inbox = self.from_below if up else self.from_above
        recv = self.below_recv if up else self.above_recv
        return pltpu.make_async_remote_copy(
            src_ref=self.sums.at[order],
            dst_ref=inbox.at[target],
            send_sem=self.send.at[order],
            recv_sem=recv.at[target],
            device_id={"shard": self.first + self.place + (1 if up else -1)},
            device_id_type=MESH,
        )

    def arrived(self, target, up):
        inbox = self.from_below if up else self.from_above
        recv = self.below_recv if up else self.above_recv
        pltpu.make_async_remote_copy(
            src_ref=inbox.at[target],
            dst_ref=inbox.at[target],
            send_sem=self.send.at[0],
            recv_sem=recv.at[target],
            device_id={"shard": self.first + self.place + (-1 if up else 1)},
            device_id_type=MESH,
        ).wait_recv()
        return to_full(inbox[target])

    def ways(self):
        return ((True, self.place > 0), (False, self.place < self.inner - 1))

    def push_free(self, order):
        target = self.targets[order]
        for up, comes in self.ways():
            heads = (target > self.place) if up else (target < self.place)

            @pl.when(heads & jnp.logical_not(comes))
            def _():
                self.copy(order, up).start()

    def push_rest(self, order):
        target = self.targets[order]
        for up, comes in self.ways():
            heads = (target > self.place) if up else (target < self.place)

            @pl.when(heads & comes)
            def _():
                self.sums[order] = to_low(
                    to_full(self.sums[order]) + self.arrived(target, up)
                )
                self.copy(order, up).start()

    def add_own(self, total):
        for up, comes in self.ways():

            @pl.when(comes)
            def _():
                total[...] += self.arrived(self.place, up)

    def finish(self):
        for order in range(self.inner - 1):
            for up in (True, False):
                target = self.targets[order]

                @pl.when((target > self.place) if up else (target < self.place))
                def _():
                    self.copy(order, up).wait_send()

    @staticmethod
    def scratch(inner, rows, width):
        sems = lambda *shape: pltpu.SemaphoreType.DMA(shape)
        return [
            pltpu.VMEM((max(1, inner - 1), rows, width), jnp.bfloat16),
            pltpu.VMEM((inner, rows, width), jnp.bfloat16),
            pltpu.VMEM((inner, rows, width), jnp.bfloat16),
            sems(max(1, inner - 1)),
            sems(inner),
            sems(inner),
        ]


class Reducer:
    def __init__(self, inner, p_ref, total, refs, make=None):
        self.inner, self.p_ref, self.total, self.make = inner, p_ref, total, make
        self.held, self.paired, self.turned, self.crossed = refs[:4]
        self.load, self.core_send, self.core_recv = refs[4:7]
        self.turn_send, self.turn_recv, self.cross_send, self.cross_recv = refs[7:11]
        self.line = LineSum(inner, *refs[11:])
        self.part = lax.axis_index("seq")
        half = self.held.shape[2] // 2
        self.spans = [pl.ds(0, half), pl.ds(half, half)]

    @staticmethod
    def scratch(inner, rows, width):
        low = jnp.bfloat16
        sems = lambda *shape: pltpu.SemaphoreType.DMA(shape)
        return [
            pltpu.VMEM((inner, 4, rows, width), low),
            pltpu.VMEM((inner, 4, rows, width), low),
            pltpu.VMEM((inner, 2, rows // 2, width), low),
            pltpu.VMEM((inner, 4, rows // 2, width), low),
            sems(inner, 4),
            sems(inner, 4),
            sems(inner, 4),
            sems(inner, 2),
            sems(inner, 2),
            sems(inner, 4),
            sems(inner, 4),
        ] + LineSum.scratch(inner, rows, width)

    EVENS = (6, 2, 4, 0)

    def to_core(self, order, slot):
        return pltpu.make_async_remote_copy(
            src_ref=self.p_ref.at[order, slot]
            if self.make
            else self.p_ref.at[
                self.line.targets[order], flipped(self.part, self.EVENS[slot] + 1)
            ],
            dst_ref=self.paired.at[order, slot],
            send_sem=self.core_send.at[order, slot],
            recv_sem=self.core_recv.at[order, slot],
            device_id={"seq": flipped(self.part, 1)},
            device_id_type=MESH,
        )

    def loading(self, order, slot):
        return pltpu.make_async_copy(
            self.p_ref.at[self.line.targets[order], flipped(self.part, self.EVENS[slot])],
            self.held.at[order, slot],
            self.load.at[order, slot],
        )

    def turn(self, order, span):
        return pltpu.make_async_remote_copy(
            src_ref=self.held.at[order, 0, self.spans[span]],
            dst_ref=self.turned.at[order, span],
            send_sem=self.turn_send.at[order, span],
            recv_sem=self.turn_recv.at[order, span],
            device_id={"seq": flipped(self.part, (2, 4)[span])},
            device_id_type=MESH,
        )

    CROSSINGS = ((1, 2, 0), (2, 4, 1), (2, 4, 0), (1, 2, 1))

    def cross(self, order, kind):
        slot, flip, span = self.CROSSINGS[kind]
        return pltpu.make_async_remote_copy(
            src_ref=self.held.at[order, slot, self.spans[span]],
            dst_ref=self.crossed.at[order, kind],
            send_sem=self.cross_send.at[order, kind],
            recv_sem=self.cross_recv.at[order, kind],
            device_id={"seq": flipped(self.part, flip)},
            device_id_type=MESH,
        )

    def begin(self):
        for order in range(self.inner):
            for slot in range(4):
                if self.make:
                    target = self.line.targets[order]
                    block = flipped(self.part, self.EVENS[slot] + 1)
                    self.make(target, block, self.p_ref.at[order, slot])
                self.to_core(order, slot).start()
                if not self.make:
                    self.loading(order, slot).start()
            if self.make:
                for slot in range(4):
                    block = flipped(self.part, self.EVENS[slot])
                    self.make(self.line.targets[order], block, self.held.at[order, slot])

    def total_of(self, order, slot):
        if not self.make:
            self.loading(order, slot).wait()
        self.to_core(order, slot).wait_recv()
        return to_full(self.held[order, slot]) + to_full(self.paired[order, slot])

    def stage_a(self, order):
        self.held[order, 0] = to_low(self.total_of(order, 0))
        for span in range(2):
            self.turn(order, span).start()
        for slot in (1, 2):
            self.held[order, slot] = to_low(self.total_of(order, slot))
            self.cross(order, slot - 1).start()

    def stage_b(self, order):
        for kind in (2, 3):
            slot, _, span = self.CROSSINGS[kind]
            self.turn(order, span).wait_recv()
            at = self.spans[span]
            self.held[order, slot, at] = to_low(
                to_full(self.held[order, slot, at]) + to_full(self.turned[order, span])
            )
            self.cross(order, kind).start()

    def stage_c(self, order):
        total = self.total_of(order, 3)
        for kind in range(4):
            self.cross(order, kind).wait_recv()
        crossed = [to_full(self.crossed[order, kind]) for kind in range(4)]
        total = total + jnp.concatenate(
            [crossed[0] + crossed[2], crossed[1] + crossed[3]], axis=0
        )
        if order == self.inner - 1:
            self.total[...] = total
        else:
            self.line.sums[order] = to_low(total)
            self.line.push_free(order)

    def stage_d(self, order):
        if order == self.inner - 1:
            self.line.add_own(self.total)
        else:
            self.line.push_rest(order)

    def step(self, count):
        for stage, late in (
            (self.stage_b, 1),
            (self.stage_a, 0),
            (self.stage_c, 2),
            (self.stage_d, 3),
        ):
            if 0 <= count - late < self.inner:
                stage(count - late)

    def steps(self):
        return self.inner + 3

    def finish(self):
        for order in range(self.inner):
            for slot in range(4):
                self.to_core(order, slot).wait_send()
            for span in range(2):
                self.turn(order, span).wait_send()
            for kind in range(4):
                self.cross(order, kind).wait_send()
        self.line.finish()

    def whole(self, depart):
        self.begin()
        depart(0)
        for count in range(self.inner + 3):
            self.step(count)
            if count >= 2:
                depart(count - 1)
        self.finish()


def reduce_kernel(inner, staged, depart, p_ref, out_ref, *scratch):
    def leave(number):
        if staged:
            depart(lambda item: item.rank == number)

    if not staged:
        depart()
    Reducer(inner, p_ref, out_ref, scratch).whole(leave)


def reduce_rows(partial, freight=()):
    inner, _, rows, width = partial.shape
    return run(
        functools.partial(reduce_kernel, inner, inner > 1),
        (partial,),
        in_specs=[pl.BlockSpec(memory_space=pl.ANY)],
        out_specs=[pl.BlockSpec(memory_space=pltpu.VMEM)],
        out_shape=[jax.ShapeDtypeStruct((rows, width), jnp.float32)],
        scratch=Reducer.scratch(inner, rows, width),
        freight=freight,
        flips=FLIPS,
        inner=inner,
        late=True,
        micros=25 * inner,
        name="reduce_rows",
    )


def plane_gather(own, target, send, recv):
    part = lax.axis_index("seq")
    half = own.shape[0] // 2
    spans = [pl.ds(0, half), pl.ds(half, half)]
    started = []

    def copy_of(kind, block, span, flip, from_own=False):
        place = target(block).at[spans[span]]
        return pltpu.make_async_remote_copy(
            src_ref=own.at[spans[span]] if from_own else place,
            dst_ref=place,
            send_sem=send.at[kind],
            recv_sem=recv.at[kind],
            device_id={"seq": flipped(part, flip)},
            device_id_type=MESH,
        )

    def push(kind, block, span, flip, from_own=False):
        copy = copy_of(kind, block, span, flip, from_own)
        copy.start()
        started.append(copy)

    def arrived(kind, block, span, flip):
        copy_of(kind, block, span, flip).wait_recv()

    def first():
        for kind, span, flip in (
            (3, 1, 2), (4, 0, 4), (2, 0, 2), (5, 1, 4), (0, 0, 1), (1, 1, 1)
        ):
            push(kind, part, span, flip, True)

    def second():
        side, over = flipped(part, 2), flipped(part, 4)
        arrived(3, side, 1, 2)
        push(6, side, 1, 4)
        arrived(4, over, 0, 4)
        push(7, over, 0, 2)
        push(9, side, 1, 1)
        push(10, over, 0, 1)
        arrived(2, side, 0, 2)
        push(8, side, 0, 1)
        arrived(5, over, 1, 4)
        push(11, over, 1, 1)

    def third():
        far = flipped(part, 6)
        arrived(6, far, 1, 4)
        push(13, far, 1, 1)
        arrived(7, far, 0, 2)
        push(12, far, 0, 1)

    def last():
        for kind, flip, span in (
            (0, 1, 0), (1, 1, 1), (9, 3, 1), (10, 5, 0), (8, 3, 0), (11, 5, 1), (13, 7, 1), (12, 7, 0)
        ):
            arrived(kind, flipped(part, flip), span, 1)
        for copy in started:
            copy.wait_send()

    return first, second, third, last


def line_gather(inner, own, target, send, recv, split=2):
    place, first = own_shard_group(inner)
    half = own.shape[0] // split
    spans = [pl.ds(span * half, half) for span in range(split)]

    def copy_of(way, step, span):
        block = place - step if way == 0 else place + step
        to = place + 1 if way == 0 else place - 1
        spot = target(block).at[spans[span]]
        return pltpu.make_async_remote_copy(
            src_ref=own.at[spans[span]] if step == 0 else spot,
            dst_ref=spot,
            send_sem=send.at[way, step, span],
            recv_sem=recv.at[way, step, span],
            device_id={"shard": first + to},
            device_id_type=MESH,
        )

    def sends(way, step):
        if way == 0:
            return (place < inner - 1) & (place >= step)
        return (place > 0) & (place + step < inner)

    def receives(way, step):
        return place >= step if way == 0 else place + step < inner

    def start(step, span):
        for way in range(2):

            @pl.when(sends(way, step))
            def _():
                copy_of(way, step, span).start()

    def begin():
        for span in range(split):
            start(0, span)

    def onward(step):
        for span in range(split):
            for way in range(2):

                @pl.when(receives(way, step))
                def _():
                    block = place - step if way == 0 else place + step
                    spot = target(block).at[spans[span]]
                    pltpu.make_async_remote_copy(
                        src_ref=spot,
                        dst_ref=spot,
                        send_sem=send.at[way, step - 1, span],
                        recv_sem=recv.at[way, step - 1, span],
                        device_id={"shard": block + first},
                        device_id_type=MESH,
                    ).wait_recv()

            if step < inner - 1:
                start(step, span)

    def finish():
        for step in range(inner - 1):
            for span in range(split):
                for way in range(2):

                    @pl.when(sends(way, step))
                    def _():
                        copy_of(way, step, span).wait_send()

    return begin, onward, finish


def group_gather(inner, own, target, sems):
    part = lax.axis_index("seq")
    place, _ = own_shard_group(inner)
    sources = [place] + peers_in_order(place, inner)
    line_send, line_recv, send, recv = sems
    line = line_gather(inner, own, lambda p: target(p, part), line_send, line_recv)
    planes = [
        plane_gather(
            own if order == 0 else target(source, part),
            lambda b, source=source: target(source, b),
            send.at[order],
            recv.at[order],
        )
        for order, source in enumerate(sources)
    ]
    return line, planes


def group_sems(inner):
    sems = lambda *shape: pltpu.SemaphoreType.DMA(shape)
    steps = max(1, inner - 1)
    return [sems(2, steps, 2), sems(2, steps, 2), sems(inner, 14), sems(inner, 14)]


def gather_kernel(inner, depart, x_ref, out_ref, own_sem, *sems):
    part = lax.axis_index("seq")
    place, _ = own_shard_group(inner)
    own = pltpu.make_async_copy(x_ref, out_ref.at[place, part], own_sem)
    (begin, onward, finish), planes = group_gather(
        inner, x_ref, lambda p, b: out_ref.at[p, b], sems
    )
    if inner > 1:
        begin()
    else:
        depart()
    planes[0][0]()
    own.start()
    planes[0][1]()
    for order in range(1, inner):
        onward(order)
        if order < inner - 1:
            depart(lambda item: item.rank == order - 1)
        else:
            depart(lambda item: item.rank >= order - 1)
        planes[order][0]()
        planes[order - 1][2]()
        planes[order][1]()
    planes[inner - 1][2]()
    for stages in planes:
        stages[3]()
    if inner > 1:
        finish()
    own.wait()


def gather_rows(x, inner, freight=()):
    rows, width = x.shape
    seq_devices = lax.axis_size("seq")
    return run(
        functools.partial(gather_kernel, inner),
        (x,),
        in_specs=[pl.BlockSpec(memory_space=pl.ANY)],
        out_specs=[pl.BlockSpec(memory_space=pl.ANY)],
        out_shape=[jax.ShapeDtypeStruct((inner, seq_devices, rows, width), x.dtype)],
        scratch=[pltpu.SemaphoreType.DMA(())] + group_sems(inner),
        freight=freight,
        flips=FLIPS,
        inner=inner,
        late=True,
        micros=25 * inner,
        name="gather_rows",
    )


def begin_kernel(
    inner,
    depart,
    x_ref,
    g_ref,
    s_ref,
    d_ref,
    in_ref,
    shared_ref,
    out_ref,
    down_ref,
    x_out,
    g_out,
    w_out,
    s_out,
    d_out,
    r_out,
    w_ref,
    r_ref,
    b_ref,
    b_line,
    b_all,
    own_sems,
    pick_sems,
    place_sems,
    *sems,
):
    part = lax.axis_index("seq")
    place, _ = own_shard_group(inner)
    rows = w_ref.shape[0]
    seq_devices = x_out.shape[0]
    picks = []

    def pick(source, target):
        picks.append(pltpu.make_async_copy(source, target, pick_sems.at[len(picks)]))

    shared = shared_ref.shape[1] // seq_devices // 2
    channels = w_ref.shape[1] // 2 - shared
    share, state = b_ref.shape
    at = 0
    for source, extent in ((in_ref, channels), (shared_ref, shared)):
        for side in range(2):
            start = pl.multiple_of((side * seq_devices + part) * extent, extent)
            pick(source.at[:, pl.ds(start, extent)], w_ref.at[:, pl.ds(at, extent)])
            at += extent
    start = pl.multiple_of(part * share, share)
    pick(in_ref.at[pl.ds(start, share), pl.ds(in_ref.shape[1] - state, state)], b_ref)
    halves = seq_devices // inner
    at = 0
    for half in range(halves):
        for source in (out_ref, down_ref):
            fine = source.shape[0] // halves // seq_devices
            start = pl.multiple_of((half * seq_devices + part) * fine, fine)
            pick(source.at[pl.ds(start, fine)], r_ref.at[pl.ds(at, fine)])
            at += fine
    for copy in picks:
        copy.start()
    targets = [
        lambda p: s_out.at[p],
        lambda p: w_out.at[pl.ds(p * rows, rows), pl.ds(0, w_ref.shape[1])],
        lambda p: r_out.at[p],
        lambda p: d_out.at[p],
        lambda p: b_line.at[pl.ds(p * share, share)],
    ]
    sources = [s_ref, w_ref, r_ref, d_ref, b_ref]
    lines = [
        line_gather(
            inner, source, target, sems[2 * order], sems[2 * order + 1], 1 if order == 4 else 2
        )
        for order, (source, target) in enumerate(zip(sources, targets))
    ]
    b_plane = plane_gather(b_line, lambda b: b_all.at[b], sems[16], sems[17])
    line, planes = group_gather(inner, g_ref, lambda p, b: g_out.at[p, b], sems[10:14])
    lines.append(line)
    x_plane = plane_gather(x_ref, lambda b: x_out.at[b], sems[14], sems[15])
    rows_line = lines.pop(2)
    lines[0][0]()
    lines[2][0]()
    lines[4][0]()
    x_plane[0]()
    planes[0][0]()
    for copy in picks:
        copy.wait()
    lines[3][0]()
    lines[1][0]()
    rows_line[0]()
    at_end = (place == 0) | (place == inner - 1)
    depart(gate=at_end)
    owns = [
        pltpu.make_async_copy(source, target(place), own_sems.at[order])
        for order, (source, target) in enumerate(zip(sources, targets))
    ]
    owns.append(pltpu.make_async_copy(x_ref, x_out.at[part], own_sems.at[5]))
    owns.append(pltpu.make_async_copy(g_ref, g_out.at[place, part], own_sems.at[6]))
    for copy in owns:
        copy.start()
    x_plane[1]()
    planes[0][1]()
    x_plane[2]()
    planes[0][2]()
    *other_lines, g_line = lines
    for step in range(1, inner):
        g_line[1](step)
        planes[step][0]()
        if step > 1:
            planes[step - 1][2]()
        planes[step][1]()
        for _, onward, _ in reversed(other_lines):
            onward(step)
        if step == 1:
            rows_line[1](1)
            depart(gate=jnp.logical_not(at_end))
    planes[inner - 1][2]()
    owns[4].wait()
    b_plane[0]()
    for step in range(2, inner):
        rows_line[1](step)
    b_plane[1]()
    b_plane[2]()
    x_plane[3]()
    for stages in planes:
        stages[3]()
    b_plane[3]()
    own_b = pltpu.make_async_copy(b_line, b_all.at[part], own_sems.at[7])
    own_b.start()
    own_b.wait()
    spread = []
    for device in range(seq_devices):
        for shard in range(inner):
            spread.append(
                pltpu.make_async_copy(
                    b_all.at[device, pl.ds(shard * share, share)],
                    w_out.at[
                        pl.ds(shard * rows + device * share, share), pl.ds(w_ref.shape[1], state)
                    ],
                    place_sems.at[device, shard],
                )
            )
    for copy in spread:
        copy.start()
    for _, _, finish in lines + [rows_line]:
        finish()
    for order, copy in enumerate(owns):
        if order != 4:
            copy.wait()
    for copy in spread:
        copy.wait()


def begin(
    x, grad, small, by_depth, w_in, w_shared, w_out, w_down, in_width, shared_part, inner, freight
):
    seq_devices = lax.axis_size("seq")
    low = jnp.bfloat16
    depth, width = w_in.shape[0], w_out.shape[1]
    columns = in_width + 2 * shared_part
    w_columns = 2 * w_out.shape[0] * inner // seq_devices + 2 * shared_part
    rows = (w_out.shape[0] + w_down.shape[0]) // seq_devices
    anywhere = pl.BlockSpec(memory_space=pl.ANY)
    sems = lambda *shape: pltpu.SemaphoreType.DMA(shape)
    line_sems = [sems(2, inner - 1, 2)] * 10
    state = in_width + 2 * shared_part - w_columns
    fine = depth // seq_devices
    return run(
        functools.partial(begin_kernel, inner),
        (x, grad, small, by_depth, w_in, w_shared, w_out, w_down),
        in_specs=[anywhere] * 8,
        out_specs=[anywhere] * 6,
        out_shape=[
            jax.ShapeDtypeStruct((seq_devices,) + x.shape, x.dtype),
            jax.ShapeDtypeStruct((inner, seq_devices) + grad.shape, grad.dtype),
            jax.ShapeDtypeStruct((inner * depth, columns), low),
            jax.ShapeDtypeStruct((inner,) + small.shape, small.dtype),
            jax.ShapeDtypeStruct((inner,) + by_depth.shape, low),
            jax.ShapeDtypeStruct((inner, rows, width), low),
        ],
        scratch=[
            pltpu.VMEM((depth, w_columns), low),
            pltpu.VMEM((rows, width), low),
            pltpu.VMEM((fine, state), low),
            pltpu.VMEM((inner * fine, state), low),
            pltpu.VMEM((seq_devices, inner * fine, state), low),
            sems(8),
            sems(5 + 2 * (seq_devices // inner)),
            sems(seq_devices, inner),
        ]
        + line_sems
        + group_sems(inner)
        + [sems(14)] * 4,
        freight=freight,
        flips=FLIPS,
        inner=inner,
        late=True,
        micros=130,
        name="begin",
    )


def settle_kernel(
    inner,
    counts,
    hidden_ref,
    small_ref,
    x_ref,
    mix_ref,
    gain_ref,
    done_ref,
    *refs,
):
    part = lax.axis_index("seq")
    place, _ = own_shard_group(inner)
    parts, refs = refs[:counts], refs[counts:]
    tokens_out, refs = refs[0], refs[1:]
    outs, refs = refs[: counts + 2], refs[counts + 2 :]
    hidden_sum, small_sum = refs[:2]
    refs = refs[2:]
    take = len(Reducer.scratch(1, 16, LANES))
    hidden = Reducer(1, hidden_ref, hidden_sum, refs[:take])
    small = Reducer(inner, small_ref, small_sum, refs[take : 2 * take])
    refs = refs[2 * take :]
    lines, totals, planes, owns = [], [], [], []
    for index in range(counts + 2):
        low, gsend, grecv, here = refs[:4]
        refs = refs[4:]
        out = outs[index]
        planes.append(plane_gather(low, lambda b, out=out: out.at[b], gsend, grecv))
        owns.append((low, pltpu.make_async_copy(low, out.at[part], here)))
    loads = []
    for index in range(counts):
        total, load = refs[:2]
        line = LineSum(inner, *refs[2:8])
        refs = refs[8:]
        lines.append(line)
        totals.append(total)
        for order in range(inner - 1):
            loads.append(
                pltpu.make_async_copy(
                    parts[index].at[line.targets[order]], line.sums.at[order], load.at[order]
                )
            )
        loads.append(
            pltpu.make_async_copy(parts[index].at[place], owns[index][0], load.at[inner - 1])
        )
    for copy in loads:
        copy.start()
    small.begin()
    hidden.begin()

    def load(index):
        for copy in loads[index * inner : (index + 1) * inner]:
            copy.wait()
        totals[index][...] = to_full(owns[index][0][...])

    def push_free(index, orders):
        for order in orders:
            lines[index].push_free(order)

    def push_rest(index, orders):
        for order in orders:
            lines[index].push_rest(order)

    def gather_part(index):
        lines[index].add_own(totals[index])
        owns[index][0][...] = to_low(totals[index][...])
        planes[index][0]()
        owns[index][1].start()

    every = range(inner - 1)
    owns[counts + 1][0][...] = done_ref[...]
    small.step(0)
    small.step(1)
    load(0)
    push_free(0, every[:1])
    for count in range(2, small.steps() - 2):
        small.step(count)
    hidden.step(0)
    push_free(0, every[1:])
    for index in range(1, counts):
        load(index)
        push_free(index, every)
    push_rest(0, every[:1])
    for count in range(small.steps() - 2, small.steps()):
        small.step(count)
    owns[counts][0][...] = to_low(small_sum[...])
    planes[counts][0]()
    owns[counts][1].start()
    planes[counts + 1][0]()
    owns[counts + 1][1].start()
    hidden.step(1)
    push_rest(0, every[1:])
    planes[counts][1]()
    planes[counts + 1][1]()
    hidden.step(2)
    hidden.step(3)
    planes[counts][2]()
    planes[counts + 1][2]()
    x = to_full(x_ref[...])
    scale = norm_scale(x)
    unit = x * scale
    scaled = hidden_sum[...] * gain_ref[...]
    mean = jnp.mean(scaled * unit, axis=1, keepdims=True)
    tokens_out[...] = to_low(mix_ref[...] + scale * (scaled - unit * mean))
    if counts > 1:
        push_rest(1, every[:1])
    gather_part(0)
    if counts > 1:
        push_rest(1, every[1:])
    for index in range(1, counts):
        planes[index - 1][1]()
        if index > 1:
            planes[index - 2][2]()
        gather_part(index)
        if index + 1 < counts:
            push_rest(index + 1, every)
    if counts > 1:
        planes[counts - 2][2]()
    planes[counts - 1][1]()
    planes[counts - 1][2]()
    for plane in planes:
        plane[3]()
    hidden.finish()
    small.finish()
    for line in lines:
        line.finish()
    for _, copy in owns:
        copy.wait()


def settle(hidden, small, x, mix, gain, done, parts, inner):
    _, _, rows, width = hidden.shape
    seq_devices = lax.axis_size("seq")
    anywhere = pl.BlockSpec(memory_space=pl.ANY)
    inside = pl.BlockSpec(memory_space=pltpu.VMEM)
    low = jnp.bfloat16
    sems = lambda *shape: pltpu.SemaphoreType.DMA(shape)
    small_rows, small_wide = small.shape[2:]
    shapes = [part.shape[1:] for part in parts] + [(small_rows, small_wide), done.shape]
    scratch = [
        pltpu.VMEM((rows, width), jnp.float32),
        pltpu.VMEM((small_rows, small_wide), jnp.float32),
    ]
    scratch += Reducer.scratch(1, rows, width)
    scratch += Reducer.scratch(inner, small_rows, small_wide)
    for shape in shapes:
        scratch += [pltpu.VMEM(shape, low), sems(14), sems(14), sems()]
    for shape in shapes[: len(parts)]:
        scratch += [pltpu.VMEM(shape, jnp.float32), sems(inner)]
        scratch += LineSum.scratch(inner, *shape)
    return run(
        functools.partial(settle_kernel, inner, len(parts)),
        (hidden, small, x, mix, gain, done) + tuple(parts),
        in_specs=[anywhere] * 2 + [inside] * 4 + [anywhere] * len(parts),
        out_specs=[inside] + [anywhere] * len(shapes),
        out_shape=[jax.ShapeDtypeStruct((rows, width), low)]
        + [jax.ShapeDtypeStruct((seq_devices,) + shape, low) for shape in shapes],
        scratch=scratch,
        flips=FLIPS,
        inner=inner,
        micros=90,
        name="settle",
    )


def params_of(limit=VMEM_BYTES):
    return pltpu.CompilerParams(vmem_limit_bytes=limit)


def project_kernel(x_ref, gain_ref, w_ref, dt_ref, hidden_ref, gate_ref, rows_ref):
    x = to_full(x_ref[...])
    hidden = to_low(x * norm_scale(x) * gain_ref[...])
    hidden_ref[...] = hidden
    gate_width = gate_ref.shape[1]
    used = 2 * gate_width
    state = rows_ref.shape[1] - LANES - gate_width
    projected = dot_full(hidden, w_ref[:, :used])
    gate_ref[...] = projected[:, :gate_width]
    rows_ref[:, :gate_width] = to_low(projected[:, gate_width:])
    rows_ref[:, gate_width : gate_width + state] = to_low(
        dot_full(hidden, w_ref[:, w_ref.shape[1] - state :])
    )
    rows_ref[:, gate_width + state :] = to_low(dot_full(hidden, dt_ref[...]))


def project(x, gain, weights, dt_weights, gate_width, columns, freight=()):
    rows, width = x.shape
    columns = columns + LANES
    tile = 256
    block = lambda extent: pl.BlockSpec((tile, extent), lambda step: (step, 0))
    return run(
        project_kernel,
        (x, gain, weights, dt_weights,),
        grid=(rows // tile,),
        in_specs=[
            block(width), whole(gain.shape), whole(weights.shape), whole(dt_weights.shape)
        ],
        out_specs=[block(width), block(gate_width), block(columns - gate_width)],
        out_shape=[
            jax.ShapeDtypeStruct((rows, width), jnp.bfloat16),
            jax.ShapeDtypeStruct((rows, gate_width), jnp.float32),
            jax.ShapeDtypeStruct((rows, columns - gate_width), jnp.bfloat16),
        ],
        freight=freight,
        micros=11,
        name="project",
    )


def put_split(columns, rows):
    lane = iota_of((rows, LANES), 1)
    result = jnp.zeros((rows, LANES), jnp.float32)
    for place, column in enumerate(columns):
        high = to_full(to_low(column))
        result = jnp.where(lane == 2 * place, high, result)
        result = jnp.where(lane == 2 * place + 1, column - high, result)
    return to_low(result)


def mix_out_kernel(y_ref, gate_ref, gain_ref, packed_ref, out_ref, w_ref, sent, *scratch):
    width = w_ref.shape[1]
    rows = out_ref.shape[0]
    unpack_rows(packed_ref, w_ref, True)

    def make(_, block, place):
        at = pl.ds(pl.multiple_of(block * rows, rows), rows)
        gated = to_full(y_ref[at, :]) * jax.nn.silu(gate_ref[at, :])
        place[:, :width] = to_low(dot_full(to_low(gated * gain_ref[...]), w_ref[...]))
        squares = jnp.sum(gated * gated, axis=1, keepdims=True)
        place[:, width:] = put_split([squares], rows)

    Reducer(1, sent, out_ref, scratch, make).whole(lambda number: None)


def mix_out(y, gate, gain, weights, blocks, freight=()):
    rows, channels = y.shape
    width = weights.shape[2]
    tile = rows // blocks
    inside = pl.BlockSpec(memory_space=pltpu.VMEM)
    return run(
        mix_out_kernel,
        (y, gate, gain, weights),
        in_specs=[inside] * 4,
        out_specs=[inside],
        out_shape=[jax.ShapeDtypeStruct((tile, width + LANES), jnp.float32)],
        scratch=[
            pltpu.VMEM((channels, width), jnp.bfloat16),
            pltpu.VMEM((1, 4, tile, width + LANES), jnp.bfloat16),
        ]
        + Reducer.scratch(1, tile, width + LANES),
        freight=freight,
        flips=FLIPS,
        micros=35,
        name="mix_out",
    )


def mix_back_kernel(
    mix_ref,
    y_ref,
    gate_ref,
    gain_ref,
    packed_ref,
    dy_ref,
    dgate_ref,
    w_grad_ref,
    gain_grad_ref,
    total,
    w_ref,
):
    step = pl.program_id(0)
    width = w_ref.shape[1]

    @pl.when(step == 0)
    def _():
        unpack_rows(packed_ref, w_ref, True)
        total[...] = jnp.zeros_like(total)
        gain_grad_ref[...] = jnp.zeros_like(gain_grad_ref)

    mix = mix_ref[0, :, :width]
    extra = to_full(mix_ref[0, :, width:])
    share = extra[:, 0:1] + extra[:, 1:2]
    scale = extra[:, 2:3] + extra[:, 3:4]
    normed_grad = dot_lanes(mix, w_ref[...])
    y = to_full(y_ref[...])
    gate = gate_ref[...]
    sig = jax.nn.sigmoid(gate)
    act = gate * sig
    unit = y * act * scale
    gain = gain_ref[...]
    gain_grad_ref[0:1, :] += jnp.sum(normed_grad * unit, axis=0, keepdims=True)
    gated_grad = scale * (normed_grad * gain - unit * share)
    dy_ref[...] = to_low(gated_grad * act)
    dgate_ref[...] = to_low(gated_grad * y * sig * (1.0 + gate * (1.0 - sig)))
    total[...] += dot_rows(to_low(unit * gain), mix)

    @pl.when(step == pl.num_programs(0) - 1)
    def _():
        w_grad_ref[...] = to_low(total[...])


def mix_back(mix, y, gate, gain, weights, freight=()):
    blocks, tile, wide = mix.shape
    rows, channels = y.shape
    shape = (channels, weights.shape[2])
    block = pl.BlockSpec((tile, channels), lambda step: (step, 0))
    return run(
        mix_back_kernel,
        (mix, y, gate, gain, weights,),
        grid=(blocks,),
        in_specs=[
            pl.BlockSpec((1, tile, wide), lambda step: (step, 0, 0)),
            block,
            block,
            whole(gain.shape),
            whole(weights.shape),
        ],
        out_specs=[block, block, whole(shape), whole((8, channels))],
        out_shape=[
            jax.ShapeDtypeStruct((rows, channels), jnp.bfloat16),
            jax.ShapeDtypeStruct((rows, channels), jnp.bfloat16),
            jax.ShapeDtypeStruct(shape, jnp.bfloat16),
            jax.ShapeDtypeStruct((8, channels), jnp.float32),
        ],
        scratch=[pltpu.VMEM(shape, jnp.float32), pltpu.VMEM(shape, jnp.bfloat16)],
        freight=freight,
        micros=12,
        name="mix_back",
    )


def project_back_kernel(
    dgate_ref, drows_ref, hidden_ref, w_ref, dt_ref, part_ref, main_grad_ref, rest_grad_ref, total
):
    step = pl.program_id(0)

    @pl.when(step == 0)
    def _():
        total[...] = jnp.zeros_like(total)

    grads = jnp.concatenate([dgate_ref[...], drows_ref[...]], axis=1)
    main = 2 * dgate_ref.shape[1]
    columns = grads.shape[1] - LANES
    state_at = w_ref.shape[1] - (columns - main)
    part_ref[0] = to_low(
        dot_lanes(grads[:, :main], w_ref[:, :main])
        + dot_lanes(grads[:, main:columns], w_ref[:, state_at:])
        + dot_lanes(grads[:, columns:], dt_ref[...])
    )
    total[...] += dot_rows(hidden_ref[...], grads)

    @pl.when(step == pl.num_programs(0) - 1)
    def _():
        main_grad_ref[...] = to_low(total[:, :main])
        rest_grad_ref[...] = to_low(total[:, main:])
        by_gain = jnp.sum(total[:, :main] * to_full(w_ref[:, :main]), axis=1, keepdims=True)
        by_gain += jnp.sum(
            total[:, main:columns] * to_full(w_ref[:, state_at:]), axis=1, keepdims=True
        )
        by_gain += jnp.sum(total[:, columns:] * to_full(dt_ref[...]), axis=1, keepdims=True)
        rest = rest_grad_ref.shape[1]
        lane = iota_of((rest_grad_ref.shape[0], LANES), 1)
        rest_grad_ref[:, rest - LANES :] = to_low(
            jnp.where(lane == LANES - 1, by_gain, total[:, columns:])
        )


def project_back(dgate, drows, hidden, weights, dt_weights, blocks, freight=()):
    rows, width = hidden.shape
    tile = rows // blocks
    main = 2 * dgate.shape[1]
    rest = dgate.shape[1] + drows.shape[1] - main
    block = lambda extent: pl.BlockSpec((tile, extent), lambda step: (step, 0))
    return run(
        project_back_kernel,
        (dgate, drows, hidden, weights, dt_weights,),
        grid=(blocks,),
        in_specs=[
            block(dgate.shape[1]),
            block(drows.shape[1]),
            block(width),
            whole(weights.shape),
            whole(dt_weights.shape),
        ],
        out_specs=[
            pl.BlockSpec((1, tile, width), lambda step: (step, 0, 0)),
            whole((width, main)),
            whole((width, rest)),
        ],
        out_shape=[
            jax.ShapeDtypeStruct((blocks, tile, width), jnp.bfloat16),
            jax.ShapeDtypeStruct((width, main), jnp.bfloat16),
            jax.ShapeDtypeStruct((width, rest), jnp.bfloat16),
        ],
        scratch=[pltpu.VMEM((width, main + rest), jnp.float32)],
        freight=freight,
        micros=25,
        name="project_back",
    )


def unpack_rows(packed_ref, held_ref, first):
    blocks, both, _ = packed_ref.shape
    fine = held_ref.shape[0] // blocks
    start = 0 if first else both - fine
    for block in range(blocks):
        held_ref[block * fine : (block + 1) * fine] = packed_ref[block, start : start + fine]


def shared_kernel(
    rows_ref,
    grad_ref,
    up_ref,
    down_ref,
    res_ref,
    back_ref,
    up_grad_ref,
    down_grad_ref,
    up_sum,
    down_sum,
    down_held,
):
    step = pl.program_id(0)

    @pl.when(step == 0)
    def _():
        up_sum[...] = jnp.zeros_like(up_sum)
        down_sum[...] = jnp.zeros_like(down_sum)
        unpack_rows(down_ref, down_held, False)

    hidden, width = down_held.shape
    rows = rows_ref[0, :, :width]
    grad = grad_ref[0]
    joined = dot_full(rows, up_ref[...])
    gate, up = joined[:, :hidden], joined[:, hidden:]
    sig = jax.nn.sigmoid(gate)
    act = gate * sig
    acted = to_low(act * up)
    res_ref[0] = to_low(dot_full(acted, down_held[...]))
    down_sum[...] += dot_rows(acted, grad)
    act_grad = dot_lanes(grad, down_held[...])
    joined_grad = to_low(
        jnp.concatenate(
            [act_grad * up * sig * (1.0 + gate * (1.0 - sig)), act_grad * act], axis=1
        )
    )
    up_sum[...] += dot_rows(rows, joined_grad)
    back_ref[0] = to_low(dot_lanes(joined_grad, up_ref[...]))

    @pl.when(step == pl.num_programs(0) - 1)
    def _():
        up_grad_ref[...] = to_low(up_sum[...])
        down_grad_ref[...] = to_low(down_sum[...])


def shared_expert(rows, grad, up, up_at, down, hidden, blocks, inner, freight=()):
    _, tile, wide = rows.shape
    width = down.shape[2]
    down_shape = (hidden, width)
    up_shape = (width, 2 * hidden)
    block = pl.BlockSpec((1, tile, width), lambda step: (step, 0, 0))
    low = jnp.bfloat16
    own = lambda extent: pl.BlockSpec(
        (1, tile, extent), lambda step: (own_shard_group(inner)[0] * blocks + step, 0, 0)
    )
    return run(
        shared_kernel,
        (rows, grad, up, down),
        grid=(blocks,),
        in_specs=[
            own(wide),
            own(width),
            pl.BlockSpec((width, up_shape[1]), lambda step: (0, up_at // up_shape[1])),
            whole(down.shape),
        ],
        out_specs=[block, block, whole(up_shape), whole(down_shape)],
        out_shape=[
            jax.ShapeDtypeStruct((blocks, tile, width), low),
            jax.ShapeDtypeStruct((blocks, tile, width), low),
            jax.ShapeDtypeStruct(up_shape, low),
            jax.ShapeDtypeStruct(down_shape, low),
        ],
        scratch=[
            pltpu.VMEM(up_shape, jnp.float32),
            pltpu.VMEM(down_shape, jnp.float32),
            pltpu.VMEM(down_shape, low),
        ],
        freight=freight,
        micros=18,
        name="shared_expert",
    )


def dispatch_kernel(
    rows_ref, grad_ref, x_ref, g_ref, picks_ref, *, top_count, slots, own_first
):
    per_device = x_ref.shape[0]
    together, tok_rows, _ = rows_ref.shape
    width = g_ref.shape[2]
    wide = width + LANES
    taken = per_device * slots
    lane = iota_of((tok_rows, LANES), 1)
    named = (lane >= 2 * top_count) & (lane < 3 * top_count)
    before = iota_of((tok_rows, tok_rows), 0) > iota_of((tok_rows, tok_rows), 1)
    before = to_low(jnp.where(before, 1.0, 0.0))
    first = own_first()
    for index in range(together):
        extra = to_full(rows_ref[index, :, width:wide])
        member = jnp.zeros((tok_rows, LANES), jnp.float32)
        for expert in range(per_device):
            own = (first + expert).astype(jnp.float32)
            hit = jnp.sum(jnp.where(named & (extra == own), 1.0, 0.0), axis=1, keepdims=True)
            member = jnp.where(lane // slots == expert, hit, member)
        ranks = dot_full(before, to_low(member))
        picks = jnp.where(
            (ranks == to_full(lane % slots)) & (member > 0.0), 1.0, 0.0
        ).astype(jnp.bfloat16)
        picks_ref[index] = picks
        rows = to_low(dot_rows(picks[:, :taken], rows_ref[index]))
        grads = to_low(dot_rows(picks[:, :taken], grad_ref[index]))
        start = index * slots
        for expert in range(per_device):
            span = slice(expert * slots, (expert + 1) * slots)
            x_ref[expert, start : start + slots] = rows[span]
            g_ref[expert, start : start + slots] = grads[span]


def dispatch(rows, grad, per_device, top_count, slots, own_first, freight=()):
    blocks, tok_rows, wide = rows.shape
    width = grad.shape[2]
    together = 4
    block = lambda extent: pl.BlockSpec((together, tok_rows, extent), lambda step: (step, 0, 0))
    taken = lambda extent: pl.BlockSpec(
        (per_device, together * slots, extent), lambda step: (0, step, 0)
    )
    return run(
        functools.partial(
            dispatch_kernel, top_count=top_count, slots=slots, own_first=own_first
        ),
        (rows, grad),
        grid=(blocks // together,),
        in_specs=[block(wide), block(width)],
        out_specs=[taken(width + LANES), taken(width), block(LANES)],
        out_shape=[
            jax.ShapeDtypeStruct((per_device, blocks * slots, width + LANES), jnp.bfloat16),
            jax.ShapeDtypeStruct((per_device, blocks * slots, width), jnp.bfloat16),
            jax.ShapeDtypeStruct((blocks, tok_rows, LANES), jnp.bfloat16),
        ],
        freight=freight,
        micros=30,
        name="dispatch",
    )


def experts_kernel(
    depart, arrive, targets, *refs, count, per_device, top_count, own_first, inner, doubles, outgoing
):
    x_ref, g_ref = refs[:2]
    total = 2 * count * per_device
    pieces, refs = refs[2 : 2 + total], refs[2 + total :]
    seconds, came = {}, list(targets)
    for number, (_, carried) in doubles.items():
        if carried:
            seconds[number] = came.pop(0)
        else:
            seconds[number], refs = refs[0], refs[1:]
    is_incoming = lambda item: item.output is None
    is_outgoing = lambda item: item.output is not None
    late = any(carried for _, carried in doubles.values())
    res_ref, dx_ref = refs[:2]
    outs = refs[2 : 2 + total]
    up_held, down_held, up_sum, down_sum, up_low, down_low, sems = refs[2 + total :]
    own_place, _ = own_shard_group(inner)
    expert, step = pl.program_id(0), pl.program_id(1)
    steps = pl.num_programs(1)
    slot = lax.rem(expert, 2)
    width, double = up_held.shape[1:]
    hidden = double // 2
    tile = x_ref.shape[1]

    def parts(which, up, down):
        result = []
        for shift in range(count):
            from_place = lax.rem(own_place + count - shift, count)
            for kind, held in enumerate((up, down)):
                extent = held.shape[0] // count
                start = pl.multiple_of(from_place * extent, extent)
                number = (shift * per_device + which) * 2 + kind
                result.append((number, held.at[pl.ds(start, extent)], (shift, kind)))
        return result

    def fetch(which, action):
        half = which % 2
        for number, held, at in parts(which, up_held.at[half], down_held.at[half]):
            sem = sems.at[half, at[0], at[1]]
            piece = pieces[number]
            if len(piece.shape) == 3:
                piece = piece.at[own_place * per_device + which]
            if number in seconds:
                early = among(own_place, doubles[number][0])
                pl.when(early)(
                    lambda: action(pltpu.make_async_copy(piece, held, sem))
                )
                pl.when(jnp.logical_not(early))(
                    lambda: action(pltpu.make_async_copy(seconds[number], held, sem))
                )
            else:
                action(pltpu.make_async_copy(piece, held, sem))

    begin_copy = lambda copy: copy.start()
    end_copy = lambda copy: copy.wait()

    for which in range(per_device):

        @pl.when((step == 0) & (expert == which))
        def _():
            if which == 0:
                fetch(0, begin_copy)
                depart(is_incoming)
            if which == 1:
                arrive(is_incoming)
                depart(is_outgoing)
                if late:
                    fetch(1, begin_copy)
            fetch(which, end_copy)
            if which + 1 < per_device and not (late and which == 0):
                fetch(which + 1, begin_copy)

    @pl.when(step == 0)
    def _():
        up_sum[...] = jnp.zeros_like(up_sum)
        down_sum[...] = jnp.zeros_like(down_sum)

    up, down = up_held.at[slot], down_held.at[slot]
    rows = x_ref[0, :, :width]
    extra = to_full(x_ref[0, :, width:])
    lane = iota_of((tile, LANES), 1)
    own = own_first() + expert
    hits = jnp.where((lane < 3 * top_count) & (extra == own.astype(jnp.float32)), 1.0, 0.0)
    gate_slot = jnp.zeros((tile, 1), jnp.float32)
    for route in range(top_count):
        place = 2 * top_count + route
        value = extra[:, 2 * route : 2 * route + 1] + extra[:, 2 * route + 1 : 2 * route + 2]
        gate_slot = gate_slot + hits[:, place : place + 1] * value
    joined = dot_full(rows, up[...])
    gate, lift = joined[:, :hidden], joined[:, hidden:]
    sig = jax.nn.sigmoid(gate)
    act = gate * sig
    acted = to_low(act * lift)
    res = to_low(dot_full(acted, down[...]))
    grads = g_ref[0]
    wide_grads = to_full(grads)
    wide_res = to_full(res)
    gate_grad = jnp.sum(wide_res * wide_grads, axis=1, keepdims=True)
    res_ref[0] = to_low(wide_res * gate_slot)
    weighted = to_low(wide_grads * gate_slot)
    act_grad = dot_lanes(weighted, down[...])
    down_sum[...] += dot_rows(acted, weighted)
    joined_grad = to_low(
        jnp.concatenate(
            [act_grad * lift * sig * (1.0 + gate * (1.0 - sig)), act_grad * act], axis=1
        )
    )
    dx_ref[0, :, :width] = to_low(dot_lanes(joined_grad, up[...]))
    high = to_full(to_low(gate_grad))
    half = LANES // 2
    dx_ref[0, :, width:] = to_low(
        jnp.where(lane == own, high, 0.0) + jnp.where(lane == own + half, gate_grad - high, 0.0)
    )
    up_sum[...] += dot_rows(rows, joined_grad)

    for which in range(per_device):

        @pl.when((step == steps - 1) & (expert == which))
        def _():
            up_low[...] = to_low(up_sum[...])
            down_low[...] = to_low(down_sum[...])
            copies = [
                pltpu.make_async_copy(held, outs[number], sems.at[2, at[0], at[1]])
                for number, held, at in parts(which, up_low, down_low)
            ]
            for copy in copies:
                copy.start()
            for copy in copies:
                copy.wait()

    if outgoing:

        @pl.when((step == steps - 1) & (expert == per_device - 1))
        def _():
            arrive(is_outgoing)


def experts(x, g, pieces, hidden, top_count, own_first, inner, doubles=(), outgoing=()):
    per_device, rows, wide = x.shape
    width = g.shape[2]
    count = len(pieces) // per_device // 2
    low = jnp.bfloat16
    shapes = [jax.ShapeDtypeStruct(piece.shape[-2:], low) for piece in pieces]
    carried = [other for _, other, _ in doubles if isinstance(other, Parcel)]
    freight = carried + [
        Parcel(shapes[key], shift, inner, output=2 + key) for key, shift in outgoing
    ]
    others = [other for _, other, _ in doubles if not isinstance(other, Parcel)]
    double = 2 * hidden
    tile = min(rows, 256)
    block = lambda extent: pl.BlockSpec((1, tile, extent), lambda e, step: (e, step, 0))
    anywhere = pl.BlockSpec(memory_space=pl.ANY)
    low = jnp.bfloat16
    outs = run(
        functools.partial(
            experts_kernel,
            count=count,
            per_device=per_device,
            top_count=top_count,
            own_first=own_first,
            inner=inner,
            doubles={
                number: (places, isinstance(other, Parcel)) for number, other, places in doubles
            },
            outgoing=outgoing,
        ),
        (x, g) + tuple(pieces) + tuple(others),
        grid=(per_device, rows // tile),
        in_specs=[block(wide), block(width)] + [anywhere] * (len(pieces) + len(others)),
        out_specs=[block(width), block(wide)] + [anywhere] * len(shapes),
        out_shape=[
            jax.ShapeDtypeStruct((per_device, rows, width), low),
            jax.ShapeDtypeStruct((per_device, rows, wide), low),
        ]
        + shapes,
        scratch=[
            pltpu.VMEM((2, width, double), low),
            pltpu.VMEM((2, hidden, width), low),
            pltpu.VMEM((width, double), jnp.float32),
            pltpu.VMEM((hidden, width), jnp.float32),
            pltpu.VMEM((width, double), low),
            pltpu.VMEM((hidden, width), low),
            pltpu.SemaphoreType.DMA((3, count, 2)),
        ],
        freight=freight,
        inner=inner if freight else 1,
        late=True,
        micros=45,
        name="experts",
    )
    sent = outs.pop()[len(carried) :] if freight else []
    return outs[0], outs[1], outs[2:], sent


def combine_kernel(
    picks_ref, res_ref, dx_ref, sres_ref, sback_ref, out_ref, back_ref, *, slots, inner
):
    step = pl.program_id(0)
    together, _, width = out_ref.shape
    per_device = res_ref.shape[0]
    blocks = sres_ref.shape[0]
    place, _ = own_shard_group(inner)
    for index in range(together):
        picks = picks_ref[index, :, : per_device * slots]
        start = index * slots
        stacked = lambda ref: jnp.concatenate(
            [ref[expert, start : start + slots] for expert in range(per_device)], axis=0
        )
        out_ref[index] = to_low(dot_full(picks, stacked(res_ref)))
        back_ref[index] = to_low(dot_full(picks, stacked(dx_ref)))

    @pl.when(lax.div(step * together, blocks) == place)
    def _():
        first = lax.rem(step * together, blocks)
        for index in range(together):
            out_ref[index] = to_low(to_full(out_ref[index]) + to_full(sres_ref[first + index]))
            back_ref[index, :, :width] = to_low(
                to_full(back_ref[index, :, :width]) + to_full(sback_ref[first + index])
            )


def combine(picks, res, dx, shared_res, shared_back, inner, freight=()):
    blocks, tok_rows, _ = picks.shape
    per_device, rows, width = res.shape
    slots = rows // blocks
    together = 4
    block = lambda extent: pl.BlockSpec((together, tok_rows, extent), lambda step: (step, 0, 0))
    taken = lambda extent: pl.BlockSpec(
        (per_device, together * slots, extent), lambda step: (0, step, 0)
    )
    return run(
        functools.partial(combine_kernel, slots=slots, inner=inner),
        (picks, res, dx, shared_res, shared_back),
        grid=(blocks // together,),
        in_specs=[
            block(LANES),
            taken(width),
            taken(width + LANES),
            whole(shared_res.shape),
            whole(shared_back.shape),
        ],
        out_specs=[block(width), block(width + LANES)],
        out_shape=[
            jax.ShapeDtypeStruct((blocks, tok_rows, width), jnp.bfloat16),
            jax.ShapeDtypeStruct((blocks, tok_rows, width + LANES), jnp.bfloat16),
        ],
        freight=freight,
        micros=30,
        name="combine",
    )


def assemble_kernel(
    main_ref, shared_in_ref, small_ref, rows_ref, w_in_ref, shared_ref, out_ref, down_ref
):
    seq_devices, rows, double = main_ref.shape
    channels = double // 2
    for device in range(seq_devices):
        for target, source in ((w_in_ref, main_ref), (shared_ref, shared_in_ref)):
            extent = source.shape[2] // 2
            for side in range(2):
                start = (side * seq_devices + device) * extent
                target[:, start : start + extent] = to_full(
                    source[device, :, side * extent : (side + 1) * extent]
                )
    start = 2 * seq_devices * channels
    w_in_ref[:, start:] = to_full(small_ref[0, :rows, : w_in_ref.shape[1] - start])
    halves, _, out_rows, _ = out_ref.shape
    down_rows = down_ref.shape[2]
    for half in range(halves):
        at = half * (out_rows + down_rows)
        out_ref[half, 0] = to_full(rows_ref[0, at : at + out_rows])
        down_ref[half, 0] = to_full(rows_ref[0, at + out_rows : at + out_rows + down_rows])


def assemble(main, shared, small, rows, columns, shared_columns, out_rows, down_rows, halves):
    seq_devices, depth_rows, _ = main.shape
    tile = depth_rows // seq_devices
    width = rows.shape[2]
    out_fine = out_rows // halves // seq_devices
    down_fine = down_rows // halves // seq_devices
    flat = lambda extent: pl.BlockSpec((tile, extent), lambda step: (step, 0))
    fine = lambda extent: pl.BlockSpec(
        (halves, 1, extent, width), lambda step: (0, step, 0, 0)
    )
    full = jnp.float32
    results = pl.pallas_call(
        assemble_kernel,
        grid=(seq_devices,),
        in_specs=[
            pl.BlockSpec((seq_devices, tile, main.shape[2]), lambda step: (0, step, 0)),
            pl.BlockSpec((seq_devices, tile, shared.shape[2]), lambda step: (0, step, 0)),
            pl.BlockSpec((1,) + small.shape[1:], lambda step: (step, 0, 0)),
            pl.BlockSpec((1,) + rows.shape[1:], lambda step: (step, 0, 0)),
        ],
        out_specs=[flat(columns), flat(shared_columns), fine(out_fine), fine(down_fine)],
        out_shape=[
            jax.ShapeDtypeStruct((depth_rows, columns), full),
            jax.ShapeDtypeStruct((depth_rows, shared_columns), full),
            jax.ShapeDtypeStruct((halves, seq_devices, out_fine, width), full),
            jax.ShapeDtypeStruct((halves, seq_devices, down_fine, width), full),
        ],
        compiler_params=params_of(),
        cost_estimate=cost_of(10),
        name="assemble",
    )(main, shared, small, rows)
    return results[0], results[1], results[2].reshape(-1, width), results[3].reshape(-1, width)


def collect_kernel(place_ref, *refs):
    del place_ref
    step = pl.program_id(0)
    up_ref, down_ref = refs[-2:]
    for order in range(len(refs) // 2 - 1):

        @pl.when(step == order)
        def _():
            up_ref[0] = to_full(refs[2 * order][...])
            down_ref[0] = to_full(refs[2 * order + 1][...])


def collect(place, pieces, per_device):
    count = len(pieces) // 2
    up, down = pieces[0].shape, pieces[1].shape

    def here(step, place):
        shift, expert = lax.div(step, per_device), lax.rem(step, per_device)
        return (
            lax.rem(place[0] + shift, count // per_device) * per_device + expert, 0, 0
        )

    still = lambda shape: pl.BlockSpec(shape, lambda step, place: (0, 0))
    return pl.pallas_call(
        collect_kernel,
        grid_spec=pltpu.PrefetchScalarGridSpec(
            num_scalar_prefetch=1,
            grid=(count,),
            in_specs=[still(up), still(down)] * count,
            out_specs=[pl.BlockSpec((1,) + up, here), pl.BlockSpec((1,) + down, here)],
        ),
        out_shape=[
            jax.ShapeDtypeStruct((count,) + up, jnp.float32),
            jax.ShapeDtypeStruct((count,) + down, jnp.float32),
        ],
        compiler_params=params_of(),
        cost_estimate=cost_of(12),
        name="collect",
    )(place, *pieces)


def route_hits(routes, route, lane):
    return lane == routes[:, route : route + 1]


def token_forward_kernel(
    mixed_ref, x_ref, gain_ref, router_ref, routes_ref, after_ref, wide_ref, gates_ref, *, inner_width, top_count
):
    width = x_ref.shape[1]
    rows = x_ref.shape[0]
    squares = mixed_ref[:, width : width + 1] + mixed_ref[:, width + 1 : width + 2]
    scale = lax.rsqrt(squares / inner_width + EPSILON)
    after = to_full(x_ref[...]) + mixed_ref[:, :width] * scale
    after_ref[...] = after
    moe_in = to_low(after * norm_scale(after) * gain_ref[...])
    wide_ref[:, :width] = moe_in
    logits = dot_full(moe_in, router_ref[...])
    lane = iota_of((rows, LANES), 1)
    routes = routes_ref[...]
    picked = [
        jnp.sum(jnp.where(route_hits(routes, k, lane), logits, 0.0), axis=1, keepdims=True)
        for k in range(top_count)
    ]
    largest = functools.reduce(jnp.maximum, picked)
    powers = [jnp.exp(value - largest) for value in picked]
    total = sum(powers)
    gates = jnp.zeros((rows, LANES), jnp.float32)
    extra = jnp.zeros((rows, LANES), jnp.float32)
    for k in range(top_count):
        value = powers[k] / total
        high = to_full(to_low(value))
        gates = jnp.where(lane == k, value, gates)
        extra = jnp.where(lane == 2 * k, high, extra)
        extra = jnp.where(lane == 2 * k + 1, value - high, extra)
        extra = jnp.where(lane == 2 * top_count + k, to_full(routes[:, k : k + 1]), extra)
    gates_ref[...] = jnp.where(lane == top_count, scale, gates)
    wide_ref[:, width:] = to_low(extra)


def token_forward(mixed, x, gain, router, routes, inner_width, top_count):
    rows, width = x.shape
    arrays = (mixed, x, gain, router, routes)
    return pl.pallas_call(
        functools.partial(
            token_forward_kernel, inner_width=inner_width, top_count=top_count
        ),
        in_specs=[whole(array.shape) for array in arrays],
        out_specs=[whole((rows, width)), whole((rows, width + LANES)), whole((rows, LANES))],
        out_shape=[
            jax.ShapeDtypeStruct((rows, width), jnp.float32),
            jax.ShapeDtypeStruct((rows, width + LANES), jnp.bfloat16),
            jax.ShapeDtypeStruct((rows, LANES), jnp.float32),
        ],
        compiler_params=params_of(),
        cost_estimate=cost_of(5),
        name="token_forward",
    )(*arrays)


def token_back_kernel(
    back_ref,
    mixed_ref,
    after_ref,
    wide_ref,
    gates_ref,
    grad_ref,
    gain_ref,
    router_ref,
    routes_ref,
    mix_ref,
    mix_wide_ref,
    router_grad_ref,
    gain_grad_ref,
    *,
    inner_width,
    top_count,
):
    rows, width = grad_ref.shape
    lane = iota_of((rows, LANES), 1)
    half = LANES // 2
    routes = routes_ref[...]
    gates = gates_ref[...]
    all_grads = back_ref[:, width:]
    values = [gates[:, k : k + 1] for k in range(top_count)]
    grads = [
        jnp.sum(
            jnp.where(
                route_hits(routes, k, lane) | route_hits(routes, k, lane - half), all_grads, 0.0
            ),
            axis=1,
            keepdims=True,
        )
        for k in range(top_count)
    ]
    common = sum(value * grad for value, grad in zip(values, grads))
    logit_grad = jnp.zeros((rows, LANES), jnp.float32)
    for k in range(top_count):
        logit_grad = jnp.where(
            route_hits(routes, k, lane), values[k] * (grads[k] - common), logit_grad
        )
    logit_grad = to_low(logit_grad)
    router_grad_ref[...] = to_low(dot_rows(wide_ref[:, :width], logit_grad))
    moe_grad = back_ref[:, :width] + dot_lanes(logit_grad, router_ref[...])
    after = after_ref[...]
    scale = norm_scale(after)
    unit = after * scale
    gain_grad_ref[...] = jnp.broadcast_to(
        jnp.sum(moe_grad * unit, axis=0, keepdims=True), (8, width)
    )
    scaled = moe_grad * gain_ref[...]
    mean = jnp.mean(scaled * unit, axis=1, keepdims=True)
    mix = to_full(grad_ref[...]) + scale * (scaled - unit * mean)
    mix_ref[...] = mix
    mix_low = to_low(mix)
    mix_wide_ref[:, :width] = mix_low
    mix_scale = gates[:, top_count : top_count + 1]
    share = jnp.sum(to_full(mix_low) * mixed_ref[:, :width], axis=1, keepdims=True)
    mix_wide_ref[:, width:] = put_split([share * mix_scale / inner_width, mix_scale], rows)


def token_back(back, mixed, after, wide, gates, grad, gain, router, routes, inner_width, top_count):
    rows, width = grad.shape
    arrays = (back, mixed, after, wide, gates, grad, gain, router, routes)
    return pl.pallas_call(
        functools.partial(token_back_kernel, inner_width=inner_width, top_count=top_count),
        in_specs=[whole(array.shape) for array in arrays],
        out_specs=[
            whole((rows, width)),
            whole((rows, width + LANES)),
            whole((width, LANES)),
            whole((8, width)),
        ],
        out_shape=[
            jax.ShapeDtypeStruct((rows, width), jnp.float32),
            jax.ShapeDtypeStruct((rows, width + LANES), jnp.bfloat16),
            jax.ShapeDtypeStruct((width, LANES), jnp.bfloat16),
            jax.ShapeDtypeStruct((8, width), jnp.float32),
        ],
        compiler_params=params_of(),
        cost_estimate=cost_of(6),
        name="token_back",
    )(*arrays)


ROWS_AFTER = 16


def pack_kernel(
    rest_ref, router_ref, conv_ref, head_ref, gate_ref, moe_ref, out_ref, wide, *, inner_width, experts, heads
):
    part = lax.axis_index("seq")
    inner, seq_devices, block_rows, columns = out_ref.shape
    depth = block_rows - ROWS_AFTER
    state = columns - LANES
    lane = iota_of((rest_ref.shape[0], LANES), 1)
    last = to_full(rest_ref[:, state:])
    steps = jnp.where(lane < heads, last, 0.0)
    extra = to_full(router_ref[...]) + pltpu.roll(steps, experts + heads * part, 1)
    extra = to_low(jnp.where(lane == LANES - 1, last, extra))
    for shard in range(inner):
        for device in range(seq_devices):
            start = (shard * seq_devices + device) * depth
            out_ref[shard, device, :depth, :state] = rest_ref[start : start + depth, :state]
            out_ref[shard, device, :depth, state:] = extra[start : start + depth]
    channels = gate_ref.shape[1]
    others = conv_ref.shape[1] - channels
    wide[...] = jnp.zeros_like(wide)
    own = pl.ds(pl.multiple_of(part * channels, channels), channels)
    wide[:8, own] = conv_ref[:, :channels]
    wide[:8, inner_width : inner_width + others] = conv_ref[:, channels:]
    wide[8:, own] = gate_ref[...]
    convs = wide[:8, :]
    gates = wide[8:, :]
    per_conv = (inner_width + others) // inner
    per_gate = inner_width // inner
    width = moe_ref.shape[1] // inner
    row = iota_of((ROWS_AFTER, columns), 0)
    blank = jnp.zeros((1, columns), jnp.float32)
    head_lane = iota_of((8, LANES), 1)
    values = jnp.where(head_lane < heads, head_ref[...], 0.0)
    values = [
        jnp.concatenate([pltpu.roll(values, heads * part, 1)[k : k + 1], blank[:, LANES:]], axis=1)
        for k in range(3)
    ]
    moe = moe_ref[...]

    def pieces(rows, at, start, extent):
        count = -(-extent // columns)
        return [rows[at : at + 1, start + k * columns : start + (k + 1) * columns] for k in range(count)]

    for shard in range(inner):
        for device in range(seq_devices):
            if device < 5:
                lines = pieces(convs, device, shard * per_conv, per_conv)
            elif device == 5:
                lines = pieces(gates, 0, shard * per_gate, per_gate)
            elif device == 6:
                lines = values
            else:
                lines = [moe[:1, shard * width : (shard + 1) * width]]
                lines = [jnp.concatenate([lines[0], blank[:, width:]], axis=1) if width < columns else lines[0]]
            tile = jnp.zeros((ROWS_AFTER, columns), jnp.float32)
            for k, line in enumerate(lines):
                tile = jnp.where(row == k, line, tile)
            out_ref[shard, device, depth:] = to_low(tile)


def pack(rest, router, conv, head, gate, moe, inner, seq_devices, inner_width, experts, heads):
    depth = rest.shape[0] // inner // seq_devices
    columns = rest.shape[1]
    arrays = (rest, router, conv, head, gate, moe)
    reach = inner_width + conv.shape[1] - gate.shape[1] + columns
    return pl.pallas_call(
        functools.partial(pack_kernel, inner_width=inner_width, experts=experts, heads=heads),
        in_specs=[whole(array.shape) for array in arrays],
        out_specs=whole((inner, seq_devices, depth + ROWS_AFTER, columns)),
        out_shape=jax.ShapeDtypeStruct(
            (inner, seq_devices, depth + ROWS_AFTER, columns), jnp.bfloat16
        ),
        scratch_shapes=[pltpu.VMEM((16, -(-reach // LANES) * LANES), jnp.float32)],
        compiler_params=params_of(),
        cost_estimate=cost_of(3),
        name="pack",
    )(*arrays)


def rows_to_send(weights, part):
    seq_devices = lax.axis_size("seq")
    halves = max(1, seq_devices // lax.axis_size("shard"))
    mine = []
    for weight in weights:
        view = weight.reshape(halves, seq_devices, -1, weight.shape[1])
        mine.append(lax.dynamic_index_in_dim(view, part, 1, keepdims=False))
    return jnp.concatenate(mine, axis=1).reshape(-1, weights[0].shape[1])


def rows_by_owner(joined):
    seq_devices = lax.axis_size("seq")
    return joined.reshape(seq_devices, -1, joined.shape[2])


def rows_of_owner(taken, weights):
    seq_devices = lax.axis_size("seq")
    halves = max(1, seq_devices // lax.axis_size("shard"))
    fine_rows = [weight.shape[0] // halves // seq_devices for weight in weights]
    width = taken.shape[2]
    taken = taken.reshape(seq_devices, -1, sum(fine_rows), width).transpose(1, 0, 2, 3)
    results, start = [], 0
    for fine in fine_rows:
        results.append(taken[:, :, start : start + fine].reshape(-1, width))
        start += fine
    return results


def rows_from_owner(grads):
    seq_devices = lax.axis_size("seq")
    shard_devices = lax.axis_size("shard")
    width = grads[0].shape[1]
    turns = shard_devices * max(1, seq_devices // shard_devices) // seq_devices
    pieces = [
        grad.reshape(turns, seq_devices, -1, width).transpose(1, 0, 2, 3) for grad in grads
    ]
    return jnp.concatenate(pieces, axis=2).reshape(seq_devices, -1, width)


def rows_of_shard(joined, weights):
    seq_devices = lax.axis_size("seq")
    halves = max(1, seq_devices // lax.axis_size("shard"))
    fine_rows = [weight.shape[0] // halves // seq_devices for weight in weights]
    width = joined.shape[2]
    spread = joined.reshape(seq_devices, halves, -1, width).transpose(1, 0, 2, 3)
    results, start = [], 0
    for fine in fine_rows:
        results.append(to_full(spread[:, :, start : start + fine]).reshape(-1, width))
        start += fine
    return results


def inner_groups(inner):
    count = lax.axis_size("shard")
    return [list(range(start, start + inner)) for start in range(0, count, inner)]


def outer_groups(inner):
    count = lax.axis_size("shard")
    return [list(range(start, count, inner)) for start in range(inner)]


def stacked_pieces(received, place, inner):
    own = jnp.stack(received)[lax.rem(place + inner - jnp.arange(inner), inner)]
    joined = lax.all_gather(own, "shard", axis_index_groups=outer_groups(inner))
    return joined.reshape(-1, joined.shape[-1])


def split_piece(grad, shift, place, inner):
    outer = lax.axis_size("shard") // inner
    rows = grad.reshape(outer, inner, -1, grad.shape[1])
    here = lax.rem(place + inner - shift, inner)
    return lax.psum_scatter(
        lax.dynamic_index_in_dim(rows, here, 1, keepdims=False),
        "shard",
        axis_index_groups=outer_groups(inner),
    )


def local(
    tokens,
    out_grad,
    deal_order,
    lengths,
    routes,
    norm_in,
    w_in,
    w_dt,
    conv_w,
    conv_b,
    dt_bias,
    a_log,
    d_skip,
    norm_gate,
    w_out,
    norm_moe,
    w_router,
    w_shared,
    w_shared_down,
    w_experts,
    w_experts_down,
):
    seq_devices = lax.axis_size("seq")
    shard_devices = lax.axis_size("shard")
    part = lax.axis_index("seq")
    shard = lax.axis_index("shard")
    inner = min(shard_devices, INNER)
    outer = shard_devices // inner
    place = lax.rem(shard, inner)
    _, tok_rows, width = tokens.shape
    group_rows = tok_rows * seq_devices
    inner_width = w_out.shape[0] * shard_devices
    channels = inner_width // seq_devices
    head_total = w_dt.shape[1]
    heads = head_total // seq_devices
    shared_width = w_shared_down.shape[0] * shard_devices
    shared_part = shared_width // seq_devices
    depth_rows = w_in.shape[0]
    expert_total = w_router.shape[1]
    local_experts, _, double = w_experts.shape
    hidden = double // 2
    hidden_rows = w_experts_down.shape[1]
    top_count = routes.shape[2]
    per_device = local_experts // inner
    blocks = inner * seq_devices
    COLLECTIVES.clear()

    def own_columns(array, start, extent):
        return lax.dynamic_slice_in_dim(array, start + part * extent, extent, 1)

    def own_rows(array, extent):
        return lax.dynamic_slice_in_dim(array, part * extent, extent, 0)

    row_wide = -(-max(conv_w.shape[0], norm_gate.shape[0]) // LANES) * LANES
    row_of = lambda piece: jnp.pad(piece, ((0, 0), (0, row_wide - piece.shape[1])))
    vectors = [conv_b, norm_gate, norm_in, norm_moe, dt_bias, a_log, d_skip]
    flat = jnp.concatenate([row_of(conv_w.T)] + [row_of(vector[None]) for vector in vectors])
    by_depth = jnp.concatenate(
        [
            w_router,
            own_columns(w_dt, 0, heads),
            jnp.zeros((depth_rows, LANES - expert_total - heads), jnp.bfloat16),
        ],
        axis=1,
    )
    weights_of = (w_experts, w_experts_down)

    def own_first():
        here, _ = own_shard_group(inner)
        return lax.axis_index("seq") * local_experts + here * per_device

    pieces = {
        (0, expert, kind): weights_of[kind] for expert in range(per_device) for kind in range(2)
    }

    last = inner - 1
    early_from = {1: range(inner // 2), last: range(inner - inner // 2, inner)} if outer == 1 else {}
    early = {}

    def parcels(*keys, first=False):
        result = []
        for shift, expert, kind in keys:
            senders = None
            if shift in early_from:
                senders = [
                    place for place in range(inner) if (place in early_from[shift]) == first
                ]
            result.append(
                Parcel(
                    weights_of[kind],
                    shift,
                    inner,
                    lambda to, expert=expert: to * per_device + expert,
                    senders=senders,
                )
            )
        return result

    def unpack(keys, arrays):
        pieces.update(zip(keys, arrays))


    in_width = 2 * channels + w_in.shape[1] - 2 * inner_width
    if outer == 1:
        flat = jnp.pad(flat, ((0, -flat.shape[0] % 32), (0, 0)))
        early_keys = [
            (shift, expert, kind)
            for expert in range(per_device)
            for kind in range(2)
            for shift in early_from
        ]
        x_group, grad_all, proj_in, joined, depth_joined, rows_joined, arrays = begin(
            tokens[0],
            out_grad[0],
            flat,
            by_depth,
            w_in,
            w_shared,
            w_out,
            w_shared_down,
            in_width,
            shared_part,
            inner,
            parcels(*early_keys, first=True),
        )
        early.update(zip(early_keys, arrays))
        x_group = x_group.reshape(group_rows, width)
    else:
        x_group = gather_rows(tokens[0], 1)[0].reshape(group_rows, width)
        grad_all = gather_rows(out_grad[0], inner)[0]
        in_columns = jnp.concatenate(
            [
                own_columns(w_in, 0, channels),
                own_columns(w_in, inner_width, channels),
                own_columns(w_shared, 0, shared_part),
                own_columns(w_shared, shared_width, shared_part),
                w_in[:, 2 * inner_width :],
            ],
            axis=1,
        )
        proj_in = lax.all_gather(in_columns, "shard", tiled=True)
        joined = lax.all_gather(flat, "shard")
        depth_joined = lax.all_gather(by_depth, "shard")
        rows_joined = lax.all_gather(rows_to_send([w_out, w_shared_down], part), "shard")
    taps = conv_w.shape[1]
    conv_rows = joined[:, :taps, : conv_w.shape[0]].transpose(1, 0, 2).reshape(taps, -1)
    conv_bias, gain_gate, gain_in, gain_moe, step_bias, decay_log, skip_gain = (
        joined[:, taps + order, : vector.shape[0]].reshape(-1)
        for order, vector in enumerate(vectors)
    )
    depth_joined = depth_joined.reshape(width, LANES)
    lane = jnp.arange(LANES)[None]
    router_wide = jnp.where(lane < expert_total, depth_joined, 0)
    dt_columns = jnp.where(lane < heads, jnp.roll(depth_joined, -expert_total, axis=1), 0)
    grad_all = grad_all.reshape(blocks, tok_rows, width)

    gain_row = to_full(gain_in)[None]
    hidden_in, gate_in, rows_in = project(
        x_group, gain_row, proj_in, dt_columns, channels, in_width
    )
    conv_all = jnp.concatenate([conv_rows, conv_bias[None]], axis=0)
    conv_table = to_full(
        jnp.pad(
            jnp.concatenate([own_columns(conv_all, 0, channels), conv_all[:, inner_width:]], axis=1),
            ((0, 3), (0, 0)),
        )
    )
    head_table = jnp.pad(
        jnp.stack(
            [
                to_full(own_rows(step_bias, heads)),
                -jnp.exp(to_full(own_rows(decay_log, heads))),
                to_full(own_rows(skip_gain, heads)),
            ]
        ),
        ((0, 5), (0, LANES - heads)),
    )
    keys = [(2, 0, DOWN), (1, 0, DOWN), (last, 0, DOWN)]
    y, seq_rows, states, (taken, *arrays) = scan_forward(
        lengths[0],
        deal_order,
        rows_in,
        conv_table,
        head_table,
        channels,
        [PlaneSwap(rows_by_owner(rows_joined))] + parcels(*keys),
    )
    unpack(keys, arrays)
    if outer > 1:
        out_rows, down_rows = rows_of_owner(taken, [w_out, w_shared_down])
        taken = jnp.concatenate(
            [
                out_rows.reshape(seq_devices, -1, width),
                down_rows.reshape(seq_devices, -1, width),
            ],
            axis=1,
        )
    own_weights = taken
    gate_gain = to_full(own_rows(gain_gate, channels))[None]
    keys = [(2, 1, DOWN), (1, 1, DOWN), (last, 1, DOWN)]
    mixed, arrays = mix_out(
        y, gate_in, gate_gain, own_weights, seq_devices, parcels(*keys)
    )
    unpack(keys, arrays)

    moe_row = to_full(gain_moe)[None]
    route_ids = jnp.pad(routes[0], ((0, 0), (0, LANES - top_count)))
    after_mix, moe_wide, gates = token_forward(
        mixed, tokens[0], moe_row, router_wide, route_ids, inner_width, top_count
    )
    keys = [(2, 0, UP), (1, 0, UP), (last, 0, UP)]
    moe_all, arrays = gather_rows(moe_wide, inner, parcels(*keys))
    unpack(keys, arrays)
    moe_all = moe_all.reshape(blocks, tok_rows, width + LANES)
    capacity = min(tok_rows, max(2, tok_rows * top_count * 5 // (expert_total * 3)))
    slots = -(-capacity // 16) * 16
    late_keys = [(1, 1, UP)] if outer == 1 else []
    keys = [key for key in [(2, 1, UP), (1, 1, UP)] if key not in late_keys]
    expert_rows, grad_rows, picks, arrays = dispatch(
        moe_all, grad_all, per_device, top_count, slots, own_first, parcels(*keys)
    )
    unpack(keys, arrays)
    keys = [(last, 1, UP)]
    shared_res, shared_back, shared_up_grad, shared_down_grad, arrays = shared_expert(
        moe_all,
        grad_all,
        proj_in,
        2 * channels,
        own_weights,
        shared_part,
        seq_devices,
        inner,
        parcels(*keys),
    )
    unpack(keys, arrays)
    order = [
        (shift, expert, kind)
        for shift in range(inner)
        for expert in range(per_device)
        for kind in range(2)
    ]
    if outer == 1:
        early_keys = [(1, 0, UP), (last, 0, DOWN)]
        expert_res, expert_back, grads, sent = experts(
            expert_rows,
            grad_rows,
            [early[key] if key in early else pieces[key] for key in order],
            hidden,
            top_count,
            own_first,
            inner,
            [
                (
                    order.index(key),
                    parcels(key)[0] if key in late_keys else pieces[key],
                    [(place_of + key[0]) % inner for place_of in early_from[key[0]]],
                )
                for key in order
                if key in early
            ],
            [(order.index(key), inner - key[0]) for key in early_keys],
        )
    else:
        for expert in range(per_device):
            for kind in range(2):
                pieces[0, expert, kind] = lax.dynamic_index_in_dim(
                    weights_of[kind], place * per_device + expert, 0, keepdims=False
                )
        early_keys, sent = [], []
        held = [
            stacked_pieces([pieces[shift, expert, kind] for shift in range(inner)], place, inner)
            for expert in range(per_device)
            for kind in range(2)
        ]
        expert_res, expert_back, grads, _ = experts(
            expert_rows, grad_rows, held, hidden, top_count, own_first, inner
        )
        grads = [
            split_piece(grads[expert * 2 + kind], shift, place, inner)
            for shift, expert, kind in order
        ]
    grads = dict(zip(order, grads))
    returned = {key: grads[key] for key in order if key[0] == 0}
    returned.update(zip(early_keys, sent))

    def back_parcels(*keys):
        keys = [key for key in keys if key not in early_keys]
        return [Parcel(grads[key], inner - key[0], inner) for key in keys]

    def unpack_back(keys, arrays):
        keys = [key for key in keys if key not in early_keys]
        returned.update(zip(keys, arrays))

    keys = [(1, 0, UP), (last, 0, DOWN), (last, 0, UP), (1, 0, DOWN)]
    out_part, back_part, arrays = combine(
        picks, expert_res, expert_back, shared_res, shared_back, inner, back_parcels(*keys)
    )
    unpack_back(keys, arrays)
    keys = [(last, 1, UP), (2, 1, DOWN), (1, 1, UP)]
    back, arrays = reduce_rows(
        back_part.reshape(inner, seq_devices, tok_rows, -1), back_parcels(*keys)
    )
    unpack_back(keys, arrays)
    mix_grad, mix_wide, router_grad, gain_moe_grad = token_back(
        back,
        mixed,
        after_mix,
        moe_wide,
        gates,
        out_grad[0],
        moe_row,
        router_wide,
        route_ids,
        inner_width,
        top_count,
    )

    keys = [(2, 0, DOWN), (last, 1, DOWN)]
    mix_group, arrays = gather_rows(mix_wide, 1, back_parcels(*keys))
    unpack_back(keys, arrays)
    keys = []
    dy, gate_in_grad, proj_out_grad, gain_gate_grad = mix_back(
        mix_group[0], y, gate_in, gate_gain, own_weights
    )
    keys = [(2, 1, UP), (2, 0, UP)]
    rows_grad, conv_grad, head_grad, out_sum, arrays = scan_backward(
        lengths[0],
        deal_order,
        seq_rows,
        states,
        dy,
        conv_table,
        head_table,
        out_part.reshape(inner, seq_devices, tok_rows, -1),
        back_parcels(*keys),
    )
    unpack_back(keys, arrays)
    layer_out = to_low(after_mix + out_sum)
    keys = [(1, 1, DOWN)]
    swap = [PlaneSwap(rows_from_owner([proj_out_grad, shared_down_grad]))]
    shared_parts = shared_up_grad.reshape(shard_devices, depth_rows, -1)
    if outer == 1:
        swap += [
            Parcel(shared_parts, shift, inner, lambda to: to) for shift in range(1, inner)
        ]
    hidden_part, main_grad, rest_grad, (taken, *arrays) = project_back(
        gate_in_grad, rows_grad, hidden_in, proj_in, dt_columns, seq_devices, swap + back_parcels(*keys)
    )
    shared_came, arrays = arrays[: len(swap) - 1], arrays[len(swap) - 1 :]
    unpack_back(keys, arrays)
    experts_grad, experts_down_grad = collect(
        place[None], [returned[key] for key in order], per_device
    )
    def spread(values, length, axis=0):
        shape = values.shape[:axis] + (length,) + values.shape[axis + 1 :]
        return lax.dynamic_update_slice_in_dim(
            jnp.zeros(shape, values.dtype), values, part * values.shape[axis], axis
        )

    state_columns = rest_grad.shape[1] - LANES
    if outer == 1:
        small = pack(
            rest_grad,
            router_grad,
            conv_grad,
            head_grad,
            gain_gate_grad,
            gain_moe_grad,
            inner,
            seq_devices,
            inner_width,
            expert_total,
            heads,
        )
        tokens_grad, main_all, rows_all, small_all, shared_all = settle(
            hidden_part[None],
            small,
            tokens[0],
            mix_grad,
            gain_row,
            to_low(
                sum(
                    map(to_full, shared_came),
                    to_full(lax.dynamic_index_in_dim(shared_parts, place, 0, keepdims=False)),
                )
            ),
            [
                main_grad.reshape(inner, depth_rows, -1),
                taken.reshape(inner, -1, width),
            ],
            inner,
        )
        w_in_grad, w_shared_grad, w_out_grad, w_shared_down_grad = assemble(
            main_all,
            shared_all,
            small_all,
            rows_all,
            w_in.shape[1],
            2 * shared_width,
            w_out.shape[0],
            w_shared_down.shape[0],
            max(1, seq_devices // shard_devices),
        )
        depth_each = small_all.shape[1] - ROWS_AFTER
        depth_sum = to_full(small_all[:, :depth_each].reshape(depth_rows, -1))
        after = to_full(small_all[:, depth_each:])
        conv_w_grad = after[:4].reshape(4, -1)[:, : conv_w.shape[0]].T
        conv_b_grad = after[4].reshape(-1)[: conv_b.shape[0]]
        norm_gate_grad = after[5].reshape(-1)[: norm_gate.shape[0]]
        here = shard * dt_bias.shape[0]
        of_heads = lax.dynamic_slice_in_dim(after[6, :3], here, dt_bias.shape[0], 1)
        dt_bias_grad, a_log_grad, d_skip_grad = of_heads[0], of_heads[1], of_heads[2]
        norm_moe_grad = after[7, 0, :depth_rows]
        last_lane = rest_grad.shape[1] - 1
    else:
        conv_rows_grad = conv_grad[:5].T
        conv_full = jnp.concatenate(
            [spread(conv_rows_grad[:channels], inner_width), conv_rows_grad[channels:]], axis=0
        )
        by_depth = [
            rest_grad[:, :state_columns],
            router_grad[:, :expert_total],
            spread(rest_grad[:, state_columns : state_columns + heads], head_total, 1),
            rest_grad[:, -1:],
            to_low(gain_moe_grad[0])[:, None],
        ]
        by_shard = [
            conv_full[:, :4],
            conv_full[:, 4],
            spread(head_grad[0, :heads], head_total),
            spread(head_grad[1, :heads], head_total),
            spread(head_grad[2, :heads], head_total),
            spread(gain_gate_grad[0], inner_width),
        ]
        shapes = [(piece.shape[0] // shard_devices,) + piece.shape[1:] for piece in by_shard]
        by_shard = jnp.concatenate(
            [to_low(piece).reshape(shard_devices, -1) for piece in by_shard], axis=1
        )
        extents = [piece.shape[1] for piece in by_depth]
        used = sum(extents)
        hidden_grad = reduce_rows(hidden_part[None])[0]
        residual = to_full(tokens[0])
        own_scale = norm_scale(residual)
        own_unit = residual * own_scale
        scaled = hidden_grad * gain_row
        tokens_grad = to_low(
            mix_grad
            + own_scale
            * (scaled - own_unit * jnp.mean(scaled * own_unit, axis=1, keepdims=True))
        )
        by_depth = jnp.concatenate(by_depth, axis=1).reshape(shard_devices, -1)
        packed = jnp.concatenate([by_depth, by_shard], axis=1)
        summed = lax.psum(lax.psum_scatter(packed, "shard", tiled=True), "seq").reshape(-1)
        count = depth_rows * used
        depth_sum = to_full(summed[:count]).reshape(depth_rows, used)
        shard_sum = summed[count:]

        def from_line(part, rows):
            own = lax.psum_scatter(part.reshape(shard_devices, rows, -1), "shard")
            return lax.all_gather(own, "seq")

        def columns_of(joined, extent):
            joined = joined.reshape(seq_devices, depth_rows, 2, extent).transpose(1, 2, 0, 3)
            return to_full(joined.reshape(depth_rows, -1))

        w_in_main = columns_of(from_line(main_grad, depth_rows), channels)
        w_in_grad = jnp.concatenate([w_in_main, depth_sum[:, :state_columns]], axis=1)
        w_shared_grad = columns_of(from_line(shared_up_grad, depth_rows), shared_part)
        rows_each = taken.shape[0] * taken.shape[1] // shard_devices
        w_out_grad, w_shared_down_grad = rows_of_shard(
            from_line(taken, rows_each), [w_out, w_shared_down]
        )
        results, start = [], 0
        for shape in shapes:
            size = 1
            for extent in shape:
                size *= extent
            results.append(to_full(shard_sum[start : start + size]).reshape(shape))
            start += size
        conv_w_grad, conv_b_grad, dt_bias_grad, a_log_grad, d_skip_grad, norm_gate_grad = results
        norm_moe_grad = depth_sum[:, used - 1]
        last_lane = used - 2
    start = state_columns
    w_router_grad = depth_sum[:, start : start + expert_total]
    start += expert_total
    w_dt_grad = depth_sum[:, start : start + head_total]
    norm_in_grad = depth_sum[:, last_lane] / to_full(norm_in)
    return (
        layer_out[None],
        tokens_grad[None],
        norm_in_grad,
        w_in_grad,
        w_dt_grad,
        conv_w_grad,
        conv_b_grad,
        dt_bias_grad,
        a_log_grad,
        d_skip_grad,
        norm_gate_grad,
        w_out_grad,
        norm_moe_grad,
        w_router_grad,
        w_shared_grad,
        w_shared_down_grad,
        experts_grad,
        experts_down_grad,
    )


def solution(mesh):
    placed = (
        P("shard", "seq", None),
        P("shard", "seq", None),
        P("shard", None),
        P("shard", None),
        P("shard", "seq", None),
        P("shard"),
        P("shard", None),
        P("shard", None),
        P("shard", None),
        P("shard"),
        P("shard"),
        P("shard"),
        P("shard"),
        P("shard"),
        P("shard", None),
        P("shard"),
        P("shard", None),
        P("shard", None),
        P("shard", None),
        P("seq", "shard", None),
        P("seq", "shard", None),
    )
    return jax.shard_map(
        local,
        mesh=mesh,
        in_specs=placed,
        out_specs=(
            P("shard", "seq", None),
            P("shard", "seq", None),
            P("shard"),
            P("shard", None),
            P("shard", None),
            P("shard", None),
            P("shard"),
            P("shard"),
            P("shard"),
            P("shard"),
            P("shard"),
            P("shard", None),
            P("shard"),
            P("shard", None),
            P("shard", None),
            P("shard", None),
            P("seq", "shard", None),
            P("seq", "shard", None),
        ),
        check_vma=False,
    )
```

```python
import functools

import jax
import jax.numpy as jnp
from jax import lax
from jax.experimental import pallas as pl
from jax.experimental.pallas import tpu as pltpu
from jax.sharding import PartitionSpec as P

STRETCH = 256
INNER = 4
UP, DOWN = 0, 1
EPSILON = 1e-05
HIGHEST = lax.Precision.HIGHEST


def matmul(left_side, right_side):
    return jnp.dot(left_side, right_side, preferred_element_type=jnp.float32)


def left_contract(left_side, right_side):
    return lax.dot_general(
        left_side, right_side, (((0,), (0,)), ((), ())), preferred_element_type=jnp.float32
    )


def right_contract(left_side, right_side):
    return lax.dot_general(
        left_side, right_side, (((1,), (1,)), ((), ())), preferred_element_type=jnp.float32
    )


def to_low(values):
    return values.astype(jnp.bfloat16)


def to_full(values):
    return values.astype(jnp.float32)


def norm_scale(values):
    return lax.rsqrt(jnp.mean(values * values, axis=-1, keepdims=True) + EPSILON)


LANES = 128
VMEM_BYTES = 56 * 1024 * 1024


def cost_of(micros):
    return pl.CostEstimate(flops=0, transcendentals=0, bytes_accessed=int(micros * 3.6e6))


def dot_rows(left_side, right_side, precision=None):
    return lax.dot_general(
        left_side,
        right_side,
        (((0,), (0,)), ((), ())),
        precision=precision,
        preferred_element_type=jnp.float32,
    )


def dot_lanes(left_side, right_side, precision=None):
    return lax.dot_general(
        left_side,
        right_side,
        (((1,), (1,)), ((), ())),
        precision=precision,
        preferred_element_type=jnp.float32,
    )


def dot_full(left_side, right_side, precision=None):
    return jnp.dot(
        left_side, right_side, precision=precision, preferred_element_type=jnp.float32
    )


def iota_of(shape, axis):
    return lax.broadcasted_iota(jnp.int32, shape, axis)


def ids_at(places, lengths_ref):
    total, end = jnp.zeros(places.shape, jnp.int32), 0
    for seq in range(lengths_ref.shape[0]):
        end = end + lengths_ref[seq]
        total = total + (places >= end).astype(jnp.int32)
    return total


def id_at(place, lengths_ref):
    total, end = jnp.int32(0), 0
    for seq in range(lengths_ref.shape[0]):
        end = end + lengths_ref[seq]
        total = total + (place >= end).astype(jnp.int32)
    return total


class Stretch:
    def __init__(self, start, rows, before, conv_ref, head_ref, lengths_ref, channels):
        length = rows.shape[0]
        self.channels = channels
        self.heads = channels // 64
        width = conv_ref.shape[1]
        state = (width - channels) // 2
        places = start + iota_of((length, 1), 0)
        self.ids = ids_at(places, lengths_ref)
        self.ids_row = ids_at(start + iota_of((1, length), 1), lengths_ref)
        inputs = rows[:, :width]
        joined = jnp.concatenate([before[:, :width], inputs], axis=0)
        self.shifted = [inputs]
        value = conv_ref[4:5, :] + inputs * conv_ref[3:4, :]
        for offset in range(1, 4):
            same = (ids_at(places - offset, lengths_ref) == self.ids) & (places >= offset)
            moved = pltpu.roll(joined, offset, 0)[8:, :]
            moved = jnp.where(same, moved, 0.0)
            self.shifted.append(moved)
            value = value + moved * conv_ref[3 - offset : 4 - offset, :]
        self.value = value
        self.sig = jax.nn.sigmoid(value)
        act = value * self.sig
        self.x = act[:, :channels]
        self.b = act[:, channels : channels + state]
        self.c = act[:, channels + state :]
        self.b_low = to_low(self.b)
        self.c_low = to_low(self.c)
        self.dt_in = rows[:, width:] + head_ref[0:1, :]
        self.dt = jnp.maximum(self.dt_in, 0.0) + jnp.log1p(jnp.exp(-jnp.abs(self.dt_in)))
        self.rate = head_ref[1:2, :]
        rows_at = iota_of((length, length), 0)
        columns_at = iota_of((length, length), 1)
        lower = (rows_at >= columns_at).astype(jnp.float32)
        self.cum = dot_full(lower, self.dt * self.rate, HIGHEST)
        self.cum_rows = self.cum.T[:8, :]
        self.dt_rows = self.dt.T[:8, :]
        self.causal = (self.ids == self.ids_row) & (rows_at >= columns_at)
        self.scores = dot_lanes(self.c_low, self.b_low)
        last_id = jnp.where(start > 0, id_at(start - 1, lengths_ref), -1)
        end_id = id_at(start + length - 1, lengths_ref)
        self.enter = jnp.where(self.ids == last_id, jnp.exp(self.cum), 0.0)
        end_cum = self.cum[length - 1 : length, :]
        self.tail = jnp.where(self.ids == end_id, jnp.exp(end_cum - self.cum), 0.0)
        self.tail_weight = self.tail * self.dt
        self.keep = jnp.where(last_id == end_id, jnp.exp(end_cum), 0.0)

    def decay(self, head):
        spread = self.cum[:, head : head + 1] - self.cum_rows[head : head + 1, :]
        return jnp.where(self.causal, jnp.exp(jnp.minimum(spread, 0.0)), 0.0)

    def per_channel(self, by_head):
        return jnp.concatenate(
            [
                jnp.broadcast_to(by_head[:, head : head + 1], (by_head.shape[0], 64))
                for head in range(self.heads)
            ],
            axis=1,
        )

    def state_keep(self):
        return jnp.concatenate(
            [
                jnp.broadcast_to(self.keep[:, head : head + 1], (64, LANES))
                for head in range(self.heads)
            ],
            axis=0,
        )


def head_lanes(channels):
    return (iota_of((channels, LANES), 0) // 64 == iota_of((channels, LANES), 1)).astype(
        jnp.float32
    )


def pick_rows(deal_ref, start, length):
    places = start + iota_of((length, 1), 0)
    return jnp.where(deal_ref[...] == places, 1.0, 0.0).astype(jnp.bfloat16)


def scan_forward_kernel(
    lengths_ref, deal_ref, rows_ref, conv_ref, head_ref, y_ref, seq_ref, states_ref, before, state, total
):
    step = pl.program_id(0)
    length = seq_ref.shape[0]
    channels = y_ref.shape[1]
    start = step * length

    @pl.when(step == 0)
    def _():
        before[...] = jnp.zeros_like(before)
        state[...] = jnp.zeros_like(state)
        total[...] = jnp.zeros_like(total)

    picks = pick_rows(deal_ref, start, length)
    rows = dot_full(picks, rows_ref[...])
    seq_ref[...] = to_low(rows)
    part = Stretch(start, rows, before[...], conv_ref, head_ref, lengths_ref, channels)
    before[...] = rows[length - 8 :, :]
    state_now = state[...]
    states_ref[0] = state_now
    x_low = to_low(part.x)
    outs = []
    lane = iota_of((length, LANES), 1)
    for pair in range(channels // LANES):
        x_pair = x_low[:, pair * LANES : (pair + 1) * LANES]
        halves = []
        for head in (2 * pair, 2 * pair + 1):
            weights = part.decay(head) * part.scores * part.dt_rows[head : head + 1, :]
            halves.append(dot_full(to_low(weights), x_pair))
        outs.append(jnp.where(lane < 64, halves[0], halves[1]))
    earlier = dot_lanes(part.c_low, to_low(state_now))
    skip = part.per_channel(head_ref[2:3, :])
    y = jnp.concatenate(outs, axis=1) + part.per_channel(part.enter) * earlier + skip * part.x
    state[...] = part.state_keep() * state_now + dot_rows(
        to_low(part.per_channel(part.tail_weight) * part.x), part.b_low
    )
    total[...] += dot_rows(picks, to_low(y))

    @pl.when(step == pl.num_programs(0) - 1)
    def _():
        y_ref[...] = to_low(total[...])


def scan_forward(lengths, deal_row, rows, conv_table, head_table, channels, freight):
    group_rows, width = rows.shape
    steps = group_rows // STRETCH
    state_rows = (channels, LANES)
    return run(
        scan_forward_kernel,
        (lengths, deal_row, rows, conv_table, head_table),
        grid=(steps,),
        in_specs=[
            pl.BlockSpec(memory_space=pltpu.SMEM),
            whole(deal_row.shape),
            whole(rows.shape),
            whole(conv_table.shape),
            whole(head_table.shape),
        ],
        out_specs=[
            whole((group_rows, channels)),
            pl.BlockSpec((STRETCH, width), lambda step: (step, 0)),
            pl.BlockSpec((1,) + state_rows, lambda step: (step, 0, 0)),
        ],
        out_shape=[
            jax.ShapeDtypeStruct((group_rows, channels), jnp.bfloat16),
            jax.ShapeDtypeStruct((group_rows, width), jnp.bfloat16),
            jax.ShapeDtypeStruct((steps,) + state_rows, jnp.float32),
        ],
        scratch=[
            pltpu.VMEM((8, width), jnp.float32),
            pltpu.VMEM(state_rows, jnp.float32),
            pltpu.VMEM((group_rows, channels), jnp.float32),
        ],
        freight=freight,
        micros=25,
        name="scan_forward",
    )


def scan_backward_kernel(
    lengths_ref,
    deal_ref,
    seq_ref,
    states_ref,
    dy_ref,
    conv_ref,
    head_ref,
    other_ref,
    drows_ref,
    conv_grad_ref,
    head_grad_ref,
    other_sum_ref,
    after,
    state_grad,
    *other_scratch,
):
    order = pl.program_id(0)
    steps = pl.num_programs(0)
    reducer = Reducer(other_ref.shape[0], other_ref, other_sum_ref, other_scratch)

    last = dy_ref.shape[0] // STRETCH - 1

    @pl.when(order == 0)
    def _():
        reducer.begin()

    for count in range(min(last + 1, reducer.inner + 3)):

        @pl.when(order == count)
        def _():
            reducer.step(count)

    step = steps - 1 - order
    length = STRETCH
    channels = dy_ref.shape[1]
    width = conv_ref.shape[1]
    state_width = (width - channels) // 2
    start = pl.multiple_of(step * length, length)

    @pl.when(order == 0)
    def _():
        after[...] = jnp.zeros_like(after)
        state_grad[...] = jnp.zeros_like(state_grad)
        drows_ref[...] = jnp.zeros_like(drows_ref)
        conv_grad_ref[...] = jnp.zeros_like(conv_grad_ref)
        head_grad_ref[...] = jnp.zeros_like(head_grad_ref)

    picks = pick_rows(deal_ref, start, length)
    dy = dot_full(picks, dy_ref[...])
    rows = seq_ref[pl.ds(start, length), :].astype(jnp.float32)
    place = pl.multiple_of(jnp.maximum(start - 16, 0), 16)
    before = seq_ref[pl.ds(place, 16), :].astype(jnp.float32)[8:, :]
    part = Stretch(start, rows, before, conv_ref, head_ref, lengths_ref, channels)
    state_now = states_ref[0]
    state_low = to_low(state_now)
    next_grad = state_grad[...]
    next_low = to_low(next_grad)
    lanes_of = head_lanes(channels)
    x_low = to_low(part.x)
    dy_low = to_low(dy)
    lane = iota_of((length, LANES), 1)

    enter = part.per_channel(part.enter)
    tail_weight = part.per_channel(part.tail_weight)
    earlier = dot_lanes(part.c_low, state_low)
    enter_grad = dot_full(dy * earlier, lanes_of, HIGHEST)
    entered = to_low(enter * dy)
    c_grad = dot_full(entered, state_low)
    state_grad[...] = part.state_keep() * next_grad + dot_rows(entered, part.c_low)
    onward = dot_lanes(part.b_low, next_low)
    x_grad = part.per_channel(head_ref[2:3, :]) * dy + tail_weight * onward
    tail_grad = dot_full(part.x * onward, lanes_of, HIGHEST)
    b_grad = dot_full(to_low(tail_weight * part.x), next_low)
    tail_part = tail_grad * part.tail_weight
    cum_grad = enter_grad * part.enter - tail_part
    dt_grad = tail_grad * part.tail
    kept = dot_lanes(jnp.ones((8, LANES), jnp.float32), next_grad * state_now, HIGHEST)
    keep_grad = dot_full(kept, lanes_of, HIGHEST)[:1, :]
    end_grad = jnp.sum(tail_part, axis=0, keepdims=True) + keep_grad * part.keep

    score_grad = jnp.zeros((length, length), jnp.float32)
    cum_columns, cum_rows, dt_rows, outs = [], [], [], []
    for pair in range(channels // LANES):
        x_pair = x_low[:, pair * LANES : (pair + 1) * LANES]
        dy_pair = dy_low[:, pair * LANES : (pair + 1) * LANES]
        halves = []
        for half, head in enumerate((2 * pair, 2 * pair + 1)):
            mine = (lane < 64) if half == 0 else (lane >= 64)
            weight_grad = dot_lanes(jnp.where(mine, dy_pair, jnp.zeros_like(dy_pair)), x_pair)
            decay = part.decay(head)
            dt_row = part.dt_rows[head : head + 1, :]
            by_decay = weight_grad * decay
            by_dt = by_decay * part.scores
            by_spread = by_dt * dt_row
            dt_rows.append(jnp.sum(by_dt, axis=0, keepdims=True))
            cum_rows.append(jnp.sum(by_spread, axis=0, keepdims=True))
            cum_columns.append(jnp.sum(by_spread, axis=1, keepdims=True))
            score_grad = score_grad + by_decay * dt_row
            halves.append(dot_rows(to_low(decay * part.scores * dt_row), dy_pair))
        outs.append(jnp.where(lane < 64, halves[0], halves[1]))
    x_grad = x_grad + jnp.concatenate(outs, axis=1)
    score_low = to_low(score_grad)
    c_grad = c_grad + dot_full(score_low, part.b_low)
    b_grad = b_grad + dot_rows(score_low, part.c_low)

    heads = len(dt_rows)
    blank = jnp.zeros((LANES - heads, length), jnp.float32)
    dt_grad = dt_grad + jnp.concatenate(dt_rows + [blank], axis=0).T
    cum_grad = cum_grad - jnp.concatenate(cum_rows + [blank], axis=0).T
    for head in range(heads):
        cum_grad = cum_grad + jnp.where(lane == head, cum_columns[head], 0.0)
    at_end = iota_of((length, 1), 0) == length - 1
    cum_grad = cum_grad + jnp.where(at_end, end_grad, 0.0)
    upper = (iota_of((length, length), 1) >= iota_of((length, length), 0)).astype(jnp.float32)
    log_grad = dot_full(upper, cum_grad, HIGHEST)
    dt_grad = dt_grad + log_grad * part.rate
    dt_in_grad = dt_grad * jax.nn.sigmoid(part.dt_in)
    dt_in_grad = jnp.where(lane < heads, dt_in_grad, 0.0)
    head_grad_ref[0:1, :] += jnp.sum(dt_in_grad, axis=0, keepdims=True)
    head_grad_ref[1:2, :] += jnp.sum(log_grad * part.dt, axis=0, keepdims=True) * part.rate
    skip_sum = jnp.broadcast_to(jnp.sum(dy * part.x, axis=0, keepdims=True), (8, channels))
    head_grad_ref[2:3, :] += dot_full(skip_sum, lanes_of, HIGHEST)[:1, :]

    act_grad = jnp.concatenate([x_grad, b_grad, c_grad], axis=1)
    value_grad = act_grad * part.sig * (1.0 + part.value * (1.0 - part.sig))
    conv_grad_ref[4:5, :] += jnp.sum(value_grad, axis=0, keepdims=True)
    for offset in range(4):
        conv_grad_ref[3 - offset : 4 - offset, :] += jnp.sum(
            value_grad * part.shifted[offset], axis=0, keepdims=True
        )
    joined = jnp.concatenate([value_grad, after[...]], axis=0)
    places = start + iota_of((length, 1), 0)
    rows_grad = value_grad * conv_ref[3:4, :]
    for offset in range(1, 4):
        moved = pltpu.roll(joined, length + 8 - offset, 0)[:length, :]
        same = (ids_at(places + offset, lengths_ref) == part.ids) & (
            places + offset < steps * length
        )
        rows_grad = rows_grad + jnp.where(same, moved, 0.0) * conv_ref[3 - offset : 4 - offset, :]
    after[...] = value_grad[:8, :]
    drows_ref[...] += to_low(
        dot_rows(picks, to_low(jnp.concatenate([rows_grad, dt_in_grad], axis=1)))
    )

    for count in range(last + 1, reducer.inner + 3):

        @pl.when(order == last)
        def _():
            reducer.step(count)

    @pl.when(order == steps - 1)
    def _():
        reducer.finish()


def scan_backward(
    lengths, deal_row, seq_rows, states, dy, conv_table, head_table, other, freight
):
    group_rows, width = seq_rows.shape
    channels = dy.shape[1]
    steps = group_rows // STRETCH
    return run(
        scan_backward_kernel,
        (lengths, deal_row, seq_rows, states, dy, conv_table, head_table, other),
        grid=(steps,),
        in_specs=[
            pl.BlockSpec(memory_space=pltpu.SMEM),
            whole(deal_row.shape),
            once(seq_rows.shape),
            pl.BlockSpec((1, channels, LANES), lambda step: (steps - 1 - step, 0, 0)),
            once(dy.shape),
            whole(conv_table.shape),
            whole(head_table.shape),
            pl.BlockSpec(memory_space=pl.ANY),
        ],
        out_specs=[
            whole((group_rows, width)),
            whole(conv_table.shape),
            whole(head_table.shape),
            whole(other.shape[2:]),
        ],
        out_shape=[
            jax.ShapeDtypeStruct((group_rows, width), jnp.bfloat16),
            jax.ShapeDtypeStruct(conv_table.shape, jnp.float32),
            jax.ShapeDtypeStruct(head_table.shape, jnp.float32),
            jax.ShapeDtypeStruct(other.shape[2:], jnp.float32),
        ],
        scratch=[
            pltpu.VMEM((8, conv_table.shape[1]), jnp.float32),
            pltpu.VMEM((channels, LANES), jnp.float32),
        ]
        + Reducer.scratch(other.shape[0], *other.shape[2:]),
        freight=freight,
        flips=FLIPS,
        inner=other.shape[0],
        micros=40,
        name="scan_backward",
    )


def whole(shape):
    return pl.BlockSpec(shape, lambda *steps: (0,) * len(shape))


def once(shape):
    return pl.BlockSpec(
        shape, lambda *steps: (0,) * len(shape), pipeline_mode=pl.Buffered(buffer_count=1)
    )


MESH = pl.DeviceIdType.MESH
FLIPS = (1, 2, 4)


def flipped(place, flip):
    result = place
    for bit in FLIPS:
        if flip & bit:
            result = result + bit - 2 * bit * lax.rem(lax.div(place, bit), 2)
    return result


def own_shard_group(inner):
    shard = lax.axis_index("shard")
    place = lax.rem(shard, inner)
    return place, shard - place


def peers_in_order(place, inner):
    if inner == 1:
        return []
    if inner == 4:
        half = lax.div(place, 2)
        return [flipped(place, 1), 2 - half, 3 - 3 * half]
    return [lax.rem(place + shift, inner) for shift in range(1, inner)]


def greet(flips, inner):
    barrier = pltpu.get_barrier_semaphore()
    part = lax.axis_index("seq")
    place, first = own_shard_group(inner)
    for flip in flips:
        pl.semaphore_signal(
            barrier, inc=1, device_id={"seq": flipped(part, flip)}, device_id_type=MESH
        )
    for peer in peers_in_order(place, inner):
        pl.semaphore_signal(
            barrier, inc=1, device_id={"shard": first + peer}, device_id_type=MESH
        )
    pl.semaphore_wait(barrier, len(flips) + inner - 1)


def among(place, places):
    if places is None:
        return None
    return functools.reduce(jnp.logical_or, [place == one for one in places])


def do_if(condition, action):
    if condition is None:
        action()
    else:
        pl.when(condition)(action)


class Parcel:
    flips = ()
    sems = 1

    def __init__(self, array, shift, inner, index=None, output=None, senders=None):
        self.array, self.shift, self.inner, self.index = array, shift, inner, index
        self.senders = senders
        self.shape = array.shape if index is None else array.shape[1:]
        self.output = output

    def moves(self, source, target):
        place, first = own_shard_group(self.inner)
        to = lax.rem(place + self.shift, self.inner)
        if self.index is not None:
            source = source.at[self.index(to)]
        return [(source, target, target, {"shard": first + to})]

    def sends(self):
        return among(own_shard_group(self.inner)[0], self.senders)

    def comes(self):
        place, _ = own_shard_group(self.inner)
        return among(lax.rem(place + self.inner - self.shift, self.inner), self.senders)

    def stays(self, source, target):
        return []


class PlaneSwap:
    flips = (1, 2, 3, 4, 5, 6, 7)
    inner = 1
    sems = 8

    output = None

    def __init__(self, array):
        self.array, self.shape = array, array.shape

    def sends(self):
        return None

    def comes(self):
        return None

    def moves(self, source, target):
        part = lax.axis_index("seq")
        return [
            (
                source.at[flipped(part, flip)],
                target.at[part],
                target.at[flipped(part, flip)],
                {"seq": flipped(part, flip)},
            )
            for flip in self.flips
        ]

    def stays(self, source, target):
        part = lax.axis_index("seq")
        return [(source.at[part], target.at[part])]


COLLECTIVES = []


def run(
    kernel,
    args,
    *,
    in_specs,
    out_specs,
    out_shape,
    name,
    micros,
    grid=(),
    scratch=(),
    freight=(),
    flips=(),
    inner=1,
    late=False,
):
    freight = list(freight)
    for place, item in enumerate(freight):
        item.rank = place
    flips = tuple(sorted(set(flips).union(*[item.flips for item in freight])))
    inner = max([inner] + [item.inner for item in freight])
    talks = bool(flips) or inner > 1
    count_in, count_out, count_scratch = len(args), len(out_shape), len(scratch)
    count = len(freight)
    loaded = [item for item in freight if item.output is None]

    def wrapped(*refs):
        ins, refs = refs[:count_in], refs[count_in:]
        sources, refs = list(refs[: len(loaded)]), refs[len(loaded) :]
        outs, refs = refs[:count_out], refs[count_out:]
        sources = [
            sources.pop(0) if item.output is None else outs[item.output] for item in freight
        ]
        targets, refs = refs[:count], refs[count:]
        own, refs = refs[:count_scratch], refs[count_scratch:]

        def remote(item, place, order, source, target, device):
            send, recv = refs[3 * place : 3 * place + 2]
            return pltpu.make_async_remote_copy(
                src_ref=source,
                dst_ref=target,
                send_sem=send.at[order],
                recv_sem=recv.at[order],
                device_id=device,
                device_id_type=MESH,
            )

        def moves(chosen):
            for place, item in enumerate(freight):
                if not chosen(item):
                    continue
                for order, move in enumerate(item.moves(sources[place], targets[place])):
                    yield item, place, order, move

        def stays(chosen):
            for place, item in enumerate(freight):
                if not chosen(item):
                    continue
                for source, target in item.stays(sources[place], targets[place]):
                    yield pltpu.make_async_copy(source, target, refs[3 * place + 2])

        def depart(chosen=lambda item: True, gate=None):
            for item, place, order, (source, target, _, device) in moves(chosen):
                allowed = item.sends()
                if gate is not None:
                    allowed = gate if allowed is None else allowed & gate
                do_if(
                    allowed,
                    lambda: remote(item, place, order, source, target, device).start(),
                )
            for copy in stays(chosen):
                copy.start()

        def arrive(chosen=lambda item: True):
            for item, place, order, (source, target, arrival, device) in moves(chosen):
                do_if(
                    item.comes(),
                    lambda: remote(item, place, order, source, arrival, device).wait_recv(),
                )
                do_if(
                    item.sends(),
                    lambda: remote(item, place, order, source, target, device).wait_send(),
                )
            for copy in stays(chosen):
                copy.wait()

        if grid:
            at = [pl.program_id(axis) for axis in range(len(grid))]
            first, last = at[0] == 0, at[0] == grid[0] - 1
            for axis in range(1, len(grid)):
                first = first & (at[axis] == 0)
                last = last & (at[axis] == grid[axis] - 1)
            if talks:

                @pl.when(first)
                def _():
                    greet(flips, inner)
                    if not late:
                        depart()

            if late:
                kernel(depart, arrive, targets, *ins, *outs, *own)
            else:
                kernel(*ins, *outs, *own)
            if talks and not late:
                pl.when(last)(arrive)
        else:
            if talks:
                greet(flips, inner)
            if late:
                kernel(depart, *ins, *outs, *own)
            else:
                depart()
                kernel(*ins, *outs, *own)
            arrive()

    anywhere = pl.BlockSpec(memory_space=pl.ANY)
    extra = {}
    if talks:
        COLLECTIVES.append(name)
        extra = dict(collective_id=len(COLLECTIVES), has_side_effects=True)
    sems = []
    for item in freight:
        sems += [
            pltpu.SemaphoreType.DMA((item.sems,)),
            pltpu.SemaphoreType.DMA((item.sems,)),
            pltpu.SemaphoreType.DMA(()),
        ]
    results = pl.pallas_call(
        wrapped,
        grid=grid,
        in_specs=list(in_specs) + [anywhere] * len(loaded),
        out_specs=list(out_specs) + [anywhere] * count,
        out_shape=list(out_shape)
        + [jax.ShapeDtypeStruct(item.shape, item.array.dtype) for item in freight],
        scratch_shapes=list(scratch) + sems,
        compiler_params=pltpu.CompilerParams(vmem_limit_bytes=VMEM_BYTES, **extra),
        cost_estimate=cost_of(micros),
        name=name,
    )(*args, *[item.array for item in loaded])
    results = list(results)
    if freight:
        return results[:count_out] + [results[count_out:]]
    return results


class LineSum:
    def __init__(self, inner, sums, from_below, from_above, send, below_recv, above_recv):
        self.inner = inner
        self.sums, self.from_below, self.from_above = sums, from_below, from_above
        self.send, self.below_recv, self.above_recv = send, below_recv, above_recv
        self.place, self.first = own_shard_group(inner)
        self.targets = list(reversed(peers_in_order(self.place, inner))) + [self.place]

    def copy(self, order, up):
        target = self.targets[order]
        inbox = self.from_below if up else self.from_above
        recv = self.below_recv if up else self.above_recv
        return pltpu.make_async_remote_copy(
            src_ref=self.sums.at[order],
            dst_ref=inbox.at[target],
            send_sem=self.send.at[order],
            recv_sem=recv.at[target],
            device_id={"shard": self.first + self.place + (1 if up else -1)},
            device_id_type=MESH,
        )

    def arrived(self, target, up):
        inbox = self.from_below if up else self.from_above
        recv = self.below_recv if up else self.above_recv
        pltpu.make_async_remote_copy(
            src_ref=inbox.at[target],
            dst_ref=inbox.at[target],
            send_sem=self.send.at[0],
            recv_sem=recv.at[target],
            device_id={"shard": self.first + self.place + (-1 if up else 1)},
            device_id_type=MESH,
        ).wait_recv()
        return to_full(inbox[target])

    def ways(self):
        return ((True, self.place > 0), (False, self.place < self.inner - 1))

    def push_free(self, order):
        target = self.targets[order]
        for up, comes in self.ways():
            heads = (target > self.place) if up else (target < self.place)

            @pl.when(heads & jnp.logical_not(comes))
            def _():
                self.copy(order, up).start()

    def push_rest(self, order):
        target = self.targets[order]
        for up, comes in self.ways():
            heads = (target > self.place) if up else (target < self.place)

            @pl.when(heads & comes)
            def _():
                self.sums[order] = to_low(
                    to_full(self.sums[order]) + self.arrived(target, up)
                )
                self.copy(order, up).start()

    def add_own(self, total):
        for up, comes in self.ways():

            @pl.when(comes)
            def _():
                total[...] += self.arrived(self.place, up)

    def finish(self):
        for order in range(self.inner - 1):
            for up in (True, False):
                target = self.targets[order]

                @pl.when((target > self.place) if up else (target < self.place))
                def _():
                    self.copy(order, up).wait_send()

    @staticmethod
    def scratch(inner, rows, width):
        sems = lambda *shape: pltpu.SemaphoreType.DMA(shape)
        return [
            pltpu.VMEM((max(1, inner - 1), rows, width), jnp.bfloat16),
            pltpu.VMEM((inner, rows, width), jnp.bfloat16),
            pltpu.VMEM((inner, rows, width), jnp.bfloat16),
            sems(max(1, inner - 1)),
            sems(inner),
            sems(inner),
        ]


class Reducer:
    def __init__(self, inner, p_ref, total, refs, make=None):
        self.inner, self.p_ref, self.total, self.make = inner, p_ref, total, make
        self.held, self.paired, self.turned, self.crossed = refs[:4]
        self.load, self.core_send, self.core_recv = refs[4:7]
        self.turn_send, self.turn_recv, self.cross_send, self.cross_recv = refs[7:11]
        self.line = LineSum(inner, *refs[11:])
        self.part = lax.axis_index("seq")
        half = self.held.shape[2] // 2
        self.spans = [pl.ds(0, half), pl.ds(half, half)]

    @staticmethod
    def scratch(inner, rows, width):
        low = jnp.bfloat16
        sems = lambda *shape: pltpu.SemaphoreType.DMA(shape)
        return [
            pltpu.VMEM((inner, 4, rows, width), low),
            pltpu.VMEM((inner, 4, rows, width), low),
            pltpu.VMEM((inner, 2, rows // 2, width), low),
            pltpu.VMEM((inner, 4, rows // 2, width), low),
            sems(inner, 4),
            sems(inner, 4),
            sems(inner, 4),
            sems(inner, 2),
            sems(inner, 2),
            sems(inner, 4),
            sems(inner, 4),
        ] + LineSum.scratch(inner, rows, width)

    EVENS = (6, 2, 4, 0)

    def to_core(self, order, slot):
        return pltpu.make_async_remote_copy(
            src_ref=self.p_ref.at[order, slot]
            if self.make
            else self.p_ref.at[
                self.line.targets[order], flipped(self.part, self.EVENS[slot] + 1)
            ],
            dst_ref=self.paired.at[order, slot],
            send_sem=self.core_send.at[order, slot],
            recv_sem=self.core_recv.at[order, slot],
            device_id={"seq": flipped(self.part, 1)},
            device_id_type=MESH,
        )

    def loading(self, order, slot):
        return pltpu.make_async_copy(
            self.p_ref.at[self.line.targets[order], flipped(self.part, self.EVENS[slot])],
            self.held.at[order, slot],
            self.load.at[order, slot],
        )

    def turn(self, order, span):
        return pltpu.make_async_remote_copy(
            src_ref=self.held.at[order, 0, self.spans[span]],
            dst_ref=self.turned.at[order, span],
            send_sem=self.turn_send.at[order, span],
            recv_sem=self.turn_recv.at[order, span],
            device_id={"seq": flipped(self.part, (2, 4)[span])},
            device_id_type=MESH,
        )

    CROSSINGS = ((1, 2, 0), (2, 4, 1), (2, 4, 0), (1, 2, 1))

    def cross(self, order, kind):
        slot, flip, span = self.CROSSINGS[kind]
        return pltpu.make_async_remote_copy(
            src_ref=self.held.at[order, slot, self.spans[span]],
            dst_ref=self.crossed.at[order, kind],
            send_sem=self.cross_send.at[order, kind],
            recv_sem=self.cross_recv.at[order, kind],
            device_id={"seq": flipped(self.part, flip)},
            device_id_type=MESH,
        )

    def begin(self):
        for order in range(self.inner):
            for slot in range(4):
                if self.make:
                    target = self.line.targets[order]
                    block = flipped(self.part, self.EVENS[slot] + 1)
                    self.make(target, block, self.p_ref.at[order, slot])
                self.to_core(order, slot).start()
                if not self.make:
                    self.loading(order, slot).start()
            if self.make:
                for slot in range(4):
                    block = flipped(self.part, self.EVENS[slot])
                    self.make(self.line.targets[order], block, self.held.at[order, slot])

    def total_of(self, order, slot):
        if not self.make:
            self.loading(order, slot).wait()
        self.to_core(order, slot).wait_recv()
        return to_full(self.held[order, slot]) + to_full(self.paired[order, slot])

    def stage_a(self, order):
        self.held[order, 0] = to_low(self.total_of(order, 0))
        for span in range(2):
            self.turn(order, span).start()
        for slot in (1, 2):
            self.held[order, slot] = to_low(self.total_of(order, slot))
            self.cross(order, slot - 1).start()

    def stage_b(self, order):
        for kind in (2, 3):
            slot, _, span = self.CROSSINGS[kind]
            self.turn(order, span).wait_recv()
            at = self.spans[span]
            self.held[order, slot, at] = to_low(
                to_full(self.held[order, slot, at]) + to_full(self.turned[order, span])
            )
            self.cross(order, kind).start()

    def stage_c(self, order):
        total = self.total_of(order, 3)
        for kind in range(4):
            self.cross(order, kind).wait_recv()
        crossed = [to_full(self.crossed[order, kind]) for kind in range(4)]
        total = total + jnp.concatenate(
            [crossed[0] + crossed[2], crossed[1] + crossed[3]], axis=0
        )
        if order == self.inner - 1:
            self.total[...] = total
        else:
            self.line.sums[order] = to_low(total)
            self.line.push_free(order)

    def stage_d(self, order):
        if order == self.inner - 1:
            self.line.add_own(self.total)
        else:
            self.line.push_rest(order)

    def step(self, count):
        for stage, late in (
            (self.stage_b, 1),
            (self.stage_a, 0),
            (self.stage_c, 2),
            (self.stage_d, 3),
        ):
            if 0 <= count - late < self.inner:
                stage(count - late)

    def steps(self):
        return self.inner + 3

    def finish(self):
        for order in range(self.inner):
            for slot in range(4):
                self.to_core(order, slot).wait_send()
            for span in range(2):
                self.turn(order, span).wait_send()
            for kind in range(4):
                self.cross(order, kind).wait_send()
        self.line.finish()

    def whole(self, depart):
        self.begin()
        depart(0)
        for count in range(self.inner + 3):
            self.step(count)
            if count >= 2:
                depart(count - 1)
        self.finish()


def reduce_kernel(inner, staged, depart, p_ref, out_ref, *scratch):
    def leave(number):
        if staged:
            depart(lambda item: item.rank == number)

    if not staged:
        depart()
    Reducer(inner, p_ref, out_ref, scratch).whole(leave)


def reduce_rows(partial, freight=()):
    inner, _, rows, width = partial.shape
    return run(
        functools.partial(reduce_kernel, inner, inner > 1),
        (partial,),
        in_specs=[pl.BlockSpec(memory_space=pl.ANY)],
        out_specs=[pl.BlockSpec(memory_space=pltpu.VMEM)],
        out_shape=[jax.ShapeDtypeStruct((rows, width), jnp.float32)],
        scratch=Reducer.scratch(inner, rows, width),
        freight=freight,
        flips=FLIPS,
        inner=inner,
        late=True,
        micros=25 * inner,
        name="reduce_rows",
    )


def plane_gather(own, target, send, recv):
    part = lax.axis_index("seq")
    half = own.shape[0] // 2
    spans = [pl.ds(0, half), pl.ds(half, half)]
    started = []

    def copy_of(kind, block, span, flip, from_own=False):
        place = target(block).at[spans[span]]
        return pltpu.make_async_remote_copy(
            src_ref=own.at[spans[span]] if from_own else place,
            dst_ref=place,
            send_sem=send.at[kind],
            recv_sem=recv.at[kind],
            device_id={"seq": flipped(part, flip)},
            device_id_type=MESH,
        )

    def push(kind, block, span, flip, from_own=False):
        copy = copy_of(kind, block, span, flip, from_own)
        copy.start()
        started.append(copy)

    def arrived(kind, block, span, flip):
        copy_of(kind, block, span, flip).wait_recv()

    def first():
        for kind, span, flip in (
            (3, 1, 2), (4, 0, 4), (2, 0, 2), (5, 1, 4), (0, 0, 1), (1, 1, 1)
        ):
            push(kind, part, span, flip, True)

    def second():
        side, over = flipped(part, 2), flipped(part, 4)
        arrived(3, side, 1, 2)
        push(6, side, 1, 4)
        arrived(4, over, 0, 4)
        push(7, over, 0, 2)
        push(9, side, 1, 1)
        push(10, over, 0, 1)
        arrived(2, side, 0, 2)
        push(8, side, 0, 1)
        arrived(5, over, 1, 4)
        push(11, over, 1, 1)

    def third():
        far = flipped(part, 6)
        arrived(6, far, 1, 4)
        push(13, far, 1, 1)
        arrived(7, far, 0, 2)
        push(12, far, 0, 1)

    def last():
        for kind, flip, span in (
            (0, 1, 0), (1, 1, 1), (9, 3, 1), (10, 5, 0), (8, 3, 0), (11, 5, 1), (13, 7, 1), (12, 7, 0)
        ):
            arrived(kind, flipped(part, flip), span, 1)
        for copy in started:
            copy.wait_send()

    return first, second, third, last


def line_gather(inner, own, target, send, recv, split=2):
    place, first = own_shard_group(inner)
    half = own.shape[0] // split
    spans = [pl.ds(span * half, half) for span in range(split)]

    def copy_of(way, step, span):
        block = place - step if way == 0 else place + step
        to = place + 1 if way == 0 else place - 1
        spot = target(block).at[spans[span]]
        return pltpu.make_async_remote_copy(
            src_ref=own.at[spans[span]] if step == 0 else spot,
            dst_ref=spot,
            send_sem=send.at[way, step, span],
            recv_sem=recv.at[way, step, span],
            device_id={"shard": first + to},
            device_id_type=MESH,
        )

    def sends(way, step):
        if way == 0:
            return (place < inner - 1) & (place >= step)
        return (place > 0) & (place + step < inner)

    def receives(way, step):
        return place >= step if way == 0 else place + step < inner

    def start(step, span):
        for way in range(2):

            @pl.when(sends(way, step))
            def _():
                copy_of(way, step, span).start()

    def begin():
        for span in range(split):
            start(0, span)

    def onward(step):
        for span in range(split):
            for way in range(2):

                @pl.when(receives(way, step))
                def _():
                    block = place - step if way == 0 else place + step
                    spot = target(block).at[spans[span]]
                    pltpu.make_async_remote_copy(
                        src_ref=spot,
                        dst_ref=spot,
                        send_sem=send.at[way, step - 1, span],
                        recv_sem=recv.at[way, step - 1, span],
                        device_id={"shard": block + first},
                        device_id_type=MESH,
                    ).wait_recv()

            if step < inner - 1:
                start(step, span)

    def finish():
        for step in range(inner - 1):
            for span in range(split):
                for way in range(2):

                    @pl.when(sends(way, step))
                    def _():
                        copy_of(way, step, span).wait_send()

    return begin, onward, finish


def group_gather(inner, own, target, sems):
    part = lax.axis_index("seq")
    place, _ = own_shard_group(inner)
    sources = [place] + peers_in_order(place, inner)
    line_send, line_recv, send, recv = sems
    line = line_gather(inner, own, lambda p: target(p, part), line_send, line_recv)
    planes = [
        plane_gather(
            own if order == 0 else target(source, part),
            lambda b, source=source: target(source, b),
            send.at[order],
            recv.at[order],
        )
        for order, source in enumerate(sources)
    ]
    return line, planes


def group_sems(inner):
    sems = lambda *shape: pltpu.SemaphoreType.DMA(shape)
    steps = max(1, inner - 1)
    return [sems(2, steps, 2), sems(2, steps, 2), sems(inner, 14), sems(inner, 14)]


def gather_kernel(inner, depart, x_ref, out_ref, own_sem, *sems):
    part = lax.axis_index("seq")
    place, _ = own_shard_group(inner)
    own = pltpu.make_async_copy(x_ref, out_ref.at[place, part], own_sem)
    (begin, onward, finish), planes = group_gather(
        inner, x_ref, lambda p, b: out_ref.at[p, b], sems
    )
    if inner > 1:
        begin()
    else:
        depart()
    planes[0][0]()
    own.start()
    planes[0][1]()
    for order in range(1, inner):
        onward(order)
        if order < inner - 1:
            depart(lambda item: item.rank == order - 1)
        else:
            depart(lambda item: item.rank >= order - 1)
        planes[order][0]()
        planes[order - 1][2]()
        planes[order][1]()
    planes[inner - 1][2]()
    for stages in planes:
        stages[3]()
    if inner > 1:
        finish()
    own.wait()


def gather_rows(x, inner, freight=()):
    rows, width = x.shape
    seq_devices = lax.axis_size("seq")
    return run(
        functools.partial(gather_kernel, inner),
        (x,),
        in_specs=[pl.BlockSpec(memory_space=pl.ANY)],
        out_specs=[pl.BlockSpec(memory_space=pl.ANY)],
        out_shape=[jax.ShapeDtypeStruct((inner, seq_devices, rows, width), x.dtype)],
        scratch=[pltpu.SemaphoreType.DMA(())] + group_sems(inner),
        freight=freight,
        flips=FLIPS,
        inner=inner,
        late=True,
        micros=25 * inner,
        name="gather_rows",
    )


def begin_kernel(
    inner,
    depart,
    x_ref,
    g_ref,
    s_ref,
    d_ref,
    in_ref,
    shared_ref,
    out_ref,
    down_ref,
    x_out,
    g_out,
    w_out,
    s_out,
    d_out,
    r_out,
    w_ref,
    r_ref,
    b_ref,
    b_line,
    b_all,
    own_sems,
    pick_sems,
    place_sems,
    *sems,
):
    part = lax.axis_index("seq")
    place, _ = own_shard_group(inner)
    rows = w_ref.shape[0]
    seq_devices = x_out.shape[0]
    picks = []

    def pick(source, target):
        picks.append(pltpu.make_async_copy(source, target, pick_sems.at[len(picks)]))

    shared = shared_ref.shape[1] // seq_devices // 2
    channels = w_ref.shape[1] // 2 - shared
    share, state = b_ref.shape
    at = 0
    for source, extent in ((in_ref, channels), (shared_ref, shared)):
        for side in range(2):
            start = pl.multiple_of((side * seq_devices + part) * extent, extent)
            pick(source.at[:, pl.ds(start, extent)], w_ref.at[:, pl.ds(at, extent)])
            at += extent
    start = pl.multiple_of(part * share, share)
    pick(in_ref.at[pl.ds(start, share), pl.ds(in_ref.shape[1] - state, state)], b_ref)
    halves = seq_devices // inner
    at = 0
    for half in range(halves):
        for source in (out_ref, down_ref):
            fine = source.shape[0] // halves // seq_devices
            start = pl.multiple_of((half * seq_devices + part) * fine, fine)
            pick(source.at[pl.ds(start, fine)], r_ref.at[pl.ds(at, fine)])
            at += fine
    for copy in picks:
        copy.start()
    targets = [
        lambda p: s_out.at[p],
        lambda p: w_out.at[pl.ds(p * rows, rows), pl.ds(0, w_ref.shape[1])],
        lambda p: r_out.at[p],
        lambda p: d_out.at[p],
        lambda p: b_line.at[pl.ds(p * share, share)],
    ]
    sources = [s_ref, w_ref, r_ref, d_ref, b_ref]
    lines = [
        line_gather(
            inner, source, target, sems[2 * order], sems[2 * order + 1], 1 if order == 4 else 2
        )
        for order, (source, target) in enumerate(zip(sources, targets))
    ]
    b_plane = plane_gather(b_line, lambda b: b_all.at[b], sems[16], sems[17])
    line, planes = group_gather(inner, g_ref, lambda p, b: g_out.at[p, b], sems[10:14])
    lines.append(line)
    x_plane = plane_gather(x_ref, lambda b: x_out.at[b], sems[14], sems[15])
    rows_line = lines.pop(2)
    lines[0][0]()
    lines[2][0]()
    lines[4][0]()
    x_plane[0]()
    planes[0][0]()
    for copy in picks:
        copy.wait()
    lines[3][0]()
    lines[1][0]()
    rows_line[0]()
    at_end = (place == 0) | (place == inner - 1)
    depart(gate=at_end)
    owns = [
        pltpu.make_async_copy(source, target(place), own_sems.at[order])
        for order, (source, target) in enumerate(zip(sources, targets))
    ]
    owns.append(pltpu.make_async_copy(x_ref, x_out.at[part], own_sems.at[5]))
    owns.append(pltpu.make_async_copy(g_ref, g_out.at[place, part], own_sems.at[6]))
    for copy in owns:
        copy.start()
    x_plane[1]()
    planes[0][1]()
    x_plane[2]()
    planes[0][2]()
    *other_lines, g_line = lines
    for step in range(1, inner):
        g_line[1](step)
        planes[step][0]()
        if step > 1:
            planes[step - 1][2]()
        planes[step][1]()
        for _, onward, _ in reversed(other_lines):
            onward(step)
        if step == 1:
            rows_line[1](1)
            depart(gate=jnp.logical_not(at_end))
    planes[inner - 1][2]()
    owns[4].wait()
    b_plane[0]()
    for step in range(2, inner):
        rows_line[1](step)
    b_plane[1]()
    b_plane[2]()
    x_plane[3]()
    for stages in planes:
        stages[3]()
    b_plane[3]()
    own_b = pltpu.make_async_copy(b_line, b_all.at[part], own_sems.at[7])
    own_b.start()
    own_b.wait()
    spread = []
    for device in range(seq_devices):
        for shard in range(inner):
            spread.append(
                pltpu.make_async_copy(
                    b_all.at[device, pl.ds(shard * share, share)],
                    w_out.at[
                        pl.ds(shard * rows + device * share, share), pl.ds(w_ref.shape[1], state)
                    ],
                    place_sems.at[device, shard],
                )
            )
    for copy in spread:
        copy.start()
    for _, _, finish in lines + [rows_line]:
        finish()
    for order, copy in enumerate(owns):
        if order != 4:
            copy.wait()
    for copy in spread:
        copy.wait()


def begin(
    x, grad, small, by_depth, w_in, w_shared, w_out, w_down, in_width, shared_part, inner, freight
):
    seq_devices = lax.axis_size("seq")
    low = jnp.bfloat16
    depth, width = w_in.shape[0], w_out.shape[1]
    columns = in_width + 2 * shared_part
    w_columns = 2 * w_out.shape[0] * inner // seq_devices + 2 * shared_part
    rows = (w_out.shape[0] + w_down.shape[0]) // seq_devices
    anywhere = pl.BlockSpec(memory_space=pl.ANY)
    sems = lambda *shape: pltpu.SemaphoreType.DMA(shape)
    line_sems = [sems(2, inner - 1, 2)] * 10
    state = in_width + 2 * shared_part - w_columns
    fine = depth // seq_devices
    return run(
        functools.partial(begin_kernel, inner),
        (x, grad, small, by_depth, w_in, w_shared, w_out, w_down),
        in_specs=[anywhere] * 8,
        out_specs=[anywhere] * 6,
        out_shape=[
            jax.ShapeDtypeStruct((seq_devices,) + x.shape, x.dtype),
            jax.ShapeDtypeStruct((inner, seq_devices) + grad.shape, grad.dtype),
            jax.ShapeDtypeStruct((inner * depth, columns), low),
            jax.ShapeDtypeStruct((inner,) + small.shape, small.dtype),
            jax.ShapeDtypeStruct((inner,) + by_depth.shape, low),
            jax.ShapeDtypeStruct((inner, rows, width), low),
        ],
        scratch=[
            pltpu.VMEM((depth, w_columns), low),
            pltpu.VMEM((rows, width), low),
            pltpu.VMEM((fine, state), low),
            pltpu.VMEM((inner * fine, state), low),
            pltpu.VMEM((seq_devices, inner * fine, state), low),
            sems(8),
            sems(5 + 2 * (seq_devices // inner)),
            sems(seq_devices, inner),
        ]
        + line_sems
        + group_sems(inner)
        + [sems(14)] * 4,
        freight=freight,
        flips=FLIPS,
        inner=inner,
        late=True,
        micros=130,
        name="begin",
    )


def settle_kernel(
    inner,
    counts,
    depart,
    hidden_ref,
    small_ref,
    x_ref,
    mix_ref,
    gain_ref,
    done_ref,
    *refs,
):
    part = lax.axis_index("seq")
    place, _ = own_shard_group(inner)
    parts, refs = refs[:counts], refs[counts:]
    tokens_out, refs = refs[0], refs[1:]
    outs, refs = refs[: counts + 2], refs[counts + 2 :]
    hidden_sum, small_sum = refs[:2]
    refs = refs[2:]
    take = len(Reducer.scratch(1, 16, LANES))
    hidden = Reducer(1, hidden_ref, hidden_sum, refs[:take])
    small = Reducer(inner, small_ref, small_sum, refs[take : 2 * take])
    refs = refs[2 * take :]
    lines, totals, planes, owns = [], [], [], []
    for index in range(counts + 2):
        low, gsend, grecv, here = refs[:4]
        refs = refs[4:]
        out = outs[index]
        planes.append(plane_gather(low, lambda b, out=out: out.at[b], gsend, grecv))
        owns.append((low, pltpu.make_async_copy(low, out.at[part], here)))
    loads = []
    for index in range(counts):
        total, load = refs[:2]
        line = LineSum(inner, *refs[2:8])
        refs = refs[8:]
        lines.append(line)
        totals.append(total)
        for order in range(inner - 1):
            loads.append(
                pltpu.make_async_copy(
                    parts[index].at[line.targets[order]], line.sums.at[order], load.at[order]
                )
            )
        loads.append(
            pltpu.make_async_copy(parts[index].at[place], owns[index][0], load.at[inner - 1])
        )
    for copy in loads:
        copy.start()
    small.begin()
    hidden.begin()

    def load(index):
        for copy in loads[index * inner : (index + 1) * inner]:
            copy.wait()
        totals[index][...] = to_full(owns[index][0][...])

    def push_free(index, orders):
        for order in orders:
            lines[index].push_free(order)

    def push_rest(index, orders):
        for order in orders:
            lines[index].push_rest(order)

    def gather_part(index):
        lines[index].add_own(totals[index])
        owns[index][0][...] = to_low(totals[index][...])
        planes[index][0]()
        owns[index][1].start()

    every = range(inner - 1)
    owns[counts + 1][0][...] = done_ref[...]
    small.step(0)
    small.step(1)
    load(0)
    push_free(0, every[:1])
    for count in range(2, small.steps() - 2):
        small.step(count)
    hidden.step(0)
    push_free(0, every[1:])
    for index in range(1, counts):
        load(index)
        push_free(index, every)
    push_rest(0, every[:1])
    for count in range(small.steps() - 2, small.steps()):
        small.step(count)
    owns[counts][0][...] = to_low(small_sum[...])
    planes[counts][0]()
    owns[counts][1].start()
    planes[counts + 1][0]()
    owns[counts + 1][1].start()
    hidden.step(1)
    push_rest(0, every[1:])
    planes[counts][1]()
    planes[counts + 1][1]()
    hidden.step(2)
    hidden.step(3)
    planes[counts][2]()
    planes[counts + 1][2]()
    x = to_full(x_ref[...])
    scale = norm_scale(x)
    unit = x * scale
    scaled = hidden_sum[...] * gain_ref[...]
    mean = jnp.mean(scaled * unit, axis=1, keepdims=True)
    tokens_out[...] = to_low(mix_ref[...] + scale * (scaled - unit * mean))
    if counts > 1:
        push_rest(1, every[:1])
    gather_part(0)
    if counts > 1:
        push_rest(1, every[1:])
    depart()
    for index in range(1, counts):
        planes[index - 1][1]()
        if index > 1:
            planes[index - 2][2]()
        gather_part(index)
        if index + 1 < counts:
            push_rest(index + 1, every)
    if counts > 1:
        planes[counts - 2][2]()
    planes[counts - 1][1]()
    planes[counts - 1][2]()
    for plane in planes:
        plane[3]()
    hidden.finish()
    small.finish()
    for line in lines:
        line.finish()
    for _, copy in owns:
        copy.wait()


def settle(hidden, small, x, mix, gain, done, parts, inner, freight):
    _, _, rows, width = hidden.shape
    seq_devices = lax.axis_size("seq")
    anywhere = pl.BlockSpec(memory_space=pl.ANY)
    inside = pl.BlockSpec(memory_space=pltpu.VMEM)
    low = jnp.bfloat16
    sems = lambda *shape: pltpu.SemaphoreType.DMA(shape)
    small_rows, small_wide = small.shape[2:]
    shapes = [part.shape[1:] for part in parts] + [(small_rows, small_wide), done.shape]
    scratch = [
        pltpu.VMEM((rows, width), jnp.float32),
        pltpu.VMEM((small_rows, small_wide), jnp.float32),
    ]
    scratch += Reducer.scratch(1, rows, width)
    scratch += Reducer.scratch(inner, small_rows, small_wide)
    for shape in shapes:
        scratch += [pltpu.VMEM(shape, low), sems(14), sems(14), sems()]
    for shape in shapes[: len(parts)]:
        scratch += [pltpu.VMEM(shape, jnp.float32), sems(inner)]
        scratch += LineSum.scratch(inner, *shape)
    return run(
        functools.partial(settle_kernel, inner, len(parts)),
        (hidden, small, x, mix, gain, done) + tuple(parts),
        in_specs=[anywhere] * 2 + [inside] * 4 + [anywhere] * len(parts),
        out_specs=[inside] + [anywhere] * len(shapes),
        out_shape=[jax.ShapeDtypeStruct((rows, width), low)]
        + [jax.ShapeDtypeStruct((seq_devices,) + shape, low) for shape in shapes],
        scratch=scratch,
        freight=freight,
        flips=FLIPS,
        inner=inner,
        late=True,
        micros=90,
        name="settle",
    )


def params_of(limit=VMEM_BYTES):
    return pltpu.CompilerParams(vmem_limit_bytes=limit)


def project_kernel(x_ref, gain_ref, w_ref, dt_ref, hidden_ref, gate_ref, rows_ref):
    x = to_full(x_ref[...])
    hidden = to_low(x * norm_scale(x) * gain_ref[...])
    hidden_ref[...] = hidden
    gate_width = gate_ref.shape[1]
    used = 2 * gate_width
    state = rows_ref.shape[1] - LANES - gate_width
    projected = dot_full(hidden, w_ref[:, :used])
    gate_ref[...] = projected[:, :gate_width]
    rows_ref[:, :gate_width] = to_low(projected[:, gate_width:])
    rows_ref[:, gate_width : gate_width + state] = to_low(
        dot_full(hidden, w_ref[:, w_ref.shape[1] - state :])
    )
    rows_ref[:, gate_width + state :] = to_low(dot_full(hidden, dt_ref[...]))


def project(x, gain, weights, dt_weights, gate_width, columns, freight=()):
    rows, width = x.shape
    columns = columns + LANES
    tile = 256
    block = lambda extent: pl.BlockSpec((tile, extent), lambda step: (step, 0))
    return run(
        project_kernel,
        (x, gain, weights, dt_weights,),
        grid=(rows // tile,),
        in_specs=[
            block(width), whole(gain.shape), whole(weights.shape), whole(dt_weights.shape)
        ],
        out_specs=[block(width), block(gate_width), block(columns - gate_width)],
        out_shape=[
            jax.ShapeDtypeStruct((rows, width), jnp.bfloat16),
            jax.ShapeDtypeStruct((rows, gate_width), jnp.float32),
            jax.ShapeDtypeStruct((rows, columns - gate_width), jnp.bfloat16),
        ],
        freight=freight,
        micros=11,
        name="project",
    )


def put_split(columns, rows):
    lane = iota_of((rows, LANES), 1)
    result = jnp.zeros((rows, LANES), jnp.float32)
    for place, column in enumerate(columns):
        high = to_full(to_low(column))
        result = jnp.where(lane == 2 * place, high, result)
        result = jnp.where(lane == 2 * place + 1, column - high, result)
    return to_low(result)


def mix_out_kernel(y_ref, gate_ref, gain_ref, packed_ref, out_ref, w_ref, sent, *scratch):
    width = w_ref.shape[1]
    rows = out_ref.shape[0]
    unpack_rows(packed_ref, w_ref, True)

    def make(_, block, place):
        at = pl.ds(pl.multiple_of(block * rows, rows), rows)
        gated = to_full(y_ref[at, :]) * jax.nn.silu(gate_ref[at, :])
        place[:, :width] = to_low(dot_full(to_low(gated * gain_ref[...]), w_ref[...]))
        squares = jnp.sum(gated * gated, axis=1, keepdims=True)
        place[:, width:] = put_split([squares], rows)

    Reducer(1, sent, out_ref, scratch, make).whole(lambda number: None)


def mix_out(y, gate, gain, weights, blocks, freight=()):
    rows, channels = y.shape
    width = weights.shape[2]
    tile = rows // blocks
    inside = pl.BlockSpec(memory_space=pltpu.VMEM)
    return run(
        mix_out_kernel,
        (y, gate, gain, weights),
        in_specs=[inside] * 4,
        out_specs=[inside],
        out_shape=[jax.ShapeDtypeStruct((tile, width + LANES), jnp.float32)],
        scratch=[
            pltpu.VMEM((channels, width), jnp.bfloat16),
            pltpu.VMEM((1, 4, tile, width + LANES), jnp.bfloat16),
        ]
        + Reducer.scratch(1, tile, width + LANES),
        freight=freight,
        flips=FLIPS,
        micros=35,
        name="mix_out",
    )


def mix_back_kernel(
    mix_ref,
    y_ref,
    gate_ref,
    gain_ref,
    packed_ref,
    dy_ref,
    dgate_ref,
    w_grad_ref,
    gain_grad_ref,
    total,
    w_ref,
):
    step = pl.program_id(0)
    width = w_ref.shape[1]

    @pl.when(step == 0)
    def _():
        unpack_rows(packed_ref, w_ref, True)
        total[...] = jnp.zeros_like(total)
        gain_grad_ref[...] = jnp.zeros_like(gain_grad_ref)

    mix = mix_ref[0, :, :width]
    extra = to_full(mix_ref[0, :, width:])
    share = extra[:, 0:1] + extra[:, 1:2]
    scale = extra[:, 2:3] + extra[:, 3:4]
    normed_grad = dot_lanes(mix, w_ref[...])
    y = to_full(y_ref[...])
    gate = gate_ref[...]
    sig = jax.nn.sigmoid(gate)
    act = gate * sig
    unit = y * act * scale
    gain = gain_ref[...]
    gain_grad_ref[0:1, :] += jnp.sum(normed_grad * unit, axis=0, keepdims=True)
    gated_grad = scale * (normed_grad * gain - unit * share)
    dy_ref[...] = to_low(gated_grad * act)
    dgate_ref[...] = to_low(gated_grad * y * sig * (1.0 + gate * (1.0 - sig)))
    total[...] += dot_rows(to_low(unit * gain), mix)

    @pl.when(step == pl.num_programs(0) - 1)
    def _():
        w_grad_ref[...] = to_low(total[...])


def mix_back(mix, y, gate, gain, weights, freight=()):
    blocks, tile, wide = mix.shape
    rows, channels = y.shape
    shape = (channels, weights.shape[2])
    block = pl.BlockSpec((tile, channels), lambda step: (step, 0))
    return run(
        mix_back_kernel,
        (mix, y, gate, gain, weights,),
        grid=(blocks,),
        in_specs=[
            pl.BlockSpec((1, tile, wide), lambda step: (step, 0, 0)),
            block,
            block,
            whole(gain.shape),
            whole(weights.shape),
        ],
        out_specs=[block, block, whole(shape), whole((8, channels))],
        out_shape=[
            jax.ShapeDtypeStruct((rows, channels), jnp.bfloat16),
            jax.ShapeDtypeStruct((rows, channels), jnp.bfloat16),
            jax.ShapeDtypeStruct(shape, jnp.bfloat16),
            jax.ShapeDtypeStruct((8, channels), jnp.float32),
        ],
        scratch=[pltpu.VMEM(shape, jnp.float32), pltpu.VMEM(shape, jnp.bfloat16)],
        freight=freight,
        micros=12,
        name="mix_back",
    )


def project_back_kernel(
    dgate_ref, drows_ref, hidden_ref, w_ref, dt_ref, part_ref, main_grad_ref, rest_grad_ref, total
):
    step = pl.program_id(0)

    @pl.when(step == 0)
    def _():
        total[...] = jnp.zeros_like(total)

    grads = jnp.concatenate([dgate_ref[...], drows_ref[...]], axis=1)
    main = 2 * dgate_ref.shape[1]
    columns = grads.shape[1] - LANES
    state_at = w_ref.shape[1] - (columns - main)
    part_ref[0] = to_low(
        dot_lanes(grads[:, :main], w_ref[:, :main])
        + dot_lanes(grads[:, main:columns], w_ref[:, state_at:])
        + dot_lanes(grads[:, columns:], dt_ref[...])
    )
    total[...] += dot_rows(hidden_ref[...], grads)

    @pl.when(step == pl.num_programs(0) - 1)
    def _():
        main_grad_ref[...] = to_low(total[:, :main])
        rest_grad_ref[...] = to_low(total[:, main:])
        by_gain = jnp.sum(total[:, :main] * to_full(w_ref[:, :main]), axis=1, keepdims=True)
        by_gain += jnp.sum(
            total[:, main:columns] * to_full(w_ref[:, state_at:]), axis=1, keepdims=True
        )
        by_gain += jnp.sum(total[:, columns:] * to_full(dt_ref[...]), axis=1, keepdims=True)
        rest = rest_grad_ref.shape[1]
        lane = iota_of((rest_grad_ref.shape[0], LANES), 1)
        rest_grad_ref[:, rest - LANES :] = to_low(
            jnp.where(lane == LANES - 1, by_gain, total[:, columns:])
        )


def project_back(dgate, drows, hidden, weights, dt_weights, blocks, freight=()):
    rows, width = hidden.shape
    tile = rows // blocks
    main = 2 * dgate.shape[1]
    rest = dgate.shape[1] + drows.shape[1] - main
    block = lambda extent: pl.BlockSpec((tile, extent), lambda step: (step, 0))
    return run(
        project_back_kernel,
        (dgate, drows, hidden, weights, dt_weights,),
        grid=(blocks,),
        in_specs=[
            block(dgate.shape[1]),
            block(drows.shape[1]),
            block(width),
            whole(weights.shape),
            whole(dt_weights.shape),
        ],
        out_specs=[
            pl.BlockSpec((1, tile, width), lambda step: (step, 0, 0)),
            whole((width, main)),
            whole((width, rest)),
        ],
        out_shape=[
            jax.ShapeDtypeStruct((blocks, tile, width), jnp.bfloat16),
            jax.ShapeDtypeStruct((width, main), jnp.bfloat16),
            jax.ShapeDtypeStruct((width, rest), jnp.bfloat16),
        ],
        scratch=[pltpu.VMEM((width, main + rest), jnp.float32)],
        freight=freight,
        micros=25,
        name="project_back",
    )


def unpack_rows(packed_ref, held_ref, first):
    blocks, both, _ = packed_ref.shape
    fine = held_ref.shape[0] // blocks
    start = 0 if first else both - fine
    for block in range(blocks):
        held_ref[block * fine : (block + 1) * fine] = packed_ref[block, start : start + fine]


def shared_kernel(
    rows_ref,
    grad_ref,
    up_ref,
    down_ref,
    res_ref,
    back_ref,
    up_grad_ref,
    down_grad_ref,
    up_sum,
    down_sum,
    down_held,
):
    step = pl.program_id(0)

    @pl.when(step == 0)
    def _():
        up_sum[...] = jnp.zeros_like(up_sum)
        down_sum[...] = jnp.zeros_like(down_sum)
        unpack_rows(down_ref, down_held, False)

    hidden, width = down_held.shape
    rows = rows_ref[0, :, :width]
    grad = grad_ref[0]
    joined = dot_full(rows, up_ref[...])
    gate, up = joined[:, :hidden], joined[:, hidden:]
    sig = jax.nn.sigmoid(gate)
    act = gate * sig
    acted = to_low(act * up)
    res_ref[0] = to_low(dot_full(acted, down_held[...]))
    down_sum[...] += dot_rows(acted, grad)
    act_grad = dot_lanes(grad, down_held[...])
    joined_grad = to_low(
        jnp.concatenate(
            [act_grad * up * sig * (1.0 + gate * (1.0 - sig)), act_grad * act], axis=1
        )
    )
    up_sum[...] += dot_rows(rows, joined_grad)
    back_ref[0] = to_low(dot_lanes(joined_grad, up_ref[...]))

    @pl.when(step == pl.num_programs(0) - 1)
    def _():
        up_grad_ref[...] = to_low(up_sum[...])
        down_grad_ref[...] = to_low(down_sum[...])


def shared_expert(rows, grad, up, up_at, down, hidden, blocks, inner, freight=()):
    _, tile, wide = rows.shape
    width = down.shape[2]
    down_shape = (hidden, width)
    up_shape = (width, 2 * hidden)
    block = pl.BlockSpec((1, tile, width), lambda step: (step, 0, 0))
    low = jnp.bfloat16
    own = lambda extent: pl.BlockSpec(
        (1, tile, extent), lambda step: (own_shard_group(inner)[0] * blocks + step, 0, 0)
    )
    return run(
        shared_kernel,
        (rows, grad, up, down),
        grid=(blocks,),
        in_specs=[
            own(wide),
            own(width),
            pl.BlockSpec((width, up_shape[1]), lambda step: (0, up_at // up_shape[1])),
            whole(down.shape),
        ],
        out_specs=[block, block, whole(up_shape), whole(down_shape)],
        out_shape=[
            jax.ShapeDtypeStruct((blocks, tile, width), low),
            jax.ShapeDtypeStruct((blocks, tile, width), low),
            jax.ShapeDtypeStruct(up_shape, low),
            jax.ShapeDtypeStruct(down_shape, low),
        ],
        scratch=[
            pltpu.VMEM(up_shape, jnp.float32),
            pltpu.VMEM(down_shape, jnp.float32),
            pltpu.VMEM(down_shape, low),
        ],
        freight=freight,
        micros=18,
        name="shared_expert",
    )


def dispatch_kernel(
    rows_ref, grad_ref, x_ref, g_ref, picks_ref, *, top_count, slots, own_first
):
    per_device = x_ref.shape[0]
    together, tok_rows, _ = rows_ref.shape
    width = g_ref.shape[2]
    wide = width + LANES
    taken = per_device * slots
    lane = iota_of((tok_rows, LANES), 1)
    named = (lane >= 2 * top_count) & (lane < 3 * top_count)
    before = iota_of((tok_rows, tok_rows), 0) > iota_of((tok_rows, tok_rows), 1)
    before = to_low(jnp.where(before, 1.0, 0.0))
    first = own_first()
    for index in range(together):
        extra = to_full(rows_ref[index, :, width:wide])
        member = jnp.zeros((tok_rows, LANES), jnp.float32)
        for expert in range(per_device):
            own = (first + expert).astype(jnp.float32)
            hit = jnp.sum(jnp.where(named & (extra == own), 1.0, 0.0), axis=1, keepdims=True)
            member = jnp.where(lane // slots == expert, hit, member)
        ranks = dot_full(before, to_low(member))
        picks = jnp.where(
            (ranks == to_full(lane % slots)) & (member > 0.0), 1.0, 0.0
        ).astype(jnp.bfloat16)
        picks_ref[index] = picks
        rows = to_low(dot_rows(picks[:, :taken], rows_ref[index]))
        grads = to_low(dot_rows(picks[:, :taken], grad_ref[index]))
        start = index * slots
        for expert in range(per_device):
            span = slice(expert * slots, (expert + 1) * slots)
            x_ref[expert, start : start + slots] = rows[span]
            g_ref[expert, start : start + slots] = grads[span]


def dispatch(rows, grad, per_device, top_count, slots, own_first, freight=()):
    blocks, tok_rows, wide = rows.shape
    width = grad.shape[2]
    together = 4
    block = lambda extent: pl.BlockSpec((together, tok_rows, extent), lambda step: (step, 0, 0))
    taken = lambda extent: pl.BlockSpec(
        (per_device, together * slots, extent), lambda step: (0, step, 0)
    )
    return run(
        functools.partial(
            dispatch_kernel, top_count=top_count, slots=slots, own_first=own_first
        ),
        (rows, grad),
        grid=(blocks // together,),
        in_specs=[block(wide), block(width)],
        out_specs=[taken(width + LANES), taken(width), block(LANES)],
        out_shape=[
            jax.ShapeDtypeStruct((per_device, blocks * slots, width + LANES), jnp.bfloat16),
            jax.ShapeDtypeStruct((per_device, blocks * slots, width), jnp.bfloat16),
            jax.ShapeDtypeStruct((blocks, tok_rows, LANES), jnp.bfloat16),
        ],
        freight=freight,
        micros=30,
        name="dispatch",
    )


def experts_kernel(
    depart, arrive, targets, *refs, count, per_device, top_count, own_first, inner, doubles, outgoing
):
    x_ref, g_ref = refs[:2]
    total = 2 * count * per_device
    pieces, refs = refs[2 : 2 + total], refs[2 + total :]
    seconds, came = {}, list(targets)
    for number, (_, carried) in doubles.items():
        if carried:
            seconds[number] = came.pop(0)
        else:
            seconds[number], refs = refs[0], refs[1:]
    is_incoming = lambda item: item.output is None
    is_outgoing = lambda item: item.output is not None
    late = any(carried for _, carried in doubles.values())
    res_ref, dx_ref = refs[:2]
    outs = refs[2 : 2 + total]
    up_held, down_held, up_sum, down_sum, up_low, down_low, sems = refs[2 + total :]
    own_place, _ = own_shard_group(inner)
    expert, step = pl.program_id(0), pl.program_id(1)
    steps = pl.num_programs(1)
    slot = lax.rem(expert, 2)
    width, double = up_held.shape[1:]
    hidden = double // 2
    tile = x_ref.shape[1]

    def parts(which, up, down):
        result = []
        for shift in range(count):
            from_place = lax.rem(own_place + count - shift, count)
            for kind, held in enumerate((up, down)):
                extent = held.shape[0] // count
                start = pl.multiple_of(from_place * extent, extent)
                number = (shift * per_device + which) * 2 + kind
                result.append((number, held.at[pl.ds(start, extent)], (shift, kind)))
        return result

    def fetch(which, action):
        half = which % 2
        for number, held, at in parts(which, up_held.at[half], down_held.at[half]):
            sem = sems.at[half, at[0], at[1]]
            piece = pieces[number]
            if len(piece.shape) == 3:
                piece = piece.at[own_place * per_device + which]
            if number in seconds:
                early = among(own_place, doubles[number][0])
                pl.when(early)(
                    lambda: action(pltpu.make_async_copy(piece, held, sem))
                )
                pl.when(jnp.logical_not(early))(
                    lambda: action(pltpu.make_async_copy(seconds[number], held, sem))
                )
            else:
                action(pltpu.make_async_copy(piece, held, sem))

    begin_copy = lambda copy: copy.start()
    end_copy = lambda copy: copy.wait()

    for which in range(per_device):

        @pl.when((step == 0) & (expert == which))
        def _():
            if which == 0:
                fetch(0, begin_copy)
                depart(is_incoming)
            if which == 1:
                arrive(is_incoming)
                depart(is_outgoing)
                if late:
                    fetch(1, begin_copy)
            fetch(which, end_copy)
            if which + 1 < per_device and not (late and which == 0):
                fetch(which + 1, begin_copy)

    @pl.when(step == 0)
    def _():
        up_sum[...] = jnp.zeros_like(up_sum)
        down_sum[...] = jnp.zeros_like(down_sum)

    up, down = up_held.at[slot], down_held.at[slot]
    rows = x_ref[0, :, :width]
    extra = to_full(x_ref[0, :, width:])
    lane = iota_of((tile, LANES), 1)
    own = own_first() + expert
    hits = jnp.where((lane < 3 * top_count) & (extra == own.astype(jnp.float32)), 1.0, 0.0)
    gate_slot = jnp.zeros((tile, 1), jnp.float32)
    for route in range(top_count):
        place = 2 * top_count + route
        value = extra[:, 2 * route : 2 * route + 1] + extra[:, 2 * route + 1 : 2 * route + 2]
        gate_slot = gate_slot + hits[:, place : place + 1] * value
    joined = dot_full(rows, up[...])
    gate, lift = joined[:, :hidden], joined[:, hidden:]
    sig = jax.nn.sigmoid(gate)
    act = gate * sig
    acted = to_low(act * lift)
    res = to_low(dot_full(acted, down[...]))
    grads = g_ref[0]
    wide_grads = to_full(grads)
    wide_res = to_full(res)
    gate_grad = jnp.sum(wide_res * wide_grads, axis=1, keepdims=True)
    res_ref[0] = to_low(wide_res * gate_slot)
    weighted = to_low(wide_grads * gate_slot)
    act_grad = dot_lanes(weighted, down[...])
    down_sum[...] += dot_rows(acted, weighted)
    joined_grad = to_low(
        jnp.concatenate(
            [act_grad * lift * sig * (1.0 + gate * (1.0 - sig)), act_grad * act], axis=1
        )
    )
    dx_ref[0, :, :width] = to_low(dot_lanes(joined_grad, up[...]))
    high = to_full(to_low(gate_grad))
    half = LANES // 2
    dx_ref[0, :, width:] = to_low(
        jnp.where(lane == own, high, 0.0) + jnp.where(lane == own + half, gate_grad - high, 0.0)
    )
    up_sum[...] += dot_rows(rows, joined_grad)

    for which in range(per_device):

        @pl.when((step == steps - 1) & (expert == which))
        def _():
            up_low[...] = to_low(up_sum[...])
            down_low[...] = to_low(down_sum[...])
            copies = [
                pltpu.make_async_copy(held, outs[number], sems.at[2, at[0], at[1]])
                for number, held, at in parts(which, up_low, down_low)
            ]
            for copy in copies:
                copy.start()
            for copy in copies:
                copy.wait()

    if outgoing:

        @pl.when((step == steps - 1) & (expert == per_device - 1))
        def _():
            arrive(is_outgoing)


def experts(x, g, pieces, hidden, top_count, own_first, inner, doubles=(), outgoing=()):
    per_device, rows, wide = x.shape
    width = g.shape[2]
    count = len(pieces) // per_device // 2
    low = jnp.bfloat16
    shapes = [jax.ShapeDtypeStruct(piece.shape[-2:], low) for piece in pieces]
    carried = [other for _, other, _ in doubles if isinstance(other, Parcel)]
    freight = carried + [
        Parcel(shapes[key], shift, inner, output=2 + key) for key, shift in outgoing
    ]
    others = [other for _, other, _ in doubles if not isinstance(other, Parcel)]
    double = 2 * hidden
    tile = min(rows, 256)
    block = lambda extent: pl.BlockSpec((1, tile, extent), lambda e, step: (e, step, 0))
    anywhere = pl.BlockSpec(memory_space=pl.ANY)
    low = jnp.bfloat16
    outs = run(
        functools.partial(
            experts_kernel,
            count=count,
            per_device=per_device,
            top_count=top_count,
            own_first=own_first,
            inner=inner,
            doubles={
                number: (places, isinstance(other, Parcel)) for number, other, places in doubles
            },
            outgoing=outgoing,
        ),
        (x, g) + tuple(pieces) + tuple(others),
        grid=(per_device, rows // tile),
        in_specs=[block(wide), block(width)] + [anywhere] * (len(pieces) + len(others)),
        out_specs=[block(width), block(wide)] + [anywhere] * len(shapes),
        out_shape=[
            jax.ShapeDtypeStruct((per_device, rows, width), low),
            jax.ShapeDtypeStruct((per_device, rows, wide), low),
        ]
        + shapes,
        scratch=[
            pltpu.VMEM((2, width, double), low),
            pltpu.VMEM((2, hidden, width), low),
            pltpu.VMEM((width, double), jnp.float32),
            pltpu.VMEM((hidden, width), jnp.float32),
            pltpu.VMEM((width, double), low),
            pltpu.VMEM((hidden, width), low),
            pltpu.SemaphoreType.DMA((3, count, 2)),
        ],
        freight=freight,
        inner=inner if freight else 1,
        late=True,
        micros=45,
        name="experts",
    )
    sent = outs.pop()[len(carried) :] if freight else []
    return outs[0], outs[1], outs[2:], sent


def combine_kernel(
    picks_ref, res_ref, dx_ref, sres_ref, sback_ref, out_ref, back_ref, *, slots, inner
):
    step = pl.program_id(0)
    together, _, width = out_ref.shape
    per_device = res_ref.shape[0]
    blocks = sres_ref.shape[0]
    place, _ = own_shard_group(inner)
    for index in range(together):
        picks = picks_ref[index, :, : per_device * slots]
        start = index * slots
        stacked = lambda ref: jnp.concatenate(
            [ref[expert, start : start + slots] for expert in range(per_device)], axis=0
        )
        out_ref[index] = to_low(dot_full(picks, stacked(res_ref)))
        back_ref[index] = to_low(dot_full(picks, stacked(dx_ref)))

    @pl.when(lax.div(step * together, blocks) == place)
    def _():
        first = lax.rem(step * together, blocks)
        for index in range(together):
            out_ref[index] = to_low(to_full(out_ref[index]) + to_full(sres_ref[first + index]))
            back_ref[index, :, :width] = to_low(
                to_full(back_ref[index, :, :width]) + to_full(sback_ref[first + index])
            )


def combine(picks, res, dx, shared_res, shared_back, inner, freight=()):
    blocks, tok_rows, _ = picks.shape
    per_device, rows, width = res.shape
    slots = rows // blocks
    together = 4
    block = lambda extent: pl.BlockSpec((together, tok_rows, extent), lambda step: (step, 0, 0))
    taken = lambda extent: pl.BlockSpec(
        (per_device, together * slots, extent), lambda step: (0, step, 0)
    )
    return run(
        functools.partial(combine_kernel, slots=slots, inner=inner),
        (picks, res, dx, shared_res, shared_back),
        grid=(blocks // together,),
        in_specs=[
            block(LANES),
            taken(width),
            taken(width + LANES),
            whole(shared_res.shape),
            whole(shared_back.shape),
        ],
        out_specs=[block(width), block(width + LANES)],
        out_shape=[
            jax.ShapeDtypeStruct((blocks, tok_rows, width), jnp.bfloat16),
            jax.ShapeDtypeStruct((blocks, tok_rows, width + LANES), jnp.bfloat16),
        ],
        freight=freight,
        micros=30,
        name="combine",
    )


def assemble_kernel(
    main_ref, shared_in_ref, small_ref, rows_ref, w_in_ref, shared_ref, out_ref, down_ref
):
    seq_devices, rows, double = main_ref.shape
    channels = double // 2
    for device in range(seq_devices):
        for target, source in ((w_in_ref, main_ref), (shared_ref, shared_in_ref)):
            extent = source.shape[2] // 2
            for side in range(2):
                start = (side * seq_devices + device) * extent
                target[:, start : start + extent] = to_full(
                    source[device, :, side * extent : (side + 1) * extent]
                )
    start = 2 * seq_devices * channels
    w_in_ref[:, start:] = to_full(small_ref[0, :rows, : w_in_ref.shape[1] - start])
    halves, _, out_rows, _ = out_ref.shape
    down_rows = down_ref.shape[2]
    for half in range(halves):
        at = half * (out_rows + down_rows)
        out_ref[half, 0] = to_full(rows_ref[0, at : at + out_rows])
        down_ref[half, 0] = to_full(rows_ref[0, at + out_rows : at + out_rows + down_rows])


def assemble(main, shared, small, rows, columns, shared_columns, out_rows, down_rows, halves):
    seq_devices, depth_rows, _ = main.shape
    tile = depth_rows // seq_devices
    width = rows.shape[2]
    out_fine = out_rows // halves // seq_devices
    down_fine = down_rows // halves // seq_devices
    flat = lambda extent: pl.BlockSpec((tile, extent), lambda step: (step, 0))
    fine = lambda extent: pl.BlockSpec(
        (halves, 1, extent, width), lambda step: (0, step, 0, 0)
    )
    full = jnp.float32
    results = pl.pallas_call(
        assemble_kernel,
        grid=(seq_devices,),
        in_specs=[
            pl.BlockSpec((seq_devices, tile, main.shape[2]), lambda step: (0, step, 0)),
            pl.BlockSpec((seq_devices, tile, shared.shape[2]), lambda step: (0, step, 0)),
            pl.BlockSpec((1,) + small.shape[1:], lambda step: (step, 0, 0)),
            pl.BlockSpec((1,) + rows.shape[1:], lambda step: (step, 0, 0)),
        ],
        out_specs=[flat(columns), flat(shared_columns), fine(out_fine), fine(down_fine)],
        out_shape=[
            jax.ShapeDtypeStruct((depth_rows, columns), full),
            jax.ShapeDtypeStruct((depth_rows, shared_columns), full),
            jax.ShapeDtypeStruct((halves, seq_devices, out_fine, width), full),
            jax.ShapeDtypeStruct((halves, seq_devices, down_fine, width), full),
        ],
        compiler_params=params_of(),
        cost_estimate=cost_of(10),
        name="assemble",
    )(main, shared, small, rows)
    return results[0], results[1], results[2].reshape(-1, width), results[3].reshape(-1, width)


def collect_kernel(place_ref, *refs):
    del place_ref
    step = pl.program_id(0)
    up_ref, down_ref = refs[-2:]
    for order in range(len(refs) // 2 - 1):

        @pl.when(step == order)
        def _():
            up_ref[0] = to_full(refs[2 * order][...])
            down_ref[0] = to_full(refs[2 * order + 1][...])


def collect(place, pieces, per_device):
    count = len(pieces) // 2
    up, down = pieces[0].shape, pieces[1].shape

    def here(step, place):
        shift, expert = lax.div(step, per_device), lax.rem(step, per_device)
        return (
            lax.rem(place[0] + shift, count // per_device) * per_device + expert, 0, 0
        )

    still = lambda shape: pl.BlockSpec(shape, lambda step, place: (0, 0))
    return pl.pallas_call(
        collect_kernel,
        grid_spec=pltpu.PrefetchScalarGridSpec(
            num_scalar_prefetch=1,
            grid=(count,),
            in_specs=[still(up), still(down)] * count,
            out_specs=[pl.BlockSpec((1,) + up, here), pl.BlockSpec((1,) + down, here)],
        ),
        out_shape=[
            jax.ShapeDtypeStruct((count,) + up, jnp.float32),
            jax.ShapeDtypeStruct((count,) + down, jnp.float32),
        ],
        compiler_params=params_of(),
        cost_estimate=cost_of(12),
        name="collect",
    )(place, *pieces)


def route_hits(routes, route, lane):
    return lane == routes[:, route : route + 1]


def token_forward_kernel(
    mixed_ref, x_ref, gain_ref, router_ref, routes_ref, after_ref, wide_ref, gates_ref, *, inner_width, top_count
):
    width = x_ref.shape[1]
    rows = x_ref.shape[0]
    squares = mixed_ref[:, width : width + 1] + mixed_ref[:, width + 1 : width + 2]
    scale = lax.rsqrt(squares / inner_width + EPSILON)
    after = to_full(x_ref[...]) + mixed_ref[:, :width] * scale
    after_ref[...] = after
    moe_in = to_low(after * norm_scale(after) * gain_ref[...])
    wide_ref[:, :width] = moe_in
    logits = dot_full(moe_in, router_ref[...])
    lane = iota_of((rows, LANES), 1)
    routes = routes_ref[...]
    picked = [
        jnp.sum(jnp.where(route_hits(routes, k, lane), logits, 0.0), axis=1, keepdims=True)
        for k in range(top_count)
    ]
    largest = functools.reduce(jnp.maximum, picked)
    powers = [jnp.exp(value - largest) for value in picked]
    total = sum(powers)
    gates = jnp.zeros((rows, LANES), jnp.float32)
    extra = jnp.zeros((rows, LANES), jnp.float32)
    for k in range(top_count):
        value = powers[k] / total
        high = to_full(to_low(value))
        gates = jnp.where(lane == k, value, gates)
        extra = jnp.where(lane == 2 * k, high, extra)
        extra = jnp.where(lane == 2 * k + 1, value - high, extra)
        extra = jnp.where(lane == 2 * top_count + k, to_full(routes[:, k : k + 1]), extra)
    gates_ref[...] = jnp.where(lane == top_count, scale, gates)
    wide_ref[:, width:] = to_low(extra)


def token_forward(mixed, x, gain, router, routes, inner_width, top_count):
    rows, width = x.shape
    arrays = (mixed, x, gain, router, routes)
    return pl.pallas_call(
        functools.partial(
            token_forward_kernel, inner_width=inner_width, top_count=top_count
        ),
        in_specs=[whole(array.shape) for array in arrays],
        out_specs=[whole((rows, width)), whole((rows, width + LANES)), whole((rows, LANES))],
        out_shape=[
            jax.ShapeDtypeStruct((rows, width), jnp.float32),
            jax.ShapeDtypeStruct((rows, width + LANES), jnp.bfloat16),
            jax.ShapeDtypeStruct((rows, LANES), jnp.float32),
        ],
        compiler_params=params_of(),
        cost_estimate=cost_of(5),
        name="token_forward",
    )(*arrays)


def token_back_kernel(
    back_ref,
    mixed_ref,
    after_ref,
    wide_ref,
    gates_ref,
    grad_ref,
    gain_ref,
    router_ref,
    routes_ref,
    mix_ref,
    mix_wide_ref,
    router_grad_ref,
    gain_grad_ref,
    *,
    inner_width,
    top_count,
):
    rows, width = grad_ref.shape
    lane = iota_of((rows, LANES), 1)
    half = LANES // 2
    routes = routes_ref[...]
    gates = gates_ref[...]
    all_grads = back_ref[:, width:]
    values = [gates[:, k : k + 1] for k in range(top_count)]
    grads = [
        jnp.sum(
            jnp.where(
                route_hits(routes, k, lane) | route_hits(routes, k, lane - half), all_grads, 0.0
            ),
            axis=1,
            keepdims=True,
        )
        for k in range(top_count)
    ]
    common = sum(value * grad for value, grad in zip(values, grads))
    logit_grad = jnp.zeros((rows, LANES), jnp.float32)
    for k in range(top_count):
        logit_grad = jnp.where(
            route_hits(routes, k, lane), values[k] * (grads[k] - common), logit_grad
        )
    logit_grad = to_low(logit_grad)
    router_grad_ref[...] = to_low(dot_rows(wide_ref[:, :width], logit_grad))
    moe_grad = back_ref[:, :width] + dot_lanes(logit_grad, router_ref[...])
    after = after_ref[...]
    scale = norm_scale(after)
    unit = after * scale
    gain_grad_ref[...] = jnp.broadcast_to(
        jnp.sum(moe_grad * unit, axis=0, keepdims=True), (8, width)
    )
    scaled = moe_grad * gain_ref[...]
    mean = jnp.mean(scaled * unit, axis=1, keepdims=True)
    mix = to_full(grad_ref[...]) + scale * (scaled - unit * mean)
    mix_ref[...] = mix
    mix_low = to_low(mix)
    mix_wide_ref[:, :width] = mix_low
    mix_scale = gates[:, top_count : top_count + 1]
    share = jnp.sum(to_full(mix_low) * mixed_ref[:, :width], axis=1, keepdims=True)
    mix_wide_ref[:, width:] = put_split([share * mix_scale / inner_width, mix_scale], rows)


def token_back(back, mixed, after, wide, gates, grad, gain, router, routes, inner_width, top_count):
    rows, width = grad.shape
    arrays = (back, mixed, after, wide, gates, grad, gain, router, routes)
    return pl.pallas_call(
        functools.partial(token_back_kernel, inner_width=inner_width, top_count=top_count),
        in_specs=[whole(array.shape) for array in arrays],
        out_specs=[
            whole((rows, width)),
            whole((rows, width + LANES)),
            whole((width, LANES)),
            whole((8, width)),
        ],
        out_shape=[
            jax.ShapeDtypeStruct((rows, width), jnp.float32),
            jax.ShapeDtypeStruct((rows, width + LANES), jnp.bfloat16),
            jax.ShapeDtypeStruct((width, LANES), jnp.bfloat16),
            jax.ShapeDtypeStruct((8, width), jnp.float32),
        ],
        compiler_params=params_of(),
        cost_estimate=cost_of(6),
        name="token_back",
    )(*arrays)


ROWS_AFTER = 16


def pack_kernel(
    rest_ref, router_ref, conv_ref, head_ref, gate_ref, moe_ref, out_ref, wide, *, inner_width, experts, heads
):
    part = lax.axis_index("seq")
    inner, seq_devices, block_rows, columns = out_ref.shape
    depth = block_rows - ROWS_AFTER
    state = columns - LANES
    lane = iota_of((rest_ref.shape[0], LANES), 1)
    last = to_full(rest_ref[:, state:])
    steps = jnp.where(lane < heads, last, 0.0)
    extra = to_full(router_ref[...]) + pltpu.roll(steps, experts + heads * part, 1)
    extra = to_low(jnp.where(lane == LANES - 1, last, extra))
    for shard in range(inner):
        for device in range(seq_devices):
            start = (shard * seq_devices + device) * depth
            out_ref[shard, device, :depth, :state] = rest_ref[start : start + depth, :state]
            out_ref[shard, device, :depth, state:] = extra[start : start + depth]
    channels = gate_ref.shape[1]
    others = conv_ref.shape[1] - channels
    wide[...] = jnp.zeros_like(wide)
    own = pl.ds(pl.multiple_of(part * channels, channels), channels)
    wide[:8, own] = conv_ref[:, :channels]
    wide[:8, inner_width : inner_width + others] = conv_ref[:, channels:]
    wide[8:, own] = gate_ref[...]
    convs = wide[:8, :]
    gates = wide[8:, :]
    per_conv = (inner_width + others) // inner
    per_gate = inner_width // inner
    width = moe_ref.shape[1] // inner
    row = iota_of((ROWS_AFTER, columns), 0)
    blank = jnp.zeros((1, columns), jnp.float32)
    head_lane = iota_of((8, LANES), 1)
    values = jnp.where(head_lane < heads, head_ref[...], 0.0)
    values = [
        jnp.concatenate([pltpu.roll(values, heads * part, 1)[k : k + 1], blank[:, LANES:]], axis=1)
        for k in range(3)
    ]
    moe = moe_ref[...]

    def pieces(rows, at, start, extent):
        count = -(-extent // columns)
        return [rows[at : at + 1, start + k * columns : start + (k + 1) * columns] for k in range(count)]

    for shard in range(inner):
        for device in range(seq_devices):
            if device < 5:
                lines = pieces(convs, device, shard * per_conv, per_conv)
            elif device == 5:
                lines = pieces(gates, 0, shard * per_gate, per_gate)
            elif device == 6:
                lines = values
            else:
                lines = [moe[:1, shard * width : (shard + 1) * width]]
                lines = [jnp.concatenate([lines[0], blank[:, width:]], axis=1) if width < columns else lines[0]]
            tile = jnp.zeros((ROWS_AFTER, columns), jnp.float32)
            for k, line in enumerate(lines):
                tile = jnp.where(row == k, line, tile)
            out_ref[shard, device, depth:] = to_low(tile)


def pack(rest, router, conv, head, gate, moe, inner, seq_devices, inner_width, experts, heads):
    depth = rest.shape[0] // inner // seq_devices
    columns = rest.shape[1]
    arrays = (rest, router, conv, head, gate, moe)
    reach = inner_width + conv.shape[1] - gate.shape[1] + columns
    return pl.pallas_call(
        functools.partial(pack_kernel, inner_width=inner_width, experts=experts, heads=heads),
        in_specs=[whole(array.shape) for array in arrays],
        out_specs=whole((inner, seq_devices, depth + ROWS_AFTER, columns)),
        out_shape=jax.ShapeDtypeStruct(
            (inner, seq_devices, depth + ROWS_AFTER, columns), jnp.bfloat16
        ),
        scratch_shapes=[pltpu.VMEM((16, -(-reach // LANES) * LANES), jnp.float32)],
        compiler_params=params_of(),
        cost_estimate=cost_of(3),
        name="pack",
    )(*arrays)


def rows_to_send(weights, part):
    seq_devices = lax.axis_size("seq")
    halves = max(1, seq_devices // lax.axis_size("shard"))
    mine = []
    for weight in weights:
        view = weight.reshape(halves, seq_devices, -1, weight.shape[1])
        mine.append(lax.dynamic_index_in_dim(view, part, 1, keepdims=False))
    return jnp.concatenate(mine, axis=1).reshape(-1, weights[0].shape[1])


def rows_by_owner(joined):
    seq_devices = lax.axis_size("seq")
    return joined.reshape(seq_devices, -1, joined.shape[2])


def rows_of_owner(taken, weights):
    seq_devices = lax.axis_size("seq")
    halves = max(1, seq_devices // lax.axis_size("shard"))
    fine_rows = [weight.shape[0] // halves // seq_devices for weight in weights]
    width = taken.shape[2]
    taken = taken.reshape(seq_devices, -1, sum(fine_rows), width).transpose(1, 0, 2, 3)
    results, start = [], 0
    for fine in fine_rows:
        results.append(taken[:, :, start : start + fine].reshape(-1, width))
        start += fine
    return results


def rows_from_owner(grads):
    seq_devices = lax.axis_size("seq")
    shard_devices = lax.axis_size("shard")
    width = grads[0].shape[1]
    turns = shard_devices * max(1, seq_devices // shard_devices) // seq_devices
    pieces = [
        grad.reshape(turns, seq_devices, -1, width).transpose(1, 0, 2, 3) for grad in grads
    ]
    return jnp.concatenate(pieces, axis=2).reshape(seq_devices, -1, width)


def rows_of_shard(joined, weights):
    seq_devices = lax.axis_size("seq")
    halves = max(1, seq_devices // lax.axis_size("shard"))
    fine_rows = [weight.shape[0] // halves // seq_devices for weight in weights]
    width = joined.shape[2]
    spread = joined.reshape(seq_devices, halves, -1, width).transpose(1, 0, 2, 3)
    results, start = [], 0
    for fine in fine_rows:
        results.append(to_full(spread[:, :, start : start + fine]).reshape(-1, width))
        start += fine
    return results


def inner_groups(inner):
    count = lax.axis_size("shard")
    return [list(range(start, start + inner)) for start in range(0, count, inner)]


def outer_groups(inner):
    count = lax.axis_size("shard")
    return [list(range(start, count, inner)) for start in range(inner)]


def stacked_pieces(received, place, inner):
    own = jnp.stack(received)[lax.rem(place + inner - jnp.arange(inner), inner)]
    joined = lax.all_gather(own, "shard", axis_index_groups=outer_groups(inner))
    return joined.reshape(-1, joined.shape[-1])


def split_piece(grad, shift, place, inner):
    outer = lax.axis_size("shard") // inner
    rows = grad.reshape(outer, inner, -1, grad.shape[1])
    here = lax.rem(place + inner - shift, inner)
    return lax.psum_scatter(
        lax.dynamic_index_in_dim(rows, here, 1, keepdims=False),
        "shard",
        axis_index_groups=outer_groups(inner),
    )


def local(
    tokens,
    out_grad,
    deal_order,
    lengths,
    routes,
    norm_in,
    w_in,
    w_dt,
    conv_w,
    conv_b,
    dt_bias,
    a_log,
    d_skip,
    norm_gate,
    w_out,
    norm_moe,
    w_router,
    w_shared,
    w_shared_down,
    w_experts,
    w_experts_down,
):
    seq_devices = lax.axis_size("seq")
    shard_devices = lax.axis_size("shard")
    part = lax.axis_index("seq")
    shard = lax.axis_index("shard")
    inner = min(shard_devices, INNER)
    outer = shard_devices // inner
    place = lax.rem(shard, inner)
    _, tok_rows, width = tokens.shape
    group_rows = tok_rows * seq_devices
    inner_width = w_out.shape[0] * shard_devices
    channels = inner_width // seq_devices
    head_total = w_dt.shape[1]
    heads = head_total // seq_devices
    shared_width = w_shared_down.shape[0] * shard_devices
    shared_part = shared_width // seq_devices
    depth_rows = w_in.shape[0]
    expert_total = w_router.shape[1]
    local_experts, _, double = w_experts.shape
    hidden = double // 2
    hidden_rows = w_experts_down.shape[1]
    top_count = routes.shape[2]
    per_device = local_experts // inner
    blocks = inner * seq_devices
    COLLECTIVES.clear()

    def own_columns(array, start, extent):
        return lax.dynamic_slice_in_dim(array, start + part * extent, extent, 1)

    def own_rows(array, extent):
        return lax.dynamic_slice_in_dim(array, part * extent, extent, 0)

    row_wide = -(-max(conv_w.shape[0], norm_gate.shape[0]) // LANES) * LANES
    row_of = lambda piece: jnp.pad(piece, ((0, 0), (0, row_wide - piece.shape[1])))
    vectors = [conv_b, norm_gate, norm_in, norm_moe, dt_bias, a_log, d_skip]
    flat = jnp.concatenate([row_of(conv_w.T)] + [row_of(vector[None]) for vector in vectors])
    by_depth = jnp.concatenate(
        [
            w_router,
            own_columns(w_dt, 0, heads),
            jnp.zeros((depth_rows, LANES - expert_total - heads), jnp.bfloat16),
        ],
        axis=1,
    )
    weights_of = (w_experts, w_experts_down)

    def own_first():
        here, _ = own_shard_group(inner)
        return lax.axis_index("seq") * local_experts + here * per_device

    pieces = {
        (0, expert, kind): weights_of[kind] for expert in range(per_device) for kind in range(2)
    }

    last = inner - 1
    early_from = {1: range(inner // 2), last: range(inner - inner // 2, inner)} if outer == 1 else {}
    early = {}

    def parcels(*keys, first=False):
        result = []
        for shift, expert, kind in keys:
            senders = None
            if shift in early_from:
                senders = [
                    place for place in range(inner) if (place in early_from[shift]) == first
                ]
            result.append(
                Parcel(
                    weights_of[kind],
                    shift,
                    inner,
                    lambda to, expert=expert: to * per_device + expert,
                    senders=senders,
                )
            )
        return result

    def unpack(keys, arrays):
        pieces.update(zip(keys, arrays))


    in_width = 2 * channels + w_in.shape[1] - 2 * inner_width
    if outer == 1:
        flat = jnp.pad(flat, ((0, -flat.shape[0] % 32), (0, 0)))
        early_keys = [
            (shift, expert, kind)
            for expert in range(per_device)
            for kind in range(2)
            for shift in early_from
        ]
        x_group, grad_all, proj_in, joined, depth_joined, rows_joined, arrays = begin(
            tokens[0],
            out_grad[0],
            flat,
            by_depth,
            w_in,
            w_shared,
            w_out,
            w_shared_down,
            in_width,
            shared_part,
            inner,
            parcels(*early_keys, first=True),
        )
        early.update(zip(early_keys, arrays))
        x_group = x_group.reshape(group_rows, width)
    else:
        x_group = gather_rows(tokens[0], 1)[0].reshape(group_rows, width)
        grad_all = gather_rows(out_grad[0], inner)[0]
        in_columns = jnp.concatenate(
            [
                own_columns(w_in, 0, channels),
                own_columns(w_in, inner_width, channels),
                own_columns(w_shared, 0, shared_part),
                own_columns(w_shared, shared_width, shared_part),
                w_in[:, 2 * inner_width :],
            ],
            axis=1,
        )
        proj_in = lax.all_gather(in_columns, "shard", tiled=True)
        joined = lax.all_gather(flat, "shard")
        depth_joined = lax.all_gather(by_depth, "shard")
        rows_joined = lax.all_gather(rows_to_send([w_out, w_shared_down], part), "shard")
    taps = conv_w.shape[1]
    conv_rows = joined[:, :taps, : conv_w.shape[0]].transpose(1, 0, 2).reshape(taps, -1)
    conv_bias, gain_gate, gain_in, gain_moe, step_bias, decay_log, skip_gain = (
        joined[:, taps + order, : vector.shape[0]].reshape(-1)
        for order, vector in enumerate(vectors)
    )
    depth_joined = depth_joined.reshape(width, LANES)
    lane = jnp.arange(LANES)[None]
    router_wide = jnp.where(lane < expert_total, depth_joined, 0)
    dt_columns = jnp.where(lane < heads, jnp.roll(depth_joined, -expert_total, axis=1), 0)
    grad_all = grad_all.reshape(blocks, tok_rows, width)

    gain_row = to_full(gain_in)[None]
    hidden_in, gate_in, rows_in = project(
        x_group, gain_row, proj_in, dt_columns, channels, in_width
    )
    conv_all = jnp.concatenate([conv_rows, conv_bias[None]], axis=0)
    conv_table = to_full(
        jnp.pad(
            jnp.concatenate([own_columns(conv_all, 0, channels), conv_all[:, inner_width:]], axis=1),
            ((0, 3), (0, 0)),
        )
    )
    head_table = jnp.pad(
        jnp.stack(
            [
                to_full(own_rows(step_bias, heads)),
                -jnp.exp(to_full(own_rows(decay_log, heads))),
                to_full(own_rows(skip_gain, heads)),
            ]
        ),
        ((0, 5), (0, LANES - heads)),
    )
    keys = [(2, 0, DOWN), (1, 0, DOWN), (last, 0, DOWN)]
    y, seq_rows, states, (taken, *arrays) = scan_forward(
        lengths[0],
        deal_order,
        rows_in,
        conv_table,
        head_table,
        channels,
        [PlaneSwap(rows_by_owner(rows_joined))] + parcels(*keys),
    )
    unpack(keys, arrays)
    if outer > 1:
        out_rows, down_rows = rows_of_owner(taken, [w_out, w_shared_down])
        taken = jnp.concatenate(
            [
                out_rows.reshape(seq_devices, -1, width),
                down_rows.reshape(seq_devices, -1, width),
            ],
            axis=1,
        )
    own_weights = taken
    gate_gain = to_full(own_rows(gain_gate, channels))[None]
    keys = [(2, 1, DOWN), (1, 1, DOWN), (last, 1, DOWN)]
    mixed, arrays = mix_out(
        y, gate_in, gate_gain, own_weights, seq_devices, parcels(*keys)
    )
    unpack(keys, arrays)

    moe_row = to_full(gain_moe)[None]
    route_ids = jnp.pad(routes[0], ((0, 0), (0, LANES - top_count)))
    after_mix, moe_wide, gates = token_forward(
        mixed, tokens[0], moe_row, router_wide, route_ids, inner_width, top_count
    )
    keys = [(2, 0, UP), (1, 0, UP), (last, 0, UP)]
    moe_all, arrays = gather_rows(moe_wide, inner, parcels(*keys))
    unpack(keys, arrays)
    moe_all = moe_all.reshape(blocks, tok_rows, width + LANES)
    capacity = min(tok_rows, max(2, tok_rows * top_count * 5 // (expert_total * 3)))
    slots = -(-capacity // 16) * 16
    late_keys = [(1, 1, UP)] if outer == 1 else []
    keys = [key for key in [(2, 1, UP), (1, 1, UP)] if key not in late_keys]
    expert_rows, grad_rows, picks, arrays = dispatch(
        moe_all, grad_all, per_device, top_count, slots, own_first, parcels(*keys)
    )
    unpack(keys, arrays)
    keys = [(last, 1, UP)]
    shared_res, shared_back, shared_up_grad, shared_down_grad, arrays = shared_expert(
        moe_all,
        grad_all,
        proj_in,
        2 * channels,
        own_weights,
        shared_part,
        seq_devices,
        inner,
        parcels(*keys),
    )
    unpack(keys, arrays)
    order = [
        (shift, expert, kind)
        for shift in range(inner)
        for expert in range(per_device)
        for kind in range(2)
    ]
    if outer == 1:
        early_keys = [(1, 0, UP), (last, 0, DOWN)]
        expert_res, expert_back, grads, sent = experts(
            expert_rows,
            grad_rows,
            [early[key] if key in early else pieces[key] for key in order],
            hidden,
            top_count,
            own_first,
            inner,
            [
                (
                    order.index(key),
                    parcels(key)[0] if key in late_keys else pieces[key],
                    [(place_of + key[0]) % inner for place_of in early_from[key[0]]],
                )
                for key in order
                if key in early
            ],
            [(order.index(key), inner - key[0]) for key in early_keys],
        )
    else:
        for expert in range(per_device):
            for kind in range(2):
                pieces[0, expert, kind] = lax.dynamic_index_in_dim(
                    weights_of[kind], place * per_device + expert, 0, keepdims=False
                )
        early_keys, sent = [], []
        held = [
            stacked_pieces([pieces[shift, expert, kind] for shift in range(inner)], place, inner)
            for expert in range(per_device)
            for kind in range(2)
        ]
        expert_res, expert_back, grads, _ = experts(
            expert_rows, grad_rows, held, hidden, top_count, own_first, inner
        )
        grads = [
            split_piece(grads[expert * 2 + kind], shift, place, inner)
            for shift, expert, kind in order
        ]
    grads = dict(zip(order, grads))
    returned = {key: grads[key] for key in order if key[0] == 0}
    returned.update(zip(early_keys, sent))

    def back_parcels(*keys):
        keys = [key for key in keys if key not in early_keys]
        return [Parcel(grads[key], inner - key[0], inner) for key in keys]

    def unpack_back(keys, arrays):
        keys = [key for key in keys if key not in early_keys]
        returned.update(zip(keys, arrays))

    keys = [(1, 0, UP), (last, 0, DOWN), (last, 0, UP), (1, 0, DOWN)]
    out_part, back_part, arrays = combine(
        picks, expert_res, expert_back, shared_res, shared_back, inner, back_parcels(*keys)
    )
    unpack_back(keys, arrays)
    keys = [(last, 1, UP), (2, 0, UP)]
    back, arrays = reduce_rows(
        back_part.reshape(inner, seq_devices, tok_rows, -1), back_parcels(*keys)
    )
    unpack_back(keys, arrays)
    mix_grad, mix_wide, router_grad, gain_moe_grad = token_back(
        back,
        mixed,
        after_mix,
        moe_wide,
        gates,
        out_grad[0],
        moe_row,
        router_wide,
        route_ids,
        inner_width,
        top_count,
    )

    keys = [(2, 0, DOWN), (last, 1, DOWN)]
    mix_group, arrays = gather_rows(mix_wide, 1, back_parcels(*keys))
    unpack_back(keys, arrays)
    keys = []
    dy, gate_in_grad, proj_out_grad, gain_gate_grad = mix_back(
        mix_group[0], y, gate_in, gate_gain, own_weights
    )
    keys = [(2, 1, UP), (1, 1, UP)]
    rows_grad, conv_grad, head_grad, out_sum, arrays = scan_backward(
        lengths[0],
        deal_order,
        seq_rows,
        states,
        dy,
        conv_table,
        head_table,
        out_part.reshape(inner, seq_devices, tok_rows, -1),
        back_parcels(*keys),
    )
    unpack_back(keys, arrays)
    layer_out = to_low(after_mix + out_sum)
    keys = [(1, 1, DOWN)] if outer == 1 else [(1, 1, DOWN), (2, 1, DOWN)]
    swap = [PlaneSwap(rows_from_owner([proj_out_grad, shared_down_grad]))]
    shared_parts = shared_up_grad.reshape(shard_devices, depth_rows, -1)
    if outer == 1:
        swap += [
            Parcel(shared_parts, shift, inner, lambda to: to) for shift in range(1, inner)
        ]
    hidden_part, main_grad, rest_grad, (taken, *arrays) = project_back(
        gate_in_grad, rows_grad, hidden_in, proj_in, dt_columns, seq_devices, swap + back_parcels(*keys)
    )
    shared_came, arrays = arrays[: len(swap) - 1], arrays[len(swap) - 1 :]
    unpack_back(keys, arrays)
    def spread(values, length, axis=0):
        shape = values.shape[:axis] + (length,) + values.shape[axis + 1 :]
        return lax.dynamic_update_slice_in_dim(
            jnp.zeros(shape, values.dtype), values, part * values.shape[axis], axis
        )

    state_columns = rest_grad.shape[1] - LANES
    if outer == 1:
        small = pack(
            rest_grad,
            router_grad,
            conv_grad,
            head_grad,
            gain_gate_grad,
            gain_moe_grad,
            inner,
            seq_devices,
            inner_width,
            expert_total,
            heads,
        )
        keys = [(2, 1, DOWN)]
        tokens_grad, main_all, rows_all, small_all, shared_all, arrays = settle(
            hidden_part[None],
            small,
            tokens[0],
            mix_grad,
            gain_row,
            to_low(
                sum(
                    map(to_full, shared_came),
                    to_full(lax.dynamic_index_in_dim(shared_parts, place, 0, keepdims=False)),
                )
            ),
            [
                main_grad.reshape(inner, depth_rows, -1),
                taken.reshape(inner, -1, width),
            ],
            inner,
            back_parcels(*keys),
        )
        unpack_back(keys, arrays)
        w_in_grad, w_shared_grad, w_out_grad, w_shared_down_grad = assemble(
            main_all,
            shared_all,
            small_all,
            rows_all,
            w_in.shape[1],
            2 * shared_width,
            w_out.shape[0],
            w_shared_down.shape[0],
            max(1, seq_devices // shard_devices),
        )
        depth_each = small_all.shape[1] - ROWS_AFTER
        depth_sum = to_full(small_all[:, :depth_each].reshape(depth_rows, -1))
        after = to_full(small_all[:, depth_each:])
        conv_w_grad = after[:4].reshape(4, -1)[:, : conv_w.shape[0]].T
        conv_b_grad = after[4].reshape(-1)[: conv_b.shape[0]]
        norm_gate_grad = after[5].reshape(-1)[: norm_gate.shape[0]]
        here = shard * dt_bias.shape[0]
        of_heads = lax.dynamic_slice_in_dim(after[6, :3], here, dt_bias.shape[0], 1)
        dt_bias_grad, a_log_grad, d_skip_grad = of_heads[0], of_heads[1], of_heads[2]
        norm_moe_grad = after[7, 0, :depth_rows]
        last_lane = rest_grad.shape[1] - 1
    else:
        conv_rows_grad = conv_grad[:5].T
        conv_full = jnp.concatenate(
            [spread(conv_rows_grad[:channels], inner_width), conv_rows_grad[channels:]], axis=0
        )
        by_depth = [
            rest_grad[:, :state_columns],
            router_grad[:, :expert_total],
            spread(rest_grad[:, state_columns : state_columns + heads], head_total, 1),
            rest_grad[:, -1:],
            to_low(gain_moe_grad[0])[:, None],
        ]
        by_shard = [
            conv_full[:, :4],
            conv_full[:, 4],
            spread(head_grad[0, :heads], head_total),
            spread(head_grad[1, :heads], head_total),
            spread(head_grad[2, :heads], head_total),
            spread(gain_gate_grad[0], inner_width),
        ]
        shapes = [(piece.shape[0] // shard_devices,) + piece.shape[1:] for piece in by_shard]
        by_shard = jnp.concatenate(
            [to_low(piece).reshape(shard_devices, -1) for piece in by_shard], axis=1
        )
        extents = [piece.shape[1] for piece in by_depth]
        used = sum(extents)
        hidden_grad = reduce_rows(hidden_part[None])[0]
        residual = to_full(tokens[0])
        own_scale = norm_scale(residual)
        own_unit = residual * own_scale
        scaled = hidden_grad * gain_row
        tokens_grad = to_low(
            mix_grad
            + own_scale
            * (scaled - own_unit * jnp.mean(scaled * own_unit, axis=1, keepdims=True))
        )
        by_depth = jnp.concatenate(by_depth, axis=1).reshape(shard_devices, -1)
        packed = jnp.concatenate([by_depth, by_shard], axis=1)
        summed = lax.psum(lax.psum_scatter(packed, "shard", tiled=True), "seq").reshape(-1)
        count = depth_rows * used
        depth_sum = to_full(summed[:count]).reshape(depth_rows, used)
        shard_sum = summed[count:]

        def from_line(part, rows):
            own = lax.psum_scatter(part.reshape(shard_devices, rows, -1), "shard")
            return lax.all_gather(own, "seq")

        def columns_of(joined, extent):
            joined = joined.reshape(seq_devices, depth_rows, 2, extent).transpose(1, 2, 0, 3)
            return to_full(joined.reshape(depth_rows, -1))

        w_in_main = columns_of(from_line(main_grad, depth_rows), channels)
        w_in_grad = jnp.concatenate([w_in_main, depth_sum[:, :state_columns]], axis=1)
        w_shared_grad = columns_of(from_line(shared_up_grad, depth_rows), shared_part)
        rows_each = taken.shape[0] * taken.shape[1] // shard_devices
        w_out_grad, w_shared_down_grad = rows_of_shard(
            from_line(taken, rows_each), [w_out, w_shared_down]
        )
        results, start = [], 0
        for shape in shapes:
            size = 1
            for extent in shape:
                size *= extent
            results.append(to_full(shard_sum[start : start + size]).reshape(shape))
            start += size
        conv_w_grad, conv_b_grad, dt_bias_grad, a_log_grad, d_skip_grad, norm_gate_grad = results
        norm_moe_grad = depth_sum[:, used - 1]
        last_lane = used - 2
    experts_grad, experts_down_grad = collect(
        place[None], [returned[key] for key in order], per_device
    )
    start = state_columns
    w_router_grad = depth_sum[:, start : start + expert_total]
    start += expert_total
    w_dt_grad = depth_sum[:, start : start + head_total]
    norm_in_grad = depth_sum[:, last_lane] / to_full(norm_in)
    return (
        layer_out[None],
        tokens_grad[None],
        norm_in_grad,
        w_in_grad,
        w_dt_grad,
        conv_w_grad,
        conv_b_grad,
        dt_bias_grad,
        a_log_grad,
        d_skip_grad,
        norm_gate_grad,
        w_out_grad,
        norm_moe_grad,
        w_router_grad,
        w_shared_grad,
        w_shared_down_grad,
        experts_grad,
        experts_down_grad,
    )


def solution(mesh):
    placed = (
        P("shard", "seq", None),
        P("shard", "seq", None),
        P("shard", None),
        P("shard", None),
        P("shard", "seq", None),
        P("shard"),
        P("shard", None),
        P("shard", None),
        P("shard", None),
        P("shard"),
        P("shard"),
        P("shard"),
        P("shard"),
        P("shard"),
        P("shard", None),
        P("shard"),
        P("shard", None),
        P("shard", None),
        P("shard", None),
        P("seq", "shard", None),
        P("seq", "shard", None),
    )
    return jax.shard_map(
        local,
        mesh=mesh,
        in_specs=placed,
        out_specs=(
            P("shard", "seq", None),
            P("shard", "seq", None),
            P("shard"),
            P("shard", None),
            P("shard", None),
            P("shard", None),
            P("shard"),
            P("shard"),
            P("shard"),
            P("shard"),
            P("shard"),
            P("shard", None),
            P("shard"),
            P("shard", None),
            P("shard", None),
            P("shard", None),
            P("seq", "shard", None),
            P("seq", "shard", None),
        ),
        check_vma=False,
    )
```
